32 devices in a mesh: section: 2 (over core), expert: 4 (over y, x), shard: 4 (over z).
Axes of the slice: x: 2, y: 2, z: 4, core: 2. Of those that a mesh axis runs over, the one named last changes fastest.
Arguments:
- x_in: bfloat16 [2, 16, 256, 768], P(None, ('expert', 'shard')), may hold values from -6 to 6
- cotangent: float32 [2, 16, 256, 768], P(None, ('expert', 'shard')), may hold values from -6 to 6
- gate_prev: bfloat16 [2, 16, 256, 8], P(None, ('expert', 'shard')), may hold values from -4 to 4
- segments: int32 [2, 16, 256], P(None, ('expert', 'shard')), may hold values from 0 to 3, never falling along the last dimension, each value on 1 to 128 neighbouring positions
- routes: int32 [2, 2, 16, 256, 2], P('section', None, ('expert', 'shard')), may hold values from 0 to 7, all different within a row
- priority: int32 [2, 2, 16, 256], P('section', None, ('expert', 'shard')), may hold values from 0 to 255, each once within a row
- attn_qkv: bfloat16 [2, 768, 2304], P('section', ('expert', 'shard')), may hold values from -0.21875 to 0.21875
- attn_out: bfloat16 [2, 768, 768], P('section', ('expert', 'shard')), may hold values from -0.875 to 0.875
- router: bfloat16 [2, 768, 8], P('section', ('expert', 'shard')), may hold values from -0.15625 to 0.15625
- const_proj: bfloat16 [2, 768, 4], P('section', ('expert', 'shard')), may hold values from -0.21875 to 0.21875
- const_vec: bfloat16 [2, 768, 2], P('section', ('expert', 'shard')), may hold values from -5 to 5
- gains: bfloat16 [2, 768, 2], P('section', ('expert', 'shard')), may hold values from 0.5 to 1.5
- gate_mix: float32 [2, 8, 8], P('section'), may hold values from -2 to 2
- expert_in: bfloat16 [2, 4, 768, 4096], P('section', 'expert', 'shard'), may hold values from -0.21875 to 0.21875
- expert_out: bfloat16 [2, 4, 2048, 768], P('section', 'expert', 'shard'), may hold values from -0.25 to 0.25
Outputs:
- section_out: bfloat16 [2, 2, 16, 256, 768], P('section', None, ('expert', 'shard'))
- section_grad: float32 [2, 2, 16, 256, 768], P('section', None, ('expert', 'shard'))
- gate_grad: float32 [2, 2, 16, 256, 8], P('section', None, ('expert', 'shard'))
- attn_qkv_grad: float32 [2, 768, 2304], P('section', ('expert', 'shard'))
- attn_out_grad: float32 [2, 768, 768], P('section', ('expert', 'shard'))
- router_grad: float32 [2, 768, 8], P('section', ('expert', 'shard'))
- const_proj_grad: float32 [2, 768, 4], P('section', ('expert', 'shard'))
- const_vec_grad: float32 [2, 768, 2], P('section', ('expert', 'shard'))
- gains_grad: float32 [2, 768, 2], P('section', ('expert', 'shard'))
- gate_mix_grad: float32 [2, 8, 8], P('section')
- expert_in_grad: float32 [2, 4, 768, 4096], P('section', 'expert', 'shard')
- expert_out_grad: float32 [2, 4, 2048, 768], P('section', 'expert', 'shard')
The draws below stay inside these ranges and needn't reach their ends.
Inputs may be any that keep to these rules, and one draw needn't show every extreme that they name: `routes`: the 2 experts of a token differ; indices below 4 are feed-forward experts, then the zero, the copy and the 2 constant experts. `priority`: each sequence's tokens hold each number once. `segments`: segment numbers never fall along a sequence.
All inputs are finite; a program needn't handle non-finite values.
Results may differ from the reference program's by a relative error of at most 0.024.
Values may be sent and summed in bfloat16 or wider, within the bound.
A program may use at most 256 MiB of HBM per device.

```python
import math
import jax
import jax.numpy as jnp
import numpy as np
from jax import lax

D = 768
HEADS = 12
HEAD = 64
HID = 2048
NCONST = 2
TOP = 2
MICRO = 2
DOCS = 4
SEQ = 256
NFFN = 4
NEXP = 8
SEQS = 16
CAP = 80


def shard_levels(own_key, shape, split, smallest, largest):
    loudness, own = 1.0, jax.random.fold_in(own_key, 6)
    for dim, blocks in split:
        draws = jnp.exp(jax.random.uniform(jax.random.fold_in(own, dim), (blocks,), jnp.float32, smallest / len(split), largest / len(split)))
        loudness = loudness * jnp.repeat(draws, shape[dim] // blocks).reshape([-1 if axis == dim else 1 for axis in range(len(shape))])
    return loudness


def different_ones(own_key, rows, number_of, top, lift):
    ranking = jax.random.permutation(jax.random.fold_in(own_key, 1), number_of)
    favour = ranking
    for power in range(3):
        favour = favour * favour // number_of
    favour = favour * lift // number_of
    lots = jax.random.randint(jax.random.fold_in(own_key, 2), (rows, number_of), 0, 4096) + favour
    sure = jax.random.permutation(jax.random.fold_in(own_key, 3), rows)[jnp.arange(number_of) % rows]
    lots = jnp.where(jnp.arange(rows)[:, None] == sure[None, :], 1 << 14, lots)
    merit = lots * number_of + jnp.arange(number_of)
    return lax.top_k(merit.astype(jnp.int32), top)[1].astype(jnp.int32)


def length_profile(amount, total, most, slope):
    portions = [(1 << 20) // math.isqrt(rank ** slope) + 1 for rank in range(2, amount + 1)]
    spare, counts = total - most - (amount - 1), [1] * (amount - 1)
    while spare > 0:
        movable = [i for i in range(amount - 1) if counts[i] < most]
        mass, remaining = sum([portions[i] for i in movable]), spare
        for i in movable:
            more = min(most - counts[i], max(1, remaining * portions[i] // mass), spare)
            counts[i] = counts[i] + more
            spare = spare - more
    return np.array([most] + counts)


def uneven_parts(own_key, number_of, total, limit, slope):
    if number_of == 2:
        one = jax.random.randint(own_key, (), max(1, total - limit), min(limit, total - 1) + 1)
        return jnp.stack([one, total - one])
    lengths = jnp.asarray(length_profile(number_of, total, limit, slope), jnp.int32)
    couples = (number_of - 1) // 2
    source_of, receiver = lengths[1:1 + 2 * couples:2], lengths[2:2 + 2 * couples:2]
    margin = jnp.minimum(source_of - 1, limit - receiver)
    shifted = jax.random.randint(jax.random.fold_in(own_key, 1), (couples,), 0, 1 << 20) % (margin + 1)
    lengths = lengths.at[1:1 + 2 * couples:2].set(source_of - shifted).at[2:2 + 2 * couples:2].set(receiver + shifted)
    return lengths[jax.random.permutation(jax.random.fold_in(own_key, 2), number_of)]


def normal_values(own_key, extent, spread, reach, split=(), kind=jnp.bfloat16):
    level = shard_levels(own_key, extent, split, -0.22, 0.18) if split else 1.0
    entries = jax.random.normal(own_key, extent, jnp.float32) * spread * level
    return jnp.minimum(jnp.maximum(entries, -reach), reach).astype(kind)


def setup_inputs(seed: int = 0) -> dict:
    streams_of = jax.random.split(jax.random.key(seed), 16)
    return {
        "x_in": normal_values(streams_of[0], (MICRO, SEQS, SEQ, D), 1.0, 6.0, ((1, 16),)),
        "cotangent": normal_values(streams_of[1], (MICRO, SEQS, SEQ, D), 1.0, 6.0, ((1, 16),), jnp.float32),
        "gate_prev": normal_values(streams_of[2], (MICRO, SEQS, SEQ, NEXP), 0.5, 4.0, ((1, 16),)),
        "segments": jax.vmap(lambda own: jnp.searchsorted(jnp.cumsum(uneven_parts(own, DOCS, SEQ, SEQ // 2, 1)), jnp.arange(SEQ), side="right"))(jax.random.split(streams_of[3], MICRO * SEQS)).reshape((MICRO, SEQS, SEQ)).astype(jnp.int32),
        "routes": different_ones(streams_of[4], 2 * MICRO * SEQS * SEQ, NEXP, TOP, 2048).reshape((2, MICRO, SEQS, SEQ, TOP)),
        "priority": jax.vmap(lambda own: jax.random.permutation(own, SEQ))(jax.random.split(streams_of[5], 2 * MICRO * SEQS)).reshape((2, MICRO, SEQS, SEQ)).astype(jnp.int32),
        "attn_qkv": normal_values(streams_of[6], (2, D, 3 * D), D ** -0.5, 0.21875, ((0, 2), (1, 16))),
        "attn_out": normal_values(streams_of[7], (2, D, D), (D // 16) ** -0.5, 0.875, ((0, 2), (1, 16))),
        "router": normal_values(streams_of[8], (2, D, NEXP), (2 * D) ** -0.5, 0.15625, ((0, 2), (1, 16))),
        "const_proj": normal_values(streams_of[9], (2, D, 2 * NCONST), D ** -0.5, 0.21875, ((0, 2), (1, 16))),
        "const_vec": normal_values(streams_of[10], (2, D, NCONST), 1.0, 5.0, ((0, 2), (1, 16))),
        "gains": jnp.clip(1.0 + 0.1 * jax.random.normal(streams_of[11], (2, D, 2), jnp.float32), 0.5, 1.5).astype(jnp.bfloat16),
        "gate_mix": normal_values(streams_of[12], (2, NEXP, NEXP), NEXP ** -0.5, 2.0, ((0, 2),), jnp.float32),
        "expert_in": normal_values(streams_of[13], (2, NFFN, D, 2 * HID), D ** -0.5, 0.21875, ((0, 2), (1, 4), (2, 4))),
        "expert_out": normal_values(streams_of[14], (2, NFFN, HID, D), (HID // 4) ** -0.5, 0.25, ((0, 2), (1, 4), (2, 4))),
    }


HIGH_PRECISION = lax.Precision.HIGHEST
norm_eps = 1e-06

@jax.custom_vjp
def low(v):
    return lax.optimization_barrier(v.astype(jnp.bfloat16)).astype(jnp.float32)

@jax.custom_vjp
def low_back(v):
    return v

def low_keep(v):
    return (low(v), None)

def low_pass(kept, grad):
    return (grad,)

def back_keep(v):
    return (v, None)

def back_low(kept, grad):
    return (low(grad),)
low.defvjp(low_keep, low_pass)
low_back.defvjp(back_keep, back_low)

def matmul(left, right):
    return jnp.dot(left, right, precision=HIGH_PRECISION)

def rms(values):
    return values * lax.rsqrt(lax.optimization_barrier(jnp.mean(values * values, axis=-1, keepdims=True)) + norm_eps)

def rotate(values, cosine, sine):
    half_head = values.shape[-1] // 2
    first = values[..., :half_head]
    second = values[..., half_head:]
    return jnp.concatenate([first * cosine - second * sine, first * sine + second * cosine], axis=-1)

def layer(params, x_here, r_here, seg, route_ids, prio):
    w_qkv, w_attn, w_router, w_const, const_values, gain_pair, mix_matrix, w_in, w_out = params
    place = jnp.arange(SEQ, dtype=jnp.int32)
    allowed = (seg[:, None] == seg[None, :]) & (place[None, :] <= place[:, None])
    positions = lax.optimization_barrier(jnp.sum(allowed.astype(jnp.float32), axis=1)) - 1.0
    rates = jnp.exp(jnp.arange(HEAD // 2, dtype=jnp.float32) * (-2.0 * math.log(10000.0) / HEAD))
    angles = positions[:, None] * rates[None, :]
    cosine = jnp.cos(angles)[:, None, :]
    sine = jnp.sin(angles)[:, None, :]
    first_b = low(rms(x_here) * gain_pair[:, 0])
    projected = low_back(matmul(first_b, w_qkv))
    queries = low(rotate(projected[:, :D].reshape(SEQ, HEADS, HEAD), cosine, sine))
    keys_rot = low(rotate(projected[:, D:2 * D].reshape(SEQ, HEADS, HEAD), cosine, sine))
    values_b = low(projected[:, 2 * D:].reshape(SEQ, HEADS, HEAD))
    scores = low_back(jnp.einsum('qhd,khd->hqk', queries, keys_rot, precision=HIGH_PRECISION) * HEAD ** (-0.5))
    scores = jnp.where(allowed[None], scores, -1e+30)
    probs_att = low(jax.nn.softmax(scores, axis=-1))
    attended = jnp.einsum('hqk,khd->qhd', probs_att, values_b, precision=HIGH_PRECISION).reshape(SEQ, D)
    attended = low(low_back(attended))
    after_attn = x_here + low_back(matmul(attended, w_attn))
    second = rms(after_attn) * gain_pair[:, 1]
    second_b = low(second)
    logits = matmul(second_b, w_router) + matmul(r_here, mix_matrix)
    probs = jax.nn.softmax(logits, axis=-1)
    choose = (route_ids[:, :, None] == jnp.arange(NEXP, dtype=jnp.int32)[None, None, :]).astype(jnp.float32)
    gate_values = jnp.einsum('ske,se->sk', choose, probs, precision=HIGH_PRECISION)
    routed = lax.optimization_barrier(jnp.sum(choose[:, :, :NFFN], axis=1))
    before = (prio[None, :] < prio[:, None]).astype(jnp.float32)
    rank = matmul(before, routed)
    rank_k = lax.optimization_barrier(jnp.sum(choose[:, :, :NFFN] * rank[:, None, :], axis=-1))
    slot = route_ids.astype(jnp.float32) * CAP + rank_k
    keep = (route_ids < NFFN) & (rank_k < CAP)
    columns = jnp.arange(NFFN * CAP, dtype=jnp.float32)
    table = (keep[:, :, None] & (slot[:, :, None] == columns[None, None, :])).astype(jnp.float32)
    dispatch = table[:, 0] + table[:, 1]
    buffer = low_back(matmul(dispatch.T, second_b)).reshape(NFFN, CAP, D)
    gate_up = low_back(jnp.einsum('ecd,edf->ecf', buffer, w_in, precision=HIGH_PRECISION))
    hidden = low(jax.nn.silu(gate_up[..., :HID]) * gate_up[..., HID:])
    made = jnp.einsum('ech,ehd->ecd', hidden, w_out, precision=HIGH_PRECISION).reshape(NFFN * CAP, D)
    made = low_back(low(made))
    mixture = jnp.zeros((SEQ, D), jnp.float32)
    for pick in range(TOP):
        picked = low_back(matmul(table[:, pick], made))
        mixture = mixture + gate_values[:, pick:pick + 1] * picked
    extra = jnp.einsum('sk,ske->se', gate_values, choose[:, :, NFFN:], precision=HIGH_PRECISION)
    const_mix = jax.nn.softmax(matmul(second_b, w_const).reshape(SEQ, NCONST, 2), axis=-1)
    mixture = mixture + extra[:, 1:2] * second
    for const_index in range(NCONST):
        term = const_mix[:, const_index, 0:1] * second + const_mix[:, const_index, 1:2] * const_values[:, const_index][None, :]
        mixture = mixture + extra[:, 2 + const_index:3 + const_index] * term
    return (after_attn + mixture, logits)

def reference(x_in, cotangent, gate_prev, segments, routes, priority, attn_qkv, attn_out, router, const_proj, const_vec, gains, gate_mix, expert_in, expert_out):
    weights = (attn_qkv, attn_out, router, const_proj, const_vec, gains, gate_mix, expert_in, expert_out)
    params = [tuple((w[s].astype(jnp.float32) for w in weights)) for s in range(2)]
    blocks = MICRO * SEQS
    items = (x_in.reshape(blocks, SEQ, D).astype(jnp.float32), cotangent.reshape(blocks, SEQ, D).astype(jnp.float32), gate_prev.reshape(blocks, SEQ, NEXP).astype(jnp.float32), segments.reshape(blocks, SEQ), jnp.moveaxis(routes.reshape(2, blocks, SEQ, TOP), 0, 1), jnp.moveaxis(priority.reshape(2, blocks, SEQ), 0, 1))

    def one_block(totals, item):
        x_blk, cot_blk, prev_blk, seg_blk, routes_blk, prio_blk = item

        def first_section(p, xx, rr):
            return layer(p, xx, rr, seg_blk, routes_blk[0], prio_blk[0])

        def second_section(p, xx, rr):
            return layer(p, xx, rr, seg_blk, routes_blk[1], prio_blk[1])
        (out_first, log_first), back_first = jax.vjp(first_section, params[0], x_blk, prev_blk)
        sent_x = low(out_first)
        sent_log = low(log_first)
        (out_second, log_second), back_second = jax.vjp(second_section, params[1], sent_x, sent_log)
        grad_p1, grad_x1, grad_r1 = back_second((cot_blk, jnp.zeros_like(log_second)))
        grad_p0, grad_x0, grad_r0 = back_first((low(grad_x1), low(grad_r1)))
        totals = (jax.tree.map(jnp.add, totals[0], grad_p0), jax.tree.map(jnp.add, totals[1], grad_p1))
        outs = (jnp.stack([out_first, out_second]).astype(jnp.bfloat16), jnp.stack([grad_x0, grad_x1]), jnp.stack([grad_r0, grad_r1]))
        return (totals, outs)
    start = (jax.tree.map(jnp.zeros_like, params[0]), jax.tree.map(jnp.zeros_like, params[1]))
    totals, outs = lax.scan(one_block, start, items)
    section_out = jnp.moveaxis(outs[0], 1, 0).reshape(2, MICRO, SEQS, SEQ, D)
    section_grad = jnp.moveaxis(outs[1], 1, 0).reshape(2, MICRO, SEQS, SEQ, D)
    gate_grad = jnp.moveaxis(outs[2], 1, 0).reshape(2, MICRO, SEQS, SEQ, NEXP)
    grads = [jnp.stack([totals[0][i], totals[1][i]]) for i in range(9)]
    return (section_out, section_grad, gate_grad, grads[0], grads[1], grads[2], grads[3], grads[4], grads[5], grads[6], grads[7], grads[8])
```

```python
import math

import jax
import jax.numpy as jnp
from jax import lax
from jax.experimental import pallas as pl
from jax.experimental.pallas import tpu as pltpu
from jax.sharding import PartitionSpec as P

HEADS = 12
HEAD = 64
TOP = 2
CHUNK = 256
LANES = 128
AT_PROJ = 16
AT_VEC = 24
AT_GAIN = 28
AT_MIX = 32

HIGH = lax.Precision.HIGHEST
norm_eps = 1e-06
masked_score = -1e30
F32 = jnp.float32
BF16 = jnp.bfloat16


def mm(a, b, contract=((1,), (0,)), precision=None):
    return lax.dot_general(a, b, (contract, ((), ())), precision=precision, preferred_element_type=F32)


NT = ((1,), (1,))
TN = ((0,), (0,))


def lane_of(rows, columns=LANES):
    return lax.broadcasted_iota(jnp.int32, (rows, columns), 1)


def inverse_norm(values):
    return lax.rsqrt(jnp.mean(values * values, axis=-1, keepdims=True) + norm_eps)


def norm_back(grad_unit, unit, inverse):
    return inverse * (grad_unit - unit * jnp.mean(grad_unit * unit, axis=-1, keepdims=True))


def roll(x, by):
    return jnp.roll(x, by, axis=1)


def turned(x, lane):
    return jnp.where(lane % HEAD < HEAD // 2, roll(x, LANES - HEAD // 2), roll(x, HEAD // 2))


def hi_lo(x):
    high = x.astype(BF16)
    return high, (x - high.astype(F32)).astype(BF16)


def attention_body(x, w_qkv, w_attn, gain_first, cosine, sine, seg_col, seg_row):
    seq_len, width = x.shape
    first_b = (x * inverse_norm(x) * gain_first).astype(BF16)
    place_q = lax.broadcasted_iota(jnp.int32, (seq_len, seq_len), 0)
    place_k = lax.broadcasted_iota(jnp.int32, (seq_len, seq_len), 1)
    allowed = (seg_col == seg_row) & (place_k <= place_q)
    lane = lane_of(seq_len)
    low_head = lane < HEAD
    parts_q, parts_k, parts_v, parts_a, parts_p = [], [], [], [], []
    for pair in range(width // LANES):
        at = pair * LANES
        q = mm(first_b, w_qkv[:, at : at + LANES])
        k = mm(first_b, w_qkv[:, width + at : width + at + LANES])
        v = mm(first_b, w_qkv[:, 2 * width + at : 2 * width + at + LANES]).astype(BF16)
        q = (q * cosine + turned(q, lane) * sine).astype(BF16)
        k = (k * cosine + turned(k, lane) * sine).astype(BF16)
        outs = []
        for keep in (low_head, ~low_head):
            scores = mm(jnp.where(keep, q, 0), k, NT) * (HEAD**-0.5)
            scores = jnp.where(allowed, scores, masked_score)
            scores = jnp.exp(scores - jnp.max(scores, axis=-1, keepdims=True))
            probs = (scores / jnp.sum(scores, axis=-1, keepdims=True)).astype(BF16)
            parts_p.append(probs)
            outs.append(mm(probs, v))
        parts_a.append(jnp.where(low_head, outs[0], outs[1]).astype(BF16))
        parts_q.append(q)
        parts_k.append(k)
        parts_v.append(v)
    attended = jnp.concatenate(parts_a, axis=1)
    qkv = jnp.concatenate(parts_q + parts_k + parts_v, axis=1)
    after = x + mm(attended, w_attn)
    return after, qkv, jnp.stack(parts_p), attended


def gating_body(after, r, small, mix, gain_second, ints, prio_row, nffn, nexp, capacity, slots):
    rows = after.shape[0]
    second = after * inverse_norm(after) * gain_second
    second_b = second.astype(BF16)
    lane = lane_of(rows)
    logits = mm(second_b, small)
    full = logits + mm(r, mix, precision=HIGH)
    inside = lane < nexp
    top = jnp.max(jnp.where(inside, full, -jnp.inf), axis=-1, keepdims=True)
    raised = jnp.where(inside, jnp.exp(jnp.where(inside, full, top) - top), 0.0)
    probs = raised / jnp.sum(raised, axis=-1, keepdims=True)
    other = jnp.where(lane % 2 == 0, roll(logits, LANES - 1), roll(logits, 1))
    bigger = jnp.maximum(logits, other)
    mine_e = jnp.exp(logits - bigger)
    mixes = mine_e / (mine_e + jnp.exp(other - bigger))
    before = (prio_row < ints[:, 2:3]).astype(BF16)
    route = (ints[:, 0:1], ints[:, 1:2])
    routed = (((lane == route[0]) | (lane == route[1])) & (lane < nffn)).astype(BF16)
    rank = mm(before, routed)
    columns = []
    dispatch = jnp.zeros((rows, slots), BF16)
    stride = slots // nffn
    for k in range(TOP):
        chosen = lane == route[k]
        gate = jnp.sum(jnp.where(chosen, probs, 0.0), axis=-1, keepdims=True)
        rank_k = jnp.sum(jnp.where(chosen, rank, 0.0), axis=-1, keepdims=True).astype(jnp.int32)
        kept = (route[k] < nffn) & (rank_k < capacity)
        slot = jnp.where(kept, route[k] * stride + rank_k, -1)
        dispatch = dispatch + (slot == lane_of(rows, slots)).astype(BF16)
        columns.append((gate, slot))
    buffer = mm(dispatch, second_b, TN).astype(BF16)
    packed = jnp.where(inside, probs, jnp.where((lane >= AT_PROJ) & (lane < AT_VEC), mixes, 0.0))
    packed = jnp.where(lane == AT_VEC, columns[0][0], packed)
    packed = jnp.where(lane == AT_VEC + 1, columns[1][0], packed)
    slot_pair = jnp.where(lane == 0, columns[0][1], columns[1][1])
    return full, packed, slot_pair, buffer


def extras(packed, ints, nffn, nconst):
    gates = (packed[:, AT_VEC : AT_VEC + 1], packed[:, AT_VEC + 1 : AT_VEC + 2])

    def of(expert):
        return sum(jnp.where(ints[:, k : k + 1] == expert, gates[k], 0.0) for k in range(TOP))

    def mixes(c):
        at = AT_PROJ + 2 * c
        return packed[:, at : at + 1], packed[:, at + 1 : at + 2]

    return gates, of(nffn + 1), [of(nffn + 2 + c) for c in range(nconst)], [mixes(c) for c in range(nconst)]


def combine_body(after, packed, slot_pair, ints, returned, gain_second, vec_rows, nffn):
    rows = after.shape[0]
    nconst = vec_rows.shape[0]
    second = after * inverse_norm(after) * gain_second
    gates, copied, const, mixes = extras(packed, ints, nffn, nconst)
    made = (returned[0].astype(F32) + returned[1].astype(F32)).astype(BF16)
    slot_lane = lane_of(rows, made.shape[0])
    picked = [mm((slot_pair[:, k : k + 1] == slot_lane).astype(BF16), made) for k in range(TOP)]
    coefficient = copied
    for c in range(nconst):
        coefficient = coefficient + const[c] * mixes[c][0]
    out = after + gates[0] * picked[0] + gates[1] * picked[1] + coefficient * second
    for c in range(nconst):
        out = out + (const[c] * mixes[c][1]) * vec_rows[c : c + 1]
    return out, [p.astype(BF16) for p in picked]


def expert_chunk(arrived, w_in):
    both = mm(arrived, w_in)
    gate, up = both[:, :CHUNK], both[:, CHUNK:]
    return gate, up, jax.nn.sigmoid(gate)


def expert_forward(arrived, w_in, w_out):
    total = 0.0
    for chunk in range(w_out.shape[0] // CHUNK):
        gate, up, sig = expert_chunk(arrived, w_in[:, 2 * CHUNK * chunk : 2 * CHUNK * (chunk + 1)])
        hidden = (gate * sig * up).astype(BF16)
        total = total + mm(hidden, w_out[CHUNK * chunk : CHUNK * (chunk + 1)])
    return total.astype(BF16)


def expert_backward(grad_made, arrived, w_in, w_out):
    total = 0.0
    grads_in, grads_out = [], []
    for chunk in range(w_out.shape[0] // CHUNK):
        piece = w_in[:, 2 * CHUNK * chunk : 2 * CHUNK * (chunk + 1)]
        gate, up, sig = expert_chunk(arrived, piece)
        hidden = (gate * sig * up).astype(BF16)
        grad_hidden = mm(grad_made, w_out[CHUNK * chunk : CHUNK * (chunk + 1)], NT)
        grads_out.append(mm(hidden, grad_made, TN).astype(BF16))
        grad_gate = grad_hidden * up * sig * (1.0 + gate * (1.0 - sig))
        grad_up = grad_hidden * gate * sig
        grad_both = jnp.concatenate([grad_gate, grad_up], axis=1).astype(BF16)
        grads_in.append(mm(arrived, grad_both, TN).astype(BF16))
        total = total + mm(grad_both, piece, NT)
    return total.astype(BF16), jnp.concatenate(grads_in, axis=1), jnp.concatenate(grads_out, axis=0)


def return_body(grad_y, packed, slot_pair, slots):
    rows = grad_y.shape[0]
    slot_lane = lane_of(rows, slots)
    total = 0.0
    for k in range(TOP):
        gate = packed[:, AT_VEC + k : AT_VEC + k + 1]
        table = (slot_pair[:, k : k + 1] == slot_lane).astype(BF16)
        total = total + mm(table, (gate * grad_y).astype(BF16), TN)
    return total.astype(BF16)


def moe_back_body(
    grad_y, grad_log_in, after, packed, slot_pair, ints, picked, returned, r, small, mix, gain_second, vec_rows, nffn, nexp
):
    rows = grad_y.shape[0]
    nconst = vec_rows.shape[0]
    lane = lane_of(rows)
    inverse = inverse_norm(after)
    unit = after * inverse
    second = unit * gain_second
    second_b = second.astype(BF16)
    gates, copied, const, mixes = extras(packed, ints, nffn, nconst)
    grad_buffer = (returned[0].astype(F32) + returned[1].astype(F32)).astype(BF16)
    slot_lane = lane_of(rows, grad_buffer.shape[0])
    dispatch = sum((slot_pair[:, k : k + 1] == slot_lane).astype(BF16) for k in range(TOP))
    grad_second = mm(dispatch, grad_buffer)
    along_second = jnp.sum(grad_y * second, axis=-1, keepdims=True)
    coefficient = copied
    grad_extra = [(nffn + 1, along_second)]
    grad_lanes = jnp.zeros((rows, LANES), F32)
    vec_grads = []
    for c in range(nconst):
        along = jnp.sum(grad_y * vec_rows[c : c + 1], axis=-1, keepdims=True)
        m0, m1 = mixes[c]
        coefficient = coefficient + const[c] * m0
        grad_extra.append((nffn + 2 + c, m0 * along_second + m1 * along))
        d0, d1 = const[c] * along_second, const[c] * along
        mean = m0 * d0 + m1 * d1
        at = AT_PROJ + 2 * c
        grad_lanes = jnp.where(lane == at, m0 * (d0 - mean), grad_lanes)
        grad_lanes = jnp.where(lane == at + 1, m1 * (d1 - mean), grad_lanes)
        vec_grads.append(jnp.sum(grad_y * (const[c] * m1), axis=0, keepdims=True))
    grad_second = grad_second + coefficient * grad_y
    grad_probs = jnp.zeros((rows, LANES), F32)
    for k in range(TOP):
        grad_gate = jnp.sum(picked[k].astype(F32) * grad_y, axis=-1, keepdims=True)
        for expert, value in grad_extra:
            grad_gate = grad_gate + jnp.where(ints[:, k : k + 1] == expert, value, 0.0)
        grad_probs = grad_probs + jnp.where(lane == ints[:, k : k + 1], grad_gate, 0.0)
    probs = jnp.where(lane < nexp, packed, 0.0)
    grad_logits = probs * (grad_probs - jnp.sum(probs * grad_probs, axis=-1, keepdims=True)) + grad_log_in
    grad_mix = mm(r, grad_logits, TN, HIGH)
    grad_r = mm(grad_logits, mix, NT, HIGH)
    high, low = hi_lo(jnp.where(lane < nexp, grad_logits, grad_lanes))
    small_rows = mm(high, second_b, TN) + mm(low, second_b, TN)
    grad_second = grad_second + mm(high, small, NT) + mm(low, small, NT)
    grad_gain = jnp.sum(grad_second * unit, axis=0, keepdims=True)
    grad_after = grad_y + norm_back(grad_second * gain_second, unit, inverse)
    row = lax.broadcasted_iota(jnp.int32, small_rows.shape, 0)
    small_rows = jnp.where(row < AT_VEC, small_rows, 0.0)
    for c in range(nconst):
        small_rows = jnp.where(row == AT_VEC + c, vec_grads[c], small_rows)
    small_rows = jnp.where(row == AT_GAIN + 1, grad_gain, small_rows)
    return grad_after, grad_r, grad_mix, small_rows


def attention_back_body(grad_after, x, qkv, probs_att, attended, small_rows, w_qkv, w_attn, gain_first, cosine, sine):
    seq_len, width = x.shape
    inverse = inverse_norm(x)
    unit = x * inverse
    first_b = (unit * gain_first).astype(BF16)
    grad_branch = grad_after.astype(BF16)
    grad_w_attn = mm(attended, grad_branch, TN).astype(BF16)
    grad_attended = mm(grad_branch, w_attn, NT).astype(BF16)
    lane = lane_of(seq_len)
    low_head = lane < HEAD
    scale = HEAD**-0.5
    parts_q, parts_k, parts_v = [], [], []
    for pair in range(width // LANES):
        at = pair * LANES
        q = qkv[:, at : at + LANES]
        k = qkv[:, width + at : width + at + LANES]
        v = qkv[:, 2 * width + at : 2 * width + at + LANES]
        g = grad_attended[:, at : at + LANES]
        dq, dk, dv = [], [], []
        for half, keep in enumerate((low_head, ~low_head)):
            probs = probs_att[2 * pair + half]
            grad_p = mm(jnp.where(keep, g, 0), v, NT)
            p = probs.astype(F32)
            grad_s = (p * (grad_p - jnp.sum(p * grad_p, axis=-1, keepdims=True))).astype(BF16)
            dv.append(mm(probs, g, TN))
            dq.append(mm(grad_s, k))
            dk.append(mm(grad_s, q, TN))
        dq = jnp.where(low_head, dq[0], dq[1]) * scale
        dk = jnp.where(low_head, dk[0], dk[1]) * scale
        parts_q.append((dq * cosine - turned(dq, lane) * sine).astype(BF16))
        parts_k.append((dk * cosine - turned(dk, lane) * sine).astype(BF16))
        parts_v.append(jnp.where(low_head, dv[0], dv[1]).astype(BF16))
    grad_qkv = jnp.concatenate(parts_q + parts_k + parts_v, axis=1)
    grad_w_qkv = mm(first_b, grad_qkv, TN).astype(BF16)
    grad_first = mm(grad_qkv, w_qkv, NT)
    grad_gain = jnp.sum(grad_first * unit, axis=0, keepdims=True)
    grad_x = grad_after + norm_back(grad_first * gain_first, unit, inverse)
    row = lax.broadcasted_iota(jnp.int32, small_rows.shape, 0)
    small_rows = jnp.where(row == AT_GAIN, grad_gain, small_rows)
    return grad_x, grad_w_qkv, grad_w_attn, small_rows.T


def local(
    x_in,
    cotangent,
    gate_prev,
    segments,
    routes,
    priority,
    attn_qkv,
    attn_out,
    router,
    const_proj,
    const_vec,
    gains,
    gate_mix,
    expert_in,
    expert_out,
):
    seq_len, width = x_in.shape[2:]
    nexp = gate_prev.shape[-1]
    owners, pieces = lax.axis_size("expert"), lax.axis_size("shard")
    nffn = owners * expert_in.shape[1]
    nconst = const_vec.shape[-1]
    capacity = (5 * TOP * seq_len + 4 * nexp - 1) // (4 * nexp)
    room = -(-capacity // 16) * 16
    slots = nffn * room
    core = lax.axis_index("section")
    first_core = core == 0

    def swap(item):
        return lax.ppermute(item, "section", [(0, 1), (1, 0)])

    def mine(stack, axis=0):
        return lax.dynamic_index_in_dim(stack, core, axis, keepdims=False)

    def others(stack, axis=0):
        return lax.dynamic_index_in_dim(stack, 1 - core, axis, keepdims=False)

    def by_section(own, other):
        return jnp.where(first_core, own, other), jnp.where(first_core, other, own)

    in_rows, columns = expert_in.shape[2:]
    hidden_here = expert_out.shape[2] // 2
    chunks = pieces * hidden_here // CHUNK
    w_in = expert_in[0, 0].reshape(in_rows, 2, pieces, 2, hidden_here)

    def as_chunks(half):
        half = half.reshape(in_rows, 2, chunks, CHUNK)
        return jnp.swapaxes(half, 1, 2).reshape(in_rows, columns // 2)

    w_out = expert_out[0, 0].reshape(2, hidden_here, width)
    ins = by_section(as_chunks(mine(w_in, 3)), swap(as_chunks(others(w_in, 3))))
    outs = by_section(mine(w_out), swap(others(w_out)))
    experts = [
        (
            lax.all_gather(ins[s], "shard", axis=0, tiled=True),
            lax.all_gather(outs[s], "shard", axis=0, tiled=True),
        )
        for s in range(2)
    ]
    rows = attn_qkv.shape[1]

    def lanes(array, upto):
        return jnp.pad(array, ((0, 0), (0, upto - array.shape[1])))

    small = jnp.concatenate(
        [
            lanes(router[0], AT_PROJ),
            lanes(const_proj[0], AT_VEC - AT_PROJ),
            lanes(const_vec[0], AT_GAIN - AT_VEC),
            lanes(gains[0], LANES - AT_GAIN),
        ],
        axis=1,
    )
    shared = jnp.concatenate([attn_qkv[0], attn_out[0], small], axis=1)
    shared = lax.all_gather(shared, ("expert", "shard"), axis=0, tiled=True)
    shared = by_section(shared, swap(shared))
    mix_own = jnp.pad(gate_mix[0], ((0, LANES - nexp), (0, LANES - nexp)))
    mix_all = by_section(mix_own, swap(mix_own))
    ints_own = jnp.concatenate([routes[0, :, 0], priority[0, :, 0, :, None]], axis=-1)
    ints_all = by_section(mine(ints_own), swap(others(ints_own)))
    x_first = mine(x_in[:, 0]).astype(F32)
    r_first = jnp.pad(mine(gate_prev[:, 0]).astype(F32), ((0, 0), (0, LANES - nexp)))
    upstream = mine(cotangent[:, 0])
    seg = mine(segments[:, 0])
    place = lax.iota(jnp.int32, seq_len)
    start = jnp.sum((seg[None, :] < seg[:, None]).astype(F32), axis=1)
    angles = (place.astype(F32) - start)[:, None] * jnp.exp(
        lax.iota(F32, HEAD // 2) * (-2.0 * math.log(10000.0) / HEAD)
    )[None, :]
    cosine, sine = jnp.cos(angles), jnp.sin(angles)
    cosine = jnp.concatenate([cosine] * 4, axis=1)
    sine = jnp.concatenate([-sine, sine, -sine, sine], axis=1)

    def to_owners(blocks):
        blocks = lax.all_to_all(
            blocks.reshape(owners, room, width), "expert", split_axis=0, concat_axis=0, tiled=True
        ).reshape(slots, width)
        return jnp.concatenate(by_section(blocks, swap(blocks)), axis=0)

    def to_tokens(blocks):
        blocks = blocks.reshape(2, slots, width)

        def back(part):
            return lax.all_to_all(
                part.reshape(owners, room, width), "expert", split_axis=0, concat_axis=0, tiled=True
            ).reshape(slots, width)

        return back(mine(blocks)), back(swap(others(blocks)))

    kept = []
    x, r = x_first, r_first
    results = []
    for s in range(2):
        packed_w = shared[s]
        w_qkv = packed_w[:, : 3 * width]
        w_attn = packed_w[:, 3 * width : 4 * width]
        w_small = packed_w[:, 4 * width :]
        small_t = w_small.astype(F32).T
        gain = (small_t[AT_GAIN : AT_GAIN + 1], small_t[AT_GAIN + 1 : AT_GAIN + 2])
        vec_rows = small_t[AT_VEC : AT_VEC + nconst]
        ints = ints_all[s]
        after, qkv, probs_att, attended = attention_body(
            x, w_qkv, w_attn, gain[0], cosine, sine, seg[:, None], seg[None, :]
        )
        logits, packed, slot_pair, buffer = gating_body(
            after, r, w_small, mix_all[s], gain[1], ints, ints[:, 2][None], nffn, nexp, capacity, slots
        )
        arrived = to_owners(buffer)
        returned = to_tokens(expert_forward(arrived, *experts[s]))
        out, picked = combine_body(after, packed, slot_pair, ints, returned, gain[1], vec_rows, nffn)
        kept.append(
            (x, r, after, qkv, probs_att, attended, packed, slot_pair, arrived, picked, w_qkv, w_attn, w_small, gain, vec_rows, ints)
        )
        sent = out.astype(BF16)
        results.append(sent)
        x = sent.astype(F32)
        r = jnp.where(lane_of(seq_len) < nexp, logits, 0.0).astype(BF16).astype(F32)
    grad_y = upstream
    grad_log = jnp.zeros((seq_len, LANES), F32)
    x_grads, r_grads, sums = [None, None], [None, None], [None, None]
    for s in (1, 0):
        x, r, after, qkv, probs_att, attended, packed, slot_pair, arrived, picked, w_qkv, w_attn, w_small, gain, vec_rows, ints = kept[s]
        grad_made = to_owners(return_body(grad_y, packed, slot_pair, slots))
        grad_arrived, grad_in, grad_out = expert_backward(grad_made, arrived, *experts[s])
        in_sum = lax.psum_scatter(grad_in, "shard", scatter_dimension=0, tiled=True)
        out_sum = lax.psum_scatter(grad_out, "shard", scatter_dimension=0, tiled=True)
        returned = to_tokens(grad_arrived)
        grad_after, grad_r, grad_mix, small_rows = moe_back_body(
            grad_y, grad_log, after, packed, slot_pair, ints, picked, returned, r, w_small, mix_all[s], gain[1], vec_rows, nffn, nexp
        )
        grad_x, grad_w_qkv, grad_w_attn, small_grads = attention_back_body(
            grad_after, x, qkv, probs_att, attended, small_rows, w_qkv, w_attn, gain[0], cosine, sine
        )
        x_grads[s] = grad_x
        r_grads[s] = grad_r[:, :nexp]
        mix_lanes = -(-nexp * nexp // rows)
        mix_flat = jnp.pad(grad_mix[:nexp, :nexp].reshape(-1), (0, rows * mix_lanes - nexp * nexp)).reshape(rows, mix_lanes)
        mix_tile = jnp.tile(mix_flat, (owners * pieces, 1))
        small_grads = small_grads.at[:, AT_MIX : AT_MIX + mix_lanes].set(mix_tile)
        grads = jnp.concatenate([grad_w_qkv, grad_w_attn, small_grads.astype(BF16)], axis=1)
        sums[s] = (grads, in_sum, out_sum)
        grad_y = grad_x.astype(BF16).astype(F32)
        grad_log = grad_r.astype(BF16).astype(F32)
    shared_own = jnp.where(first_core, sums[0][0], sums[1][0])
    shared_other = jnp.where(first_core, sums[1][0], sums[0][0])
    shared_sum = (shared_own.astype(F32) + swap(shared_other).astype(F32)).astype(BF16)
    shared_sum = lax.psum_scatter(shared_sum, ("expert", "shard"), scatter_dimension=0, tiled=True).astype(F32)

    def halves(index):
        own = jnp.where(first_core, sums[0][index], sums[1][index])
        got = swap(jnp.where(first_core, sums[1][index], sums[0][index]))
        return jnp.where(first_core, own, got).astype(F32), jnp.where(first_core, got, own).astype(F32)

    in_halves = [
        jnp.swapaxes(half.reshape(in_rows, chunks, 2, CHUNK), 1, 2).reshape(in_rows, 2, pieces, hidden_here)
        for half in halves(1)
    ]
    in_grad = jnp.stack(in_halves, axis=3).reshape(in_rows, columns)
    out_grad = jnp.concatenate(halves(2), axis=0)

    def both_batches(pair):
        own = jnp.where(first_core, pair[0], pair[1])
        got = swap(jnp.where(first_core, pair[1], pair[0]))
        return jnp.stack(by_section(own, got))[None, :, None]

    small_sum = shared_sum[:, 4 * width :]
    mix_grad = small_sum[:, AT_MIX : AT_MIX + mix_lanes].reshape(-1)[: nexp * nexp].reshape(nexp, nexp)
    return (
        both_batches(results),
        both_batches(x_grads),
        both_batches(r_grads),
        shared_sum[None, :, : 3 * width],
        shared_sum[None, :, 3 * width : 4 * width],
        small_sum[None, :, :nexp],
        small_sum[None, :, AT_PROJ : AT_PROJ + const_proj.shape[-1]],
        small_sum[None, :, AT_VEC : AT_VEC + nconst],
        small_sum[None, :, AT_GAIN : AT_GAIN + 2],
        mix_grad[None],
        in_grad[None, None],
        out_grad[None, None],
    )


def solution(mesh):
    placed = (
        P(None, ("expert", "shard"), None, None),
        P(None, ("expert", "shard"), None, None),
        P(None, ("expert", "shard"), None, None),
        P(None, ("expert", "shard"), None),
        P("section", None, ("expert", "shard"), None, None),
        P("section", None, ("expert", "shard"), None),
        P("section", ("expert", "shard"), None),
        P("section", ("expert", "shard"), None),
        P("section", ("expert", "shard"), None),
        P("section", ("expert", "shard"), None),
        P("section", ("expert", "shard"), None),
        P("section", ("expert", "shard"), None),
        P("section", None, None),
        P("section", "expert", "shard", None),
        P("section", "expert", "shard", None),
    )
    return jax.shard_map(
        local,
        mesh=mesh,
        in_specs=placed,
        out_specs=(
            P("section", None, ("expert", "shard"), None, None),
            P("section", None, ("expert", "shard"), None, None),
            P("section", None, ("expert", "shard"), None, None),
            P("section", ("expert", "shard"), None),
            P("section", ("expert", "shard"), None),
            P("section", ("expert", "shard"), None),
            P("section", ("expert", "shard"), None),
            P("section", ("expert", "shard"), None),
            P("section", ("expert", "shard"), None),
            P("section", None, None),
            P("section", "expert", "shard", None),
            P("section", "expert", "shard", None),
        ),
        check_vma=False,
    )
```

```python
import functools
import math

import jax
import jax.numpy as jnp
from jax import lax
from jax.experimental import pallas as pl
from jax.experimental.pallas import tpu as pltpu
from jax.sharding import PartitionSpec as P

HEADS = 12
HEAD = 64
TOP = 2
CHUNK = 256
LANES = 128
AT_PROJ = 16
AT_VEC = 24
AT_GAIN = 28
AT_MIX = 32

HIGH = lax.Precision.HIGHEST
norm_eps = 1e-06
masked_score = -1e30
F32 = jnp.float32
BF16 = jnp.bfloat16


VMEM_BYTES = 56 * 1024 * 1024


def mm(a, b, contract=((1,), (0,)), precision=None):
    return lax.dot_general(a, b, (contract, ((), ())), precision=precision, preferred_element_type=F32)


NT = ((1,), (1,))
TN = ((0,), (0,))


def lane_of(rows, columns=LANES):
    return lax.broadcasted_iota(jnp.int32, (rows, columns), 1)


def inverse_norm(values):
    return lax.rsqrt(jnp.mean(values * values, axis=-1, keepdims=True) + norm_eps)


def norm_back(grad_unit, unit, inverse):
    return inverse * (grad_unit - unit * jnp.mean(grad_unit * unit, axis=-1, keepdims=True))


def roll(x, by):
    return pltpu.roll(x, by, 1)


def turned(x, lane):
    return jnp.where(lane % HEAD < HEAD // 2, roll(x, LANES - HEAD // 2), roll(x, HEAD // 2))


def hi_lo(x):
    high = x.astype(BF16)
    return high, (x - high.astype(F32)).astype(BF16)


def ones_where(condition):
    return jnp.where(condition, 1.0, 0.0).astype(BF16)


def small_rows_of(w, width):
    rows = w[:, 4 * width :].astype(F32).T
    return rows[AT_GAIN : AT_GAIN + 1], rows[AT_GAIN + 1 : AT_GAIN + 2], rows[AT_VEC:AT_GAIN]


def attention(x, w, gain_first, cosine, sine, seg_col, seg_row, qkv, probs_att, attended):
    seq_len, width = x.shape
    first_b = (x * inverse_norm(x) * gain_first).astype(BF16)
    place_q = lax.broadcasted_iota(jnp.int32, (seq_len, seq_len), 0)
    place_k = lax.broadcasted_iota(jnp.int32, (seq_len, seq_len), 1)
    bias = jnp.where((seg_col == seg_row) & (place_k <= place_q), 0.0, masked_score)
    lane = lane_of(seq_len)
    low_head = lane < HEAD
    for pair in range(width // LANES):
        at = pair * LANES
        q = mm(first_b, w[:, at : at + LANES])
        k = mm(first_b, w[:, width + at : width + at + LANES])
        v = mm(first_b, w[:, 2 * width + at : 2 * width + at + LANES]).astype(BF16)
        q = q * cosine + turned(q, lane) * sine
        k = (k * cosine + turned(k, lane) * sine).astype(BF16)
        outs = []
        for half in range(2):
            one = jnp.where(low_head if half == 0 else lane >= HEAD, q, 0.0).astype(BF16)
            scores = mm(one, k, NT) * (HEAD**-0.5) + bias
            scores = jnp.exp(scores - jnp.max(scores, axis=-1, keepdims=True))
            probs = (scores * (1.0 / jnp.sum(scores, axis=-1, keepdims=True))).astype(BF16)
            probs_att[2 * pair + half] = probs
            outs.append(mm(probs, v))
        attended[:, at : at + LANES] = jnp.where(low_head, outs[0], outs[1]).astype(BF16)
        qkv[:, at : at + LANES] = q.astype(BF16)
        qkv[:, width + at : width + at + LANES] = k
        qkv[:, 2 * width + at : 2 * width + at + LANES] = v
    return x + mm(attended[...], w[:, 3 * width : 4 * width])


def gating(after, r, small, mix, gain_second, ints, prio_row, dims, packed_ref, slot_ref, r_next, buffer):
    nffn, nexp, capacity, slots = dims
    rows = after.shape[0]
    second_b = (after * inverse_norm(after) * gain_second).astype(BF16)
    lane = lane_of(rows)
    logits = mm(second_b, small)
    full = logits + mm(r, mix, precision=HIGH)
    inside = lane < nexp
    full = jnp.where(inside, full, masked_score)
    raised = jnp.exp(full - jnp.max(full, axis=-1, keepdims=True))
    probs = raised / jnp.sum(raised, axis=-1, keepdims=True)
    other = jnp.where(lane % 2 == 0, roll(logits, LANES - 1), roll(logits, 1))
    bigger = jnp.maximum(logits, other)
    mine_e = jnp.exp(logits - bigger)
    mixes = mine_e / (mine_e + jnp.exp(other - bigger))
    before = ones_where(prio_row < ints[:, 2:3])
    route = (ints[:, 0:1], ints[:, 1:2])
    routed = ones_where(((lane == route[0]) | (lane == route[1])) & (lane < nffn))
    rank = mm(before, routed)
    gates, places = [], []
    dispatch = 0.0
    stride = slots // nffn
    for k in range(TOP):
        chosen = lane == route[k]
        gates.append(jnp.sum(jnp.where(chosen, probs, 0.0), axis=-1, keepdims=True))
        rank_k = jnp.sum(jnp.where(chosen, rank, 0.0), axis=-1, keepdims=True).astype(jnp.int32)
        kept = (route[k] < nffn) & (rank_k < capacity)
        places.append(jnp.where(kept, route[k] * stride + rank_k, -1))
        dispatch = dispatch + jnp.where(places[k] == lane_of(rows, slots), 1.0, 0.0)
    buffer[...] = mm(dispatch.astype(BF16), second_b, TN).astype(BF16)
    packed = jnp.where(inside, probs, jnp.where((lane >= AT_PROJ) & (lane < AT_VEC), mixes, 0.0))
    packed = jnp.where(lane == AT_VEC, gates[0], packed)
    packed_ref[...] = jnp.where(lane == AT_VEC + 1, gates[1], packed)
    slot_ref[...] = jnp.where(lane == 0, places[0], places[1])
    if r_next is not None:
        r_next[...] = jnp.where(inside, full, 0.0).astype(BF16)


def extras(packed, ints, nffn, nconst):
    gates = (packed[:, AT_VEC : AT_VEC + 1], packed[:, AT_VEC + 1 : AT_VEC + 2])

    def of(expert):
        return sum(jnp.where(ints[:, k : k + 1] == expert, gates[k], 0.0) for k in range(TOP))

    def mixes(c):
        at = AT_PROJ + 2 * c
        return packed[:, at : at + 1], packed[:, at + 1 : at + 2]

    return gates, of(nffn + 1), [of(nffn + 2 + c) for c in range(nconst)], [mixes(c) for c in range(nconst)]


def combine(after, packed, slot_pair, ints, parts, gain_second, vec_rows, dims, picked_ref):
    nffn, nexp, _, slots = dims
    nconst = nexp - nffn - 2
    rows = after.shape[0]
    second = after * inverse_norm(after) * gain_second
    gates, copied, const, mixes = extras(packed, ints, nffn, nconst)
    made = (parts[0][...].astype(F32) + parts[1][...].astype(F32)).astype(BF16)
    slot_lane = lane_of(rows, slots)
    coefficient = copied
    for c in range(nconst):
        coefficient = coefficient + const[c] * mixes[c][0]
    out = after + coefficient * second
    for k in range(TOP):
        picked = mm(ones_where(slot_pair[:, k : k + 1] == slot_lane), made)
        picked_ref[k] = picked.astype(BF16)
        out = out + gates[k] * picked
    for c in range(nconst):
        out = out + (const[c] * mixes[c][1]) * vec_rows[c : c + 1]
    return out


def give_back(grad_y, packed, slot_pair, dims, buffer):
    slots = dims[3]
    slot_lane = lane_of(grad_y.shape[0], slots)
    total = 0.0
    for k in range(TOP):
        gate = packed[:, AT_VEC + k : AT_VEC + k + 1]
        table = ones_where(slot_pair[:, k : k + 1] == slot_lane)
        total = total + mm(table, (gate * grad_y).astype(BF16), TN)
    buffer[...] = total.astype(BF16)


def moe_back(
    grad_y, grad_log_in, after, packed, slot_pair, ints, picked, parts, r, small, mix, gain_second, vec_rows, dims
):
    nffn, nexp, _, slots = dims
    nconst = nexp - nffn - 2
    rows = grad_y.shape[0]
    lane = lane_of(rows)
    inverse = inverse_norm(after)
    unit = after * inverse
    second = unit * gain_second
    second_b = second.astype(BF16)
    gates, copied, const, mixes = extras(packed, ints, nffn, nconst)
    grad_buffer = (parts[0][...].astype(F32) + parts[1][...].astype(F32)).astype(BF16)
    slot_lane = lane_of(rows, slots)
    dispatch = sum(jnp.where(slot_pair[:, k : k + 1] == slot_lane, 1.0, 0.0) for k in range(TOP))
    grad_second = mm(dispatch.astype(BF16), grad_buffer)
    along_second = jnp.sum(grad_y * second, axis=-1, keepdims=True)
    coefficient = copied
    grad_extra = [(nffn + 1, along_second)]
    grad_lanes = jnp.zeros((rows, LANES), F32)
    vec_grads = []
    for c in range(nconst):
        along = jnp.sum(grad_y * vec_rows[c : c + 1], axis=-1, keepdims=True)
        m0, m1 = mixes[c]
        coefficient = coefficient + const[c] * m0
        grad_extra.append((nffn + 2 + c, m0 * along_second + m1 * along))
        d0, d1 = const[c] * along_second, const[c] * along
        mean = m0 * d0 + m1 * d1
        at = AT_PROJ + 2 * c
        grad_lanes = jnp.where(lane == at, m0 * (d0 - mean), grad_lanes)
        grad_lanes = jnp.where(lane == at + 1, m1 * (d1 - mean), grad_lanes)
        vec_grads.append(jnp.sum(grad_y * (const[c] * m1), axis=0, keepdims=True))
    grad_second = grad_second + coefficient * grad_y
    grad_probs = jnp.zeros((rows, LANES), F32)
    for k in range(TOP):
        grad_gate = jnp.sum(picked[k].astype(F32) * grad_y, axis=-1, keepdims=True)
        for expert, value in grad_extra:
            grad_gate = grad_gate + jnp.where(ints[:, k : k + 1] == expert, value, 0.0)
        grad_probs = grad_probs + jnp.where(lane == ints[:, k : k + 1], grad_gate, 0.0)
    probs = jnp.where(lane < nexp, packed, 0.0)
    grad_logits = probs * (grad_probs - jnp.sum(probs * grad_probs, axis=-1, keepdims=True)) + grad_log_in
    grad_mix = mm(r, grad_logits, TN, HIGH)
    grad_r = mm(grad_logits, mix, NT, HIGH)
    high, low = hi_lo(jnp.where(lane < nexp, grad_logits, grad_lanes))
    small_rows = mm(high, second_b, TN) + mm(low, second_b, TN)
    grad_second = grad_second + mm(high, small, NT) + mm(low, small, NT)
    grad_gain = jnp.sum(grad_second * unit, axis=0, keepdims=True)
    grad_after = grad_y + norm_back(grad_second * gain_second, unit, inverse)
    row = lax.broadcasted_iota(jnp.int32, small_rows.shape, 0)
    small_rows = jnp.where(row < AT_VEC, small_rows, 0.0)
    for c in range(nconst):
        small_rows = jnp.where(row == AT_VEC + c, vec_grads[c], small_rows)
    small_rows = jnp.where(row == AT_GAIN + 1, grad_gain, small_rows)
    return grad_after, grad_r, grad_mix, small_rows


def attention_back(grad_after, x, qkv, probs_att, attended, small_rows, w, gain_first, cosine, sine, grads, grad_qkv):
    seq_len, width = x.shape
    inverse = inverse_norm(x)
    unit = x * inverse
    first_b = (unit * gain_first).astype(BF16)
    grad_branch = grad_after.astype(BF16)
    grads[:, 3 * width : 4 * width] = mm(attended[...], grad_branch, TN).astype(BF16)
    lane = lane_of(seq_len)
    low_head = lane < HEAD
    masks = (ones_where(low_head), ones_where(lane >= HEAD))
    scale = HEAD**-0.5
    for pair in range(width // LANES):
        at = pair * LANES
        q = qkv[:, at : at + LANES]
        k = qkv[:, width + at : width + at + LANES]
        v = qkv[:, 2 * width + at : 2 * width + at + LANES]
        g = mm(grad_branch, w[at : at + LANES, 3 * width : 4 * width], NT).astype(BF16)
        dq, dk, dv = [], [], []
        for half in range(2):
            probs = probs_att[2 * pair + half]
            grad_p = mm(g * masks[half], v, NT)
            p = probs.astype(F32)
            grad_s = (p * (grad_p - jnp.sum(p * grad_p, axis=-1, keepdims=True))).astype(BF16)
            dv.append(mm(probs, g, TN))
            dq.append(mm(grad_s, k))
            dk.append(mm(grad_s, q, TN))
        dq = jnp.where(low_head, dq[0], dq[1]) * scale
        dk = jnp.where(low_head, dk[0], dk[1]) * scale
        grad_qkv[:, at : at + LANES] = (dq * cosine - turned(dq, lane) * sine).astype(BF16)
        grad_qkv[:, width + at : width + at + LANES] = (dk * cosine - turned(dk, lane) * sine).astype(BF16)
        grad_qkv[:, 2 * width + at : 2 * width + at + LANES] = jnp.where(low_head, dv[0], dv[1]).astype(BF16)
    grads[:, : 3 * width] = mm(first_b, grad_qkv[...], TN).astype(BF16)
    grad_first = mm(grad_qkv[...], w[:, : 3 * width], NT)
    grad_gain = jnp.sum(grad_first * unit, axis=0, keepdims=True)
    grad_x = grad_after + norm_back(grad_first * gain_first, unit, inverse)
    row = lax.broadcasted_iota(jnp.int32, small_rows.shape, 0)
    small_rows = jnp.where(row == AT_GAIN, grad_gain, small_rows)
    grads[:, 4 * width :] = small_rows.T.astype(BF16)
    return grad_x


def attend_kernel(
    dims, x, r, w, mix, cosine, sine, seg_col, seg_row, ints, prio_row,
    after, qkv, probs_att, attended, packed, slot_pair, r_next, buffer,
):
    width = x.shape[1]
    gain_first, gain_second, _ = small_rows_of(w, width)
    after_v = attention(
        x[...].astype(F32), w, gain_first, cosine[...], sine[...], seg_col[...], seg_row[...], qkv, probs_att, attended
    )
    after[...] = after_v
    gating(
        after_v, r[...].astype(F32), w[:, 4 * width :], mix[...], gain_second, ints[...], prio_row[...], dims,
        packed, slot_pair, r_next, buffer,
    )


def combine_kernel(dims, after, packed, slot_pair, ints, part_0, part_1, w, out, picked):
    width = after.shape[1]
    _, gain_second, vec_rows = small_rows_of(w, width)
    out[...] = combine(
        after[...], packed[...], slot_pair[...], ints[...], (part_0, part_1), gain_second, vec_rows, dims, picked
    ).astype(BF16)


def give_back_kernel(dims, grad_y, packed, slot_pair, buffer):
    give_back(grad_y[...].astype(F32), packed[...], slot_pair[...], dims, buffer)


def back_kernel(
    dims, grad_y, grad_log, after, packed, slot_pair, ints, picked, part_0, part_1, r, w, mix,
    x, qkv, probs_att, attended, cosine, sine,
    grad_x, grad_r, grad_mix, grads, grad_qkv,
):
    width = x.shape[1]
    gain_first, gain_second, vec_rows = small_rows_of(w, width)
    grad_after, grad_r_v, grad_mix_v, small_rows = moe_back(
        grad_y[...].astype(F32), grad_log[...].astype(F32), after[...], packed[...], slot_pair[...], ints[...], picked,
        (part_0, part_1), r[...].astype(F32), w[:, 4 * width :], mix[...], gain_second, vec_rows, dims,
    )
    grad_r[...] = grad_r_v
    grad_mix[...] = grad_mix_v
    grad_x[...] = attention_back(
        grad_after, x[...].astype(F32), qkv, probs_att, attended, small_rows, w, gain_first, cosine[...], sine[...],
        grads, grad_qkv,
    )


def expert_kernel(arrived_0, arrived_1, w_in, w_out, made_0, made_1, total):
    slots = arrived_0.shape[0]
    step = pl.program_id(0)
    for part, arrived in enumerate((arrived_0, arrived_1)):
        at = part * slots
        both = mm(arrived[...], w_in[...])
        gate = both[:, :CHUNK]
        hidden = (gate * jax.nn.sigmoid(gate) * both[:, CHUNK:]).astype(BF16)
        more = mm(hidden, w_out[...])

        @pl.when(step == 0)
        def _():
            total[at : at + slots] = more

        @pl.when(step > 0)
        def _():
            total[at : at + slots] += more

    @pl.when(step == pl.num_programs(0) - 1)
    def _():
        made_0[...] = total[:slots].astype(BF16)
        made_1[...] = total[slots:].astype(BF16)


def expert_back_kernel(
    arrived_0, arrived_1, grad_0, grad_1, w_in, w_out, given_0, given_1, grad_in, grad_out, total
):
    slots = arrived_0.shape[0]
    step = pl.program_id(0)
    arrived = jnp.concatenate([arrived_0[...], arrived_1[...]], axis=0)
    grad_made = jnp.concatenate([grad_0[...], grad_1[...]], axis=0)
    both = mm(arrived, w_in[...])
    gate, up = both[:, :CHUNK], both[:, CHUNK:]
    sig = jax.nn.sigmoid(gate)
    hidden = (gate * sig * up).astype(BF16)
    grad_hidden = mm(grad_made, w_out[...], NT)
    grad_out[...] = mm(hidden, grad_made, TN).astype(BF16)
    grad_gate = grad_hidden * up * sig * (1.0 + gate * (1.0 - sig))
    grad_up = grad_hidden * gate * sig
    grad_both = jnp.concatenate([grad_gate, grad_up], axis=1).astype(BF16)
    grad_in[...] = mm(arrived, grad_both, TN).astype(BF16)
    more = mm(grad_both, w_in[...], NT)

    @pl.when(step == 0)
    def _():
        total[...] = more

    @pl.when(step > 0)
    def _():
        total[...] += more

    @pl.when(step == pl.num_programs(0) - 1)
    def _():
        given_0[...] = total[:slots].astype(BF16)
        given_1[...] = total[slots:].astype(BF16)


def shaped(shape, dtype):
    return jax.ShapeDtypeStruct(shape, dtype)


def run(kernel, out, args, flops=0):
    return pl.pallas_call(
        kernel,
        out_shape=out,
        compiler_params=pltpu.CompilerParams(vmem_limit_bytes=VMEM_BYTES),
        cost_estimate=pl.CostEstimate(flops=flops, bytes_accessed=8 << 20, transcendentals=0),
    )(*args)


def expert_specs(slots, width):
    whole = pl.BlockSpec((slots, width), lambda i: (0, 0))
    w_in = pl.BlockSpec((width, 2 * CHUNK), lambda i: (0, i))
    w_out = pl.BlockSpec((CHUNK, width), lambda i: (i, 0))
    return whole, w_in, w_out


def expert_forward(arrived, w_in, w_out):
    slots, width = arrived[0].shape
    whole, in_spec, out_spec = expert_specs(slots, width)
    return pl.pallas_call(
        expert_kernel,
        grid=(w_out.shape[0] // CHUNK,),
        in_specs=[whole, whole, in_spec, out_spec],
        out_specs=[whole, whole],
        out_shape=[shaped((slots, width), BF16)] * 2,
        scratch_shapes=[pltpu.VMEM((2 * slots, width), F32)],
        compiler_params=pltpu.CompilerParams(vmem_limit_bytes=VMEM_BYTES),
        cost_estimate=pl.CostEstimate(flops=12 * slots * width * w_out.shape[0], bytes_accessed=8 << 20, transcendentals=0),
    )(*arrived, w_in, w_out)


def expert_backward(grad_made, arrived, w_in, w_out):
    slots, width = arrived[0].shape
    whole, in_spec, out_spec = expert_specs(slots, width)
    return pl.pallas_call(
        expert_back_kernel,
        grid=(w_out.shape[0] // CHUNK,),
        in_specs=[whole, whole, whole, whole, in_spec, out_spec],
        out_specs=[whole, whole, in_spec, out_spec],
        out_shape=[shaped((slots, width), BF16)] * 2 + [shaped(w_in.shape, BF16), shaped(w_out.shape, BF16)],
        scratch_shapes=[pltpu.VMEM((2 * slots, width), F32)],
        compiler_params=pltpu.CompilerParams(vmem_limit_bytes=VMEM_BYTES),
        cost_estimate=pl.CostEstimate(flops=32 * slots * width * w_out.shape[0], bytes_accessed=16 << 20, transcendentals=0),
    )(*arrived, *grad_made, w_in, w_out)

def local(
    x_in,
    cotangent,
    gate_prev,
    segments,
    routes,
    priority,
    attn_qkv,
    attn_out,
    router,
    const_proj,
    const_vec,
    gains,
    gate_mix,
    expert_in,
    expert_out,
):
    seq_len, width = x_in.shape[2:]
    nexp = gate_prev.shape[-1]
    owners, pieces = lax.axis_size("expert"), lax.axis_size("shard")
    nffn = owners * expert_in.shape[1]
    nconst = const_vec.shape[-1]
    capacity = (5 * TOP * seq_len + 4 * nexp - 1) // (4 * nexp)
    room = -(-capacity // 16) * 16
    slots = nffn * room
    core = lax.axis_index("section")
    first_core = core == 0

    def swap(item):
        return lax.ppermute(item, "section", [(0, 1), (1, 0)])

    def mine(stack, axis=0):
        return lax.dynamic_index_in_dim(stack, core, axis, keepdims=False)

    def others(stack, axis=0):
        return lax.dynamic_index_in_dim(stack, 1 - core, axis, keepdims=False)

    def by_section(own, other):
        return jnp.where(first_core, own, other), jnp.where(first_core, other, own)

    in_rows, columns = expert_in.shape[2:]
    hidden_here = expert_out.shape[2] // 2
    chunks = pieces * hidden_here // CHUNK
    w_in = expert_in[0, 0].reshape(in_rows, 2, pieces, 2, hidden_here)

    def as_chunks(half):
        half = half.reshape(in_rows, 2, chunks, CHUNK)
        return jnp.swapaxes(half, 1, 2).reshape(in_rows, columns // 2)

    w_out = expert_out[0, 0].reshape(2, hidden_here, width)
    ins = by_section(as_chunks(mine(w_in, 3)), swap(as_chunks(others(w_in, 3))))
    outs = by_section(mine(w_out), swap(others(w_out)))
    experts = [
        (
            lax.all_gather(ins[s], "shard", axis=0, tiled=True),
            lax.all_gather(outs[s], "shard", axis=0, tiled=True),
        )
        for s in range(2)
    ]
    rows = attn_qkv.shape[1]

    def lanes(array, upto):
        return jnp.pad(array, ((0, 0), (0, upto - array.shape[1])))

    small = jnp.concatenate(
        [
            lanes(router[0], AT_PROJ),
            lanes(const_proj[0], AT_VEC - AT_PROJ),
            lanes(const_vec[0], AT_GAIN - AT_VEC),
            lanes(gains[0], LANES - AT_GAIN),
        ],
        axis=1,
    )
    shared = jnp.concatenate([attn_qkv[0], attn_out[0], small], axis=1)
    shared = lax.all_gather(shared, ("expert", "shard"), axis=0, tiled=True)
    shared = by_section(shared, swap(shared))
    mix_own = jnp.pad(gate_mix[0], ((0, LANES - nexp), (0, LANES - nexp)))
    mix_all = by_section(mix_own, swap(mix_own))
    ints_own = jnp.concatenate([routes[0, :, 0], priority[0, :, 0, :, None]], axis=-1)
    ints_all = by_section(mine(ints_own), swap(others(ints_own)))
    x_first = mine(x_in[:, 0])
    r_first = jnp.pad(mine(gate_prev[:, 0]), ((0, 0), (0, LANES - nexp)))
    upstream = mine(cotangent[:, 0])
    seg = mine(segments[:, 0])
    place = lax.iota(jnp.int32, seq_len)
    start = jnp.sum((seg[None, :] < seg[:, None]).astype(F32), axis=1)
    angles = (place.astype(F32) - start)[:, None] * jnp.exp(
        lax.iota(F32, HEAD // 2) * (-2.0 * math.log(10000.0) / HEAD)
    )[None, :]
    cosine, sine = jnp.cos(angles), jnp.sin(angles)
    cosine = jnp.concatenate([cosine] * 4, axis=1)
    sine = jnp.concatenate([-sine, sine, -sine, sine], axis=1)

    dims = (nffn, nexp, capacity, slots)
    heads = width // HEAD

    def exchanged(blocks):
        return lax.all_to_all(
            blocks.reshape(owners, room, width), "expert", split_axis=0, concat_axis=0, tiled=True
        ).reshape(slots, width)

    def to_owners(blocks):
        blocks = exchanged(blocks)
        return blocks, swap(blocks)

    def to_tokens(parts):
        return exchanged(parts[0]), exchanged(swap(parts[1]))

    kept = []
    x, r = x_first, r_first
    results = []
    seg_col, seg_row = seg[:, None], seg[None, :]
    for s in range(2):
        w, ints = shared[s], ints_all[s]
        after, qkv, probs_att, attended, packed, slot_pair, r_next, buffer = run(
            functools.partial(attend_kernel, dims),
            [
                shaped((seq_len, width), F32),
                shaped((seq_len, 3 * width), BF16),
                shaped((heads, seq_len, seq_len), BF16),
                shaped((seq_len, width), BF16),
                shaped((seq_len, LANES), F32),
                shaped((seq_len, LANES), jnp.int32),
                shaped((seq_len, LANES), BF16),
                shaped((slots, width), BF16),
            ],
            (x, r, w, mix_all[s], cosine, sine, seg_col, seg_row, ints, ints[:, 2][None]),
            flops=2 << 30,
        )
        arrived = to_owners(buffer)
        parts = to_tokens(expert_forward(arrived, *experts[s]))
        out, picked = run(
            functools.partial(combine_kernel, dims),
            [shaped((seq_len, width), BF16), shaped((TOP, seq_len, width), BF16)],
            (after, packed, slot_pair, ints, *parts, w),
        )
        kept.append((x, r, w, ints, after, qkv, probs_att, attended, packed, slot_pair, arrived, picked))
        results.append(out)
        x, r = out, r_next
    grad_y = upstream
    grad_log = jnp.zeros((seq_len, LANES), F32)
    x_grads, r_grads, sums = [None, None], [None, None], [None, None]
    for s in (1, 0):
        x, r, w, ints, after, qkv, probs_att, attended, packed, slot_pair, arrived, picked = kept[s]
        (buffer,) = run(
            functools.partial(give_back_kernel, dims),
            [shaped((slots, width), BF16)],
            (grad_y, packed, slot_pair),
        )
        given_0, given_1, grad_in, grad_out = expert_backward(to_owners(buffer), arrived, *experts[s])
        in_sum = lax.psum_scatter(grad_in, "shard", scatter_dimension=0, tiled=True)
        out_sum = lax.psum_scatter(grad_out, "shard", scatter_dimension=0, tiled=True)
        parts = to_tokens((given_0, given_1))
        grad_x, grad_r, grad_mix, grads, _ = run(
            functools.partial(back_kernel, dims),
            [
                shaped((seq_len, width), F32),
                shaped((seq_len, LANES), F32),
                shaped((LANES, LANES), F32),
                shaped(w.shape, BF16),
                shaped((seq_len, 3 * width), BF16),
            ],
            (
                grad_y, grad_log, after, packed, slot_pair, ints, picked, *parts, r, w, mix_all[s],
                x, qkv, probs_att, attended, cosine, sine,
            ),
            flops=5 << 30,
        )
        x_grads[s] = grad_x
        r_grads[s] = grad_r[:, :nexp]
        mix_lanes = -(-nexp * nexp // rows)
        mix_flat = jnp.pad(grad_mix[:nexp, :nexp].reshape(-1), (0, rows * mix_lanes - nexp * nexp)).reshape(rows, mix_lanes)
        mix_tile = jnp.tile(mix_flat, (owners * pieces, 1)).astype(BF16)
        at = 4 * width + AT_MIX
        grads = lax.dynamic_update_slice(grads, mix_tile, (0, at))
        sums[s] = (grads, in_sum, out_sum)
        grad_y = grad_x.astype(BF16)
        grad_log = grad_r.astype(BF16)
    shared_own = jnp.where(first_core, sums[0][0], sums[1][0])
    shared_other = jnp.where(first_core, sums[1][0], sums[0][0])
    shared_sum = (shared_own.astype(F32) + swap(shared_other).astype(F32)).astype(BF16)
    shared_sum = lax.psum_scatter(shared_sum, ("expert", "shard"), scatter_dimension=0, tiled=True).astype(F32)

    def halves(index):
        own = jnp.where(first_core, sums[0][index], sums[1][index])
        got = swap(jnp.where(first_core, sums[1][index], sums[0][index]))
        return jnp.where(first_core, own, got).astype(F32), jnp.where(first_core, got, own).astype(F32)

    in_halves = [
        jnp.swapaxes(half.reshape(in_rows, chunks, 2, CHUNK), 1, 2).reshape(in_rows, 2, pieces, hidden_here)
        for half in halves(1)
    ]
    in_grad = jnp.stack(in_halves, axis=3).reshape(in_rows, columns)
    out_grad = jnp.concatenate(halves(2), axis=0)

    def both_batches(pair):
        own = jnp.where(first_core, pair[0], pair[1])
        got = swap(jnp.where(first_core, pair[1], pair[0]))
        return jnp.stack(by_section(own, got))[None, :, None]

    small_sum = shared_sum[:, 4 * width :]
    mix_grad = small_sum[:, AT_MIX : AT_MIX + mix_lanes].reshape(-1)[: nexp * nexp].reshape(nexp, nexp)
    return (
        both_batches(results),
        both_batches(x_grads),
        both_batches(r_grads),
        shared_sum[None, :, : 3 * width],
        shared_sum[None, :, 3 * width : 4 * width],
        small_sum[None, :, :nexp],
        small_sum[None, :, AT_PROJ : AT_PROJ + const_proj.shape[-1]],
        small_sum[None, :, AT_VEC : AT_VEC + nconst],
        small_sum[None, :, AT_GAIN : AT_GAIN + 2],
        mix_grad[None],
        in_grad[None, None],
        out_grad[None, None],
    )


def solution(mesh):
    placed = (
        P(None, ("expert", "shard"), None, None),
        P(None, ("expert", "shard"), None, None),
        P(None, ("expert", "shard"), None, None),
        P(None, ("expert", "shard"), None),
        P("section", None, ("expert", "shard"), None, None),
        P("section", None, ("expert", "shard"), None),
        P("section", ("expert", "shard"), None),
        P("section", ("expert", "shard"), None),
        P("section", ("expert", "shard"), None),
        P("section", ("expert", "shard"), None),
        P("section", ("expert", "shard"), None),
        P("section", ("expert", "shard"), None),
        P("section", None, None),
        P("section", "expert", "shard", None),
        P("section", "expert", "shard", None),
    )
    return jax.shard_map(
        local,
        mesh=mesh,
        in_specs=placed,
        out_specs=(
            P("section", None, ("expert", "shard"), None, None),
            P("section", None, ("expert", "shard"), None, None),
            P("section", None, ("expert", "shard"), None, None),
            P("section", ("expert", "shard"), None),
            P("section", ("expert", "shard"), None),
            P("section", ("expert", "shard"), None),
            P("section", ("expert", "shard"), None),
            P("section", ("expert", "shard"), None),
            P("section", ("expert", "shard"), None),
            P("section", None, None),
            P("section", "expert", "shard", None),
            P("section", "expert", "shard", None),
        ),
        check_vma=False,
    )
```

```python
import functools
import math

import jax
import jax.numpy as jnp
from jax import lax
from jax.experimental import pallas as pl
from jax.experimental.pallas import tpu as pltpu
from jax.sharding import PartitionSpec as P

HEADS = 12
HEAD = 64
TOP = 2
CHUNK = 256
LANES = 128
AT_PROJ = 16
AT_VEC = 24
AT_GAIN = 28
AT_MIX = 32

HIGH = lax.Precision.HIGHEST
norm_eps = 1e-06
masked_score = -1e30
F32 = jnp.float32
BF16 = jnp.bfloat16


VMEM_BYTES = 56 * 1024 * 1024


def mm(a, b, contract=((1,), (0,)), precision=None):
    return lax.dot_general(a, b, (contract, ((), ())), precision=precision, preferred_element_type=F32)


NT = ((1,), (1,))
TN = ((0,), (0,))


def lane_of(rows, columns=LANES):
    return lax.broadcasted_iota(jnp.int32, (rows, columns), 1)


def inverse_norm(values):
    return lax.rsqrt(jnp.mean(values * values, axis=-1, keepdims=True) + norm_eps)


def norm_back(grad_unit, unit, inverse):
    return inverse * (grad_unit - unit * jnp.mean(grad_unit * unit, axis=-1, keepdims=True))


def roll(x, by):
    return pltpu.roll(x, by, 1)


def turned(x, lane):
    return jnp.where(lane % HEAD < HEAD // 2, roll(x, LANES - HEAD // 2), roll(x, HEAD // 2))


def hi_lo(x):
    high = x.astype(BF16)
    return high, (x - high.astype(F32)).astype(BF16)


def ones_where(condition):
    return jnp.where(condition, 1.0, 0.0).astype(BF16)


def small_rows_of(small):
    rows = small[...].astype(F32).T
    return rows[AT_GAIN : AT_GAIN + 1], rows[AT_GAIN + 1 : AT_GAIN + 2], rows[AT_VEC:AT_GAIN]


def attention(x, w, gain_first, cosine, sine, seg_col, seg_row, qkv, probs_att, attended):
    seq_len, width = x.shape
    first_b = (x * inverse_norm(x) * gain_first).astype(BF16)
    place_q = lax.broadcasted_iota(jnp.int32, (seq_len, seq_len), 0)
    place_k = lax.broadcasted_iota(jnp.int32, (seq_len, seq_len), 1)
    bias = jnp.where((seg_col == seg_row) & (place_k <= place_q), 0.0, masked_score)
    lane = lane_of(seq_len)
    low_head = lane < HEAD
    for pair in range(width // LANES):
        at = pair * LANES
        q = mm(first_b, w[:, at : at + LANES])
        k = mm(first_b, w[:, width + at : width + at + LANES])
        v = mm(first_b, w[:, 2 * width + at : 2 * width + at + LANES]).astype(BF16)
        q = q * cosine + turned(q, lane) * sine
        k = (k * cosine + turned(k, lane) * sine).astype(BF16)
        outs = []
        for half in range(2):
            one = jnp.where(low_head if half == 0 else lane >= HEAD, q, 0.0).astype(BF16)
            scores = mm(one, k, NT) * (HEAD**-0.5) + bias
            scores = jnp.exp(scores - jnp.max(scores, axis=-1, keepdims=True))
            probs = (scores * (1.0 / jnp.sum(scores, axis=-1, keepdims=True))).astype(BF16)
            probs_att[2 * pair + half] = probs
            outs.append(mm(probs, v))
        attended[:, at : at + LANES] = jnp.where(low_head, outs[0], outs[1]).astype(BF16)
        qkv[:, at : at + LANES] = q.astype(BF16)
        qkv[:, width + at : width + at + LANES] = k
        qkv[:, 2 * width + at : 2 * width + at + LANES] = v
    return x + mm(attended[...], w[:, 3 * width : 4 * width])


def gating(after, r, small, mix, gain_second, ints, prio_row, dims, packed_ref, slot_ref, r_next, buffer):
    nffn, nexp, capacity, slots = dims
    rows = after.shape[0]
    second_b = (after * inverse_norm(after) * gain_second).astype(BF16)
    lane = lane_of(rows)
    logits = mm(second_b, small)
    full = logits + mm(r, mix, precision=HIGH)
    inside = lane < nexp
    full = jnp.where(inside, full, masked_score)
    raised = jnp.exp(full - jnp.max(full, axis=-1, keepdims=True))
    probs = raised / jnp.sum(raised, axis=-1, keepdims=True)
    other = jnp.where(lane % 2 == 0, roll(logits, LANES - 1), roll(logits, 1))
    bigger = jnp.maximum(logits, other)
    mine_e = jnp.exp(logits - bigger)
    mixes = mine_e / (mine_e + jnp.exp(other - bigger))
    before = ones_where(prio_row < ints[:, 2:3])
    route = (ints[:, 0:1], ints[:, 1:2])
    routed = ones_where(((lane == route[0]) | (lane == route[1])) & (lane < nffn))
    rank = mm(before, routed)
    gates, places = [], []
    dispatch = 0.0
    stride = slots // nffn
    for k in range(TOP):
        chosen = lane == route[k]
        gates.append(jnp.sum(jnp.where(chosen, probs, 0.0), axis=-1, keepdims=True))
        rank_k = jnp.sum(jnp.where(chosen, rank, 0.0), axis=-1, keepdims=True).astype(jnp.int32)
        kept = (route[k] < nffn) & (rank_k < capacity)
        places.append(jnp.where(kept, route[k] * stride + rank_k, -1))
        dispatch = dispatch + jnp.where(places[k] == lane_of(rows, slots), 1.0, 0.0)
    buffer[...] = mm(dispatch.astype(BF16), second_b, TN).astype(BF16)
    packed = jnp.where(inside, probs, jnp.where((lane >= AT_PROJ) & (lane < AT_VEC), mixes, 0.0))
    packed = jnp.where(lane == AT_VEC, gates[0], packed)
    packed_ref[...] = jnp.where(lane == AT_VEC + 1, gates[1], packed)
    slot_ref[...] = jnp.where(lane == 0, places[0], places[1])
    if r_next is not None:
        r_next[...] = jnp.where(inside, full, 0.0).astype(BF16)


def extras(packed, ints, nffn, nconst):
    gates = (packed[:, AT_VEC : AT_VEC + 1], packed[:, AT_VEC + 1 : AT_VEC + 2])

    def of(expert):
        return sum(jnp.where(ints[:, k : k + 1] == expert, gates[k], 0.0) for k in range(TOP))

    def mixes(c):
        at = AT_PROJ + 2 * c
        return packed[:, at : at + 1], packed[:, at + 1 : at + 2]

    return gates, of(nffn + 1), [of(nffn + 2 + c) for c in range(nconst)], [mixes(c) for c in range(nconst)]


def combine(after, packed, slot_pair, ints, blocks, gain_second, vec_rows, dims, picked_ref):
    nffn, nexp, _, slots = dims
    nconst = nexp - nffn - 2
    rows = after.shape[0]
    second = after * inverse_norm(after) * gain_second
    gates, copied, const, mixes = extras(packed, ints, nffn, nconst)
    made = blocks[...]
    slot_lane = lane_of(rows, slots)
    coefficient = copied
    for c in range(nconst):
        coefficient = coefficient + const[c] * mixes[c][0]
    out = after + coefficient * second
    for k in range(TOP):
        picked = mm(ones_where(slot_pair[:, k : k + 1] == slot_lane), made)
        picked_ref[k] = picked.astype(BF16)
        out = out + gates[k] * picked
    for c in range(nconst):
        out = out + (const[c] * mixes[c][1]) * vec_rows[c : c + 1]
    return out


def give_back(grad_y, packed, slot_pair, dims, buffer):
    slots = dims[3]
    slot_lane = lane_of(grad_y.shape[0], slots)
    total = 0.0
    for k in range(TOP):
        gate = packed[:, AT_VEC + k : AT_VEC + k + 1]
        table = ones_where(slot_pair[:, k : k + 1] == slot_lane)
        total = total + mm(table, (gate * grad_y).astype(BF16), TN)
    buffer[...] = total.astype(BF16)


def moe_back(
    grad_y, grad_log_in, after, packed, slot_pair, ints, picked, blocks, r, small, mix, gain_second, vec_rows, dims
):
    nffn, nexp, _, slots = dims
    nconst = nexp - nffn - 2
    rows = grad_y.shape[0]
    lane = lane_of(rows)
    inverse = inverse_norm(after)
    unit = after * inverse
    second = unit * gain_second
    second_b = second.astype(BF16)
    gates, copied, const, mixes = extras(packed, ints, nffn, nconst)
    grad_buffer = blocks[...]
    slot_lane = lane_of(rows, slots)
    dispatch = sum(jnp.where(slot_pair[:, k : k + 1] == slot_lane, 1.0, 0.0) for k in range(TOP))
    grad_second = mm(dispatch.astype(BF16), grad_buffer)
    along_second = jnp.sum(grad_y * second, axis=-1, keepdims=True)
    coefficient = copied
    grad_extra = [(nffn + 1, along_second)]
    grad_lanes = jnp.zeros((rows, LANES), F32)
    vec_grads = []
    for c in range(nconst):
        along = jnp.sum(grad_y * vec_rows[c : c + 1], axis=-1, keepdims=True)
        m0, m1 = mixes[c]
        coefficient = coefficient + const[c] * m0
        grad_extra.append((nffn + 2 + c, m0 * along_second + m1 * along))
        d0, d1 = const[c] * along_second, const[c] * along
        mean = m0 * d0 + m1 * d1
        at = AT_PROJ + 2 * c
        grad_lanes = jnp.where(lane == at, m0 * (d0 - mean), grad_lanes)
        grad_lanes = jnp.where(lane == at + 1, m1 * (d1 - mean), grad_lanes)
        vec_grads.append(jnp.sum(grad_y * (const[c] * m1), axis=0, keepdims=True))
    grad_second = grad_second + coefficient * grad_y
    grad_probs = jnp.zeros((rows, LANES), F32)
    for k in range(TOP):
        grad_gate = jnp.sum(picked[k].astype(F32) * grad_y, axis=-1, keepdims=True)
        for expert, value in grad_extra:
            grad_gate = grad_gate + jnp.where(ints[:, k : k + 1] == expert, value, 0.0)
        grad_probs = grad_probs + jnp.where(lane == ints[:, k : k + 1], grad_gate, 0.0)
    probs = jnp.where(lane < nexp, packed, 0.0)
    grad_logits = probs * (grad_probs - jnp.sum(probs * grad_probs, axis=-1, keepdims=True)) + grad_log_in
    grad_mix = mm(r, grad_logits, TN, HIGH)
    grad_r = mm(grad_logits, mix, NT, HIGH)
    high, low = hi_lo(jnp.where(lane < nexp, grad_logits, grad_lanes))
    small_rows = mm(high, second_b, TN) + mm(low, second_b, TN)
    grad_second = grad_second + mm(high, small, NT) + mm(low, small, NT)
    grad_gain = jnp.sum(grad_second * unit, axis=0, keepdims=True)
    grad_after = grad_y + norm_back(grad_second * gain_second, unit, inverse)
    row = lax.broadcasted_iota(jnp.int32, small_rows.shape, 0)
    small_rows = jnp.where(row < AT_VEC, small_rows, 0.0)
    for c in range(nconst):
        small_rows = jnp.where(row == AT_VEC + c, vec_grads[c], small_rows)
    small_rows = jnp.where(row == AT_GAIN + 1, grad_gain, small_rows)
    return grad_after, grad_r, grad_mix, small_rows


def attention_back(grad_after, x, qkv, probs_att, attended, small_rows, w, gain_first, cosine, sine, grads, grad_qkv):
    seq_len, width = x.shape
    inverse = inverse_norm(x)
    unit = x * inverse
    first_b = (unit * gain_first).astype(BF16)
    grad_branch = grad_after.astype(BF16)
    grads[:, 3 * width : 4 * width] = mm(attended[...], grad_branch, TN).astype(BF16)
    lane = lane_of(seq_len)
    low_head = lane < HEAD
    masks = (ones_where(low_head), ones_where(lane >= HEAD))
    scale = HEAD**-0.5
    for pair in range(width // LANES):
        at = pair * LANES
        q = qkv[:, at : at + LANES]
        k = qkv[:, width + at : width + at + LANES]
        v = qkv[:, 2 * width + at : 2 * width + at + LANES]
        g = mm(grad_branch, w[at : at + LANES, 3 * width : 4 * width], NT).astype(BF16)
        dq, dk, dv = [], [], []
        for half in range(2):
            probs = probs_att[2 * pair + half]
            grad_p = mm(g * masks[half], v, NT)
            p = probs.astype(F32)
            grad_s = (p * (grad_p - jnp.sum(p * grad_p, axis=-1, keepdims=True))).astype(BF16)
            dv.append(mm(probs, g, TN))
            dq.append(mm(grad_s, k))
            dk.append(mm(grad_s, q, TN))
        dq = jnp.where(low_head, dq[0], dq[1]) * scale
        dk = jnp.where(low_head, dk[0], dk[1]) * scale
        grad_qkv[:, at : at + LANES] = (dq * cosine - turned(dq, lane) * sine).astype(BF16)
        grad_qkv[:, width + at : width + at + LANES] = (dk * cosine - turned(dk, lane) * sine).astype(BF16)
        grad_qkv[:, 2 * width + at : 2 * width + at + LANES] = jnp.where(low_head, dv[0], dv[1]).astype(BF16)
    grads[:, : 3 * width] = mm(first_b, grad_qkv[...], TN).astype(BF16)
    grad_first = mm(grad_qkv[...], w[:, : 3 * width], NT)
    grad_gain = jnp.sum(grad_first * unit, axis=0, keepdims=True)
    grad_x = grad_after + norm_back(grad_first * gain_first, unit, inverse)
    row = lax.broadcasted_iota(jnp.int32, small_rows.shape, 0)
    small_rows = jnp.where(row == AT_GAIN, grad_gain, small_rows)
    grads[:, 4 * width :] = small_rows.T.astype(BF16)
    return grad_x


def attend_kernel(
    dims, x, r, w, small, mix, cosine, sine, seg_col, seg_row, ints, prio_row,
    after, qkv, probs_att, attended, packed, slot_pair, r_next, buffer,
):
    gain_first, gain_second, _ = small_rows_of(small)
    after_v = attention(
        x[...].astype(F32), w, gain_first, cosine[...], sine[...], seg_col[...], seg_row[...], qkv, probs_att, attended
    )
    after[...] = after_v
    gating(
        after_v, r[...].astype(F32), small[...], mix[...], gain_second, ints[...], prio_row[...], dims,
        packed, slot_pair, r_next, buffer,
    )


def middle_kernel(
    dims, after_0, packed_0, slots_0, ints_0, blocks_0, small_0,
    r, w, small, mix, cosine, sine, seg_col, seg_row, ints, prio_row, grad_y,
    out, picked, after, qkv, probs_att, attended, packed, slot_pair, buffer, grad_buffer,
):
    _, gain_second, vec_rows = small_rows_of(small_0)
    out[...] = combine(
        after_0[...], packed_0[...], slots_0[...], ints_0[...], blocks_0, gain_second, vec_rows, dims, picked
    ).astype(BF16)
    attend_kernel(
        dims, out, r, w, small, mix, cosine, sine, seg_col, seg_row, ints, prio_row,
        after, qkv, probs_att, attended, packed, slot_pair, None, buffer,
    )
    give_back(grad_y[...], packed[...], slot_pair[...], dims, grad_buffer)


def turn_kernel(
    dims, grad_y, after, packed, slot_pair, ints, made, blocks, r, w, small, mix, x, qkv, probs_att, attended,
    cosine, sine, packed_0, slots_0,
    out, grad_x, grad_r, grad_mix, grads, buffer, grad_qkv, picked,
):
    _, gain_second, vec_rows = small_rows_of(small)
    out[...] = combine(
        after[...], packed[...], slot_pair[...], ints[...], made, gain_second, vec_rows, dims, picked
    ).astype(BF16)
    back_kernel(
        dims, grad_y, None, after, packed, slot_pair, ints, picked, blocks, r, w, small, mix, x, qkv, probs_att, attended,
        cosine, sine, grad_x, grad_r, grad_mix, grads, grad_qkv,
    )
    give_back(grad_x[...].astype(BF16).astype(F32), packed_0[...], slots_0[...], dims, buffer)


def back_kernel(
    dims, grad_y, grad_log, after, packed, slot_pair, ints, picked, blocks, r, w, small, mix, x, qkv, probs_att, attended,
    cosine, sine, grad_x, grad_r, grad_mix, grads, grad_qkv,
):
    gain_first, gain_second, vec_rows = small_rows_of(small)
    grad_log_v = 0.0 if grad_log is None else grad_log[...].astype(BF16).astype(F32)
    grad_y_v = grad_y[...] if grad_log is None else grad_y[...].astype(BF16).astype(F32)
    grad_after, grad_r_v, grad_mix_v, small_rows = moe_back(
        grad_y_v, grad_log_v, after[...], packed[...], slot_pair[...], ints[...], picked,
        blocks, r[...].astype(F32), small[...], mix[...], gain_second, vec_rows, dims,
    )
    grad_r[...] = grad_r_v
    grad_mix[...] = grad_mix_v
    grad_x[...] = attention_back(
        grad_after, x[...].astype(F32), qkv, probs_att, attended, small_rows, w, gain_first, cosine[...], sine[...],
        grads, grad_qkv,
    )


def shaped(shape, dtype):
    return jax.ShapeDtypeStruct(shape, dtype)


def run(kernel, out, args, flops=0, scratch=()):
    return pl.pallas_call(
        kernel,
        out_shape=out,
        in_specs=[pl.BlockSpec(memory_space=pltpu.VMEM) for _ in args],
        out_specs=[pl.BlockSpec(memory_space=pltpu.VMEM) for _ in out],
        scratch_shapes=list(scratch),
        compiler_params=pltpu.CompilerParams(vmem_limit_bytes=VMEM_BYTES),
        cost_estimate=pl.CostEstimate(flops=flops, bytes_accessed=8 << 20, transcendentals=0),
    )(*args)


MESH = pl.DeviceIdType.MESH


class Exchange:
    def __init__(self, stream, sent, groups, partial, sibling_part, onward, pair_part, summed, result, sems):
        self.stream, self.sent, self.groups = stream, sent, groups
        self.partial, self.sibling_part, self.onward = partial, sibling_part, onward
        self.pair_part, self.summed, self.result = pair_part, summed, result
        (self.column_s, self.column_r, self.pair_s, self.pair_r, self.core_s, self.core_r, self.last_s, self.last_r,
         self.local_sem, self.back_s, self.back_r, self.over_s, self.over_r, self.home_s, self.home_r) = sems
        self.core, self.column, self.place = lax.axis_index("section"), lax.axis_index("expert"), lax.axis_index("shard")
        self.owners = lax.axis_size("expert")
        self.sibling = (1 - self.core, self.column, self.place)
        self.pair = (self.core, self.column, self.place + 1 - 2 * lax.rem(self.place, 2))

    def peer(self, column):
        return (self.core, column, self.place)

    def turn(self, by):
        return lax.rem(self.column + by + self.owners, self.owners)

    def to_column(self, by):
        return pltpu.make_async_remote_copy(
            self.sent.at[self.turn(by)], self.groups.at[0, self.column],
            self.column_s.at[self.stream, by], self.column_r.at[self.stream, by],
            device_id=self.peer(self.turn(by)), device_id_type=MESH,
        )

    def from_column(self, by):
        source = self.turn(-by)
        return pltpu.make_async_remote_copy(
            self.sent.at[source], self.groups.at[0, source],
            self.column_s.at[self.stream, by], self.column_r.at[self.stream, by],
            device_id=self.peer(source), device_id_type=MESH,
        )

    def own_block(self):
        return pltpu.make_async_copy(
            self.sent.at[self.column], self.groups.at[0, self.column], self.local_sem.at[self.stream]
        )

    def forward(self, by, here, there, device, send, recv):
        block = self.turn(-by)
        return pltpu.make_async_remote_copy(
            self.groups.at[here, block], self.groups.at[there, block],
            send.at[self.stream, by], recv.at[self.stream, by], device_id=device, device_id_type=MESH,
        )

    def to_pair(self, by):
        return self.forward(by, 0, 2, self.pair, self.pair_s, self.pair_r)

    def to_core(self, by):
        return self.forward(by, 0, 1, self.sibling, self.core_s, self.core_r)

    def to_core_last(self, by):
        return self.forward(by, 2, 3, self.sibling, self.last_s, self.last_r)

    def start(self):
        for by in range(1, self.owners):
            self.to_column(by).start()
        self.own_block().start()

    def spread(self):
        for by in range(self.owners):
            if by:
                self.from_column(by).wait_recv()
            else:
                self.own_block().wait()
            self.to_pair(by).start()
            self.to_core(by).start()

    def near_ready(self):
        for by in range(self.owners):
            self.to_core(by).wait_recv()

    def spread_far(self):
        for by in range(self.owners):
            self.to_pair(by).wait_recv()
            self.to_core_last(by).start()

    def far_ready(self):
        for by in range(self.owners):
            self.to_core_last(by).wait_recv()

    def finish_dispatch(self):
        for by in range(self.owners):
            if by:
                self.to_column(by).wait_send()
            self.to_pair(by).wait_send()
            self.to_core(by).wait_send()
            self.to_core_last(by).wait_send()

    def to_sibling(self, half):
        return pltpu.make_async_remote_copy(
            self.partial.at[2 * half + 1], self.sibling_part.at[half],
            self.back_s.at[self.stream, half], self.back_r.at[self.stream, half],
            device_id=self.sibling, device_id_type=MESH,
        )

    def over_pair(self):
        return pltpu.make_async_remote_copy(
            self.onward, self.pair_part, self.over_s.at[self.stream], self.over_r.at[self.stream],
            device_id=self.pair, device_id_type=MESH,
        )

    def home(self, by):
        return pltpu.make_async_remote_copy(
            self.summed.at[self.turn(by)], self.result.at[self.column],
            self.home_s.at[self.stream, by], self.home_r.at[self.stream, by],
            device_id=self.peer(self.turn(by)), device_id_type=MESH,
        )

    def home_here(self, by):
        source = self.turn(-by)
        return pltpu.make_async_remote_copy(
            self.summed.at[source], self.result.at[source],
            self.home_s.at[self.stream, by], self.home_r.at[self.stream, by],
            device_id=self.peer(source), device_id_type=MESH,
        )

    def return_far(self):
        self.to_sibling(1).wait_recv()
        self.onward[...] = (self.partial[2].astype(F32) + self.sibling_part[1].astype(F32)).astype(BF16)
        self.over_pair().start()

    def return_home(self):
        self.to_sibling(0).wait_recv()
        near = self.partial[0].astype(F32) + self.sibling_part[0].astype(F32)
        self.over_pair().wait_recv()
        self.summed[...] = (near + self.pair_part[...].astype(F32)).astype(BF16)
        for by in range(1, self.owners):
            self.home(by).start()
        self.result[self.column] = self.summed[self.column]

    def finish(self):
        for by in range(1, self.owners):
            self.home_here(by).wait_recv()
            self.home(by).wait_send()
        self.over_pair().wait_send()
        self.to_sibling(0).wait_send()
        self.to_sibling(1).wait_send()


def greet(exchange):
    barrier = pltpu.get_barrier_semaphore()
    owners = exchange.owners
    for by in range(1, owners):
        pl.semaphore_signal(barrier, inc=1, device_id=exchange.peer(exchange.turn(by)), device_id_type=MESH)
    pl.semaphore_signal(barrier, inc=1, device_id=exchange.sibling, device_id_type=MESH)
    pl.semaphore_signal(barrier, inc=1, device_id=exchange.pair, device_id_type=MESH)
    pl.semaphore_wait(barrier, owners + 1)


def exchange_scratch(streams, owners, room, width):
    block = (owners, room, width)
    shapes = []
    for _ in range(streams):
        shapes += [
            pltpu.VMEM((4,) + block, BF16),
            pltpu.VMEM((4,) + block, BF16),
            pltpu.VMEM((2,) + block, BF16),
            pltpu.VMEM(block, BF16),
            pltpu.VMEM(block, BF16),
            pltpu.VMEM(block, BF16),
            pltpu.VMEM(block, BF16),
        ]
    dma = pltpu.SemaphoreType.DMA
    shapes += [dma((streams, owners)) for _ in range(8)] + [dma((streams,))]
    shapes += [dma((streams, 2)) for _ in range(2)] + [dma((streams,)) for _ in range(2)] + [dma((streams, owners)) for _ in range(2)]
    return shapes


def exchanges(streams, sent, scratch):
    sems = scratch[7 * streams :]
    return [Exchange(i, sent[i], *scratch[7 * i : 7 * i + 7], sems) for i in range(streams)]


def half_rows(ref, half):
    groups, owners, room, width = ref.shape
    return ref[2 * half : 2 * half + 2].reshape(2 * owners * room, width)


def set_half(ref, half, value):
    groups, owners, room, width = ref.shape
    ref[2 * half : 2 * half + 2] = value.astype(BF16).reshape(2, owners, room, width)


def experts_forward_half(rows, w_in, w_out):
    total = 0.0
    for chunk in range(w_out.shape[0] // CHUNK):
        both = mm(rows, w_in[:, 2 * CHUNK * chunk : 2 * CHUNK * (chunk + 1)])
        gate = both[:, :CHUNK]
        hidden = (gate * jax.nn.sigmoid(gate) * both[:, CHUNK:]).astype(BF16)
        total = total + mm(hidden, w_out[CHUNK * chunk : CHUNK * (chunk + 1)])
    return total


def experts_kernel(buffer, w_in, w_out, returned, arrived, *scratch):
    (tokens,) = exchanges(1, [buffer], scratch)
    greet(tokens)
    tokens.start()
    tokens.spread()
    tokens.near_ready()
    set_half(tokens.partial, 0, experts_forward_half(half_rows(tokens.groups, 0), w_in, w_out))
    tokens.to_sibling(0).start()
    tokens.spread_far()
    tokens.far_ready()
    set_half(tokens.partial, 1, experts_forward_half(half_rows(tokens.groups, 1), w_in, w_out))
    tokens.to_sibling(1).start()
    tokens.return_far()
    arrived[...] = tokens.groups[...]
    tokens.return_home()
    tokens.finish_dispatch()
    tokens.finish()
    returned[...] = tokens.result[...]


def keep_forward(half, rows, w_in, both_ref, hidden_ref):
    count = rows.shape[0]
    at = half * count
    for chunk in range(hidden_ref.shape[1] // CHUNK):
        columns = slice(2 * CHUNK * chunk, 2 * CHUNK * (chunk + 1))
        both = mm(rows, w_in[:, columns])
        gate = both[:, :CHUNK]
        both_ref[at : at + count, columns] = both
        hidden_ref[at : at + count, CHUNK * chunk : CHUNK * (chunk + 1)] = (
            gate * jax.nn.sigmoid(gate) * both[:, CHUNK:]
        ).astype(BF16)


def made_half(half, count, hidden_ref, w_out):
    return mm(hidden_ref[half * count : (half + 1) * count], w_out[...])


def back_half(half, grad_rows, w_in, w_out, both_ref, grad_ref):
    count = grad_rows.shape[0]
    at = half * count
    total = 0.0
    for chunk in range(w_out.shape[0] // CHUNK):
        columns = slice(2 * CHUNK * chunk, 2 * CHUNK * (chunk + 1))
        both = both_ref[at : at + count, columns]
        gate, up = both[:, :CHUNK], both[:, CHUNK:]
        sig = jax.nn.sigmoid(gate)
        grad_hidden = mm(grad_rows, w_out[CHUNK * chunk : CHUNK * (chunk + 1)], NT)
        grad_gate = grad_hidden * up * sig * (1.0 + gate * (1.0 - sig))
        grad_both = jnp.concatenate([grad_gate, grad_hidden * gate * sig], axis=1).astype(BF16)
        grad_ref[at : at + count, columns] = grad_both
        total = total + mm(grad_both, w_in[:, columns], NT)
    return total


def all_rows(ref):
    groups, owners, room, width = ref.shape
    return ref[...].reshape(groups * owners * room, width)


def experts_both_kernel(buffer, grad_buffer, w_in, w_out, made, returned, grad_in, grad_out, both_ref, hidden_ref, grad_ref, *scratch):
    tokens, grads = exchanges(2, [buffer, grad_buffer], scratch)
    count = both_ref.shape[0] // 2
    greet(tokens)
    tokens.start()
    grads.start()
    tokens.spread()
    grads.spread()
    tokens.near_ready()
    keep_forward(0, half_rows(tokens.groups, 0), w_in, both_ref, hidden_ref)
    set_half(tokens.partial, 0, made_half(0, count, hidden_ref, w_out))
    tokens.to_sibling(0).start()
    grads.near_ready()
    set_half(grads.partial, 0, back_half(0, half_rows(grads.groups, 0), w_in, w_out, both_ref, grad_ref))
    grads.to_sibling(0).start()
    tokens.spread_far()
    grads.spread_far()
    tokens.far_ready()
    keep_forward(1, half_rows(tokens.groups, 1), w_in, both_ref, hidden_ref)
    set_half(tokens.partial, 1, made_half(1, count, hidden_ref, w_out))
    tokens.to_sibling(1).start()
    grads.far_ready()
    set_half(grads.partial, 1, back_half(1, half_rows(grads.groups, 1), w_in, w_out, both_ref, grad_ref))
    grads.to_sibling(1).start()
    tokens.return_far()
    grads.return_far()
    grad_out[...] = mm(hidden_ref[...], all_rows(grads.groups), TN).astype(BF16)
    tokens.return_home()
    grads.return_home()
    for chunk in range(grad_in.shape[1] // (2 * CHUNK)):
        columns = slice(2 * CHUNK * chunk, 2 * CHUNK * (chunk + 1))
        grad_in[:, columns] = mm(all_rows(tokens.groups), grad_ref[:, columns], TN).astype(BF16)
    for one in (tokens, grads):
        one.finish_dispatch()
        one.finish()
    made[...] = tokens.result[...]
    returned[...] = grads.result[...]


def experts_back_kernel(grad_buffer, arrived, w_in, w_out, returned, grad_in, grad_out, both_ref, hidden_ref, grad_ref, *scratch):
    (grads,) = exchanges(1, [grad_buffer], scratch)
    greet(grads)
    grads.start()
    grads.spread()
    keep_forward(0, half_rows(arrived, 0), w_in, both_ref, hidden_ref)
    grads.near_ready()
    set_half(grads.partial, 0, back_half(0, half_rows(grads.groups, 0), w_in, w_out, both_ref, grad_ref))
    grads.to_sibling(0).start()
    grads.spread_far()
    keep_forward(1, half_rows(arrived, 1), w_in, both_ref, hidden_ref)
    grads.far_ready()
    set_half(grads.partial, 1, back_half(1, half_rows(grads.groups, 1), w_in, w_out, both_ref, grad_ref))
    grads.to_sibling(1).start()
    grads.return_far()
    grad_out[...] = mm(hidden_ref[...], all_rows(grads.groups), TN).astype(BF16)
    grads.return_home()
    for chunk in range(grad_in.shape[1] // (2 * CHUNK)):
        columns = slice(2 * CHUNK * chunk, 2 * CHUNK * (chunk + 1))
        grad_in[:, columns] = mm(all_rows(arrived), grad_ref[:, columns], TN).astype(BF16)
    grads.finish_dispatch()
    grads.finish()
    returned[...] = grads.result[...]


def run_experts(kernel, identity, streams, blocks, args, out, kept=(), flops=0):
    owners, room, width = blocks
    return pl.pallas_call(
        kernel,
        out_shape=out,
        in_specs=[pl.BlockSpec(memory_space=pltpu.VMEM) for _ in args],
        out_specs=[pl.BlockSpec(memory_space=pltpu.VMEM) for _ in out],
        scratch_shapes=list(kept) + exchange_scratch(streams, owners, room, width),
        compiler_params=pltpu.CompilerParams(
            vmem_limit_bytes=VMEM_BYTES, collective_id=identity, has_side_effects=True
        ),
        cost_estimate=pl.CostEstimate(flops=flops, bytes_accessed=16 << 20, transcendentals=0),
    )(*args)


def local(
    x_in,
    cotangent,
    gate_prev,
    segments,
    routes,
    priority,
    attn_qkv,
    attn_out,
    router,
    const_proj,
    const_vec,
    gains,
    gate_mix,
    expert_in,
    expert_out,
):
    seq_len, width = x_in.shape[2:]
    nexp = gate_prev.shape[-1]
    owners, pieces = lax.axis_size("expert"), lax.axis_size("shard")
    nffn = owners * expert_in.shape[1]
    nconst = const_vec.shape[-1]
    capacity = (5 * TOP * seq_len + 4 * nexp - 1) // (4 * nexp)
    room = -(-capacity // 16) * 16
    slots = nffn * room
    core = lax.axis_index("section")
    first_core = core == 0

    def swap(item):
        return lax.ppermute(item, "section", [(0, 1), (1, 0)])

    def mine(stack, axis=0):
        return lax.dynamic_index_in_dim(stack, core, axis, keepdims=False)

    def others(stack, axis=0):
        return lax.dynamic_index_in_dim(stack, 1 - core, axis, keepdims=False)

    def by_section(own, other):
        return jnp.where(first_core, own, other), jnp.where(first_core, other, own)

    in_rows, columns = expert_in.shape[2:]
    hidden_here = expert_out.shape[2] // 2
    pairs = pieces // 2
    quarter = pairs * hidden_here
    chunks = quarter // CHUNK
    pair_index = lax.axis_index("shard") // 2
    w_in = expert_in[0, 0].reshape(in_rows, 2, pairs, 2, 2, hidden_here)

    def as_chunks(half):
        half = jnp.moveaxis(half, 3, 0).reshape(2, in_rows, 2, chunks, CHUNK)
        return jnp.swapaxes(half, 2, 3).reshape(2, in_rows, 2 * quarter)

    w_out = expert_out[0, 0].reshape(2, hidden_here, width)
    ins = by_section(as_chunks(mine(w_in, 4)), swap(as_chunks(others(w_in, 4))))
    outs = by_section(mine(w_out), swap(others(w_out)))

    def across(piece, hops):
        return lax.ppermute(piece, "shard", [(i, (i + 2 * hops) % pieces) for i in range(pieces)])

    def whole_experts(in_pieces, out_piece):
        sent = jnp.tile(in_pieces, (pairs, 1, 1))
        got = lax.all_to_all(sent, "shard", split_axis=0, concat_axis=0, tiled=True)
        parts = jnp.stack([out_piece] + [across(out_piece, hops) for hops in range(1, pairs)])
        parts = jnp.stack(
            [lax.dynamic_index_in_dim(parts, (pair_index - i) % pairs, 0, False) for i in range(pairs)]
        )
        return got.reshape(pieces * in_rows, 2 * quarter), parts.reshape(quarter, width)

    def split_grads(grad_in, grad_out):
        got = lax.all_to_all(
            grad_in.reshape(pieces, in_rows, 2 * quarter), "shard", split_axis=0, concat_axis=0, tiled=True
        )
        in_sum = jnp.sum(got.reshape(pairs, 2, in_rows, 2 * quarter).astype(F32), axis=0).astype(BF16)
        grad_out = grad_out.reshape(pairs, hidden_here, width)

        def piece(hops):
            return lax.dynamic_index_in_dim(grad_out, (pair_index + hops) % pairs, 0, False)

        out_sum = piece(0).astype(F32)
        for hops in range(1, pairs):
            out_sum = out_sum + across(piece(hops), hops).astype(F32)
        return in_sum, out_sum.astype(BF16)

    experts = [whole_experts(ins[s], outs[s]) for s in range(2)]
    rows = attn_qkv.shape[1]

    def lanes(array, upto):
        return jnp.pad(array, ((0, 0), (0, upto - array.shape[1])))

    small = jnp.concatenate(
        [
            lanes(router[0], AT_PROJ),
            lanes(const_proj[0], AT_VEC - AT_PROJ),
            lanes(const_vec[0], AT_GAIN - AT_VEC),
            lanes(gains[0], LANES - AT_GAIN),
        ],
        axis=1,
    )
    shared = jnp.concatenate([attn_qkv[0], attn_out[0], small], axis=1)
    shared = lax.all_gather(shared, ("expert", "shard"), axis=0, tiled=True)
    shared = by_section(shared, swap(shared))
    mix_own = jnp.pad(gate_mix[0], ((0, LANES - nexp), (0, LANES - nexp)))
    mix_all = by_section(mix_own, swap(mix_own))
    ints_own = jnp.concatenate([routes[0, :, 0], priority[0, :, 0, :, None]], axis=-1)
    ints_all = by_section(mine(ints_own), swap(others(ints_own)))
    x_first = mine(x_in[:, 0])
    r_first = jnp.pad(mine(gate_prev[:, 0]), ((0, 0), (0, LANES - nexp)))
    upstream = mine(cotangent[:, 0])
    seg = mine(segments[:, 0])
    place = lax.iota(jnp.int32, seq_len)
    start = jnp.sum((seg[None, :] < seg[:, None]).astype(F32), axis=1)
    angles = (place.astype(F32) - start)[:, None] * jnp.exp(
        lax.iota(F32, HEAD // 2) * (-2.0 * math.log(10000.0) / HEAD)
    )[None, :]
    cosine, sine = jnp.cos(angles), jnp.sin(angles)
    cosine = jnp.concatenate([cosine] * 4, axis=1)
    sine = jnp.concatenate([-sine, sine, -sine, sine], axis=1)

    dims = (nffn, nexp, capacity, slots)
    heads = width // HEAD
    blocks = (owners, room, width)
    seg_col, seg_row = seg[:, None], seg[None, :]
    smalls = [w[:, 4 * width :] for w in shared]
    token_f32 = shaped((seq_len, width), F32)
    token_b16 = shaped((seq_len, width), BF16)
    lanes_f32 = shaped((seq_len, LANES), F32)
    slot_shape = shaped((slots, width), BF16)
    block_shape = shaped(blocks, BF16)
    attend_out = [
        token_f32,
        shaped((seq_len, 3 * width), BF16),
        shaped((heads, seq_len, seq_len), BF16),
        token_b16,
        lanes_f32,
        shaped((seq_len, LANES), jnp.int32),
    ]
    back_out = [token_f32, lanes_f32, shaped((LANES, LANES), F32), shaped(shared[0].shape, BF16)]
    grad_qkv = pltpu.VMEM((seq_len, 3 * width), BF16)
    prio = [ints[:, 2][None] for ints in ints_all]
    rows_there = 4 * slots
    kept = [
        pltpu.VMEM((rows_there, 2 * quarter), F32),
        pltpu.VMEM((rows_there, quarter), BF16),
        pltpu.VMEM((rows_there, 2 * quarter), BF16),
    ]
    grad_shapes = [shaped((width, 2 * quarter), BF16), shaped((quarter, width), BF16)]
    work = 2 * rows_there * width * quarter

    w, ints = shared[0], ints_all[0]
    after_0, qkv_0, probs_0, attended_0, packed_0, slots_0, r_next, buffer = run(
        functools.partial(attend_kernel, dims),
        attend_out + [shaped((seq_len, LANES), BF16), slot_shape],
        (x_first, r_first, w, smalls[0], mix_all[0], cosine, sine, seg_col, seg_row, ints, prio[0]),
        flops=2 << 30,
    )
    returned, arrived = run_experts(
        experts_kernel, 0, 1, blocks, (buffer.reshape(blocks), *experts[0]),
        [block_shape, shaped((4,) + blocks, BF16)], flops=3 * work,
    )
    out_0, picked_0, after_1, qkv_1, probs_1, attended_1, packed_1, slots_1, buffer, grad_buffer = run(
        functools.partial(middle_kernel, dims),
        [token_b16, shaped((TOP, seq_len, width), BF16)] + attend_out + [slot_shape, slot_shape],
        (
            after_0, packed_0, slots_0, ints, returned.reshape(slots, width), smalls[0],
            r_next, shared[1], smalls[1], mix_all[1], cosine, sine, seg_col, seg_row, ints_all[1], prio[1], upstream,
        ),
        flops=3 << 30,
    )
    made, returned, grad_in_1, grad_out_1 = run_experts(
        experts_both_kernel, 1, 2, blocks, (buffer.reshape(blocks), grad_buffer.reshape(blocks), *experts[1]),
        [block_shape, block_shape] + grad_shapes, kept, flops=9 * work,
    )
    sums_1 = split_grads(grad_in_1, grad_out_1)
    out_1, grad_x_1, grad_r_1, grad_mix_1, grads_1, buffer = run(
        functools.partial(turn_kernel, dims),
        [token_b16] + back_out + [slot_shape],
        (
            upstream, after_1, packed_1, slots_1, ints_all[1], made.reshape(slots, width), returned.reshape(slots, width),
            r_next, shared[1], smalls[1], mix_all[1], out_0, qkv_1, probs_1, attended_1, cosine, sine, packed_0, slots_0,
        ),
        flops=5 << 30,
        scratch=[grad_qkv, pltpu.VMEM((TOP, seq_len, width), BF16)],
    )
    returned, grad_in_0, grad_out_0 = run_experts(
        experts_back_kernel, 2, 1, blocks, (buffer.reshape(blocks), arrived, *experts[0]),
        [block_shape] + grad_shapes, kept, flops=9 * work,
    )
    sums_0 = split_grads(grad_in_0, grad_out_0)
    grad_x_0, grad_r_0, grad_mix_0, grads_0 = run(
        functools.partial(back_kernel, dims),
        back_out,
        (
            grad_x_1, grad_r_1, after_0, packed_0, slots_0, ints, picked_0, returned.reshape(slots, width),
            r_first, w, smalls[0], mix_all[0], x_first, qkv_0, probs_0, attended_0, cosine, sine,
        ),
        flops=5 << 30,
        scratch=[grad_qkv],
    )
    results, x_grads = (out_0, out_1), (grad_x_0, grad_x_1)
    r_grads = (grad_r_0[:, :nexp], grad_r_1[:, :nexp])
    sums = []
    for grads, grad_mix, expert_sums in ((grads_0, grad_mix_0, sums_0), (grads_1, grad_mix_1, sums_1)):
        mix_lanes = -(-nexp * nexp // rows)
        mix_flat = jnp.pad(grad_mix[:nexp, :nexp].reshape(-1), (0, rows * mix_lanes - nexp * nexp)).reshape(rows, mix_lanes)
        mix_tile = jnp.tile(mix_flat, (owners * pieces, 1)).astype(BF16)
        at = 4 * width + AT_MIX
        grads = lax.dynamic_update_slice(grads, mix_tile, (0, at))
        sums.append((grads, *expert_sums))
    shared_own = jnp.where(first_core, sums[0][0], sums[1][0])
    shared_other = jnp.where(first_core, sums[1][0], sums[0][0])
    shared_sum = (shared_own.astype(F32) + swap(shared_other).astype(F32)).astype(BF16)
    shared_sum = lax.psum_scatter(shared_sum, ("expert", "shard"), scatter_dimension=0, tiled=True).astype(F32)

    def halves(index):
        own = jnp.where(first_core, sums[0][index], sums[1][index])
        got = swap(jnp.where(first_core, sums[1][index], sums[0][index]))
        return jnp.where(first_core, own, got).astype(F32), jnp.where(first_core, got, own).astype(F32)

    def from_chunks(half):
        half = jnp.swapaxes(half.reshape(2, in_rows, chunks, 2, CHUNK), 2, 3)
        return jnp.moveaxis(half.reshape(2, in_rows, 2, pairs, hidden_here), 0, 3)

    in_grad = jnp.stack([from_chunks(half) for half in halves(1)], axis=4).reshape(in_rows, columns)
    out_grad = jnp.concatenate(halves(2), axis=0)

    def both_batches(pair):
        own = jnp.where(first_core, pair[0], pair[1])
        got = swap(jnp.where(first_core, pair[1], pair[0]))
        return jnp.stack(by_section(own, got))[None, :, None]

    small_sum = shared_sum[:, 4 * width :]
    mix_grad = small_sum[:, AT_MIX : AT_MIX + mix_lanes].reshape(-1)[: nexp * nexp].reshape(nexp, nexp)
    return (
        both_batches(results),
        both_batches(x_grads),
        both_batches(r_grads),
        shared_sum[None, :, : 3 * width],
        shared_sum[None, :, 3 * width : 4 * width],
        small_sum[None, :, :nexp],
        small_sum[None, :, AT_PROJ : AT_PROJ + const_proj.shape[-1]],
        small_sum[None, :, AT_VEC : AT_VEC + nconst],
        small_sum[None, :, AT_GAIN : AT_GAIN + 2],
        mix_grad[None],
        in_grad[None, None],
        out_grad[None, None],
    )


def solution(mesh):
    placed = (
        P(None, ("expert", "shard"), None, None),
        P(None, ("expert", "shard"), None, None),
        P(None, ("expert", "shard"), None, None),
        P(None, ("expert", "shard"), None),
        P("section", None, ("expert", "shard"), None, None),
        P("section", None, ("expert", "shard"), None),
        P("section", ("expert", "shard"), None),
        P("section", ("expert", "shard"), None),
        P("section", ("expert", "shard"), None),
        P("section", ("expert", "shard"), None),
        P("section", ("expert", "shard"), None),
        P("section", ("expert", "shard"), None),
        P("section", None, None),
        P("section", "expert", "shard", None),
        P("section", "expert", "shard", None),
    )
    return jax.shard_map(
        local,
        mesh=mesh,
        in_specs=placed,
        out_specs=(
            P("section", None, ("expert", "shard"), None, None),
            P("section", None, ("expert", "shard"), None, None),
            P("section", None, ("expert", "shard"), None, None),
            P("section", ("expert", "shard"), None),
            P("section", ("expert", "shard"), None),
            P("section", ("expert", "shard"), None),
            P("section", ("expert", "shard"), None),
            P("section", ("expert", "shard"), None),
            P("section", ("expert", "shard"), None),
            P("section", None, None),
            P("section", "expert", "shard", None),
            P("section", "expert", "shard", None),
        ),
        check_vma=False,
    )
```

```python
import functools
import math

import jax
import jax.numpy as jnp
from jax import lax
from jax.experimental import pallas as pl
from jax.experimental.pallas import tpu as pltpu
from jax.sharding import PartitionSpec as P

HEADS = 12
HEAD = 64
TOP = 2
CHUNK = 256
LANES = 128
AT_PROJ = 16
AT_VEC = 24
AT_GAIN = 28
AT_MIX = 32

HIGH = lax.Precision.HIGHEST
norm_eps = 1e-06
masked_score = -1e30
F32 = jnp.float32
BF16 = jnp.bfloat16


VMEM_BYTES = 56 * 1024 * 1024


def mm(a, b, contract=((1,), (0,)), precision=None):
    return lax.dot_general(a, b, (contract, ((), ())), precision=precision, preferred_element_type=F32)


NT = ((1,), (1,))
TN = ((0,), (0,))


def lane_of(rows, columns=LANES):
    return lax.broadcasted_iota(jnp.int32, (rows, columns), 1)


def inverse_norm(values):
    return lax.rsqrt(jnp.mean(values * values, axis=-1, keepdims=True) + norm_eps)


def norm_back(grad_unit, unit, inverse):
    return inverse * (grad_unit - unit * jnp.mean(grad_unit * unit, axis=-1, keepdims=True))


def roll(x, by):
    return pltpu.roll(x, by, 1)


def turned(x, lane):
    return jnp.where(lane % HEAD < HEAD // 2, roll(x, LANES - HEAD // 2), roll(x, HEAD // 2))


def hi_lo(x):
    high = x.astype(BF16)
    return high, (x - high.astype(F32)).astype(BF16)


def ones_where(condition):
    return jnp.where(condition, 1.0, 0.0).astype(BF16)


def small_rows_of(small):
    rows = small[...].astype(F32).T
    return rows[AT_GAIN : AT_GAIN + 1], rows[AT_GAIN + 1 : AT_GAIN + 2], rows[AT_VEC:AT_GAIN]


def attention(x, w, gain_first, cosine, sine, seg_col, seg_row, qkv, probs_att, attended):
    seq_len, width = x.shape
    first_b = (x * inverse_norm(x) * gain_first).astype(BF16)
    place_q = lax.broadcasted_iota(jnp.int32, (seq_len, seq_len), 0)
    place_k = lax.broadcasted_iota(jnp.int32, (seq_len, seq_len), 1)
    bias = jnp.where((seg_col == seg_row) & (place_k <= place_q), 0.0, masked_score)
    lane = lane_of(seq_len)
    low_head = lane < HEAD
    for pair in range(width // LANES):
        at = pair * LANES
        q = mm(first_b, w[:, at : at + LANES])
        k = mm(first_b, w[:, width + at : width + at + LANES])
        v = mm(first_b, w[:, 2 * width + at : 2 * width + at + LANES]).astype(BF16)
        q = q * cosine + turned(q, lane) * sine
        k = (k * cosine + turned(k, lane) * sine).astype(BF16)
        outs = []
        for half in range(2):
            one = jnp.where(low_head if half == 0 else lane >= HEAD, q, 0.0).astype(BF16)
            scores = mm(one, k, NT) * (HEAD**-0.5) + bias
            scores = jnp.exp(scores - jnp.max(scores, axis=-1, keepdims=True))
            probs = (scores * (1.0 / jnp.sum(scores, axis=-1, keepdims=True))).astype(BF16)
            probs_att[2 * pair + half] = probs
            outs.append(mm(probs, v))
        attended[:, at : at + LANES] = jnp.where(low_head, outs[0], outs[1]).astype(BF16)
        qkv[:, at : at + LANES] = q.astype(BF16)
        qkv[:, width + at : width + at + LANES] = k
        qkv[:, 2 * width + at : 2 * width + at + LANES] = v
    return x + mm(attended[...], w[:, 3 * width : 4 * width])


def gating(after, r, small, mix, gain_second, ints, prio_row, dims, packed_ref, slot_ref, r_next, buffer):
    nffn, nexp, capacity, slots = dims
    rows = after.shape[0]
    second_b = (after * inverse_norm(after) * gain_second).astype(BF16)
    lane = lane_of(rows)
    logits = mm(second_b, small)
    full = logits + mm(r, mix, precision=HIGH)
    inside = lane < nexp
    full = jnp.where(inside, full, masked_score)
    raised = jnp.exp(full - jnp.max(full, axis=-1, keepdims=True))
    probs = raised / jnp.sum(raised, axis=-1, keepdims=True)
    other = jnp.where(lane % 2 == 0, roll(logits, LANES - 1), roll(logits, 1))
    bigger = jnp.maximum(logits, other)
    mine_e = jnp.exp(logits - bigger)
    mixes = mine_e / (mine_e + jnp.exp(other - bigger))
    before = ones_where(prio_row < ints[:, 2:3])
    route = (ints[:, 0:1], ints[:, 1:2])
    routed = ones_where(((lane == route[0]) | (lane == route[1])) & (lane < nffn))
    rank = mm(before, routed)
    gates, places = [], []
    dispatch = 0.0
    stride = slots // nffn
    for k in range(TOP):
        chosen = lane == route[k]
        gates.append(jnp.sum(jnp.where(chosen, probs, 0.0), axis=-1, keepdims=True))
        rank_k = jnp.sum(jnp.where(chosen, rank, 0.0), axis=-1, keepdims=True).astype(jnp.int32)
        kept = (route[k] < nffn) & (rank_k < capacity)
        places.append(jnp.where(kept, route[k] * stride + rank_k, -1))
        dispatch = dispatch + jnp.where(places[k] == lane_of(rows, slots), 1.0, 0.0)
    buffer[...] = mm(dispatch.astype(BF16), second_b, TN).astype(BF16).reshape(buffer.shape)
    packed = jnp.where(inside, probs, jnp.where((lane >= AT_PROJ) & (lane < AT_VEC), mixes, 0.0))
    packed = jnp.where(lane == AT_VEC, gates[0], packed)
    packed_ref[...] = jnp.where(lane == AT_VEC + 1, gates[1], packed)
    slot_ref[...] = jnp.where(lane == 0, places[0], places[1])
    if r_next is not None:
        r_next[...] = jnp.where(inside, full, 0.0).astype(BF16)


def extras(packed, ints, nffn, nconst):
    gates = (packed[:, AT_VEC : AT_VEC + 1], packed[:, AT_VEC + 1 : AT_VEC + 2])

    def of(expert):
        return sum(jnp.where(ints[:, k : k + 1] == expert, gates[k], 0.0) for k in range(TOP))

    def mixes(c):
        at = AT_PROJ + 2 * c
        return packed[:, at : at + 1], packed[:, at + 1 : at + 2]

    return gates, of(nffn + 1), [of(nffn + 2 + c) for c in range(nconst)], [mixes(c) for c in range(nconst)]


def combine(after, packed, slot_pair, ints, blocks, gain_second, vec_rows, dims, picked_ref):
    nffn, nexp, _, slots = dims
    nconst = nexp - nffn - 2
    rows = after.shape[0]
    second = after * inverse_norm(after) * gain_second
    gates, copied, const, mixes = extras(packed, ints, nffn, nconst)
    made = blocks[...].reshape(slots, after.shape[1])
    slot_lane = lane_of(rows, slots)
    coefficient = copied
    for c in range(nconst):
        coefficient = coefficient + const[c] * mixes[c][0]
    out = after + coefficient * second
    for k in range(TOP):
        picked = mm(ones_where(slot_pair[:, k : k + 1] == slot_lane), made)
        picked_ref[k] = picked.astype(BF16)
        out = out + gates[k] * picked
    for c in range(nconst):
        out = out + (const[c] * mixes[c][1]) * vec_rows[c : c + 1]
    return out


def give_back(grad_y, packed, slot_pair, dims, buffer):
    slots = dims[3]
    slot_lane = lane_of(grad_y.shape[0], slots)
    total = 0.0
    for k in range(TOP):
        gate = packed[:, AT_VEC + k : AT_VEC + k + 1]
        table = ones_where(slot_pair[:, k : k + 1] == slot_lane)
        total = total + mm(table, (gate * grad_y).astype(BF16), TN)
    buffer[...] = total.astype(BF16).reshape(buffer.shape)


def moe_back(
    grad_y, grad_log_in, after, packed, slot_pair, ints, picked, blocks, r, small, mix, gain_second, vec_rows, dims
):
    nffn, nexp, _, slots = dims
    nconst = nexp - nffn - 2
    rows = grad_y.shape[0]
    lane = lane_of(rows)
    inverse = inverse_norm(after)
    unit = after * inverse
    second = unit * gain_second
    second_b = second.astype(BF16)
    gates, copied, const, mixes = extras(packed, ints, nffn, nconst)
    grad_buffer = blocks[...].reshape(slots, after.shape[1])
    slot_lane = lane_of(rows, slots)
    dispatch = sum(jnp.where(slot_pair[:, k : k + 1] == slot_lane, 1.0, 0.0) for k in range(TOP))
    grad_second = mm(dispatch.astype(BF16), grad_buffer)
    along_second = jnp.sum(grad_y * second, axis=-1, keepdims=True)
    coefficient = copied
    grad_extra = [(nffn + 1, along_second)]
    grad_lanes = jnp.zeros((rows, LANES), F32)
    vec_grads = []
    for c in range(nconst):
        along = jnp.sum(grad_y * vec_rows[c : c + 1], axis=-1, keepdims=True)
        m0, m1 = mixes[c]
        coefficient = coefficient + const[c] * m0
        grad_extra.append((nffn + 2 + c, m0 * along_second + m1 * along))
        d0, d1 = const[c] * along_second, const[c] * along
        mean = m0 * d0 + m1 * d1
        at = AT_PROJ + 2 * c
        grad_lanes = jnp.where(lane == at, m0 * (d0 - mean), grad_lanes)
        grad_lanes = jnp.where(lane == at + 1, m1 * (d1 - mean), grad_lanes)
        vec_grads.append(jnp.sum(grad_y * (const[c] * m1), axis=0, keepdims=True))
    grad_second = grad_second + coefficient * grad_y
    grad_probs = jnp.zeros((rows, LANES), F32)
    for k in range(TOP):
        grad_gate = jnp.sum(picked[k].astype(F32) * grad_y, axis=-1, keepdims=True)
        for expert, value in grad_extra:
            grad_gate = grad_gate + jnp.where(ints[:, k : k + 1] == expert, value, 0.0)
        grad_probs = grad_probs + jnp.where(lane == ints[:, k : k + 1], grad_gate, 0.0)
    probs = jnp.where(lane < nexp, packed, 0.0)
    grad_logits = probs * (grad_probs - jnp.sum(probs * grad_probs, axis=-1, keepdims=True)) + grad_log_in
    grad_mix = mm(r, grad_logits, TN, HIGH)
    grad_r = mm(grad_logits, mix, NT, HIGH)
    high, low = hi_lo(jnp.where(lane < nexp, grad_logits, grad_lanes))
    small_rows = mm(high, second_b, TN) + mm(low, second_b, TN)
    grad_second = grad_second + mm(high, small, NT) + mm(low, small, NT)
    grad_gain = jnp.sum(grad_second * unit, axis=0, keepdims=True)
    grad_after = grad_y + norm_back(grad_second * gain_second, unit, inverse)
    row = lax.broadcasted_iota(jnp.int32, small_rows.shape, 0)
    small_rows = jnp.where(row < AT_VEC, small_rows, 0.0)
    for c in range(nconst):
        small_rows = jnp.where(row == AT_VEC + c, vec_grads[c], small_rows)
    small_rows = jnp.where(row == AT_GAIN + 1, grad_gain, small_rows)
    return grad_after, grad_r, grad_mix, small_rows


def attention_back(grad_after, x, qkv, probs_att, attended, small_rows, w, gain_first, cosine, sine, grads, grad_qkv):
    seq_len, width = x.shape
    inverse = inverse_norm(x)
    unit = x * inverse
    first_b = (unit * gain_first).astype(BF16)
    grad_branch = grad_after.astype(BF16)
    grads[:, 3 * width : 4 * width] = mm(attended[...], grad_branch, TN).astype(BF16)
    lane = lane_of(seq_len)
    low_head = lane < HEAD
    masks = (ones_where(low_head), ones_where(lane >= HEAD))
    scale = HEAD**-0.5
    for pair in range(width // LANES):
        at = pair * LANES
        q = qkv[:, at : at + LANES]
        k = qkv[:, width + at : width + at + LANES]
        v = qkv[:, 2 * width + at : 2 * width + at + LANES]
        g = mm(grad_branch, w[at : at + LANES, 3 * width : 4 * width], NT).astype(BF16)
        dq, dk, dv = [], [], []
        for half in range(2):
            probs = probs_att[2 * pair + half]
            grad_p = mm(g * masks[half], v, NT)
            p = probs.astype(F32)
            grad_s = (p * (grad_p - jnp.sum(p * grad_p, axis=-1, keepdims=True))).astype(BF16)
            dv.append(mm(probs, g, TN))
            dq.append(mm(grad_s, k))
            dk.append(mm(grad_s, q, TN))
        dq = jnp.where(low_head, dq[0], dq[1]) * scale
        dk = jnp.where(low_head, dk[0], dk[1]) * scale
        grad_qkv[:, at : at + LANES] = (dq * cosine - turned(dq, lane) * sine).astype(BF16)
        grad_qkv[:, width + at : width + at + LANES] = (dk * cosine - turned(dk, lane) * sine).astype(BF16)
        grad_qkv[:, 2 * width + at : 2 * width + at + LANES] = jnp.where(low_head, dv[0], dv[1]).astype(BF16)
    grads[:, : 3 * width] = mm(first_b, grad_qkv[...], TN).astype(BF16)
    grad_first = mm(grad_qkv[...], w[:, : 3 * width], NT)
    grad_gain = jnp.sum(grad_first * unit, axis=0, keepdims=True)
    grad_x = grad_after + norm_back(grad_first * gain_first, unit, inverse)
    row = lax.broadcasted_iota(jnp.int32, small_rows.shape, 0)
    small_rows = jnp.where(row == AT_GAIN, grad_gain, small_rows)
    grads[:, 4 * width :] = small_rows.T.astype(BF16)
    return grad_x


def attend_kernel(
    dims, x, r, w, small, mix, cosine, sine, seg_col, seg_row, ints, prio_row,
    after, qkv, probs_att, attended, packed, slot_pair, r_next, buffer,
):
    gain_first, gain_second, _ = small_rows_of(small)
    after_v = attention(
        x[...].astype(F32), w, gain_first, cosine[...], sine[...], seg_col[...], seg_row[...], qkv, probs_att, attended
    )
    after[...] = after_v
    gating(
        after_v, r[...].astype(F32), small[...], mix[...], gain_second, ints[...], prio_row[...], dims,
        packed, slot_pair, r_next, buffer,
    )


def middle_kernel(
    dims, after_0, packed_0, slots_0, ints_0, blocks_0, small_0,
    r, w, small, mix, cosine, sine, seg_col, seg_row, ints, prio_row, grad_y,
    out, picked, after, qkv, probs_att, attended, packed, slot_pair, buffer, grad_buffer,
):
    _, gain_second, vec_rows = small_rows_of(small_0)
    out[...] = combine(
        after_0[...], packed_0[...], slots_0[...], ints_0[...], blocks_0, gain_second, vec_rows, dims, picked
    ).astype(BF16)
    attend_kernel(
        dims, out, r, w, small, mix, cosine, sine, seg_col, seg_row, ints, prio_row,
        after, qkv, probs_att, attended, packed, slot_pair, None, buffer,
    )
    give_back(grad_y[...], packed[...], slot_pair[...], dims, grad_buffer)


def turn_kernel(
    dims, grad_y, after, packed, slot_pair, ints, made, blocks, r, w, small, mix, x, qkv, probs_att, attended,
    cosine, sine, packed_0, slots_0,
    out, grad_x, grad_r, grad_mix, grads, buffer, grad_qkv, picked,
):
    _, gain_second, vec_rows = small_rows_of(small)
    out[...] = combine(
        after[...], packed[...], slot_pair[...], ints[...], made, gain_second, vec_rows, dims, picked
    ).astype(BF16)
    back_kernel(
        dims, grad_y, None, after, packed, slot_pair, ints, picked, blocks, r, w, small, mix, x, qkv, probs_att, attended,
        cosine, sine, grad_x, grad_r, grad_mix, grads, grad_qkv,
    )
    give_back(grad_x[...].astype(BF16).astype(F32), packed_0[...], slots_0[...], dims, buffer)


def back_kernel(
    dims, grad_y, grad_log, after, packed, slot_pair, ints, picked, blocks, r, w, small, mix, x, qkv, probs_att, attended,
    cosine, sine, grad_x, grad_r, grad_mix, grads, grad_qkv,
):
    gain_first, gain_second, vec_rows = small_rows_of(small)
    grad_log_v = 0.0 if grad_log is None else grad_log[...].astype(BF16).astype(F32)
    grad_y_v = grad_y[...] if grad_log is None else grad_y[...].astype(BF16).astype(F32)
    grad_after, grad_r_v, grad_mix_v, small_rows = moe_back(
        grad_y_v, grad_log_v, after[...], packed[...], slot_pair[...], ints[...], picked,
        blocks, r[...].astype(F32), small[...], mix[...], gain_second, vec_rows, dims,
    )
    grad_r[...] = grad_r_v
    grad_mix[...] = grad_mix_v
    grad_x[...] = attention_back(
        grad_after, x[...].astype(F32), qkv, probs_att, attended, small_rows, w, gain_first, cosine[...], sine[...],
        grads, grad_qkv,
    )


def shaped(shape, dtype):
    return jax.ShapeDtypeStruct(shape, dtype)


def run(kernel, out, args, flops=0, scratch=()):
    return pl.pallas_call(
        kernel,
        out_shape=out,
        in_specs=[pl.BlockSpec(memory_space=pltpu.VMEM) for _ in args],
        out_specs=[pl.BlockSpec(memory_space=pltpu.VMEM) for _ in out],
        scratch_shapes=list(scratch),
        compiler_params=pltpu.CompilerParams(vmem_limit_bytes=VMEM_BYTES),
        cost_estimate=pl.CostEstimate(flops=flops, bytes_accessed=8 << 20, transcendentals=0),
    )(*args)


MESH = pl.DeviceIdType.MESH


class Exchange:
    def __init__(self, stream, sent, groups, partial, sibling_part, onward, pair_part, summed, result, sems):
        self.stream, self.sent, self.groups = stream, sent, groups
        self.partial, self.sibling_part, self.onward = partial, sibling_part, onward
        self.pair_part, self.summed, self.result = pair_part, summed, result
        (self.column_s, self.column_r, self.pair_s, self.pair_r, self.core_s, self.core_r, self.last_s, self.last_r,
         self.local_sem, self.back_s, self.back_r, self.over_s, self.over_r, self.home_s, self.home_r) = sems
        self.core, self.column, self.place = lax.axis_index("section"), lax.axis_index("expert"), lax.axis_index("shard")
        self.owners = lax.axis_size("expert")
        self.sibling = (1 - self.core, self.column, self.place)
        self.pair = (self.core, self.column, self.place + 1 - 2 * lax.rem(self.place, 2))

    def peer(self, column):
        return (self.core, column, self.place)

    def turn(self, by):
        return lax.rem(self.column + by + self.owners, self.owners)

    def to_column(self, by):
        return pltpu.make_async_remote_copy(
            self.sent.at[self.turn(by)], self.groups.at[0, self.column],
            self.column_s.at[self.stream, by], self.column_r.at[self.stream, by],
            device_id=self.peer(self.turn(by)), device_id_type=MESH,
        )

    def from_column(self, by):
        source = self.turn(-by)
        return pltpu.make_async_remote_copy(
            self.sent.at[source], self.groups.at[0, source],
            self.column_s.at[self.stream, by], self.column_r.at[self.stream, by],
            device_id=self.peer(source), device_id_type=MESH,
        )

    def own_block(self):
        return pltpu.make_async_copy(
            self.sent.at[self.column], self.groups.at[0, self.column], self.local_sem.at[self.stream]
        )

    def forward(self, by, here, there, device, send, recv):
        block = self.turn(-by)
        return pltpu.make_async_remote_copy(
            self.groups.at[here, block], self.groups.at[there, block],
            send.at[self.stream, by], recv.at[self.stream, by], device_id=device, device_id_type=MESH,
        )

    def to_pair(self, by):
        return self.forward(by, 0, 2, self.pair, self.pair_s, self.pair_r)

    def to_core(self, by):
        return self.forward(by, 0, 1, self.sibling, self.core_s, self.core_r)

    def to_core_last(self, by):
        return self.forward(by, 2, 3, self.sibling, self.last_s, self.last_r)

    def start(self):
        for by in range(1, self.owners):
            self.to_column(by).start()
        self.own_block().start()

    def spread(self):
        for by in range(self.owners):
            if by:
                self.from_column(by).wait_recv()
            else:
                self.own_block().wait()
            self.to_pair(by).start()
            self.to_core(by).start()

    def near_ready(self):
        for by in range(self.owners):
            self.to_core(by).wait_recv()

    def spread_far(self):
        for by in range(self.owners):
            self.to_pair(by).wait_recv()
            self.to_core_last(by).start()

    def far_ready(self):
        for by in range(self.owners):
            self.to_core_last(by).wait_recv()

    def finish_dispatch(self):
        for by in range(self.owners):
            if by:
                self.to_column(by).wait_send()
            self.to_pair(by).wait_send()
            self.to_core(by).wait_send()
            self.to_core_last(by).wait_send()

    def to_sibling(self, half):
        return pltpu.make_async_remote_copy(
            self.partial.at[2 * half + 1], self.sibling_part.at[half],
            self.back_s.at[self.stream, half], self.back_r.at[self.stream, half],
            device_id=self.sibling, device_id_type=MESH,
        )

    def over_pair(self):
        return pltpu.make_async_remote_copy(
            self.onward, self.pair_part, self.over_s.at[self.stream], self.over_r.at[self.stream],
            device_id=self.pair, device_id_type=MESH,
        )

    def home(self, by):
        return pltpu.make_async_remote_copy(
            self.summed.at[self.turn(by)], self.result.at[self.column],
            self.home_s.at[self.stream, by], self.home_r.at[self.stream, by],
            device_id=self.peer(self.turn(by)), device_id_type=MESH,
        )

    def home_here(self, by):
        source = self.turn(-by)
        return pltpu.make_async_remote_copy(
            self.summed.at[source], self.result.at[source],
            self.home_s.at[self.stream, by], self.home_r.at[self.stream, by],
            device_id=self.peer(source), device_id_type=MESH,
        )

    def return_far(self):
        self.to_sibling(1).wait_recv()
        self.onward[...] = (self.partial[2].astype(F32) + self.sibling_part[1].astype(F32)).astype(BF16)
        self.over_pair().start()

    def return_home(self):
        self.to_sibling(0).wait_recv()
        near = self.partial[0].astype(F32) + self.sibling_part[0].astype(F32)
        self.over_pair().wait_recv()
        self.summed[...] = (near + self.pair_part[...].astype(F32)).astype(BF16)
        for by in range(1, self.owners):
            self.home(by).start()
        self.result[self.column] = self.summed[self.column]

    def finish(self):
        for by in range(1, self.owners):
            self.home_here(by).wait_recv()
            self.home(by).wait_send()
        self.over_pair().wait_send()
        self.to_sibling(0).wait_send()
        self.to_sibling(1).wait_send()


def greet(exchange):
    barrier = pltpu.get_barrier_semaphore()
    owners = exchange.owners
    for by in range(1, owners):
        pl.semaphore_signal(barrier, inc=1, device_id=exchange.peer(exchange.turn(by)), device_id_type=MESH)
    pl.semaphore_signal(barrier, inc=1, device_id=exchange.sibling, device_id_type=MESH)
    pl.semaphore_signal(barrier, inc=1, device_id=exchange.pair, device_id_type=MESH)
    pl.semaphore_wait(barrier, owners + 1)


def exchange_scratch(streams, owners, room, width):
    block = (owners, room, width)
    shapes = []
    for _ in range(streams):
        shapes += [
            pltpu.VMEM((4,) + block, BF16),
            pltpu.VMEM((4,) + block, BF16),
            pltpu.VMEM((2,) + block, BF16),
            pltpu.VMEM(block, BF16),
            pltpu.VMEM(block, BF16),
            pltpu.VMEM(block, BF16),
            pltpu.VMEM(block, BF16),
        ]
    dma = pltpu.SemaphoreType.DMA
    shapes += [dma((streams, owners)) for _ in range(8)] + [dma((streams,))]
    shapes += [dma((streams, 2)) for _ in range(2)] + [dma((streams,)) for _ in range(2)] + [dma((streams, owners)) for _ in range(2)]
    return shapes


def exchanges(streams, sent, scratch):
    sems = scratch[7 * streams :]
    return [Exchange(i, sent[i], *scratch[7 * i : 7 * i + 7], sems) for i in range(streams)]


def half_rows(ref, half):
    groups, owners, room, width = ref.shape
    return ref[2 * half : 2 * half + 2].reshape(2 * owners * room, width)


def set_half(ref, half, value):
    groups, owners, room, width = ref.shape
    ref[2 * half : 2 * half + 2] = value.astype(BF16).reshape(2, owners, room, width)


def experts_forward_half(rows, w_in, w_out):
    total = 0.0
    for chunk in range(w_out.shape[0] // CHUNK):
        both = mm(rows, w_in[:, 2 * CHUNK * chunk : 2 * CHUNK * (chunk + 1)])
        gate = both[:, :CHUNK]
        hidden = (gate * jax.nn.sigmoid(gate) * both[:, CHUNK:]).astype(BF16)
        total = total + mm(hidden, w_out[CHUNK * chunk : CHUNK * (chunk + 1)])
    return total


def experts_kernel(buffer, w_in, w_out, returned, arrived, *scratch):
    (tokens,) = exchanges(1, [buffer], scratch)
    greet(tokens)
    tokens.start()
    tokens.spread()
    tokens.near_ready()
    set_half(tokens.partial, 0, experts_forward_half(half_rows(tokens.groups, 0), w_in, w_out))
    tokens.to_sibling(0).start()
    tokens.spread_far()
    tokens.far_ready()
    set_half(tokens.partial, 1, experts_forward_half(half_rows(tokens.groups, 1), w_in, w_out))
    tokens.to_sibling(1).start()
    tokens.return_far()
    arrived[...] = tokens.groups[...]
    tokens.return_home()
    tokens.finish_dispatch()
    tokens.finish()
    returned[...] = tokens.result[...]


def keep_forward(half, rows, w_in, both_ref, hidden_ref):
    count = rows.shape[0]
    at = half * count
    for chunk in range(hidden_ref.shape[1] // CHUNK):
        columns = slice(2 * CHUNK * chunk, 2 * CHUNK * (chunk + 1))
        both = mm(rows, w_in[:, columns])
        gate = both[:, :CHUNK]
        both_ref[at : at + count, columns] = both
        hidden_ref[at : at + count, CHUNK * chunk : CHUNK * (chunk + 1)] = (
            gate * jax.nn.sigmoid(gate) * both[:, CHUNK:]
        ).astype(BF16)


def made_half(half, count, hidden_ref, w_out):
    return mm(hidden_ref[half * count : (half + 1) * count], w_out[...])


def back_half(half, grad_rows, w_in, w_out, both_ref, grad_ref):
    count = grad_rows.shape[0]
    at = half * count
    total = 0.0
    for chunk in range(w_out.shape[0] // CHUNK):
        columns = slice(2 * CHUNK * chunk, 2 * CHUNK * (chunk + 1))
        both = both_ref[at : at + count, columns]
        gate, up = both[:, :CHUNK], both[:, CHUNK:]
        sig = jax.nn.sigmoid(gate)
        grad_hidden = mm(grad_rows, w_out[CHUNK * chunk : CHUNK * (chunk + 1)], NT)
        grad_gate = grad_hidden * up * sig * (1.0 + gate * (1.0 - sig))
        grad_both = jnp.concatenate([grad_gate, grad_hidden * gate * sig], axis=1).astype(BF16)
        grad_ref[at : at + count, columns] = grad_both
        total = total + mm(grad_both, w_in[:, columns], NT)
    return total


def all_rows(ref):
    groups, owners, room, width = ref.shape
    return ref[...].reshape(groups * owners * room, width)


def experts_both_kernel(buffer, grad_buffer, w_in, w_out, made, returned, grad_in, grad_out, both_ref, hidden_ref, grad_ref, *scratch):
    tokens, grads = exchanges(2, [buffer, grad_buffer], scratch)
    count = both_ref.shape[0] // 2
    greet(tokens)
    tokens.start()
    grads.start()
    tokens.spread()
    grads.spread()
    tokens.near_ready()
    keep_forward(0, half_rows(tokens.groups, 0), w_in, both_ref, hidden_ref)
    set_half(tokens.partial, 0, made_half(0, count, hidden_ref, w_out))
    tokens.to_sibling(0).start()
    grads.near_ready()
    set_half(grads.partial, 0, back_half(0, half_rows(grads.groups, 0), w_in, w_out, both_ref, grad_ref))
    grads.to_sibling(0).start()
    tokens.spread_far()
    grads.spread_far()
    tokens.far_ready()
    keep_forward(1, half_rows(tokens.groups, 1), w_in, both_ref, hidden_ref)
    set_half(tokens.partial, 1, made_half(1, count, hidden_ref, w_out))
    tokens.to_sibling(1).start()
    grads.far_ready()
    set_half(grads.partial, 1, back_half(1, half_rows(grads.groups, 1), w_in, w_out, both_ref, grad_ref))
    grads.to_sibling(1).start()
    tokens.return_far()
    grads.return_far()
    grad_out[...] = mm(hidden_ref[...], all_rows(grads.groups), TN).astype(BF16)
    tokens.return_home()
    grads.return_home()
    for chunk in range(grad_in.shape[1] // (2 * CHUNK)):
        columns = slice(2 * CHUNK * chunk, 2 * CHUNK * (chunk + 1))
        grad_in[:, columns] = mm(all_rows(tokens.groups), grad_ref[:, columns], TN).astype(BF16)
    for one in (tokens, grads):
        one.finish_dispatch()
        one.finish()
    made[...] = tokens.result[...]
    returned[...] = grads.result[...]


def experts_back_kernel(grad_buffer, arrived, w_in, w_out, returned, grad_in, grad_out, both_ref, hidden_ref, grad_ref, *scratch):
    (grads,) = exchanges(1, [grad_buffer], scratch)
    greet(grads)
    grads.start()
    grads.spread()
    keep_forward(0, half_rows(arrived, 0), w_in, both_ref, hidden_ref)
    grads.near_ready()
    set_half(grads.partial, 0, back_half(0, half_rows(grads.groups, 0), w_in, w_out, both_ref, grad_ref))
    grads.to_sibling(0).start()
    grads.spread_far()
    keep_forward(1, half_rows(arrived, 1), w_in, both_ref, hidden_ref)
    grads.far_ready()
    set_half(grads.partial, 1, back_half(1, half_rows(grads.groups, 1), w_in, w_out, both_ref, grad_ref))
    grads.to_sibling(1).start()
    grads.return_far()
    grad_out[...] = mm(hidden_ref[...], all_rows(grads.groups), TN).astype(BF16)
    grads.return_home()
    for chunk in range(grad_in.shape[1] // (2 * CHUNK)):
        columns = slice(2 * CHUNK * chunk, 2 * CHUNK * (chunk + 1))
        grad_in[:, columns] = mm(all_rows(arrived), grad_ref[:, columns], TN).astype(BF16)
    grads.finish_dispatch()
    grads.finish()
    returned[...] = grads.result[...]


def run_experts(kernel, identity, streams, blocks, args, out, kept=(), flops=0):
    owners, room, width = blocks
    return pl.pallas_call(
        kernel,
        out_shape=out,
        in_specs=[pl.BlockSpec(memory_space=pltpu.VMEM) for _ in args],
        out_specs=[pl.BlockSpec(memory_space=pltpu.VMEM) for _ in out],
        scratch_shapes=list(kept) + exchange_scratch(streams, owners, room, width),
        compiler_params=pltpu.CompilerParams(
            vmem_limit_bytes=VMEM_BYTES, collective_id=identity, has_side_effects=True
        ),
        cost_estimate=pl.CostEstimate(flops=flops, bytes_accessed=16 << 20, transcendentals=0),
    )(*args)


class Spread:
    def __init__(self, packed, in_pieces, out_pieces, attn, w_in, w_out, sems):
        self.packed, self.in_pieces, self.out_pieces = packed, in_pieces, out_pieces
        self.attn, self.w_in, self.w_out = attn, w_in, w_out
        (self.own_sem, self.z_s, self.z_r, self.plane_s, self.plane_r, self.core_s, self.core_r,
         self.in_s, self.in_r, self.out_s, self.out_r, self.own_in, self.own_out) = sems
        self.core, self.column, self.place = lax.axis_index("section"), lax.axis_index("expert"), lax.axis_index("shard")
        self.owners, self.pieces = lax.axis_size("expert"), lax.axis_size("shard")

    def spot(self, column, place):
        rows = self.packed.shape[0]
        return pl.ds(pl.multiple_of((column * self.pieces + place) * rows, rows), rows)

    def column_by(self, by):
        return lax.rem(self.column + by + self.owners, self.owners)

    def place_by(self, by):
        return lax.rem(self.place + by + self.pieces, self.pieces)

    def copy(self, source, target, send, recv, device):
        return pltpu.make_async_remote_copy(source, target, send, recv, device_id=device, device_id_type=MESH)

    def own(self):
        return pltpu.make_async_copy(self.packed, self.attn.at[self.core, self.spot(self.column, self.place)], self.own_sem)

    def along(self, by):
        block = self.attn.at[self.core, self.spot(self.column, self.place)]
        return self.copy(self.packed, block, self.z_s.at[by], self.z_r.at[by], (self.core, self.column, self.place_by(by)))

    def along_in(self, by):
        block = self.attn.at[self.core, self.spot(self.column, self.place_by(-by))]
        return self.copy(self.packed, block, self.z_s.at[by], self.z_r.at[by], (self.core, self.column, self.place_by(-by)))

    def plane(self, back, by):
        block = self.attn.at[self.core, self.spot(self.column, self.place_by(-back))]
        source = self.packed if back == 0 else block
        return self.copy(
            source, block, self.plane_s.at[back, by], self.plane_r.at[back, by], (self.core, self.column_by(by), self.place)
        )

    def plane_in(self, back, by):
        block = self.attn.at[self.core, self.spot(self.column_by(-by), self.place_by(-back))]
        return self.copy(
            block, block, self.plane_s.at[back, by], self.plane_r.at[back, by], (self.core, self.column_by(-by), self.place)
        )

    def over(self, back, by, section):
        block = self.attn.at[section, self.spot(self.column_by(-by), self.place_by(-back))]
        source = self.packed if back == 0 and by == 0 else block
        return self.copy(
            source, block, self.core_s.at[back, by], self.core_r.at[back, by], (1 - self.core, self.column, self.place)
        )

    def begin(self):
        self.own().start()
        for by in range(1, self.pieces):
            self.along(by).start()
        for by in range(1, self.owners):
            self.plane(0, by).start()
        self.over(0, 0, self.core).start()

    def pass_on(self):
        for back in range(1, self.pieces):
            self.along_in(back).wait_recv()
            for by in range(1, self.owners):
                self.plane(back, by).start()
            self.over(back, 0, self.core).start()

    def pass_over(self):
        for back in range(self.pieces):
            for by in range(1, self.owners):
                self.plane_in(back, by).wait_recv()
                self.over(back, by, self.core).start()
        self.own().wait()

    def over_ready(self):
        for back in range(self.pieces):
            for by in range(self.owners):
                self.over(back, by, 1 - self.core).wait_recv()

    def finish_attn(self):
        for by in range(1, self.pieces):
            self.along(by).wait_send()
        for back in range(self.pieces):
            for by in range(1, self.owners):
                self.plane(back, by).wait_send()
            for by in range(self.owners):
                self.over(back, by, self.core).wait_send()

    def in_rows(self, place):
        rows = self.in_pieces.shape[2]
        return pl.ds(pl.multiple_of(place * rows, rows), rows)

    def out_rows(self, place):
        rows = self.out_pieces.shape[1]
        return pl.ds(pl.multiple_of(lax.div(place, 2) * rows, rows), rows)

    def in_copy(self, cross, by):
        core = 1 - self.core if cross else self.core
        place = self.place_by(by)
        return self.copy(
            self.in_pieces.at[core, lax.rem(place, 2)], self.w_in.at[self.core, self.in_rows(self.place)],
            self.in_s.at[cross, by], self.in_r.at[cross, by], (core, self.column, place),
        )

    def in_here(self, cross, by):
        core = 1 - self.core if cross else self.core
        place = self.place_by(-by)
        return self.copy(
            self.in_pieces.at[core, lax.rem(place, 2)], self.w_in.at[core, self.in_rows(place)],
            self.in_s.at[cross, by], self.in_r.at[cross, by], (core, self.column, place),
        )

    def out_copy(self, cross, by):
        core = 1 - self.core if cross else self.core
        return self.copy(
            self.out_pieces.at[core], self.w_out.at[self.core, self.out_rows(self.place)],
            self.out_s.at[cross, by // 2], self.out_r.at[cross, by // 2], (core, self.column, self.place_by(by)),
        )

    def out_here(self, cross, by):
        core = 1 - self.core if cross else self.core
        place = self.place_by(-by)
        return self.copy(
            self.out_pieces.at[core], self.w_out.at[core, self.out_rows(place)],
            self.out_s.at[cross, by // 2], self.out_r.at[cross, by // 2], (core, self.column, place),
        )

    def own_pieces(self):
        return (
            pltpu.make_async_copy(
                self.in_pieces.at[self.core, lax.rem(self.place, 2)],
                self.w_in.at[self.core, self.in_rows(self.place)], self.own_in,
            ),
            pltpu.make_async_copy(
                self.out_pieces.at[self.core], self.w_out.at[self.core, self.out_rows(self.place)], self.own_out
            ),
        )

    def expert_routes(self):
        for by in range(self.pieces):
            for cross in (0, 1):
                if by or cross:
                    yield cross, by

    def begin_experts(self):
        for one in self.own_pieces():
            one.start()
        for cross, by in self.expert_routes():
            self.in_copy(cross, by).start()
            if by % 2 == 0:
                self.out_copy(cross, by).start()

    def experts_ready(self, cross):
        for way, by in self.expert_routes():
            if way == cross:
                self.in_here(cross, by).wait_recv()
                if by % 2 == 0:
                    self.out_here(cross, by).wait_recv()
        if not cross:
            for one in self.own_pieces():
                one.wait()

    def finish_experts(self):
        for cross, by in self.expert_routes():
            self.in_copy(cross, by).wait_send()
            if by % 2 == 0:
                self.out_copy(cross, by).wait_send()


def spread_scratch(owners, pieces):
    dma = pltpu.SemaphoreType.DMA
    return [
        dma, dma((pieces,)), dma((pieces,)), dma((pieces, owners)), dma((pieces, owners)), dma((pieces, owners)),
        dma((pieces, owners)), dma((2, pieces)), dma((2, pieces)), dma((2, pieces // 2)), dma((2, pieces // 2)), dma, dma,
    ]


SPREAD_SEMS = 13


def greet_all(spread):
    barrier = pltpu.get_barrier_semaphore()
    for by in range(1, spread.owners):
        pl.semaphore_signal(
            barrier, inc=1, device_id=(spread.core, spread.column_by(by), spread.place), device_id_type=MESH
        )
    for cross, by in spread.expert_routes():
        core = 1 - spread.core if cross else spread.core
        pl.semaphore_signal(barrier, inc=1, device_id=(core, spread.column, spread.place_by(by)), device_id_type=MESH)
    pl.semaphore_wait(barrier, spread.owners - 1 + 2 * spread.pieces - 1)


def front_kernel(
    dims, inside,
    packed, in_pieces, out_pieces, x, r, mix, cosine, sine, seg_col, seg_row, ints, prio_row, grad_y, *rest,
):
    if inside:
        attn, *rest = rest
    else:
        attn, *rest = rest
    (w_in, w_out, arrived, after_0, qkv_0, probs_0, attended_0, packed_0, slots_0, r_next,
     out, picked, after_1, qkv_1, probs_1, attended_1, packed_1, slots_1, buffer, grad_buffer, *scratch) = rest
    small, first_buffer = scratch[:2]
    width = x.shape[1]
    spread = Spread(packed, in_pieces, out_pieces, attn, w_in, w_out, scratch[2 : 2 + SPREAD_SEMS])
    (tokens,) = exchanges(1, [first_buffer], scratch[2 + SPREAD_SEMS :])
    first, second = spread.core == 0, spread.core == 1
    greet_all(spread)

    @pl.when(first)
    def _():
        if inside:
            spread.begin()
            spread.pass_on()
            spread.pass_over()
        spread.begin_experts()

    @pl.when(second)
    def _():
        if inside:
            spread.over_ready()
            spread.begin()

    small[0] = attn[0, :, 4 * width :]
    attend_kernel(
        dims, x, r, attn.at[0], small.at[0], mix.at[0], cosine, sine, seg_col, seg_row, ints.at[0], prio_row.at[0],
        after_0, qkv_0, probs_0, attended_0, packed_0, slots_0, r_next, first_buffer,
    )
    tokens.start()

    @pl.when(second)
    def _():
        if inside:
            spread.pass_on()

    tokens.spread()

    @pl.when(second)
    def _():
        if inside:
            spread.pass_over()
        spread.begin_experts()

    @pl.when(first)
    def _():
        spread.experts_ready(0)

    @pl.when(second)
    def _():
        spread.experts_ready(1)

    tokens.near_ready()
    set_half(tokens.partial, 0, experts_forward_half(half_rows(tokens.groups, 0), w_in.at[0], w_out.at[0]))
    tokens.to_sibling(0).start()
    tokens.spread_far()
    tokens.far_ready()
    set_half(tokens.partial, 1, experts_forward_half(half_rows(tokens.groups, 1), w_in.at[0], w_out.at[0]))
    tokens.to_sibling(1).start()
    tokens.return_far()
    arrived[...] = tokens.groups[...]
    tokens.return_home()
    tokens.finish_dispatch()
    tokens.finish()
    if inside:

        @pl.when(first)
        def _():
            spread.over_ready()

    small[1] = attn[1, :, 4 * width :]
    middle_kernel(
        dims, after_0, packed_0, slots_0, ints.at[0], tokens.result, small.at[0],
        r_next, attn.at[1], small.at[1], mix.at[1], cosine, sine, seg_col, seg_row, ints.at[1], prio_row.at[1], grad_y,
        out, picked, after_1, qkv_1, probs_1, attended_1, packed_1, slots_1, buffer, grad_buffer,
    )

    @pl.when(first)
    def _():
        spread.experts_ready(1)

    @pl.when(second)
    def _():
        spread.experts_ready(0)

    if inside:
        spread.finish_attn()
    spread.finish_experts()


def run_front(dims, inside, args, out, owners, pieces, blocks, width):
    vmem, anywhere = pl.BlockSpec(memory_space=pltpu.VMEM), pl.BlockSpec(memory_space=pl.ANY)
    in_specs = [vmem] * len(args)
    in_specs[1] = in_specs[2] = anywhere
    return pl.pallas_call(
        functools.partial(front_kernel, dims, inside),
        out_shape=out,
        in_specs=in_specs,
        out_specs=[vmem] * len(out),
        scratch_shapes=[pltpu.VMEM((2, width, LANES), BF16), pltpu.VMEM(blocks, BF16)]
        + spread_scratch(owners, pieces)
        + exchange_scratch(1, *blocks),
        compiler_params=pltpu.CompilerParams(
            vmem_limit_bytes=VMEM_BYTES, collective_id=0, has_side_effects=True
        ),
        cost_estimate=pl.CostEstimate(flops=8 << 30, bytes_accessed=40 << 20, transcendentals=0),
    )(*args)


def local(
    x_in,
    cotangent,
    gate_prev,
    segments,
    routes,
    priority,
    attn_qkv,
    attn_out,
    router,
    const_proj,
    const_vec,
    gains,
    gate_mix,
    expert_in,
    expert_out,
):
    seq_len, width = x_in.shape[2:]
    nexp = gate_prev.shape[-1]
    owners, pieces = lax.axis_size("expert"), lax.axis_size("shard")
    nffn = owners * expert_in.shape[1]
    nconst = const_vec.shape[-1]
    capacity = (5 * TOP * seq_len + 4 * nexp - 1) // (4 * nexp)
    room = -(-capacity // 16) * 16
    slots = nffn * room
    core = lax.axis_index("section")
    first_core = core == 0

    def swap(item):
        return lax.ppermute(item, "section", [(0, 1), (1, 0)])

    def mine(stack, axis=0):
        return lax.dynamic_index_in_dim(stack, core, axis, keepdims=False)

    def others(stack, axis=0):
        return lax.dynamic_index_in_dim(stack, 1 - core, axis, keepdims=False)

    def by_section(own, other):
        return jnp.where(first_core, own, other), jnp.where(first_core, other, own)

    in_rows, columns = expert_in.shape[2:]
    hidden_here = expert_out.shape[2] // 2
    pairs = pieces // 2
    quarter = pairs * hidden_here
    chunks = quarter // CHUNK
    pair_index = lax.axis_index("shard") // 2
    w_in = expert_in[0, 0].reshape(in_rows, 2, pairs, 2, 2, hidden_here)

    def as_chunks(half):
        half = jnp.moveaxis(half, 3, 0).reshape(2, in_rows, 2, chunks, CHUNK)
        return jnp.swapaxes(half, 2, 3).reshape(2, in_rows, 2 * quarter)

    w_out = expert_out[0, 0].reshape(2, hidden_here, width)
    in_pieces = jnp.stack([as_chunks(w_in[:, :, :, :, half]) for half in range(2)])

    def across(piece, hops):
        return lax.ppermute(piece, "shard", [(i, (i + 2 * hops) % pieces) for i in range(pieces)])

    def split_grads(grad_in, grad_out):
        got = lax.all_to_all(
            grad_in.reshape(pieces, in_rows, 2 * quarter), "shard", split_axis=0, concat_axis=0, tiled=True
        )
        in_sum = jnp.sum(got.reshape(pairs, 2, in_rows, 2 * quarter).astype(F32), axis=0).astype(BF16)
        grad_out = grad_out.reshape(pairs, hidden_here, width)

        def piece(hops):
            return lax.dynamic_index_in_dim(grad_out, (pair_index + hops) % pairs, 0, False)

        out_sum = piece(0).astype(F32)
        for hops in range(1, pairs):
            out_sum = out_sum + across(piece(hops), hops).astype(F32)
        return in_sum, out_sum.astype(BF16)

    rows = attn_qkv.shape[1]

    def lanes(array, upto):
        return jnp.pad(array, ((0, 0), (0, upto - array.shape[1])))

    small = jnp.concatenate(
        [
            lanes(router[0], AT_PROJ),
            lanes(const_proj[0], AT_VEC - AT_PROJ),
            lanes(const_vec[0], AT_GAIN - AT_VEC),
            lanes(gains[0], LANES - AT_GAIN),
        ],
        axis=1,
    )
    packed = jnp.concatenate([attn_qkv[0], attn_out[0], small], axis=1)
    inside = rows % 16 == 0
    given = []
    if not inside:
        shared = lax.all_gather(packed, ("expert", "shard"), axis=0, tiled=True)
        given = [jnp.stack(by_section(shared, swap(shared)))]
    mix_own = jnp.pad(gate_mix[0], ((0, LANES - nexp), (0, LANES - nexp)))
    mix_all = jnp.stack(by_section(mix_own, swap(mix_own)))
    ints_own = jnp.concatenate([routes[0, :, 0], priority[0, :, 0, :, None]], axis=-1)
    ints_all = jnp.stack(by_section(mine(ints_own), swap(others(ints_own))))
    x_first = mine(x_in[:, 0])
    r_first = jnp.pad(mine(gate_prev[:, 0]), ((0, 0), (0, LANES - nexp)))
    upstream = mine(cotangent[:, 0])
    seg = mine(segments[:, 0])
    place = lax.iota(jnp.int32, seq_len)
    start = jnp.sum((seg[None, :] < seg[:, None]).astype(F32), axis=1)
    angles = (place.astype(F32) - start)[:, None] * jnp.exp(
        lax.iota(F32, HEAD // 2) * (-2.0 * math.log(10000.0) / HEAD)
    )[None, :]
    cosine, sine = jnp.cos(angles), jnp.sin(angles)
    cosine = jnp.concatenate([cosine] * 4, axis=1)
    sine = jnp.concatenate([-sine, sine, -sine, sine], axis=1)

    dims = (nffn, nexp, capacity, slots)
    heads = width // HEAD
    blocks = (owners, room, width)
    seg_col, seg_row = seg[:, None], seg[None, :]
    token_f32 = shaped((seq_len, width), F32)
    token_b16 = shaped((seq_len, width), BF16)
    lanes_f32 = shaped((seq_len, LANES), F32)
    slot_shape = shaped((slots, width), BF16)
    block_shape = shaped(blocks, BF16)
    attend_out = [
        token_f32,
        shaped((seq_len, 3 * width), BF16),
        shaped((heads, seq_len, seq_len), BF16),
        token_b16,
        lanes_f32,
        shaped((seq_len, LANES), jnp.int32),
    ]
    attn_shape = shaped((width, 4 * width + LANES), BF16)
    back_out = [token_f32, lanes_f32, shaped((LANES, LANES), F32), attn_shape]
    grad_qkv = pltpu.VMEM((seq_len, 3 * width), BF16)
    prio = ints_all[:, None, :, 2]
    rows_there = 4 * slots
    kept = [
        pltpu.VMEM((rows_there, 2 * quarter), F32),
        pltpu.VMEM((rows_there, quarter), BF16),
        pltpu.VMEM((rows_there, 2 * quarter), BF16),
    ]
    grad_shapes = [shaped((width, 2 * quarter), BF16), shaped((quarter, width), BF16)]
    work = 2 * rows_there * width * quarter

    middle_out = [token_b16, shaped((TOP, seq_len, width), BF16)] + attend_out + [slot_shape, slot_shape]
    outs = [shaped((2, width, 2 * quarter), BF16), shaped((2, quarter, width), BF16), shaped((4,) + blocks, BF16)]
    outs += attend_out + [shaped((seq_len, LANES), BF16)] + middle_out
    if inside:
        outs = [shaped((2,) + attn_shape.shape, BF16)] + outs
    got = run_front(
        dims, inside,
        [packed, in_pieces, w_out, x_first, r_first, mix_all, cosine, sine, seg_col, seg_row, ints_all, prio, upstream] + given,
        outs, owners, pieces, blocks, width,
    )
    (attn_all, w_in_all, w_out_all, arrived, after_0, qkv_0, probs_0, attended_0, packed_0, slots_0, r_next,
     out_0, picked_0, after_1, qkv_1, probs_1, attended_1, packed_1, slots_1, buffer, grad_buffer) = given + list(got)
    shared = (attn_all[0], attn_all[1])
    smalls = [w[:, 4 * width :] for w in shared]
    experts = [(w_in_all[s], w_out_all[s]) for s in range(2)]
    w, ints = shared[0], ints_all[0]
    made, returned, grad_in_1, grad_out_1 = run_experts(
        experts_both_kernel, 1, 2, blocks, (buffer.reshape(blocks), grad_buffer.reshape(blocks), *experts[1]),
        [block_shape, block_shape] + grad_shapes, kept, flops=9 * work,
    )
    sums_1 = split_grads(grad_in_1, grad_out_1)
    out_1, grad_x_1, grad_r_1, grad_mix_1, grads_1, buffer = run(
        functools.partial(turn_kernel, dims),
        [token_b16] + back_out + [slot_shape],
        (
            upstream, after_1, packed_1, slots_1, ints_all[1], made.reshape(slots, width), returned.reshape(slots, width),
            r_next, shared[1], smalls[1], mix_all[1], out_0, qkv_1, probs_1, attended_1, cosine, sine, packed_0, slots_0,
        ),
        flops=5 << 30,
        scratch=[grad_qkv, pltpu.VMEM((TOP, seq_len, width), BF16)],
    )
    returned, grad_in_0, grad_out_0 = run_experts(
        experts_back_kernel, 2, 1, blocks, (buffer.reshape(blocks), arrived, *experts[0]),
        [block_shape] + grad_shapes, kept, flops=9 * work,
    )
    sums_0 = split_grads(grad_in_0, grad_out_0)
    grad_x_0, grad_r_0, grad_mix_0, grads_0 = run(
        functools.partial(back_kernel, dims),
        back_out,
        (
            grad_x_1, grad_r_1, after_0, packed_0, slots_0, ints, picked_0, returned.reshape(slots, width),
            r_first, w, smalls[0], mix_all[0], x_first, qkv_0, probs_0, attended_0, cosine, sine,
        ),
        flops=5 << 30,
        scratch=[grad_qkv],
    )
    results, x_grads = (out_0, out_1), (grad_x_0, grad_x_1)
    r_grads = (grad_r_0[:, :nexp], grad_r_1[:, :nexp])
    sums = []
    for grads, grad_mix, expert_sums in ((grads_0, grad_mix_0, sums_0), (grads_1, grad_mix_1, sums_1)):
        mix_lanes = -(-nexp * nexp // rows)
        mix_flat = jnp.pad(grad_mix[:nexp, :nexp].reshape(-1), (0, rows * mix_lanes - nexp * nexp)).reshape(rows, mix_lanes)
        mix_tile = jnp.tile(mix_flat, (owners * pieces, 1)).astype(BF16)
        at = 4 * width + AT_MIX
        grads = lax.dynamic_update_slice(grads, mix_tile, (0, at))
        sums.append((grads, *expert_sums))
    shared_own = jnp.where(first_core, sums[0][0], sums[1][0])
    shared_other = jnp.where(first_core, sums[1][0], sums[0][0])
    shared_sum = (shared_own.astype(F32) + swap(shared_other).astype(F32)).astype(BF16)
    shared_sum = lax.psum_scatter(shared_sum, ("expert", "shard"), scatter_dimension=0, tiled=True).astype(F32)

    def halves(index):
        own = jnp.where(first_core, sums[0][index], sums[1][index])
        got = swap(jnp.where(first_core, sums[1][index], sums[0][index]))
        return jnp.where(first_core, own, got).astype(F32), jnp.where(first_core, got, own).astype(F32)

    def from_chunks(half):
        half = jnp.swapaxes(half.reshape(2, in_rows, chunks, 2, CHUNK), 2, 3)
        return jnp.moveaxis(half.reshape(2, in_rows, 2, pairs, hidden_here), 0, 3)

    in_grad = jnp.stack([from_chunks(half) for half in halves(1)], axis=4).reshape(in_rows, columns)
    out_grad = jnp.concatenate(halves(2), axis=0)

    def both_batches(pair):
        own = jnp.where(first_core, pair[0], pair[1])
        got = swap(jnp.where(first_core, pair[1], pair[0]))
        return jnp.stack(by_section(own, got))[None, :, None]

    small_sum = shared_sum[:, 4 * width :]
    mix_grad = small_sum[:, AT_MIX : AT_MIX + mix_lanes].reshape(-1)[: nexp * nexp].reshape(nexp, nexp)
    return (
        both_batches(results),
        both_batches(x_grads),
        both_batches(r_grads),
        shared_sum[None, :, : 3 * width],
        shared_sum[None, :, 3 * width : 4 * width],
        small_sum[None, :, :nexp],
        small_sum[None, :, AT_PROJ : AT_PROJ + const_proj.shape[-1]],
        small_sum[None, :, AT_VEC : AT_VEC + nconst],
        small_sum[None, :, AT_GAIN : AT_GAIN + 2],
        mix_grad[None],
        in_grad[None, None],
        out_grad[None, None],
    )


def solution(mesh):
    placed = (
        P(None, ("expert", "shard"), None, None),
        P(None, ("expert", "shard"), None, None),
        P(None, ("expert", "shard"), None, None),
        P(None, ("expert", "shard"), None),
        P("section", None, ("expert", "shard"), None, None),
        P("section", None, ("expert", "shard"), None),
        P("section", ("expert", "shard"), None),
        P("section", ("expert", "shard"), None),
        P("section", ("expert", "shard"), None),
        P("section", ("expert", "shard"), None),
        P("section", ("expert", "shard"), None),
        P("section", ("expert", "shard"), None),
        P("section", None, None),
        P("section", "expert", "shard", None),
        P("section", "expert", "shard", None),
    )
    return jax.shard_map(
        local,
        mesh=mesh,
        in_specs=placed,
        out_specs=(
            P("section", None, ("expert", "shard"), None, None),
            P("section", None, ("expert", "shard"), None, None),
            P("section", None, ("expert", "shard"), None, None),
            P("section", ("expert", "shard"), None),
            P("section", ("expert", "shard"), None),
            P("section", ("expert", "shard"), None),
            P("section", ("expert", "shard"), None),
            P("section", ("expert", "shard"), None),
            P("section", ("expert", "shard"), None),
            P("section", None, None),
            P("section", "expert", "shard", None),
            P("section", "expert", "shard", None),
        ),
        check_vma=False,
    )
```

```python
import functools
import math

import jax
import jax.numpy as jnp
from jax import lax
from jax.experimental import pallas as pl
from jax.experimental.pallas import tpu as pltpu
from jax.sharding import PartitionSpec as P

HEADS = 12
HEAD = 64
TOP = 2
CHUNK = 256
LANES = 128
AT_PROJ = 16
AT_VEC = 24
AT_GAIN = 28
AT_MIX = 32

HIGH = lax.Precision.HIGHEST
norm_eps = 1e-06
masked_score = -1e30
F32 = jnp.float32
BF16 = jnp.bfloat16


VMEM_BYTES = 56 * 1024 * 1024


def mm(a, b, contract=((1,), (0,)), precision=None):
    return lax.dot_general(a, b, (contract, ((), ())), precision=precision, preferred_element_type=F32)


NT = ((1,), (1,))
TN = ((0,), (0,))


def lane_of(rows, columns=LANES):
    return lax.broadcasted_iota(jnp.int32, (rows, columns), 1)


def inverse_norm(values):
    return lax.rsqrt(jnp.mean(values * values, axis=-1, keepdims=True) + norm_eps)


def norm_back(grad_unit, unit, inverse):
    return inverse * (grad_unit - unit * jnp.mean(grad_unit * unit, axis=-1, keepdims=True))


def roll(x, by):
    return pltpu.roll(x, by, 1)


def turned(x, lane):
    return jnp.where(lane % HEAD < HEAD // 2, roll(x, LANES - HEAD // 2), roll(x, HEAD // 2))


def hi_lo(x):
    high = x.astype(BF16)
    return high, (x - high.astype(F32)).astype(BF16)


def ones_where(condition):
    return jnp.where(condition, 1.0, 0.0).astype(BF16)


def small_rows_of(small):
    rows = small[...].astype(F32).T
    return rows[AT_GAIN : AT_GAIN + 1], rows[AT_GAIN + 1 : AT_GAIN + 2], rows[AT_VEC:AT_GAIN]


def attention(x, w, gain_first, cosine, sine, seg_col, seg_row, qkv, probs_att, attended):
    seq_len, width = x.shape
    first_b = (x * inverse_norm(x) * gain_first).astype(BF16)
    place_q = lax.broadcasted_iota(jnp.int32, (seq_len, seq_len), 0)
    place_k = lax.broadcasted_iota(jnp.int32, (seq_len, seq_len), 1)
    bias = jnp.where((seg_col == seg_row) & (place_k <= place_q), 0.0, masked_score)
    lane = lane_of(seq_len)
    low_head = lane < HEAD
    for pair in range(width // LANES):
        at = pair * LANES
        q = mm(first_b, w[:, at : at + LANES])
        k = mm(first_b, w[:, width + at : width + at + LANES])
        v = mm(first_b, w[:, 2 * width + at : 2 * width + at + LANES]).astype(BF16)
        q = q * cosine + turned(q, lane) * sine
        k = (k * cosine + turned(k, lane) * sine).astype(BF16)
        outs = []
        for half in range(2):
            one = jnp.where(low_head if half == 0 else lane >= HEAD, q, 0.0).astype(BF16)
            scores = mm(one, k, NT) * (HEAD**-0.5) + bias
            scores = jnp.exp(scores - jnp.max(scores, axis=-1, keepdims=True))
            probs = (scores * (1.0 / jnp.sum(scores, axis=-1, keepdims=True))).astype(BF16)
            probs_att[2 * pair + half] = probs
            outs.append(mm(probs, v))
        attended[:, at : at + LANES] = jnp.where(low_head, outs[0], outs[1]).astype(BF16)
        qkv[:, at : at + LANES] = q.astype(BF16)
        qkv[:, width + at : width + at + LANES] = k
        qkv[:, 2 * width + at : 2 * width + at + LANES] = v
    return x + mm(attended[...], w[:, 3 * width : 4 * width])


def gating(after, r, small, mix, gain_second, ints, prio_row, dims, packed_ref, slot_ref, r_next, buffer):
    nffn, nexp, capacity, slots, _ = dims
    rows = after.shape[0]
    second_b = (after * inverse_norm(after) * gain_second).astype(BF16)
    lane = lane_of(rows)
    logits = mm(second_b, small)
    full = logits + mm(r, mix, precision=HIGH)
    inside = lane < nexp
    full = jnp.where(inside, full, masked_score)
    raised = jnp.exp(full - jnp.max(full, axis=-1, keepdims=True))
    probs = raised / jnp.sum(raised, axis=-1, keepdims=True)
    other = jnp.where(lane % 2 == 0, roll(logits, LANES - 1), roll(logits, 1))
    bigger = jnp.maximum(logits, other)
    mine_e = jnp.exp(logits - bigger)
    mixes = mine_e / (mine_e + jnp.exp(other - bigger))
    before = ones_where(prio_row < ints[:, 2:3])
    route = (ints[:, 0:1], ints[:, 1:2])
    routed = ones_where(((lane == route[0]) | (lane == route[1])) & (lane < nffn))
    rank = mm(before, routed)
    gates, places = [], []
    dispatch = 0.0
    stride = slots // nffn
    for k in range(TOP):
        chosen = lane == route[k]
        gates.append(jnp.sum(jnp.where(chosen, probs, 0.0), axis=-1, keepdims=True))
        rank_k = jnp.sum(jnp.where(chosen, rank, 0.0), axis=-1, keepdims=True).astype(jnp.int32)
        kept = (route[k] < nffn) & (rank_k < capacity)
        places.append(jnp.where(kept, route[k] * stride + rank_k, -1))
        dispatch = dispatch + jnp.where(places[k] == lane_of(rows, slots), 1.0, 0.0)
    buffer[...] = mm(dispatch.astype(BF16), second_b, TN).astype(BF16).reshape(buffer.shape)
    packed = jnp.where(inside, probs, jnp.where((lane >= AT_PROJ) & (lane < AT_VEC), mixes, 0.0))
    packed = jnp.where(lane == AT_VEC, gates[0], packed)
    packed_ref[...] = jnp.where(lane == AT_VEC + 1, gates[1], packed)
    slot_ref[...] = jnp.where(lane == 0, places[0], places[1])
    if r_next is not None:
        r_next[...] = jnp.where(inside, full, 0.0).astype(BF16)


def extras(packed, ints, nffn, nconst):
    gates = (packed[:, AT_VEC : AT_VEC + 1], packed[:, AT_VEC + 1 : AT_VEC + 2])

    def of(expert):
        return sum(jnp.where(ints[:, k : k + 1] == expert, gates[k], 0.0) for k in range(TOP))

    def mixes(c):
        at = AT_PROJ + 2 * c
        return packed[:, at : at + 1], packed[:, at + 1 : at + 2]

    return gates, of(nffn + 1), [of(nffn + 2 + c) for c in range(nconst)], [mixes(c) for c in range(nconst)]


def combine(after, packed, slot_pair, ints, blocks, gain_second, vec_rows, dims, picked_ref):
    nffn, nexp, _, slots, _ = dims
    nconst = nexp - nffn - 2
    rows = after.shape[0]
    second = after * inverse_norm(after) * gain_second
    gates, copied, const, mixes = extras(packed, ints, nffn, nconst)
    made = blocks[...].reshape(slots, after.shape[1])
    slot_lane = lane_of(rows, slots)
    coefficient = copied
    for c in range(nconst):
        coefficient = coefficient + const[c] * mixes[c][0]
    out = after + coefficient * second
    for k in range(TOP):
        picked = mm(ones_where(slot_pair[:, k : k + 1] == slot_lane), made)
        picked_ref[k] = picked.astype(BF16)
        out = out + gates[k] * picked
    for c in range(nconst):
        out = out + (const[c] * mixes[c][1]) * vec_rows[c : c + 1]
    return out


def give_back(grad_y, packed, slot_pair, dims, buffer):
    slots = dims[3]
    slot_lane = lane_of(grad_y.shape[0], slots)
    total = 0.0
    for k in range(TOP):
        gate = packed[:, AT_VEC + k : AT_VEC + k + 1]
        table = ones_where(slot_pair[:, k : k + 1] == slot_lane)
        total = total + mm(table, (gate * grad_y).astype(BF16), TN)
    buffer[...] = total.astype(BF16).reshape(buffer.shape)


def moe_back(
    grad_y, grad_log_in, after, packed, slot_pair, ints, picked, blocks, r, small, mix, gain_second, vec_rows, dims
):
    nffn, nexp, _, slots, _ = dims
    nconst = nexp - nffn - 2
    rows = grad_y.shape[0]
    lane = lane_of(rows)
    inverse = inverse_norm(after)
    unit = after * inverse
    second = unit * gain_second
    second_b = second.astype(BF16)
    gates, copied, const, mixes = extras(packed, ints, nffn, nconst)
    grad_buffer = blocks[...].reshape(slots, after.shape[1])
    slot_lane = lane_of(rows, slots)
    dispatch = sum(jnp.where(slot_pair[:, k : k + 1] == slot_lane, 1.0, 0.0) for k in range(TOP))
    grad_second = mm(dispatch.astype(BF16), grad_buffer)
    along_second = jnp.sum(grad_y * second, axis=-1, keepdims=True)
    coefficient = copied
    grad_extra = [(nffn + 1, along_second)]
    grad_lanes = jnp.zeros((rows, LANES), F32)
    vec_grads = []
    for c in range(nconst):
        along = jnp.sum(grad_y * vec_rows[c : c + 1], axis=-1, keepdims=True)
        m0, m1 = mixes[c]
        coefficient = coefficient + const[c] * m0
        grad_extra.append((nffn + 2 + c, m0 * along_second + m1 * along))
        d0, d1 = const[c] * along_second, const[c] * along
        mean = m0 * d0 + m1 * d1
        at = AT_PROJ + 2 * c
        grad_lanes = jnp.where(lane == at, m0 * (d0 - mean), grad_lanes)
        grad_lanes = jnp.where(lane == at + 1, m1 * (d1 - mean), grad_lanes)
        vec_grads.append(jnp.sum(grad_y * (const[c] * m1), axis=0, keepdims=True))
    grad_second = grad_second + coefficient * grad_y
    grad_probs = jnp.zeros((rows, LANES), F32)
    for k in range(TOP):
        grad_gate = jnp.sum(picked[k].astype(F32) * grad_y, axis=-1, keepdims=True)
        for expert, value in grad_extra:
            grad_gate = grad_gate + jnp.where(ints[:, k : k + 1] == expert, value, 0.0)
        grad_probs = grad_probs + jnp.where(lane == ints[:, k : k + 1], grad_gate, 0.0)
    probs = jnp.where(lane < nexp, packed, 0.0)
    grad_logits = probs * (grad_probs - jnp.sum(probs * grad_probs, axis=-1, keepdims=True)) + grad_log_in
    grad_mix = mm(jnp.where(lane < nexp, r, 0.0), jnp.where(lane < nexp, grad_logits, 0.0), TN, HIGH)
    grad_r = mm(grad_logits, mix, NT, HIGH)
    high, low = hi_lo(jnp.where(lane < nexp, grad_logits, grad_lanes))
    small_rows = mm(high, second_b, TN) + mm(low, second_b, TN)
    grad_second = grad_second + mm(high, small, NT) + mm(low, small, NT)
    grad_gain = jnp.sum(grad_second * unit, axis=0, keepdims=True)
    grad_after = grad_y + norm_back(grad_second * gain_second, unit, inverse)
    row = lax.broadcasted_iota(jnp.int32, small_rows.shape, 0)
    small_rows = jnp.where(row < AT_VEC, small_rows, 0.0)
    for c in range(nconst):
        small_rows = jnp.where(row == AT_VEC + c, vec_grads[c], small_rows)
    small_rows = jnp.where(row == AT_GAIN + 1, grad_gain, small_rows)
    return grad_after, grad_r, grad_mix, small_rows


def attention_back(grad_after, x, qkv, probs_att, attended, small_rows, mix_tile, w, gain_first, cosine, sine, grads, grad_qkv):
    seq_len, width = x.shape
    inverse = inverse_norm(x)
    unit = x * inverse
    first_b = (unit * gain_first).astype(BF16)
    grad_branch = grad_after.astype(BF16)
    grads[:, 3 * width : 4 * width] = mm(attended[...], grad_branch, TN).astype(BF16)
    lane = lane_of(seq_len)
    low_head = lane < HEAD
    masks = (ones_where(low_head), ones_where(lane >= HEAD))
    scale = HEAD**-0.5
    for pair in range(width // LANES):
        at = pair * LANES
        q = qkv[:, at : at + LANES]
        k = qkv[:, width + at : width + at + LANES]
        v = qkv[:, 2 * width + at : 2 * width + at + LANES]
        g = mm(grad_branch, w[at : at + LANES, 3 * width : 4 * width], NT).astype(BF16)
        dq, dk, dv = [], [], []
        for half in range(2):
            probs = probs_att[2 * pair + half]
            grad_p = mm(g * masks[half], v, NT)
            p = probs.astype(F32)
            grad_s = (p * (grad_p - jnp.sum(p * grad_p, axis=-1, keepdims=True))).astype(BF16)
            dv.append(mm(probs, g, TN))
            dq.append(mm(grad_s, k))
            dk.append(mm(grad_s, q, TN))
        dq = jnp.where(low_head, dq[0], dq[1]) * scale
        dk = jnp.where(low_head, dk[0], dk[1]) * scale
        grad_qkv[:, at : at + LANES] = (dq * cosine - turned(dq, lane) * sine).astype(BF16)
        grad_qkv[:, width + at : width + at + LANES] = (dk * cosine - turned(dk, lane) * sine).astype(BF16)
        grad_qkv[:, 2 * width + at : 2 * width + at + LANES] = jnp.where(low_head, dv[0], dv[1]).astype(BF16)
    grads[:, : 3 * width] = mm(first_b, grad_qkv[...], TN).astype(BF16)
    grad_first = mm(grad_qkv[...], w[:, : 3 * width], NT)
    grad_gain = jnp.sum(grad_first * unit, axis=0, keepdims=True)
    grad_x = grad_after + norm_back(grad_first * gain_first, unit, inverse)
    row = lax.broadcasted_iota(jnp.int32, small_rows.shape, 0)
    small_rows = jnp.where(row == AT_GAIN, grad_gain, small_rows)
    grads[:, 4 * width :] = (small_rows.T + mix_tile).astype(BF16)
    return grad_x


def attend_kernel(
    dims, x, r, w, small, mix, cosine, sine, seg_col, seg_row, ints, prio_row,
    after, qkv, probs_att, attended, packed, slot_pair, r_next, buffer,
):
    gain_first, gain_second, _ = small_rows_of(small)
    after_v = attention(
        x[...].astype(F32), w, gain_first, cosine[...], sine[...], seg_col[...], seg_row[...], qkv, probs_att, attended
    )
    after[...] = after_v
    gating(
        after_v, r[...].astype(F32), small[...], mix[...], gain_second, ints[...], prio_row[...], dims,
        packed, slot_pair, r_next, buffer,
    )


def middle_kernel(
    dims, after_0, packed_0, slots_0, ints_0, blocks_0, small_0,
    r, w, small, mix, cosine, sine, seg_col, seg_row, ints, prio_row, grad_y,
    out, picked, after, qkv, probs_att, attended, packed, slot_pair, buffer, grad_buffer,
):
    _, gain_second, vec_rows = small_rows_of(small_0)
    out[...] = combine(
        after_0[...], packed_0[...], slots_0[...], ints_0[...], blocks_0, gain_second, vec_rows, dims, picked
    ).astype(BF16)
    attend_kernel(
        dims, out, r, w, small, mix, cosine, sine, seg_col, seg_row, ints, prio_row,
        after, qkv, probs_att, attended, packed, slot_pair, None, buffer,
    )
    give_back(grad_y[...], packed[...], slot_pair[...], dims, grad_buffer)


def turn_kernel(
    dims, grad_y, after, packed, slot_pair, ints, made, blocks, r, w, small, mix, x, qkv, probs_att, attended,
    cosine, sine, packed_0, slots_0,
    out, grad_x, grad_r, grad_mix, grads, buffer, grad_qkv, picked,
):
    _, gain_second, vec_rows = small_rows_of(small)
    out[...] = combine(
        after[...], packed[...], slot_pair[...], ints[...], made, gain_second, vec_rows, dims, picked
    ).astype(BF16)
    back_kernel(
        dims, grad_y, None, after, packed, slot_pair, ints, picked, blocks, r, w, small, mix, x, qkv, probs_att, attended,
        cosine, sine, grad_x, grad_r, grad_mix, grads, grad_qkv,
    )
    give_back(grad_x[...].astype(BF16).astype(F32), packed_0[...], slots_0[...], dims, buffer)


def back_kernel(
    dims, grad_y, grad_log, after, packed, slot_pair, ints, picked, blocks, r, w, small, mix, x, qkv, probs_att, attended,
    cosine, sine, grad_x, grad_r, grad_mix, grads, grad_qkv,
):
    gain_first, gain_second, vec_rows = small_rows_of(small)
    grad_log_v = 0.0 if grad_log is None else grad_log[...].astype(BF16).astype(F32)
    grad_y_v = grad_y[...] if grad_log is None else grad_y[...].astype(BF16).astype(F32)
    grad_after, grad_r_v, grad_mix_v, small_rows = moe_back(
        grad_y_v, grad_log_v, after[...], packed[...], slot_pair[...], ints[...], picked,
        blocks, r[...].astype(F32), small[...], mix[...], gain_second, vec_rows, dims,
    )
    grad_r[...] = grad_r_v
    grad_mix[...] = grad_mix_v
    rows = dims[4]
    mix_tile = 0.0
    if rows:
        mix_tile = jnp.concatenate([roll(grad_mix_v, AT_MIX)[:rows]] * (x.shape[1] // rows), axis=0)
    grad_x[...] = attention_back(
        grad_after, x[...].astype(F32), qkv, probs_att, attended, small_rows, mix_tile, w, gain_first,
        cosine[...], sine[...], grads, grad_qkv,
    )


def shaped(shape, dtype):
    return jax.ShapeDtypeStruct(shape, dtype)


def run(kernel, out, args, flops=0, scratch=()):
    return pl.pallas_call(
        kernel,
        out_shape=out,
        in_specs=[pl.BlockSpec(memory_space=pltpu.VMEM) for _ in args],
        out_specs=[pl.BlockSpec(memory_space=pltpu.VMEM) for _ in out],
        scratch_shapes=list(scratch),
        compiler_params=pltpu.CompilerParams(vmem_limit_bytes=VMEM_BYTES),
        cost_estimate=pl.CostEstimate(flops=flops, bytes_accessed=8 << 20, transcendentals=0),
    )(*args)


MESH = pl.DeviceIdType.MESH


class Exchange:
    def __init__(self, stream, sent, groups, partial, sibling_part, onward, pair_part, summed, result, sems):
        self.stream, self.sent, self.groups = stream, sent, groups
        self.partial, self.sibling_part, self.onward = partial, sibling_part, onward
        self.pair_part, self.summed, self.result = pair_part, summed, result
        (self.column_s, self.column_r, self.pair_s, self.pair_r, self.core_s, self.core_r, self.last_s, self.last_r,
         self.local_sem, self.back_s, self.back_r, self.over_s, self.over_r, self.home_s, self.home_r) = sems
        self.core, self.column, self.place = lax.axis_index("section"), lax.axis_index("expert"), lax.axis_index("shard")
        self.owners = lax.axis_size("expert")
        self.sibling = (1 - self.core, self.column, self.place)
        self.pair = (self.core, self.column, self.place + 1 - 2 * lax.rem(self.place, 2))

    def peer(self, column):
        return (self.core, column, self.place)

    def turn(self, by):
        return lax.rem(self.column + by + self.owners, self.owners)

    def to_column(self, by):
        return pltpu.make_async_remote_copy(
            self.sent.at[self.turn(by)], self.groups.at[0, self.column],
            self.column_s.at[self.stream, by], self.column_r.at[self.stream, by],
            device_id=self.peer(self.turn(by)), device_id_type=MESH,
        )

    def from_column(self, by):
        source = self.turn(-by)
        return pltpu.make_async_remote_copy(
            self.sent.at[source], self.groups.at[0, source],
            self.column_s.at[self.stream, by], self.column_r.at[self.stream, by],
            device_id=self.peer(source), device_id_type=MESH,
        )

    def own_block(self):
        return pltpu.make_async_copy(
            self.sent.at[self.column], self.groups.at[0, self.column], self.local_sem.at[self.stream]
        )

    def forward(self, by, here, there, device, send, recv):
        block = self.turn(-by)
        return pltpu.make_async_remote_copy(
            self.groups.at[here, block], self.groups.at[there, block],
            send.at[self.stream, by], recv.at[self.stream, by], device_id=device, device_id_type=MESH,
        )

    def to_pair(self, by):
        return self.forward(by, 0, 2, self.pair, self.pair_s, self.pair_r)

    def to_core(self, by):
        return self.forward(by, 0, 1, self.sibling, self.core_s, self.core_r)

    def to_core_last(self, by):
        return self.forward(by, 2, 3, self.sibling, self.last_s, self.last_r)

    def start(self):
        for by in range(1, self.owners):
            self.to_column(by).start()
        self.own_block().start()

    def spread(self):
        for by in range(self.owners):
            if by:
                self.from_column(by).wait_recv()
            else:
                self.own_block().wait()
            self.to_pair(by).start()
            self.to_core(by).start()

    def near_ready(self):
        for by in range(self.owners):
            self.to_core(by).wait_recv()

    def spread_far(self):
        for by in range(self.owners):
            self.to_pair(by).wait_recv()
            self.to_core_last(by).start()

    def far_ready(self):
        for by in range(self.owners):
            self.to_core_last(by).wait_recv()

    def finish_dispatch(self):
        for by in range(self.owners):
            if by:
                self.to_column(by).wait_send()
            self.to_pair(by).wait_send()
            self.to_core(by).wait_send()
            self.to_core_last(by).wait_send()

    def to_sibling(self, half):
        return pltpu.make_async_remote_copy(
            self.partial.at[2 * half + 1], self.sibling_part.at[half],
            self.back_s.at[self.stream, half], self.back_r.at[self.stream, half],
            device_id=self.sibling, device_id_type=MESH,
        )

    def over_pair(self):
        return pltpu.make_async_remote_copy(
            self.onward, self.pair_part, self.over_s.at[self.stream], self.over_r.at[self.stream],
            device_id=self.pair, device_id_type=MESH,
        )

    def home(self, by):
        return pltpu.make_async_remote_copy(
            self.summed.at[self.turn(by)], self.result.at[self.column],
            self.home_s.at[self.stream, by], self.home_r.at[self.stream, by],
            device_id=self.peer(self.turn(by)), device_id_type=MESH,
        )

    def home_here(self, by):
        source = self.turn(-by)
        return pltpu.make_async_remote_copy(
            self.summed.at[source], self.result.at[source],
            self.home_s.at[self.stream, by], self.home_r.at[self.stream, by],
            device_id=self.peer(source), device_id_type=MESH,
        )

    def return_far(self):
        self.to_sibling(1).wait_recv()
        self.onward[...] = (self.partial[2].astype(F32) + self.sibling_part[1].astype(F32)).astype(BF16)
        self.over_pair().start()

    def return_home(self):
        self.to_sibling(0).wait_recv()
        near = self.partial[0].astype(F32) + self.sibling_part[0].astype(F32)
        self.over_pair().wait_recv()
        self.summed[...] = (near + self.pair_part[...].astype(F32)).astype(BF16)
        for by in range(1, self.owners):
            self.home(by).start()
        self.result[self.column] = self.summed[self.column]

    def finish(self):
        for by in range(1, self.owners):
            self.home_here(by).wait_recv()
            self.home(by).wait_send()
        self.over_pair().wait_send()
        self.to_sibling(0).wait_send()
        self.to_sibling(1).wait_send()


def greet(exchange):
    barrier = pltpu.get_barrier_semaphore()
    owners = exchange.owners
    for by in range(1, owners):
        pl.semaphore_signal(barrier, inc=1, device_id=exchange.peer(exchange.turn(by)), device_id_type=MESH)
    pl.semaphore_signal(barrier, inc=1, device_id=exchange.sibling, device_id_type=MESH)
    pl.semaphore_signal(barrier, inc=1, device_id=exchange.pair, device_id_type=MESH)
    pl.semaphore_wait(barrier, owners + 1)


def exchange_scratch(streams, owners, room, width):
    block = (owners, room, width)
    shapes = []
    for _ in range(streams):
        shapes += [
            pltpu.VMEM((4,) + block, BF16),
            pltpu.VMEM((4,) + block, BF16),
            pltpu.VMEM((2,) + block, BF16),
            pltpu.VMEM(block, BF16),
            pltpu.VMEM(block, BF16),
            pltpu.VMEM(block, BF16),
            pltpu.VMEM(block, BF16),
        ]
    dma = pltpu.SemaphoreType.DMA
    shapes += [dma((streams, owners)) for _ in range(8)] + [dma((streams,))]
    shapes += [dma((streams, 2)) for _ in range(2)] + [dma((streams,)) for _ in range(2)] + [dma((streams, owners)) for _ in range(2)]
    return shapes


def exchanges(streams, sent, scratch):
    sems = scratch[7 * streams :]
    return [Exchange(i, sent[i], *scratch[7 * i : 7 * i + 7], sems) for i in range(streams)]


def half_rows(ref, half):
    groups, owners, room, width = ref.shape
    return ref[2 * half : 2 * half + 2].reshape(2 * owners * room, width)


def set_half(ref, half, value):
    groups, owners, room, width = ref.shape
    ref[2 * half : 2 * half + 2] = value.astype(BF16).reshape(2, owners, room, width)


def experts_forward_half(rows, w_in, w_out):
    total = 0.0
    for chunk in range(w_out.shape[0] // CHUNK):
        both = mm(rows, w_in[:, 2 * CHUNK * chunk : 2 * CHUNK * (chunk + 1)])
        gate = both[:, :CHUNK]
        hidden = (gate * jax.nn.sigmoid(gate) * both[:, CHUNK:]).astype(BF16)
        total = total + mm(hidden, w_out[CHUNK * chunk : CHUNK * (chunk + 1)])
    return total


def experts_kernel(buffer, w_in, w_out, returned, arrived, *scratch):
    (tokens,) = exchanges(1, [buffer], scratch)
    greet(tokens)
    tokens.start()
    tokens.spread()
    tokens.near_ready()
    set_half(tokens.partial, 0, experts_forward_half(half_rows(tokens.groups, 0), w_in, w_out))
    tokens.to_sibling(0).start()
    tokens.spread_far()
    tokens.far_ready()
    set_half(tokens.partial, 1, experts_forward_half(half_rows(tokens.groups, 1), w_in, w_out))
    tokens.to_sibling(1).start()
    tokens.return_far()
    arrived[...] = tokens.groups[...]
    tokens.return_home()
    tokens.finish_dispatch()
    tokens.finish()
    returned[...] = tokens.result[...]


def keep_forward(half, rows, w_in, both_ref, hidden_ref):
    count = rows.shape[0]
    at = half * count
    for chunk in range(hidden_ref.shape[1] // CHUNK):
        columns = slice(2 * CHUNK * chunk, 2 * CHUNK * (chunk + 1))
        both = mm(rows, w_in[:, columns])
        gate = both[:, :CHUNK]
        both_ref[at : at + count, columns] = both
        hidden_ref[at : at + count, CHUNK * chunk : CHUNK * (chunk + 1)] = (
            gate * jax.nn.sigmoid(gate) * both[:, CHUNK:]
        ).astype(BF16)


def made_half(half, count, hidden_ref, w_out):
    return mm(hidden_ref[half * count : (half + 1) * count], w_out[...])


def back_half(half, grad_rows, w_in, w_out, both_ref, grad_ref):
    count = grad_rows.shape[0]
    at = half * count
    total = 0.0
    for chunk in range(w_out.shape[0] // CHUNK):
        columns = slice(2 * CHUNK * chunk, 2 * CHUNK * (chunk + 1))
        both = both_ref[at : at + count, columns]
        gate, up = both[:, :CHUNK], both[:, CHUNK:]
        sig = jax.nn.sigmoid(gate)
        grad_hidden = mm(grad_rows, w_out[CHUNK * chunk : CHUNK * (chunk + 1)], NT)
        grad_gate = grad_hidden * up * sig * (1.0 + gate * (1.0 - sig))
        grad_both = jnp.concatenate([grad_gate, grad_hidden * gate * sig], axis=1).astype(BF16)
        grad_ref[at : at + count, columns] = grad_both
        total = total + mm(grad_both, w_in[:, columns], NT)
    return total


def all_rows(ref):
    groups, owners, room, width = ref.shape
    return ref[...].reshape(groups * owners * room, width)


def experts_both_kernel(buffer, grad_buffer, w_in, w_out, made, returned, grad_in, grad_out, both_ref, hidden_ref, grad_ref, *scratch):
    tokens, grads = exchanges(2, [buffer, grad_buffer], scratch)
    count = both_ref.shape[0] // 2
    greet(tokens)
    tokens.start()
    grads.start()
    tokens.spread()
    grads.spread()
    tokens.near_ready()
    keep_forward(0, half_rows(tokens.groups, 0), w_in, both_ref, hidden_ref)
    set_half(tokens.partial, 0, made_half(0, count, hidden_ref, w_out))
    tokens.to_sibling(0).start()
    grads.near_ready()
    set_half(grads.partial, 0, back_half(0, half_rows(grads.groups, 0), w_in, w_out, both_ref, grad_ref))
    grads.to_sibling(0).start()
    tokens.spread_far()
    grads.spread_far()
    tokens.far_ready()
    keep_forward(1, half_rows(tokens.groups, 1), w_in, both_ref, hidden_ref)
    set_half(tokens.partial, 1, made_half(1, count, hidden_ref, w_out))
    tokens.to_sibling(1).start()
    grads.far_ready()
    set_half(grads.partial, 1, back_half(1, half_rows(grads.groups, 1), w_in, w_out, both_ref, grad_ref))
    grads.to_sibling(1).start()
    tokens.return_far()
    grads.return_far()
    grad_out[...] = mm(hidden_ref[...], all_rows(grads.groups), TN).astype(BF16)
    tokens.return_home()
    grads.return_home()
    for chunk in range(grad_in.shape[1] // (2 * CHUNK)):
        columns = slice(2 * CHUNK * chunk, 2 * CHUNK * (chunk + 1))
        grad_in[:, columns] = mm(all_rows(tokens.groups), grad_ref[:, columns], TN).astype(BF16)
    for one in (tokens, grads):
        one.finish_dispatch()
        one.finish()
    made[...] = tokens.result[...]
    returned[...] = grads.result[...]


def experts_back_kernel(grad_buffer, arrived, w_in, w_out, returned, grad_in, grad_out, both_ref, hidden_ref, grad_ref, *scratch):
    (grads,) = exchanges(1, [grad_buffer], scratch)
    greet(grads)
    grads.start()
    grads.spread()
    keep_forward(0, half_rows(arrived, 0), w_in, both_ref, hidden_ref)
    grads.near_ready()
    set_half(grads.partial, 0, back_half(0, half_rows(grads.groups, 0), w_in, w_out, both_ref, grad_ref))
    grads.to_sibling(0).start()
    grads.spread_far()
    keep_forward(1, half_rows(arrived, 1), w_in, both_ref, hidden_ref)
    grads.far_ready()
    set_half(grads.partial, 1, back_half(1, half_rows(grads.groups, 1), w_in, w_out, both_ref, grad_ref))
    grads.to_sibling(1).start()
    grads.return_far()
    grad_out[...] = mm(hidden_ref[...], all_rows(grads.groups), TN).astype(BF16)
    grads.return_home()
    for chunk in range(grad_in.shape[1] // (2 * CHUNK)):
        columns = slice(2 * CHUNK * chunk, 2 * CHUNK * (chunk + 1))
        grad_in[:, columns] = mm(all_rows(arrived), grad_ref[:, columns], TN).astype(BF16)
    grads.finish_dispatch()
    grads.finish()
    returned[...] = grads.result[...]


def run_experts(kernel, identity, streams, blocks, args, out, kept=(), flops=0):
    owners, room, width = blocks
    return pl.pallas_call(
        kernel,
        out_shape=out,
        in_specs=[pl.BlockSpec(memory_space=pltpu.VMEM) for _ in args],
        out_specs=[pl.BlockSpec(memory_space=pltpu.VMEM) for _ in out],
        scratch_shapes=list(kept) + exchange_scratch(streams, owners, room, width),
        compiler_params=pltpu.CompilerParams(
            vmem_limit_bytes=VMEM_BYTES, collective_id=identity, has_side_effects=True
        ),
        cost_estimate=pl.CostEstimate(flops=flops, bytes_accessed=16 << 20, transcendentals=0),
    )(*args)


class Spread:
    def __init__(self, packed, in_pieces, out_pieces, attn, w_in, w_out, sems):
        self.packed, self.in_pieces, self.out_pieces = packed, in_pieces, out_pieces
        self.attn, self.w_in, self.w_out = attn, w_in, w_out
        (self.own_sem, self.z_s, self.z_r, self.plane_s, self.plane_r, self.core_s, self.core_r,
         self.in_s, self.in_r, self.out_s, self.out_r, self.own_in, self.own_out) = sems
        self.core, self.column, self.place = lax.axis_index("section"), lax.axis_index("expert"), lax.axis_index("shard")
        self.owners, self.pieces = lax.axis_size("expert"), lax.axis_size("shard")

    def spot(self, column, place):
        rows = self.packed.shape[0]
        return pl.ds(pl.multiple_of((column * self.pieces + place) * rows, rows), rows)

    def column_by(self, by):
        return lax.rem(self.column + by + self.owners, self.owners)

    def place_by(self, by):
        return lax.rem(self.place + by + self.pieces, self.pieces)

    def copy(self, source, target, send, recv, device):
        return pltpu.make_async_remote_copy(source, target, send, recv, device_id=device, device_id_type=MESH)

    def own(self):
        return pltpu.make_async_copy(self.packed, self.attn.at[self.core, self.spot(self.column, self.place)], self.own_sem)

    def along(self, by):
        block = self.attn.at[self.core, self.spot(self.column, self.place)]
        return self.copy(self.packed, block, self.z_s.at[by], self.z_r.at[by], (self.core, self.column, self.place_by(by)))

    def along_in(self, by):
        block = self.attn.at[self.core, self.spot(self.column, self.place_by(-by))]
        return self.copy(self.packed, block, self.z_s.at[by], self.z_r.at[by], (self.core, self.column, self.place_by(-by)))

    def plane(self, back, by):
        block = self.attn.at[self.core, self.spot(self.column, self.place_by(-back))]
        source = self.packed if back == 0 else block
        return self.copy(
            source, block, self.plane_s.at[back, by], self.plane_r.at[back, by], (self.core, self.column_by(by), self.place)
        )

    def plane_in(self, back, by):
        block = self.attn.at[self.core, self.spot(self.column_by(-by), self.place_by(-back))]
        return self.copy(
            block, block, self.plane_s.at[back, by], self.plane_r.at[back, by], (self.core, self.column_by(-by), self.place)
        )

    def over(self, back, by, section):
        block = self.attn.at[section, self.spot(self.column_by(-by), self.place_by(-back))]
        source = self.packed if back == 0 and by == 0 else block
        return self.copy(
            source, block, self.core_s.at[back, by], self.core_r.at[back, by], (1 - self.core, self.column, self.place)
        )

    def begin(self):
        self.own().start()
        for by in range(1, self.pieces):
            self.along(by).start()
        for by in range(1, self.owners):
            self.plane(0, by).start()
        self.over(0, 0, self.core).start()

    def pass_on(self):
        for back in range(1, self.pieces):
            self.along_in(back).wait_recv()
            for by in range(1, self.owners):
                self.plane(back, by).start()
            self.over(back, 0, self.core).start()

    def pass_over(self):
        for back in range(self.pieces):
            for by in range(1, self.owners):
                self.plane_in(back, by).wait_recv()
                self.over(back, by, self.core).start()
        self.own().wait()

    def over_ready(self):
        for back in range(self.pieces):
            for by in range(self.owners):
                self.over(back, by, 1 - self.core).wait_recv()

    def finish_attn(self):
        for by in range(1, self.pieces):
            self.along(by).wait_send()
        for back in range(self.pieces):
            for by in range(1, self.owners):
                self.plane(back, by).wait_send()
            for by in range(self.owners):
                self.over(back, by, self.core).wait_send()

    def in_rows(self, place):
        rows = self.in_pieces.shape[2]
        return pl.ds(pl.multiple_of(place * rows, rows), rows)

    def out_rows(self, place):
        rows = self.out_pieces.shape[1]
        return pl.ds(pl.multiple_of(lax.div(place, 2) * rows, rows), rows)

    def in_copy(self, cross, by):
        core = 1 - self.core if cross else self.core
        place = self.place_by(by)
        return self.copy(
            self.in_pieces.at[core, lax.rem(place, 2)], self.w_in.at[self.core, self.in_rows(self.place)],
            self.in_s.at[cross, by], self.in_r.at[cross, by], (core, self.column, place),
        )

    def in_here(self, cross, by):
        core = 1 - self.core if cross else self.core
        place = self.place_by(-by)
        return self.copy(
            self.in_pieces.at[core, lax.rem(place, 2)], self.w_in.at[core, self.in_rows(place)],
            self.in_s.at[cross, by], self.in_r.at[cross, by], (core, self.column, place),
        )

    def out_copy(self, cross, by):
        core = 1 - self.core if cross else self.core
        return self.copy(
            self.out_pieces.at[core], self.w_out.at[self.core, self.out_rows(self.place)],
            self.out_s.at[cross, by // 2], self.out_r.at[cross, by // 2], (core, self.column, self.place_by(by)),
        )

    def out_here(self, cross, by):
        core = 1 - self.core if cross else self.core
        place = self.place_by(-by)
        return self.copy(
            self.out_pieces.at[core], self.w_out.at[core, self.out_rows(place)],
            self.out_s.at[cross, by // 2], self.out_r.at[cross, by // 2], (core, self.column, place),
        )

    def own_pieces(self):
        return (
            pltpu.make_async_copy(
                self.in_pieces.at[self.core, lax.rem(self.place, 2)],
                self.w_in.at[self.core, self.in_rows(self.place)], self.own_in,
            ),
            pltpu.make_async_copy(
                self.out_pieces.at[self.core], self.w_out.at[self.core, self.out_rows(self.place)], self.own_out
            ),
        )

    def expert_routes(self):
        for by in range(self.pieces):
            for cross in (0, 1):
                if by or cross:
                    yield cross, by

    def begin_experts(self):
        for one in self.own_pieces():
            one.start()
        for cross, by in self.expert_routes():
            self.in_copy(cross, by).start()
            if by % 2 == 0:
                self.out_copy(cross, by).start()

    def experts_ready(self, cross):
        for way, by in self.expert_routes():
            if way == cross:
                self.in_here(cross, by).wait_recv()
                if by % 2 == 0:
                    self.out_here(cross, by).wait_recv()
        if not cross:
            for one in self.own_pieces():
                one.wait()

    def finish_experts(self):
        for cross, by in self.expert_routes():
            self.in_copy(cross, by).wait_send()
            if by % 2 == 0:
                self.out_copy(cross, by).wait_send()


def spread_scratch(owners, pieces):
    dma = pltpu.SemaphoreType.DMA
    return [
        dma, dma((pieces,)), dma((pieces,)), dma((pieces, owners)), dma((pieces, owners)), dma((pieces, owners)),
        dma((pieces, owners)), dma((2, pieces)), dma((2, pieces)), dma((2, pieces // 2)), dma((2, pieces // 2)), dma, dma,
    ]


SPREAD_SEMS = 13


def greet_all(spread):
    barrier = pltpu.get_barrier_semaphore()
    for by in range(1, spread.owners):
        pl.semaphore_signal(
            barrier, inc=1, device_id=(spread.core, spread.column_by(by), spread.place), device_id_type=MESH
        )
    for cross, by in spread.expert_routes():
        core = 1 - spread.core if cross else spread.core
        pl.semaphore_signal(barrier, inc=1, device_id=(core, spread.column, spread.place_by(by)), device_id_type=MESH)
    pl.semaphore_wait(barrier, spread.owners - 1 + 2 * spread.pieces - 1)


def front_kernel(
    dims, inside,
    packed, in_pieces, out_pieces, x, r, mix, cosine, sine, seg_col, seg_row, ints, prio_row, grad_y, *rest,
):
    if inside:
        attn, *rest = rest
    else:
        attn, *rest = rest
    (w_in, w_out, arrived, after_0, qkv_0, probs_0, attended_0, packed_0, slots_0, r_next,
     out, picked, after_1, qkv_1, probs_1, attended_1, packed_1, slots_1, buffer, grad_buffer, *scratch) = rest
    small, first_buffer = scratch[:2]
    width = x.shape[1]
    spread = Spread(packed, in_pieces, out_pieces, attn, w_in, w_out, scratch[2 : 2 + SPREAD_SEMS])
    (tokens,) = exchanges(1, [first_buffer], scratch[2 + SPREAD_SEMS :])
    first, second = spread.core == 0, spread.core == 1
    greet_all(spread)

    @pl.when(first)
    def _():
        if inside:
            spread.begin()
            spread.pass_on()
        spread.begin_experts()
        if inside:
            spread.pass_over()

    @pl.when(second)
    def _():
        if inside:
            spread.over_ready()

    small[0] = attn[0, :, 4 * width :]
    attend_kernel(
        dims, x, r, attn.at[0], small.at[0], mix.at[0], cosine, sine, seg_col, seg_row, ints.at[0], prio_row.at[0],
        after_0, qkv_0, probs_0, attended_0, packed_0, slots_0, r_next, first_buffer,
    )
    tokens.start()

    @pl.when(second)
    def _():
        if inside:
            spread.begin()

    tokens.spread()

    @pl.when(first)
    def _():
        spread.experts_ready(0)

    @pl.when(second)
    def _():
        if inside:
            spread.pass_on()
        spread.experts_ready(1)

    tokens.near_ready()
    set_half(tokens.partial, 0, experts_forward_half(half_rows(tokens.groups, 0), w_in.at[0], w_out.at[0]))
    tokens.to_sibling(0).start()
    tokens.spread_far()
    tokens.far_ready()
    set_half(tokens.partial, 1, experts_forward_half(half_rows(tokens.groups, 1), w_in.at[0], w_out.at[0]))
    tokens.to_sibling(1).start()
    tokens.return_far()

    @pl.when(second)
    def _():
        if inside:
            spread.pass_over()
        spread.begin_experts()

    arrived[...] = tokens.groups[...]
    tokens.return_home()
    tokens.finish_dispatch()
    tokens.finish()
    if inside:

        @pl.when(first)
        def _():
            spread.over_ready()

    small[1] = attn[1, :, 4 * width :]
    middle_kernel(
        dims, after_0, packed_0, slots_0, ints.at[0], tokens.result, small.at[0],
        r_next, attn.at[1], small.at[1], mix.at[1], cosine, sine, seg_col, seg_row, ints.at[1], prio_row.at[1], grad_y,
        out, picked, after_1, qkv_1, probs_1, attended_1, packed_1, slots_1, buffer, grad_buffer,
    )

    @pl.when(first)
    def _():
        spread.experts_ready(1)

    @pl.when(second)
    def _():
        spread.experts_ready(0)

    if inside:
        spread.finish_attn()
    spread.finish_experts()


def run_front(dims, inside, args, out, owners, pieces, blocks, width):
    vmem, anywhere = pl.BlockSpec(memory_space=pltpu.VMEM), pl.BlockSpec(memory_space=pl.ANY)
    in_specs = [vmem] * len(args)
    in_specs[1] = in_specs[2] = anywhere
    return pl.pallas_call(
        functools.partial(front_kernel, dims, inside),
        out_shape=out,
        in_specs=in_specs,
        out_specs=[vmem] * len(out),
        scratch_shapes=[pltpu.VMEM((2, width, LANES), BF16), pltpu.VMEM(blocks, BF16)]
        + spread_scratch(owners, pieces)
        + exchange_scratch(1, *blocks),
        compiler_params=pltpu.CompilerParams(
            vmem_limit_bytes=VMEM_BYTES, collective_id=0, has_side_effects=True
        ),
        cost_estimate=pl.CostEstimate(flops=8 << 30, bytes_accessed=40 << 20, transcendentals=0),
    )(*args)


def place_of():
    return lax.axis_index("section"), lax.axis_index("expert"), lax.axis_index("shard")


def remote(source, target, send, recv, device):
    return pltpu.make_async_remote_copy(source, target, send, recv, device_id=device, device_id_type=MESH)


class ExpertSum:
    def __init__(self, grad_in, grad_out, got_in, got_out, sems):
        self.grad_in, self.grad_out, self.got_in, self.got_out = grad_in, grad_out, got_in, got_out
        self.in_s, self.in_r, self.out_s, self.out_r = sems
        self.core, self.column, self.place = place_of()
        self.pieces = lax.axis_size("shard")

    def place_by(self, by):
        return lax.rem(self.place + by + self.pieces, self.pieces)

    def in_rows(self, place):
        rows = self.got_in.shape[1]
        return pl.ds(pl.multiple_of(place * rows, rows), rows)

    def out_rows(self, place):
        rows = self.got_out.shape[1]
        return pl.ds(pl.multiple_of(lax.div(place, 2) * rows, rows), rows)

    def in_copy(self, by, way=1):
        place = self.place_by(way * by)
        return remote(
            self.grad_in.at[self.in_rows(place)], self.got_in.at[by - 1], self.in_s.at[by - 1], self.in_r.at[by - 1],
            (self.core, self.column, place),
        )

    def out_copy(self, by, way=1):
        place = self.place_by(way * by)
        at = by // 2 - 1
        return remote(
            self.grad_out.at[self.out_rows(place)], self.got_out.at[at], self.out_s.at[at], self.out_r.at[at],
            (self.core, self.column, place),
        )

    def start(self):
        for by in range(1, self.pieces):
            self.in_copy(by).start()
            if by % 2 == 0:
                self.out_copy(by).start()

    def wait(self):
        for by in range(1, self.pieces):
            self.in_copy(by, -1).wait_recv()
            self.in_copy(by).wait_send()
            if by % 2 == 0:
                self.out_copy(by, -1).wait_recv()
                self.out_copy(by).wait_send()


def expert_sum_sems(pieces):
    dma = pltpu.SemaphoreType.DMA
    return [dma((pieces - 1,)), dma((pieces - 1,)), dma((max(pieces // 2 - 1, 1),)), dma((max(pieces // 2 - 1, 1),))]


class AttnSum:
    def __init__(self, grads, own, from_core, summed, from_plane, through, from_z, sems):
        self.grads, self.own, self.from_core, self.summed = grads, own, from_core, summed
        self.from_plane, self.through, self.from_z = from_plane, through, from_z
        self.own_sem, self.core_s, self.core_r, self.plane_s, self.plane_r, self.z_s, self.z_r = sems
        self.core, self.column, self.place = place_of()
        self.owners, self.pieces = lax.axis_size("expert"), lax.axis_size("shard")

    def block(self, column, k, core):
        rows = self.own.shape[2]
        return self.grads.at[pl.ds(pl.multiple_of((column * self.pieces + 2 * k + core) * rows, rows), rows)]

    def each(self):
        return [(column, k) for column in range(self.owners) for k in range(self.pieces // 2)]

    def load(self, column, k):
        return pltpu.make_async_copy(self.block(column, k, self.core), self.own.at[column, k], self.own_sem.at[column, k])

    def to_core(self, column, k):
        return remote(
            self.block(column, k, 1 - self.core), self.from_core.at[column, k], self.core_s.at[column, k],
            self.core_r.at[column, k], (1 - self.core, self.column, self.place),
        )

    def to_plane(self, by, way=1):
        column = lax.rem(self.column + way * by + self.owners, self.owners)
        return remote(
            self.summed.at[column], self.from_plane.at[by - 1], self.plane_s.at[by - 1], self.plane_r.at[by - 1],
            (self.core, column, self.place),
        )

    def place_by(self, by):
        return lax.rem(self.place + by + self.pieces, self.pieces)

    def along(self, by, way=1):
        place = self.place_by(way * by)
        return remote(
            self.through.at[lax.div(place, 2)], self.from_z.at[by - 1], self.z_s.at[by - 1], self.z_r.at[by - 1],
            (self.core, self.column, place),
        )

    def holds(self, place):
        return lax.rem(place, 2) == self.core

    def start(self):
        for column, k in self.each():
            self.to_core(column, k).start()
        for column, k in self.each():
            self.load(column, k).start()

    def add_cores(self):
        for column, k in self.each():
            self.load(column, k).wait()
            self.to_core(column, k).wait_recv()
        for column in range(self.owners):
            for k in range(self.pieces // 2):
                self.summed[column, k] = (
                    self.own[column, k].astype(F32) + self.from_core[column, k].astype(F32)
                ).astype(BF16)
        for by in range(1, self.owners):
            self.to_plane(by).start()

    def add_plane(self):
        total = self.summed[self.column].astype(F32)
        for by in range(1, self.owners):
            self.to_plane(by, -1).wait_recv()
            total = total + self.from_plane[by - 1].astype(F32)
        self.through[...] = total.astype(BF16)
        for by in range(1, self.pieces):

            @pl.when(self.holds(self.place_by(by)))
            def _():
                self.along(by).start()

    def add_z(self, target):
        @pl.when(self.holds(self.place))
        def _():
            total = self.through[lax.div(self.place, 2)].astype(F32)
            for by in range(1, self.pieces):
                self.along(by, -1).wait_recv()
                total = total + self.from_z[by - 1].astype(F32)
            target[...] = total

    def finish(self):
        for column, k in self.each():
            self.to_core(column, k).wait_send()
        for by in range(1, self.owners):
            self.to_plane(by).wait_send()
        for by in range(1, self.pieces):

            @pl.when(self.holds(self.place_by(by)))
            def _():
                self.along(by).wait_send()


def attn_sum_scratch(owners, pieces, rows, columns):
    blocks = (owners, pieces // 2, rows, columns)
    dma = pltpu.SemaphoreType.DMA
    return [
        pltpu.VMEM(blocks, BF16), pltpu.VMEM(blocks, BF16), pltpu.VMEM(blocks, BF16),
        pltpu.VMEM((owners - 1,) + blocks[1:], BF16), pltpu.VMEM(blocks[1:], BF16),
        pltpu.VMEM((pieces - 1,) + blocks[2:], BF16),
    ], [
        dma(blocks[:2]), dma(blocks[:2]), dma(blocks[:2]), dma((owners - 1,)), dma((owners - 1,)),
        dma((pieces - 1,)), dma((pieces - 1,)),
    ]


def greet_last(inside):
    core, column, place = place_of()
    owners, pieces = lax.axis_size("expert"), lax.axis_size("shard")
    barrier = pltpu.get_barrier_semaphore()
    others = [(1 - core, column, place)]
    others += [(core, column, lax.rem(place + by, pieces)) for by in range(1, pieces)]
    if inside:
        others += [(core, lax.rem(column + by, owners), place) for by in range(1, owners)]
    for device in others:
        pl.semaphore_signal(barrier, inc=1, device_id=device, device_id_type=MESH)
    pl.semaphore_wait(barrier, len(others))


def spread_columns(target, halves_at, hidden_here):
    rows, columns = target.shape
    hidden = columns // 2
    pieces = hidden // (2 * hidden_here)
    parity = lax.rem(lax.axis_index("shard"), 2)
    for first_parity in range(2):

        @pl.when(parity == first_parity)
        def _():
            for half in range(2):
                for q in range(2):
                    odd = first_parity if q == 0 else 1 - first_parity
                    for pair in range(pieces // 2):
                        for side in range(2):
                            for ahead in range(0, hidden_here, CHUNK):
                                at = side * hidden + (2 * pair + odd) * 2 * hidden_here + half * hidden_here + ahead
                                source = 2 * (pair * hidden_here + ahead) + side * CHUNK
                                target[:, at : at + CHUNK] = halves_at(half, q)[:, source : source + CHUNK].astype(F32)


def last_kernel(
    inside, wide, out_0, out_1, grad_x_0, grad_x_1, grad_r_0, grad_r_1, in_0, gout_0, in_1, gout_1, attn_0, attn_1, *rest
):
    (both_out, both_x, both_r, in_total, out_total, attn_total, got_in_0, got_out_0, got_in_1, got_out_1, *scratch) = rest
    (in_mine, out_mine, in_sent, out_sent, in_got, out_got, own_in, own_out, attn_sum_0, attn_sum_1,
     swap_s, swap_r, local_sem, final_s, final_r, own_sems, *scratch) = scratch
    core, column, place = place_of()
    pieces = lax.axis_size("shard")
    sibling = (1 - core, column, place)
    experts = [
        ExpertSum(in_0, gout_0, got_in_0, got_out_0, scratch[:4]),
        ExpertSum(in_1, gout_1, got_in_1, got_out_1, scratch[4:8]),
    ]
    scratch = scratch[8:]
    attn = []
    if inside:
        attn = [AttnSum(attn_0, *scratch[:6], scratch[6:13]), AttnSum(attn_1, *scratch[13:19], scratch[19:26])]
    greet_last(inside)
    pairs = ((out_0, out_1, both_out), (grad_x_0, grad_x_1, both_x), (grad_r_0, grad_r_1, both_r))

    def swaps(section):
        for i, (zero, one, both) in enumerate(pairs):
            own, other = (zero, one) if section == 0 else (one, zero)
            yield (
                remote(other, both.at[section], swap_s.at[i], swap_r.at[i], sibling),
                pltpu.make_async_copy(own, both.at[section], local_sem.at[i]),
            )

    def each_core(action):
        for section in range(2):

            @pl.when(core == section)
            def _():
                action(section)

    for one in reversed(attn):
        one.start()
    experts[1].start()

    @each_core
    def _(section):
        for away, here in swaps(section):
            away.start()
            here.start()

    for one in reversed(attn):
        one.add_cores()
    experts[0].start()
    loads = []
    for s in (1, 0):
        e = experts[s]
        loads.append((
            pltpu.make_async_copy(e.grad_in.at[e.in_rows(place)], own_in.at[s, 0], own_sems.at[s, 0]),
            pltpu.make_async_copy(e.grad_out.at[e.out_rows(place)], own_out.at[s, 0], own_sems.at[s, 1]),
        ))
        for one in loads[-1]:
            one.start()
    for one in reversed(attn):
        one.add_plane()
    for n, s in enumerate((1, 0)):
        e = experts[s]
        e.wait()
        for one in loads[n]:
            one.wait()
        copies = [pltpu.make_async_copy(e.got_in, own_in.at[s, pl.ds(1, pieces - 1)], own_sems.at[s, 2])]
        if pieces > 2:
            copies.append(pltpu.make_async_copy(e.got_out, own_out.at[s, pl.ds(1, pieces // 2 - 1)], own_sems.at[s, 3]))
        for one in copies:
            one.start()
        for one in copies:
            one.wait()
        in_sum = [sum(own_in[s, by].astype(F32) for by in range(q, pieces, 2)) for q in range(2)]
        out_sum = sum(own_out[s, i].astype(F32) for i in range(pieces // 2))

        @pl.when(core == s)
        def _():
            for q in range(2):
                in_mine[q] = in_sum[q]
            out_mine[...] = out_sum

        @pl.when(core != s)
        def _():
            for q in range(2):
                in_sent[q] = in_sum[q].astype(BF16)
            out_sent[...] = out_sum.astype(BF16)

    finals = [
        remote(in_sent, in_got, final_s.at[0], final_r.at[0], sibling),
        remote(out_sent, out_got, final_s.at[1], final_r.at[1], sibling),
    ]
    for one in finals:
        one.start()
    if inside:
        attn[1].add_z(attn_sum_1)
        attn[0].add_z(attn_sum_0)
        holder = attn[0].holds(place)
        for section in range(2):
            mine, other = (attn_sum_0, attn_sum_1) if section == 0 else (attn_sum_1, attn_sum_0)
            home = remote(other, attn_total, final_s.at[2], final_r.at[2], sibling)

            @pl.when(holder & (core == section))
            def _():
                home.start()
                attn_total[...] = mine[...]
                home.wait_send()

            @pl.when(jnp.logical_not(holder) & (core == section))
            def _():
                home.wait_recv()

    for one in finals:
        one.wait()
    for half in range(2):

        @pl.when(core == half)
        def _():
            if wide:
                hidden_here = out_mine.shape[0]
                spread_columns(
                    in_total, lambda at, q: in_mine[q] if at == half else in_got[q], hidden_here
                )
            else:
                for q in range(2):
                    in_total[half, q] = in_mine[q]
                    in_total[1 - half, q] = in_got[q].astype(F32)
            count = out_mine.shape[0]
            out_total[half * count : (half + 1) * count] = out_mine[...]
            out_total[(1 - half) * count : (2 - half) * count] = out_got[...].astype(F32)

    @each_core
    def _(section):
        for away, here in swaps(section):
            away.wait()
            here.wait()

    for one in attn:
        one.finish()


def run_last(inside, wide, args, owners, pieces, hidden_here, rows):
    vmem, anywhere = pl.BlockSpec(memory_space=pltpu.VMEM), pl.BlockSpec(memory_space=pl.ANY)
    seq_len, width = args[0].shape
    columns = args[6].shape[1]
    in_rows = width // pieces
    attn_columns = args[10].shape[1]
    in_shape = (in_rows, 4 * columns) if wide else (2, 2, in_rows, columns)
    got = [
        shaped((pieces - 1, in_rows, columns), BF16), shaped((max(pieces // 2 - 1, 1), hidden_here, width), BF16)
    ] * 2
    attn_shape = (rows, attn_columns) if inside else (8, LANES)
    out = [
        shaped((2,) + args[0].shape, BF16), shaped((2,) + args[2].shape, F32), shaped((2,) + args[4].shape, F32),
        shaped(in_shape, F32), shaped((2 * hidden_here, width), F32), shaped(attn_shape, F32),
    ] + got
    dma = pltpu.SemaphoreType.DMA
    scratch = [
        pltpu.VMEM((2, in_rows, columns), F32), pltpu.VMEM((hidden_here, width), F32),
        pltpu.VMEM((2, in_rows, columns), BF16), pltpu.VMEM((hidden_here, width), BF16),
        pltpu.VMEM((2, in_rows, columns), BF16), pltpu.VMEM((hidden_here, width), BF16),
        pltpu.VMEM((2, pieces, in_rows, columns), BF16), pltpu.VMEM((2, pieces // 2, hidden_here, width), BF16),
        pltpu.VMEM(attn_shape, F32), pltpu.VMEM(attn_shape, F32),
        dma((3,)), dma((3,)), dma((3,)), dma((3,)), dma((3,)), dma((2, 4)),
    ]
    for _ in range(2):
        scratch += expert_sum_sems(pieces)
    if inside:
        for _ in range(2):
            buffers, sems = attn_sum_scratch(owners, pieces, rows, attn_columns)
            scratch += buffers + sems
    specs = [anywhere] * 3 + [vmem] * 3 + [anywhere] * 4
    return pl.pallas_call(
        functools.partial(last_kernel, inside, wide),
        out_shape=out,
        in_specs=[anywhere] * len(args),
        out_specs=specs,
        scratch_shapes=scratch,
        compiler_params=pltpu.CompilerParams(
            vmem_limit_bytes=VMEM_BYTES, collective_id=3, has_side_effects=True
        ),
        cost_estimate=pl.CostEstimate(flops=1 << 28, bytes_accessed=40 << 20, transcendentals=0),
    )(*args)


def local(
    x_in,
    cotangent,
    gate_prev,
    segments,
    routes,
    priority,
    attn_qkv,
    attn_out,
    router,
    const_proj,
    const_vec,
    gains,
    gate_mix,
    expert_in,
    expert_out,
):
    seq_len, width = x_in.shape[2:]
    nexp = gate_prev.shape[-1]
    owners, pieces = lax.axis_size("expert"), lax.axis_size("shard")
    nffn = owners * expert_in.shape[1]
    nconst = const_vec.shape[-1]
    capacity = (5 * TOP * seq_len + 4 * nexp - 1) // (4 * nexp)
    room = -(-capacity // 16) * 16
    slots = nffn * room
    core = lax.axis_index("section")
    first_core = core == 0

    def swap(item):
        return lax.ppermute(item, "section", [(0, 1), (1, 0)])

    def mine(stack, axis=0):
        return lax.dynamic_index_in_dim(stack, core, axis, keepdims=False)

    def others(stack, axis=0):
        return lax.dynamic_index_in_dim(stack, 1 - core, axis, keepdims=False)

    def by_section(own, other):
        return jnp.where(first_core, own, other), jnp.where(first_core, other, own)

    in_rows, columns = expert_in.shape[2:]
    hidden_here = expert_out.shape[2] // 2
    pairs = pieces // 2
    quarter = pairs * hidden_here
    chunks = quarter // CHUNK
    pair_index = lax.axis_index("shard") // 2
    w_in = expert_in[0, 0].reshape(in_rows, 2, pairs, 2, 2, hidden_here)

    def as_chunks(half):
        half = jnp.moveaxis(half, 3, 0).reshape(2, in_rows, 2, chunks, CHUNK)
        return jnp.swapaxes(half, 2, 3).reshape(2, in_rows, 2 * quarter)

    w_out = expert_out[0, 0].reshape(2, hidden_here, width)
    in_pieces = jnp.stack([as_chunks(w_in[:, :, :, :, half]) for half in range(2)])

    rows = attn_qkv.shape[1]

    def lanes(array, upto):
        return jnp.pad(array, ((0, 0), (0, upto - array.shape[1])))

    small = jnp.concatenate(
        [
            lanes(router[0], AT_PROJ),
            lanes(const_proj[0], AT_VEC - AT_PROJ),
            lanes(const_vec[0], AT_GAIN - AT_VEC),
            lanes(gains[0], LANES - AT_GAIN),
        ],
        axis=1,
    )
    packed = jnp.concatenate([attn_qkv[0], attn_out[0], small], axis=1)
    inside = rows % 16 == 0
    given = []
    if not inside:
        shared = lax.all_gather(packed, ("expert", "shard"), axis=0, tiled=True)
        given = [jnp.stack(by_section(shared, swap(shared)))]
    mix_own = jnp.pad(gate_mix[0], ((0, LANES - nexp), (0, LANES - nexp)))
    mix_all = jnp.stack(by_section(mix_own, swap(mix_own)))
    ints_own = jnp.concatenate([routes[0, :, 0], priority[0, :, 0, :, None]], axis=-1)
    ints_all = jnp.stack(by_section(mine(ints_own), swap(others(ints_own))))
    x_first = mine(x_in[:, 0])
    r_first = jnp.pad(mine(gate_prev[:, 0]), ((0, 0), (0, LANES - nexp)))
    upstream = mine(cotangent[:, 0])
    seg = mine(segments[:, 0])
    place = lax.iota(jnp.int32, seq_len)
    start = jnp.sum((seg[None, :] < seg[:, None]).astype(F32), axis=1)
    angles = (place.astype(F32) - start)[:, None] * jnp.exp(
        lax.iota(F32, HEAD // 2) * (-2.0 * math.log(10000.0) / HEAD)
    )[None, :]
    cosine, sine = jnp.cos(angles), jnp.sin(angles)
    cosine = jnp.concatenate([cosine] * 4, axis=1)
    sine = jnp.concatenate([-sine, sine, -sine, sine], axis=1)

    dims = (nffn, nexp, capacity, slots, rows if inside else 0)
    heads = width // HEAD
    blocks = (owners, room, width)
    seg_col, seg_row = seg[:, None], seg[None, :]
    token_f32 = shaped((seq_len, width), F32)
    token_b16 = shaped((seq_len, width), BF16)
    lanes_f32 = shaped((seq_len, LANES), F32)
    slot_shape = shaped((slots, width), BF16)
    block_shape = shaped(blocks, BF16)
    attend_out = [
        token_f32,
        shaped((seq_len, 3 * width), BF16),
        shaped((heads, seq_len, seq_len), BF16),
        token_b16,
        lanes_f32,
        shaped((seq_len, LANES), jnp.int32),
    ]
    attn_shape = shaped((width, 4 * width + LANES), BF16)
    back_out = [token_f32, lanes_f32, shaped((LANES, LANES), F32), attn_shape]
    grad_qkv = pltpu.VMEM((seq_len, 3 * width), BF16)
    prio = ints_all[:, None, :, 2]
    rows_there = 4 * slots
    kept = [
        pltpu.VMEM((rows_there, 2 * quarter), F32),
        pltpu.VMEM((rows_there, quarter), BF16),
        pltpu.VMEM((rows_there, 2 * quarter), BF16),
    ]
    grad_shapes = [shaped((width, 2 * quarter), BF16), shaped((quarter, width), BF16)]
    work = 2 * rows_there * width * quarter

    middle_out = [token_b16, shaped((TOP, seq_len, width), BF16)] + attend_out + [slot_shape, slot_shape]
    outs = [shaped((2, width, 2 * quarter), BF16), shaped((2, quarter, width), BF16), shaped((4,) + blocks, BF16)]
    outs += attend_out + [shaped((seq_len, LANES), BF16)] + middle_out
    if inside:
        outs = [shaped((2,) + attn_shape.shape, BF16)] + outs
    got = run_front(
        dims, inside,
        [packed, in_pieces, w_out, x_first, r_first, mix_all, cosine, sine, seg_col, seg_row, ints_all, prio, upstream] + given,
        outs, owners, pieces, blocks, width,
    )
    (attn_all, w_in_all, w_out_all, arrived, after_0, qkv_0, probs_0, attended_0, packed_0, slots_0, r_next,
     out_0, picked_0, after_1, qkv_1, probs_1, attended_1, packed_1, slots_1, buffer, grad_buffer) = given + list(got)
    shared = (attn_all[0], attn_all[1])
    smalls = [w[:, 4 * width :] for w in shared]
    experts = [(w_in_all[s], w_out_all[s]) for s in range(2)]
    w, ints = shared[0], ints_all[0]
    made, returned, grad_in_1, grad_out_1 = run_experts(
        experts_both_kernel, 1, 2, blocks, (buffer.reshape(blocks), grad_buffer.reshape(blocks), *experts[1]),
        [block_shape, block_shape] + grad_shapes, kept, flops=9 * work,
    )
    out_1, grad_x_1, grad_r_1, grad_mix_1, grads_1, buffer = run(
        functools.partial(turn_kernel, dims),
        [token_b16] + back_out + [slot_shape],
        (
            upstream, after_1, packed_1, slots_1, ints_all[1], made.reshape(slots, width), returned.reshape(slots, width),
            r_next, shared[1], smalls[1], mix_all[1], out_0, qkv_1, probs_1, attended_1, cosine, sine, packed_0, slots_0,
        ),
        flops=5 << 30,
        scratch=[grad_qkv, pltpu.VMEM((TOP, seq_len, width), BF16)],
    )
    returned, grad_in_0, grad_out_0 = run_experts(
        experts_back_kernel, 2, 1, blocks, (buffer.reshape(blocks), arrived, *experts[0]),
        [block_shape] + grad_shapes, kept, flops=9 * work,
    )
    grad_x_0, grad_r_0, grad_mix_0, grads_0 = run(
        functools.partial(back_kernel, dims),
        back_out,
        (
            grad_x_1, grad_r_1, after_0, packed_0, slots_0, ints, picked_0, returned.reshape(slots, width),
            r_first, w, smalls[0], mix_all[0], x_first, qkv_0, probs_0, attended_0, cosine, sine,
        ),
        flops=5 << 30,
        scratch=[grad_qkv],
    )
    wide = hidden_here % CHUNK == 0
    both_out, both_x, both_r, in_grad, out_grad, shared_sum, *_ = run_last(
        inside, wide,
        (out_0, out_1, grad_x_0, grad_x_1, grad_r_0, grad_r_1, grad_in_0, grad_out_0, grad_in_1, grad_out_1, grads_0, grads_1),
        owners, pieces, hidden_here, rows,
    )
    if not wide:
        odd = lax.axis_index("shard") % 2
        in_grad = jnp.where(odd == 0, in_grad, in_grad[:, ::-1])
        in_grad = jnp.swapaxes(in_grad.reshape(2, 2, in_rows, chunks, 2, CHUNK), 3, 4)
        in_grad = in_grad.reshape(2, 2, in_rows, 2, pairs, hidden_here)
        in_grad = jnp.transpose(in_grad, (2, 3, 4, 1, 0, 5)).reshape(in_rows, columns)
    if inside:
        mix_grad = shared_sum[:nexp, 4 * width + AT_MIX : 4 * width + AT_MIX + nexp]
    else:
        own = jnp.where(first_core, grads_0, grads_1)
        shared_sum = own.astype(F32) + swap(jnp.where(first_core, grads_1, grads_0)).astype(F32)
        shared_sum = lax.psum_scatter(
            shared_sum.astype(BF16), ("expert", "shard"), scatter_dimension=0, tiled=True
        ).astype(F32)
        own = jnp.where(first_core, grad_mix_0, grad_mix_1)
        mix_grad = own + swap(jnp.where(first_core, grad_mix_1, grad_mix_0))
        mix_grad = lax.psum(mix_grad, ("expert", "shard"))[:nexp, :nexp]
    small_sum = shared_sum[:, 4 * width :]
    return (
        both_out[None, :, None],
        both_x[None, :, None],
        both_r[None, :, None, :, :nexp],
        shared_sum[None, :, : 3 * width],
        shared_sum[None, :, 3 * width : 4 * width],
        small_sum[None, :, :nexp],
        small_sum[None, :, AT_PROJ : AT_PROJ + const_proj.shape[-1]],
        small_sum[None, :, AT_VEC : AT_VEC + nconst],
        small_sum[None, :, AT_GAIN : AT_GAIN + 2],
        mix_grad[None],
        in_grad[None, None],
        out_grad[None, None],
    )


def solution(mesh):
    placed = (
        P(None, ("expert", "shard"), None, None),
        P(None, ("expert", "shard"), None, None),
        P(None, ("expert", "shard"), None, None),
        P(None, ("expert", "shard"), None),
        P("section", None, ("expert", "shard"), None, None),
        P("section", None, ("expert", "shard"), None),
        P("section", ("expert", "shard"), None),
        P("section", ("expert", "shard"), None),
        P("section", ("expert", "shard"), None),
        P("section", ("expert", "shard"), None),
        P("section", ("expert", "shard"), None),
        P("section", ("expert", "shard"), None),
        P("section", None, None),
        P("section", "expert", "shard", None),
        P("section", "expert", "shard", None),
    )
    return jax.shard_map(
        local,
        mesh=mesh,
        in_specs=placed,
        out_specs=(
            P("section", None, ("expert", "shard"), None, None),
            P("section", None, ("expert", "shard"), None, None),
            P("section", None, ("expert", "shard"), None, None),
            P("section", ("expert", "shard"), None),
            P("section", ("expert", "shard"), None),
            P("section", ("expert", "shard"), None),
            P("section", ("expert", "shard"), None),
            P("section", ("expert", "shard"), None),
            P("section", ("expert", "shard"), None),
            P("section", None, None),
            P("section", "expert", "shard", None),
            P("section", "expert", "shard", None),
        ),
        check_vma=False,
    )
```

```python
import math
import types

import jax
import jax.numpy as jnp
from jax import lax
from jax.experimental import pallas as pl
from jax.experimental.pallas import tpu as pltpu
from jax.sharding import PartitionSpec as P

HEADS = 12
HEAD = 64
TOP = 2
CHUNK = 256
LANES = 128
AT_PROJ = 16
AT_VEC = 24
AT_GAIN = 28
AT_MIX = 32

HIGH = lax.Precision.HIGHEST
norm_eps = 1e-06
masked_score = -1e30
F32 = jnp.float32
BF16 = jnp.bfloat16


VMEM_BYTES = 60 * 1024 * 1024


def mm(a, b, contract=((1,), (0,)), precision=None):
    return lax.dot_general(a, b, (contract, ((), ())), precision=precision, preferred_element_type=F32)


NT = ((1,), (1,))
TN = ((0,), (0,))


def lane_of(rows, columns=LANES):
    return lax.broadcasted_iota(jnp.int32, (rows, columns), 1)


def inverse_norm(values):
    return lax.rsqrt(jnp.mean(values * values, axis=-1, keepdims=True) + norm_eps)


def norm_back(grad_unit, unit, inverse):
    return inverse * (grad_unit - unit * jnp.mean(grad_unit * unit, axis=-1, keepdims=True))


def roll(x, by):
    return pltpu.roll(x, by, 1)


def turned(x, lane):
    return jnp.where(lane % HEAD < HEAD // 2, roll(x, LANES - HEAD // 2), roll(x, HEAD // 2))


def hi_lo(x):
    high = x.astype(BF16)
    return high, (x - high.astype(F32)).astype(BF16)


def ones_where(condition):
    return jnp.where(condition, 1.0, 0.0).astype(BF16)


def small_rows_of(small):
    rows = small[...].astype(F32).T
    return rows[AT_GAIN : AT_GAIN + 1], rows[AT_GAIN + 1 : AT_GAIN + 2], rows[AT_VEC:AT_GAIN]


def attention(x, w, gain_first, cosine, sine, seg_col, seg_row, qkv, probs_att, attended):
    seq_len, width = x.shape
    first_b = (x * inverse_norm(x) * gain_first).astype(BF16)
    place_q = lax.broadcasted_iota(jnp.int32, (seq_len, seq_len), 0)
    place_k = lax.broadcasted_iota(jnp.int32, (seq_len, seq_len), 1)
    bias = jnp.where((seg_col == seg_row) & (place_k <= place_q), 0.0, masked_score)
    lane = lane_of(seq_len)
    low_head = lane < HEAD
    for pair in range(width // LANES):
        at = pair * LANES
        q = mm(first_b, w[:, at : at + LANES])
        k = mm(first_b, w[:, width + at : width + at + LANES])
        v = mm(first_b, w[:, 2 * width + at : 2 * width + at + LANES]).astype(BF16)
        q = q * cosine + turned(q, lane) * sine
        k = (k * cosine + turned(k, lane) * sine).astype(BF16)
        outs = []
        for half in range(2):
            one = jnp.where(low_head if half == 0 else lane >= HEAD, q, 0.0).astype(BF16)
            scores = mm(one, k, NT) * (HEAD**-0.5) + bias
            scores = jnp.exp(scores - jnp.max(scores, axis=-1, keepdims=True))
            probs = (scores * (1.0 / jnp.sum(scores, axis=-1, keepdims=True))).astype(BF16)
            probs_att[2 * pair + half] = probs
            outs.append(mm(probs, v))
        attended[:, at : at + LANES] = jnp.where(low_head, outs[0], outs[1]).astype(BF16)
        qkv[:, at : at + LANES] = q.astype(BF16)
        qkv[:, width + at : width + at + LANES] = k
        qkv[:, 2 * width + at : 2 * width + at + LANES] = v
    return x + mm(attended[...], w[:, 3 * width : 4 * width])


def gating(after, r, small, mix, gain_second, ints, prio_row, dims, packed_ref, slot_ref, r_next, buffer):
    nffn, nexp, capacity, slots, _ = dims
    rows = after.shape[0]
    second_b = (after * inverse_norm(after) * gain_second).astype(BF16)
    lane = lane_of(rows)
    logits = mm(second_b, small)
    full = logits + mm(r, mix, precision=HIGH)
    inside = lane < nexp
    full = jnp.where(inside, full, masked_score)
    raised = jnp.exp(full - jnp.max(full, axis=-1, keepdims=True))
    probs = raised / jnp.sum(raised, axis=-1, keepdims=True)
    other = jnp.where(lane % 2 == 0, roll(logits, LANES - 1), roll(logits, 1))
    bigger = jnp.maximum(logits, other)
    mine_e = jnp.exp(logits - bigger)
    mixes = mine_e / (mine_e + jnp.exp(other - bigger))
    before = ones_where(prio_row < column_of(prio_row).astype(jnp.int32))
    route = (ints[:, 0:1], ints[:, 1:2])
    routed = ones_where(((lane == route[0]) | (lane == route[1])) & (lane < nffn))
    rank = mm(before, routed)
    gates, places = [], []
    dispatch = 0.0
    stride = slots // nffn
    for k in range(TOP):
        chosen = lane == route[k]
        gates.append(jnp.sum(jnp.where(chosen, probs, 0.0), axis=-1, keepdims=True))
        rank_k = jnp.sum(jnp.where(chosen, rank, 0.0), axis=-1, keepdims=True).astype(jnp.int32)
        kept = (route[k] < nffn) & (rank_k < capacity)
        places.append(jnp.where(kept, route[k] * stride + rank_k, -1))
        dispatch = dispatch + jnp.where(places[k] == lane_of(rows, slots), 1.0, 0.0)
    buffer[...] = mm(dispatch.astype(BF16), second_b, TN).astype(BF16).reshape(buffer.shape)
    packed = jnp.where(inside, probs, jnp.where((lane >= AT_PROJ) & (lane < AT_VEC), mixes, 0.0))
    packed = jnp.where(lane == AT_VEC, gates[0], packed)
    packed_ref[...] = jnp.where(lane == AT_VEC + 1, gates[1], packed)
    slot_ref[...] = jnp.where(lane == 0, places[0], places[1])
    if r_next is not None:
        r_next[...] = jnp.where(inside, full, 0.0).astype(BF16)


def extras(packed, ints, nffn, nconst):
    gates = (packed[:, AT_VEC : AT_VEC + 1], packed[:, AT_VEC + 1 : AT_VEC + 2])

    def of(expert):
        return sum(jnp.where(ints[:, k : k + 1] == expert, gates[k], 0.0) for k in range(TOP))

    def mixes(c):
        at = AT_PROJ + 2 * c
        return packed[:, at : at + 1], packed[:, at + 1 : at + 2]

    return gates, of(nffn + 1), [of(nffn + 2 + c) for c in range(nconst)], [mixes(c) for c in range(nconst)]


def combine(after, packed, slot_pair, ints, blocks, gain_second, vec_rows, dims, picked_ref):
    nffn, nexp, _, slots, _ = dims
    nconst = nexp - nffn - 2
    rows = after.shape[0]
    second = after * inverse_norm(after) * gain_second
    gates, copied, const, mixes = extras(packed, ints, nffn, nconst)
    made = blocks[...].reshape(slots, after.shape[1])
    slot_lane = lane_of(rows, slots)
    coefficient = copied
    for c in range(nconst):
        coefficient = coefficient + const[c] * mixes[c][0]
    out = after + coefficient * second
    for k in range(TOP):
        picked = mm(ones_where(slot_pair[:, k : k + 1] == slot_lane), made)
        picked_ref[k] = picked.astype(BF16)
        out = out + gates[k] * picked
    for c in range(nconst):
        out = out + (const[c] * mixes[c][1]) * vec_rows[c : c + 1]
    return out


def give_back(grad_y, packed, slot_pair, dims, buffer):
    slots = dims[3]
    slot_lane = lane_of(grad_y.shape[0], slots)
    total = 0.0
    for k in range(TOP):
        gate = packed[:, AT_VEC + k : AT_VEC + k + 1]
        table = ones_where(slot_pair[:, k : k + 1] == slot_lane)
        total = total + mm(table, (gate * grad_y).astype(BF16), TN)
    buffer[...] = total.astype(BF16).reshape(buffer.shape)


def moe_back(
    grad_y, grad_log_in, after, packed, slot_pair, ints, picked, blocks, r, small, mix, gain_second, vec_rows, dims
):
    nffn, nexp, _, slots, _ = dims
    nconst = nexp - nffn - 2
    rows = grad_y.shape[0]
    lane = lane_of(rows)
    inverse = inverse_norm(after)
    unit = after * inverse
    second = unit * gain_second
    second_b = second.astype(BF16)
    gates, copied, const, mixes = extras(packed, ints, nffn, nconst)
    grad_buffer = blocks[...].reshape(slots, after.shape[1])
    slot_lane = lane_of(rows, slots)
    dispatch = sum(jnp.where(slot_pair[:, k : k + 1] == slot_lane, 1.0, 0.0) for k in range(TOP))
    grad_second = mm(dispatch.astype(BF16), grad_buffer)
    along_second = jnp.sum(grad_y * second, axis=-1, keepdims=True)
    coefficient = copied
    grad_extra = [(nffn + 1, along_second)]
    grad_lanes = jnp.zeros((rows, LANES), F32)
    vec_grads = []
    for c in range(nconst):
        along = jnp.sum(grad_y * vec_rows[c : c + 1], axis=-1, keepdims=True)
        m0, m1 = mixes[c]
        coefficient = coefficient + const[c] * m0
        grad_extra.append((nffn + 2 + c, m0 * along_second + m1 * along))
        d0, d1 = const[c] * along_second, const[c] * along
        mean = m0 * d0 + m1 * d1
        at = AT_PROJ + 2 * c
        grad_lanes = jnp.where(lane == at, m0 * (d0 - mean), grad_lanes)
        grad_lanes = jnp.where(lane == at + 1, m1 * (d1 - mean), grad_lanes)
        vec_grads.append(jnp.sum(grad_y * (const[c] * m1), axis=0, keepdims=True))
    grad_second = grad_second + coefficient * grad_y
    grad_probs = jnp.zeros((rows, LANES), F32)
    for k in range(TOP):
        grad_gate = jnp.sum(picked[k].astype(F32) * grad_y, axis=-1, keepdims=True)
        for expert, value in grad_extra:
            grad_gate = grad_gate + jnp.where(ints[:, k : k + 1] == expert, value, 0.0)
        grad_probs = grad_probs + jnp.where(lane == ints[:, k : k + 1], grad_gate, 0.0)
    probs = jnp.where(lane < nexp, packed, 0.0)
    grad_logits = probs * (grad_probs - jnp.sum(probs * grad_probs, axis=-1, keepdims=True)) + grad_log_in
    grad_mix = mm(jnp.where(lane < nexp, r, 0.0), jnp.where(lane < nexp, grad_logits, 0.0), TN, HIGH)
    grad_r = mm(grad_logits, mix, NT, HIGH)
    high, low = hi_lo(jnp.where(lane < nexp, grad_logits, grad_lanes))
    small_rows = mm(high, second_b, TN) + mm(low, second_b, TN)
    grad_second = grad_second + mm(high, small, NT) + mm(low, small, NT)
    grad_gain = jnp.sum(grad_second * unit, axis=0, keepdims=True)
    grad_after = grad_y + norm_back(grad_second * gain_second, unit, inverse)
    row = lax.broadcasted_iota(jnp.int32, small_rows.shape, 0)
    small_rows = jnp.where(row < AT_VEC, small_rows, 0.0)
    for c in range(nconst):
        small_rows = jnp.where(row == AT_VEC + c, vec_grads[c], small_rows)
    small_rows = jnp.where(row == AT_GAIN + 1, grad_gain, small_rows)
    return grad_after, grad_r, grad_mix, small_rows


def attention_back(
    grad_after, x, qkv, probs_att, attended, small_rows, mix_tile, w, gain_first, cosine, sine, grads, grad_qkv, grad_x, between
):
    seq_len, width = x.shape
    inverse = inverse_norm(x)
    unit = x * inverse
    first_b = (unit * gain_first).astype(BF16)
    grad_branch = grad_after.astype(BF16)
    lane = lane_of(seq_len)
    low_head = lane < HEAD
    masks = (ones_where(low_head), ones_where(lane >= HEAD))
    scale = HEAD**-0.5
    for pair in range(width // LANES):
        at = pair * LANES
        q = qkv[:, at : at + LANES]
        k = qkv[:, width + at : width + at + LANES]
        v = qkv[:, 2 * width + at : 2 * width + at + LANES]
        g = mm(grad_branch, w[at : at + LANES, 3 * width : 4 * width], NT).astype(BF16)
        dq, dk, dv = [], [], []
        for half in range(2):
            probs = probs_att[2 * pair + half]
            grad_p = mm(g * masks[half], v, NT)
            p = probs.astype(F32)
            grad_s = (p * (grad_p - jnp.sum(p * grad_p, axis=-1, keepdims=True))).astype(BF16)
            dv.append(mm(probs, g, TN))
            dq.append(mm(grad_s, k))
            dk.append(mm(grad_s, q, TN))
        dq = jnp.where(low_head, dq[0], dq[1]) * scale
        dk = jnp.where(low_head, dk[0], dk[1]) * scale
        grad_qkv[:, at : at + LANES] = (dq * cosine - turned(dq, lane) * sine).astype(BF16)
        grad_qkv[:, width + at : width + at + LANES] = (dk * cosine - turned(dk, lane) * sine).astype(BF16)
        grad_qkv[:, 2 * width + at : 2 * width + at + LANES] = jnp.where(low_head, dv[0], dv[1]).astype(BF16)
    grad_first = mm(grad_qkv[...], w[:, : 3 * width], NT)
    grad_gain = jnp.sum(grad_first * unit, axis=0, keepdims=True)
    grad_x[...] = grad_after + norm_back(grad_first * gain_first, unit, inverse)
    between()
    grads[:, 3 * width : 4 * width] = mm(attended[...], grad_branch, TN).astype(BF16)
    grads[:, : 3 * width] = mm(first_b, grad_qkv[...], TN).astype(BF16)
    row = lax.broadcasted_iota(jnp.int32, small_rows.shape, 0)
    small_rows = jnp.where(row == AT_GAIN, grad_gain, small_rows)
    grads[:, 4 * width :] = (small_rows.T + mix_tile).astype(BF16)


def attend_kernel(
    dims, x, r, w, small, mix, cosine, sine, seg_col, seg_row, ints, prio_row,
    after, qkv, probs_att, attended, packed, slot_pair, r_next, buffer,
):
    gain_first, gain_second, _ = small_rows_of(small)
    after_v = attention(
        x[...].astype(F32), w, gain_first, cosine[...], sine[...], seg_col, seg_row, qkv, probs_att, attended
    )
    after[...] = after_v
    gating(
        after_v, r[...].astype(F32), small[...], mix[...], gain_second, ints[...], prio_row[...], dims,
        packed, slot_pair, r_next, buffer,
    )


def middle_kernel(
    dims, after_0, packed_0, slots_0, ints_0, blocks_0, small_0,
    r, w, small, mix, cosine, sine, seg_col, seg_row, ints, prio_row, grad_y,
    out, picked, after, qkv, probs_att, attended, packed, slot_pair, buffer, grad_buffer,
):
    _, gain_second, vec_rows = small_rows_of(small_0)
    out[...] = combine(
        after_0[...], packed_0[...], slots_0[...], ints_0[...], blocks_0, gain_second, vec_rows, dims, picked
    ).astype(BF16)
    attend_kernel(
        dims, out, r, w, small, mix, cosine, sine, seg_col, seg_row, ints, prio_row,
        after, qkv, probs_att, attended, packed, slot_pair, None, buffer,
    )
    give_back(grad_y[...], packed[...], slot_pair[...], dims, grad_buffer)


def back_body(
    dims, grad_y, grad_log, after, packed, slot_pair, ints, picked, blocks, r, w, small, mix, x, qkv, probs_att, attended,
    cosine, sine, grad_x, grad_r, grad_mix, grads, grad_qkv, loading, between=lambda: None,
):
    gain_first, gain_second, vec_rows = small_rows_of(small)
    grad_log_v = 0.0 if grad_log is None else grad_log[...].astype(BF16).astype(F32)
    grad_y_v = grad_y[...] if grad_log is None else grad_y[...].astype(BF16).astype(F32)
    grad_after, grad_r_v, grad_mix_v, small_rows = moe_back(
        grad_y_v, grad_log_v, after[...], packed[...], slot_pair[...], ints[...], picked,
        blocks, r[...].astype(F32), small[...], mix[...], gain_second, vec_rows, dims,
    )
    grad_r[...] = grad_r_v
    grad_mix[...] = grad_mix_v
    rows = dims[4]
    mix_tile = 0.0
    if rows:
        mix_tile = jnp.concatenate([roll(grad_mix_v, AT_MIX)[:rows]] * (x.shape[1] // rows), axis=0)
    loading.wait()
    attention_back(
        grad_after, x[...].astype(F32), qkv, probs_att, attended, small_rows, mix_tile, w, gain_first,
        cosine[...], sine[...], grads, grad_qkv, grad_x, between,
    )


def shaped(shape, dtype):
    return jax.ShapeDtypeStruct(shape, dtype)


def call(kernel, identity, ins, outs, scratch, far, flops):
    groups = {name: value if isinstance(value, list) else None for name, value in scratch.items()}
    flat = []
    for value in scratch.values():
        flat += value if isinstance(value, list) else [value]

    def body(*refs):
        refs = list(refs)
        named = {name: refs.pop(0) for name in list(ins) + list(outs)}
        for name, group in groups.items():
            named[name] = refs.pop(0) if group is None else [refs.pop(0) for _ in group]
        kernel(types.SimpleNamespace(**named))

    def spaces(names):
        return [pl.BlockSpec(memory_space=pl.ANY if name in far else pltpu.VMEM) for name in names]

    got = pl.pallas_call(
        body,
        out_shape=list(outs.values()),
        in_specs=spaces(ins),
        out_specs=spaces(outs),
        scratch_shapes=flat,
        compiler_params=pltpu.CompilerParams(
            vmem_limit_bytes=VMEM_BYTES, collective_id=identity, has_side_effects=True
        ),
        cost_estimate=pl.CostEstimate(flops=flops, bytes_accessed=40 << 20, transcendentals=0),
    )(*ins.values())
    return types.SimpleNamespace(**dict(zip(outs, got)))


MESH = pl.DeviceIdType.MESH


class Exchange:
    def __init__(self, stream, sent, groups, partial, sibling_part, onward, pair_part, summed, result, sems):
        self.stream, self.sent, self.groups = stream, sent, groups
        self.partial, self.sibling_part, self.onward = partial, sibling_part, onward
        self.pair_part, self.summed, self.result = pair_part, summed, result
        (self.column_s, self.column_r, self.pair_s, self.pair_r, self.core_s, self.core_r, self.last_s, self.last_r,
         self.local_sem, self.back_s, self.back_r, self.over_s, self.over_r, self.home_s, self.home_r) = sems
        self.core, self.column, self.place = lax.axis_index("section"), lax.axis_index("expert"), lax.axis_index("shard")
        self.owners = lax.axis_size("expert")
        self.sibling = (1 - self.core, self.column, self.place)
        self.pair = (self.core, self.column, self.place + 1 - 2 * lax.rem(self.place, 2))

    def peer(self, column):
        return (self.core, column, self.place)

    def turn(self, by):
        return lax.rem(self.column + by + self.owners, self.owners)

    def to_column(self, by):
        return pltpu.make_async_remote_copy(
            self.sent.at[self.turn(by)], self.groups.at[0, self.column],
            self.column_s.at[self.stream, by], self.column_r.at[self.stream, by],
            device_id=self.peer(self.turn(by)), device_id_type=MESH,
        )

    def from_column(self, by):
        source = self.turn(-by)
        return pltpu.make_async_remote_copy(
            self.sent.at[source], self.groups.at[0, source],
            self.column_s.at[self.stream, by], self.column_r.at[self.stream, by],
            device_id=self.peer(source), device_id_type=MESH,
        )

    def own_block(self):
        return pltpu.make_async_copy(
            self.sent.at[self.column], self.groups.at[0, self.column], self.local_sem.at[self.stream]
        )

    def forward(self, by, here, there, device, send, recv):
        block = self.turn(-by)
        return pltpu.make_async_remote_copy(
            self.groups.at[here, block], self.groups.at[there, block],
            send.at[self.stream, by], recv.at[self.stream, by], device_id=device, device_id_type=MESH,
        )

    def to_pair(self, by):
        return self.forward(by, 0, 2, self.pair, self.pair_s, self.pair_r)

    def to_core(self, by):
        return self.forward(by, 0, 1, self.sibling, self.core_s, self.core_r)

    def to_core_last(self, by):
        return self.forward(by, 2, 3, self.sibling, self.last_s, self.last_r)

    def start(self):
        for by in range(1, self.owners):
            self.to_column(by).start()
        self.own_block().start()

    def spread(self):
        for by in range(self.owners):
            if by:
                self.from_column(by).wait_recv()
            else:
                self.own_block().wait()
            self.to_pair(by).start()
            self.to_core(by).start()

    def near_ready(self):
        for by in range(self.owners):
            self.to_core(by).wait_recv()

    def spread_far(self):
        for by in range(self.owners):
            self.to_pair(by).wait_recv()
            self.to_core_last(by).start()

    def far_ready(self):
        for by in range(self.owners):
            self.to_core_last(by).wait_recv()

    def finish_dispatch(self):
        for by in range(self.owners):
            if by:
                self.to_column(by).wait_send()
            self.to_pair(by).wait_send()
            self.to_core(by).wait_send()
            self.to_core_last(by).wait_send()

    def to_sibling(self, half):
        return pltpu.make_async_remote_copy(
            self.partial.at[2 * half + 1], self.sibling_part.at[half],
            self.back_s.at[self.stream, half], self.back_r.at[self.stream, half],
            device_id=self.sibling, device_id_type=MESH,
        )

    def over_pair(self):
        return pltpu.make_async_remote_copy(
            self.onward, self.pair_part, self.over_s.at[self.stream], self.over_r.at[self.stream],
            device_id=self.pair, device_id_type=MESH,
        )

    def home(self, by):
        return pltpu.make_async_remote_copy(
            self.summed.at[self.turn(by)], self.result.at[self.column],
            self.home_s.at[self.stream, by], self.home_r.at[self.stream, by],
            device_id=self.peer(self.turn(by)), device_id_type=MESH,
        )

    def home_here(self, by):
        source = self.turn(-by)
        return pltpu.make_async_remote_copy(
            self.summed.at[source], self.result.at[source],
            self.home_s.at[self.stream, by], self.home_r.at[self.stream, by],
            device_id=self.peer(source), device_id_type=MESH,
        )

    def return_far(self):
        self.to_sibling(1).wait_recv()
        self.onward[...] = (self.partial[2].astype(F32) + self.sibling_part[1].astype(F32)).astype(BF16)
        self.over_pair().start()

    def return_home(self):
        self.to_sibling(0).wait_recv()
        near = self.partial[0].astype(F32) + self.sibling_part[0].astype(F32)
        self.over_pair().wait_recv()
        self.summed[...] = (near + self.pair_part[...].astype(F32)).astype(BF16)
        for by in range(1, self.owners):
            self.home(by).start()
        self.result[self.column] = self.summed[self.column]

    def finish(self):
        for by in range(1, self.owners):
            self.home_here(by).wait_recv()
            self.home(by).wait_send()
        self.over_pair().wait_send()
        self.to_sibling(0).wait_send()
        self.to_sibling(1).wait_send()


def home_buffers(owners, room, width):
    block = (owners, room, width)
    return [pltpu.VMEM((4,) + block, BF16), pltpu.VMEM((2,) + block, BF16)] + [pltpu.VMEM(block, BF16)] * 3


def exchange_sems(streams, owners):
    dma = pltpu.SemaphoreType.DMA
    shapes = [dma((streams, owners))] * 8 + [dma((streams,))] + [dma((streams, 2))] * 2
    return shapes + [dma((streams,))] * 2 + [dma((streams, owners))] * 2


def half_rows(ref, half):
    groups, owners, room, width = ref.shape
    return ref[2 * half : 2 * half + 2].reshape(2 * owners * room, width)


def set_half(ref, half, value):
    groups, owners, room, width = ref.shape
    ref[2 * half : 2 * half + 2] = value.astype(BF16).reshape(2, owners, room, width)


def experts_forward_half(rows, w_in, w_out):
    total = 0.0
    for chunk in range(w_out.shape[0] // CHUNK):
        both = mm(rows, w_in[:, 2 * CHUNK * chunk : 2 * CHUNK * (chunk + 1)])
        gate = both[:, :CHUNK]
        hidden = (gate * jax.nn.sigmoid(gate) * both[:, CHUNK:]).astype(BF16)
        total = total + mm(hidden, w_out[CHUNK * chunk : CHUNK * (chunk + 1)])
    return total


def keep_forward(half, rows, w_in, both_ref, hidden_ref):
    count = rows.shape[0]
    at = half * count
    for chunk in range(hidden_ref.shape[1] // CHUNK):
        columns = slice(2 * CHUNK * chunk, 2 * CHUNK * (chunk + 1))
        both = mm(rows, w_in[:, columns])
        gate = both[:, :CHUNK]
        both_ref[at : at + count, columns] = both
        hidden_ref[at : at + count, CHUNK * chunk : CHUNK * (chunk + 1)] = (
            gate * jax.nn.sigmoid(gate) * both[:, CHUNK:]
        ).astype(BF16)


def back_half(half, grad_rows, w_in, w_out, both_ref, grad_ref):
    count = grad_rows.shape[0]
    at = half * count
    total = 0.0
    for chunk in range(w_out.shape[0] // CHUNK):
        columns = slice(2 * CHUNK * chunk, 2 * CHUNK * (chunk + 1))
        both = both_ref[at : at + count, columns]
        gate, up = both[:, :CHUNK], both[:, CHUNK:]
        sig = jax.nn.sigmoid(gate)
        grad_hidden = mm(grad_rows, w_out[CHUNK * chunk : CHUNK * (chunk + 1)], NT)
        grad_gate = grad_hidden * up * sig * (1.0 + gate * (1.0 - sig))
        grad_both = jnp.concatenate([grad_gate, grad_hidden * gate * sig], axis=1).astype(BF16)
        grad_ref[at : at + count, columns] = grad_both
        total = total + mm(grad_both, w_in[:, columns], NT)
    return total


def all_rows(ref):
    groups, owners, room, width = ref.shape
    return ref[...].reshape(groups * owners * room, width)


def both_half(half, rows, grad_rows, w_in, w_out, hidden_ref, grad_ref):
    count = rows.shape[0]
    at = half * count
    made, back = 0.0, 0.0
    for chunk in range(w_out.shape[0] // CHUNK):
        columns = slice(2 * CHUNK * chunk, 2 * CHUNK * (chunk + 1))
        units = slice(CHUNK * chunk, CHUNK * (chunk + 1))
        both = mm(rows, w_in[:, columns])
        gate, up = both[:, :CHUNK], both[:, CHUNK:]
        sig = jax.nn.sigmoid(gate)
        hidden = (gate * sig * up).astype(BF16)
        hidden_ref[at : at + count, units] = hidden
        made = made + mm(hidden, w_out[units])
        grad_hidden = mm(grad_rows, w_out[units], NT)
        grad_gate = grad_hidden * up * sig * (1.0 + gate * (1.0 - sig))
        grad_both = jnp.concatenate([grad_gate, grad_hidden * gate * sig], axis=1).astype(BF16)
        grad_ref[at : at + count, columns] = grad_both
        back = back + mm(grad_both, w_in[:, columns], NT)
    return made, back


def weight_grads_in(rows, grad_ref, grad_in):
    for chunk in range(grad_in.shape[1] // (2 * CHUNK)):
        columns = slice(2 * CHUNK * chunk, 2 * CHUNK * (chunk + 1))
        grad_in[:, columns] = mm(rows, grad_ref[:, columns], TN).astype(BF16)


class Spread:
    def __init__(self, wide, packed, in_pieces, out_pieces, attn, w_in, w_out, sems):
        self.wide = wide
        self.packed, self.in_pieces, self.out_pieces = packed, in_pieces, out_pieces
        self.attn, self.w_in, self.w_out = attn, w_in, w_out
        (self.own_sem, self.z_s, self.z_r, self.plane_s, self.plane_r, self.core_s, self.core_r,
         self.in_s, self.in_r, self.out_s, self.out_r, self.own_in, self.own_out) = sems
        self.core, self.column, self.place = lax.axis_index("section"), lax.axis_index("expert"), lax.axis_index("shard")
        self.owners, self.pieces = lax.axis_size("expert"), lax.axis_size("shard")

    def spot(self, column, place):
        rows = self.packed.shape[0]
        return pl.ds(pl.multiple_of((column * self.pieces + place) * rows, rows), rows)

    def column_by(self, by):
        return lax.rem(self.column + by + self.owners, self.owners)

    def place_by(self, by):
        return lax.rem(self.place + by + self.pieces, self.pieces)

    def copy(self, source, target, send, recv, device):
        return pltpu.make_async_remote_copy(source, target, send, recv, device_id=device, device_id_type=MESH)

    def own(self):
        return pltpu.make_async_copy(self.packed, self.attn.at[self.core, self.spot(self.column, self.place)], self.own_sem)

    def along(self, by):
        block = self.attn.at[self.core, self.spot(self.column, self.place)]
        return self.copy(self.packed, block, self.z_s.at[by], self.z_r.at[by], (self.core, self.column, self.place_by(by)))

    def along_in(self, by):
        block = self.attn.at[self.core, self.spot(self.column, self.place_by(-by))]
        return self.copy(self.packed, block, self.z_s.at[by], self.z_r.at[by], (self.core, self.column, self.place_by(-by)))

    def plane(self, back, by):
        block = self.attn.at[self.core, self.spot(self.column, self.place_by(-back))]
        source = self.packed if back == 0 else block
        return self.copy(
            source, block, self.plane_s.at[back, by], self.plane_r.at[back, by], (self.core, self.column_by(by), self.place)
        )

    def plane_in(self, back, by):
        block = self.attn.at[self.core, self.spot(self.column_by(-by), self.place_by(-back))]
        return self.copy(
            block, block, self.plane_s.at[back, by], self.plane_r.at[back, by], (self.core, self.column_by(-by), self.place)
        )

    def over(self, back, by, section):
        block = self.attn.at[section, self.spot(self.column_by(-by), self.place_by(-back))]
        source = self.packed if back == 0 and by == 0 else block
        return self.copy(
            source, block, self.core_s.at[back, by], self.core_r.at[back, by], (1 - self.core, self.column, self.place)
        )

    def begin(self):
        self.own().start()
        for by in range(1, self.pieces):
            self.along(by).start()
        for by in range(1, self.owners):
            self.plane(0, by).start()
        self.over(0, 0, self.core).start()

    def pass_on(self):
        for back in range(1, self.pieces):
            self.along_in(back).wait_recv()
            for by in range(1, self.owners):
                self.plane(back, by).start()
            self.over(back, 0, self.core).start()

    def pass_over(self):
        for back in range(self.pieces):
            for by in range(1, self.owners):
                self.plane_in(back, by).wait_recv()
                self.over(back, by, self.core).start()
        self.own().wait()

    def over_ready(self):
        for back in range(self.pieces):
            for by in range(self.owners):
                self.over(back, by, 1 - self.core).wait_recv()

    def finish_attn(self):
        for by in range(1, self.pieces):
            self.along(by).wait_send()
        for back in range(self.pieces):
            for by in range(1, self.owners):
                self.plane(back, by).wait_send()
            for by in range(self.owners):
                self.over(back, by, self.core).wait_send()

    def in_rows(self, place):
        rows = self.w_in.shape[1] // self.pieces
        return pl.ds(pl.multiple_of(place * rows, rows), rows)

    def out_rows(self, place):
        rows = self.out_pieces.shape[1]
        return pl.ds(pl.multiple_of(lax.div(place, 2) * rows, rows), rows)

    def parts(self, core, place, section, rows):
        if not self.wide:
            return [(self.in_pieces.at[core, lax.rem(place, 2)], self.w_in.at[section, rows])]
        hidden = self.in_pieces.shape[1] // 2
        half = self.out_pieces.shape[1]
        pairs = []
        for pair in range(self.pieces // 2):
            for side in range(2):
                for ahead in range(0, half, CHUNK):
                    at = side * hidden + (2 * pair + lax.rem(place, 2)) * 2 * half + core * half + ahead
                    to = 2 * (pair * half + ahead) + side * CHUNK
                    pairs.append((
                        self.in_pieces.at[:, pl.ds(pl.multiple_of(at, CHUNK), CHUNK)],
                        self.w_in.at[section, rows, pl.ds(to, CHUNK)],
                    ))
        return pairs

    def in_copies(self, cross, by):
        core = 1 - self.core if cross else self.core
        place = self.place_by(by)
        return [
            self.copy(source, target, self.in_s.at[cross, by, i], self.in_r.at[cross, by, i], (core, self.column, place))
            for i, (source, target) in enumerate(self.parts(core, place, self.core, self.in_rows(self.place)))
        ]

    def in_here(self, cross, by):
        core = 1 - self.core if cross else self.core
        place = self.place_by(-by)
        return [
            self.copy(source, target, self.in_s.at[cross, by, i], self.in_r.at[cross, by, i], (core, self.column, place))
            for i, (source, target) in enumerate(self.parts(self.core, self.place, core, self.in_rows(place)))
        ]

    def out_copy(self, cross, by):
        core = 1 - self.core if cross else self.core
        return self.copy(
            self.out_pieces.at[core], self.w_out.at[self.core, self.out_rows(self.place)],
            self.out_s.at[cross, by // 2], self.out_r.at[cross, by // 2], (core, self.column, self.place_by(by)),
        )

    def out_here(self, cross, by):
        core = 1 - self.core if cross else self.core
        place = self.place_by(-by)
        return self.copy(
            self.out_pieces.at[core], self.w_out.at[core, self.out_rows(place)],
            self.out_s.at[cross, by // 2], self.out_r.at[cross, by // 2], (core, self.column, place),
        )

    def own_pieces(self):
        copies = [
            pltpu.make_async_copy(source, target, self.own_in.at[i])
            for i, (source, target) in enumerate(self.parts(self.core, self.place, self.core, self.in_rows(self.place)))
        ]
        return copies + [
            pltpu.make_async_copy(
                self.out_pieces.at[self.core], self.w_out.at[self.core, self.out_rows(self.place)], self.own_out
            )
        ]

    def expert_routes(self):
        for by in range(self.pieces):
            for cross in (0, 1):
                if by or cross:
                    yield cross, by

    def begin_experts(self):
        for one in self.own_pieces():
            one.start()
        for cross, by in self.expert_routes():
            for one in self.in_copies(cross, by):
                one.start()
            if by % 2 == 0:
                self.out_copy(cross, by).start()

    def experts_ready(self, cross):
        for way, by in self.expert_routes():
            if way == cross:
                for one in self.in_here(cross, by):
                    one.wait_recv()
                if by % 2 == 0:
                    self.out_here(cross, by).wait_recv()
        if not cross:
            for one in self.own_pieces():
                one.wait()

    def finish_experts(self):
        for cross, by in self.expert_routes():
            for one in self.in_copies(cross, by):
                one.wait_send()
            if by % 2 == 0:
                self.out_copy(cross, by).wait_send()


def spread_scratch(owners, pieces, parts):
    dma = pltpu.SemaphoreType.DMA
    return [dma, dma((pieces,)), dma((pieces,))] + [dma((pieces, owners))] * 4 + [
        dma((2, pieces, parts)), dma((2, pieces, parts)), dma((2, pieces // 2)), dma((2, pieces // 2)), dma((parts,)), dma,
    ]


def place_of():
    return lax.axis_index("section"), lax.axis_index("expert"), lax.axis_index("shard")


def remote(source, target, send, recv, device):
    return pltpu.make_async_remote_copy(source, target, send, recv, device_id=device, device_id_type=MESH)


class ExpertSum:
    def __init__(self, grad_in, grad_out, got_even, got_odd, got_out, sems):
        self.grad_in, self.grad_out = grad_in, grad_out
        self.got_even, self.got_odd, self.got_out = got_even, got_odd, got_out
        self.in_s, self.in_r, self.out_s, self.out_r = sems
        self.core, self.column, self.place = place_of()
        self.pieces = lax.axis_size("shard")

    def place_by(self, by):
        return lax.rem(self.place + by + self.pieces, self.pieces)

    def in_rows(self, place):
        rows = self.grad_in.shape[0] // self.pieces
        return pl.ds(pl.multiple_of(place * rows, rows), rows)

    def out_rows(self, place):
        rows = self.grad_out.shape[0] // (self.pieces // 2)
        return pl.ds(pl.multiple_of(lax.div(place, 2) * rows, rows), rows)

    def in_copy(self, by, way):
        place = self.place_by(way * by)
        target = self.got_even.at[by // 2 - 1] if by % 2 == 0 else self.got_odd.at[by // 2]
        return remote(
            self.grad_in.at[self.in_rows(place)], target, self.in_s.at[by - 1], self.in_r.at[by - 1],
            (self.core, self.column, place),
        )

    def out_copy(self, by, way):
        place = self.place_by(way * by)
        at = by // 2 - 1
        return remote(
            self.grad_out.at[self.out_rows(place)], self.got_out.at[at], self.out_s.at[at], self.out_r.at[at],
            (self.core, self.column, place),
        )

    def even(self, way=1):
        return [self.in_copy(by, way) for by in range(2, self.pieces, 2)]

    def odd(self, way=1):
        copies = [self.in_copy(by, way) for by in range(1, self.pieces, 2)]
        return copies + [self.out_copy(by, way) for by in range(2, self.pieces, 2)]


def start_all(copies):
    for one in copies:
        one.start()


def wait_all(sent, arriving):
    for one in arriving:
        one.wait_recv()
    for one in sent:
        one.wait_send()


def expert_sum_sems(pieces):
    dma = pltpu.SemaphoreType.DMA
    return [dma((pieces - 1,)), dma((pieces - 1,)), dma((max(pieces // 2 - 1, 1),)), dma((max(pieces // 2 - 1, 1),))]


def got_shapes(pieces, in_rows, columns, out_rows, width):
    spare = max(pieces // 2 - 1, 1)
    return (
        shaped((spare, in_rows, columns), BF16), shaped((pieces // 2, in_rows, columns), BF16),
        shaped((spare, out_rows, width), BF16),
    )


def greet_these(devices):
    barrier = pltpu.get_barrier_semaphore()
    for device in devices:
        pl.semaphore_signal(barrier, inc=1, device_id=device, device_id_type=MESH)
    pl.semaphore_wait(barrier, len(devices))


def along_z():
    core, column, place = place_of()
    pieces = lax.axis_size("shard")
    return [(core, column, lax.rem(place + by, pieces)) for by in range(1, pieces)]


def in_plane():
    core, column, place = place_of()
    owners = lax.axis_size("expert")
    return [(core, lax.rem(column + by, owners), place) for by in range(1, owners)]


def other_core():
    core, column, place = place_of()
    return [(1 - core, column, place)]


def load_weights(attn, section, w, small, sems):
    width = w.shape[0]
    first = pltpu.make_async_copy(attn.at[section, :, pl.ds(4 * width, LANES)], small, sems.at[0])
    then = pltpu.make_async_copy(attn.at[section], w, sems.at[1])
    first.start()
    then.start()
    first.wait()
    return then


class AttnSum:
    def __init__(self, grads, buffers, sems):
        self.grads = grads
        self.from_core, self.summed, self.from_plane, self.through, self.from_z = buffers
        self.core_s, self.core_r, self.plane_s, self.plane_r, self.z_s, self.z_r = sems
        self.core, self.column, self.place = place_of()
        self.owners, self.pieces = lax.axis_size("expert"), lax.axis_size("shard")

    def block(self, column, k, core):
        rows = self.summed.shape[2]
        return pl.ds(pl.multiple_of((column * self.pieces + 2 * k + core) * rows, rows), rows)

    def each(self):
        return [(column, k) for column in range(self.owners) for k in range(self.pieces // 2)]

    def to_core(self, column, k):
        return remote(
            self.grads.at[self.block(column, k, 1 - self.core)], self.from_core.at[column, k], self.core_s.at[column, k],
            self.core_r.at[column, k], (1 - self.core, self.column, self.place),
        )

    def to_plane(self, by, way=1):
        column = lax.rem(self.column + way * by + self.owners, self.owners)
        return remote(
            self.summed.at[column], self.from_plane.at[by - 1], self.plane_s.at[by - 1], self.plane_r.at[by - 1],
            (self.core, column, self.place),
        )

    def place_by(self, by):
        return lax.rem(self.place + by + self.pieces, self.pieces)

    def along(self, by, way=1):
        place = self.place_by(way * by)
        return remote(
            self.through.at[lax.div(place, 2)], self.from_z.at[by - 1], self.z_s.at[by - 1], self.z_r.at[by - 1],
            (self.core, self.column, place),
        )

    def holds(self, place):
        return lax.rem(place, 2) == self.core

    def start(self):
        for column, k in self.each():
            self.to_core(column, k).start()

    def add_cores(self):
        for column, k in self.each():
            self.to_core(column, k).wait_recv()
        for column, k in self.each():
            own = self.grads[self.block(column, k, self.core), :]
            self.summed[column, k] = (own.astype(F32) + self.from_core[column, k].astype(F32)).astype(BF16)
        for by in range(1, self.owners):
            self.to_plane(by).start()

    def plane_ready(self):
        for by in range(1, self.owners):
            self.to_plane(by, -1).wait_recv()

    def add_plane(self):
        total = self.summed[self.column].astype(F32)
        for by in range(1, self.owners):
            total = total + self.from_plane[by - 1].astype(F32)
        self.through[...] = total.astype(BF16)
        for by in range(1, self.pieces):

            @pl.when(self.holds(self.place_by(by)))
            def _():
                self.along(by).start()

    def z_ready(self):
        @pl.when(self.holds(self.place))
        def _():
            for by in range(1, self.pieces):
                self.along(by, -1).wait_recv()

    def add_z(self, target):
        @pl.when(self.holds(self.place))
        def _():
            total = self.through[lax.div(self.place, 2)].astype(F32)
            for by in range(1, self.pieces):
                total = total + self.from_z[by - 1].astype(F32)
            target[...] = total

    def finish_near(self):
        for column, k in self.each():
            self.to_core(column, k).wait_send()
        for by in range(1, self.owners):
            self.to_plane(by).wait_send()

    def finish_z(self):
        for by in range(1, self.pieces):

            @pl.when(self.holds(self.place_by(by)))
            def _():
                self.along(by).wait_send()


def attn_sum_scratch(owners, pieces, rows, columns):
    blocks = (owners, pieces // 2, rows, columns)
    dma = pltpu.SemaphoreType.DMA
    return [
        pltpu.VMEM(blocks, BF16), pltpu.VMEM(blocks, BF16), pltpu.VMEM((owners - 1,) + blocks[1:], BF16),
        pltpu.VMEM(blocks[1:], BF16), pltpu.VMEM((pieces - 1,) + blocks[2:], BF16),
    ], [dma(blocks[:2])] * 2 + [dma((owners - 1,))] * 2 + [dma((pieces - 1,))] * 2


def column_devices():
    core, column, place = place_of()
    pieces = lax.axis_size("shard")
    return [
        (one, column, lax.rem(place + by, pieces))
        for by in range(pieces)
        for one in (core, 1 - core)
    ][1:]


def column_of(row):
    return jnp.broadcast_to(row.astype(F32), (LANES, row.shape[1])).T[:, :1]


def tables_of(seg_row, cosine, sine):
    seq_len = seg_row.shape[1]
    seg_col = column_of(seg_row).astype(jnp.int32)
    start = jnp.sum(jnp.where(seg_row < seg_col, 1.0, 0.0), axis=1, keepdims=True)
    place = lax.broadcasted_iota(jnp.int32, (seq_len, LANES), 0).astype(F32)
    lane = lane_of(seq_len)
    rate = jnp.exp((lane % (HEAD // 2)).astype(F32) * (-2.0 * math.log(10000.0) / HEAD))
    angles = (place - start) * rate
    cosine[...] = jnp.cos(angles)
    sine[...] = jnp.where(lane % HEAD < HEAD // 2, -jnp.sin(angles), jnp.sin(angles))
    return seg_col


def front_kernel(dims, inside, wide, n):
    width = n.x_in.shape[2]
    core, column, place = place_of()
    nffn, nexp = dims[:2]
    packed_w = n.packed_w
    if inside:
        packed_w[:, : 3 * width] = n.w_qkv[...]
        packed_w[:, 3 * width : 4 * width] = n.w_attn[...]
        packed_w[:, 4 * width :] = jnp.zeros((packed_w.shape[0], LANES), BF16)
        for array, at in ((n.router, 0), (n.const_proj, AT_PROJ), (n.const_vec, AT_VEC), (n.gains, AT_GAIN)):
            packed_w[:, 4 * width + at : 4 * width + at + array.shape[1]] = array[...]
    spread = Spread(wide, packed_w, n.in_pieces, n.w_out_here, n.attn, n.w_in, n.w_out, n.spread_sems)
    first, second = core == 0, core == 1
    tokens = Exchange(0, n.buffer_0, n.arrived, *n.token_home, n.made, n.sems)
    tokens_1 = Exchange(1, n.buffer_0, n.groups_1, *n.token_home, n.made, n.sems)
    grads_1 = Exchange(2, n.buffer_2, n.groups_2, *n.grad_home, n.returned, n.sems)
    greet_these(column_devices() + in_plane())

    @pl.when(first)
    def _():
        if inside:
            spread.begin()

    sibling = (1 - core, column, place)
    n.mix_own[...] = jnp.zeros(n.mix_own.shape, F32)
    n.mix_own[:nexp, :nexp] = n.gate_mix[...]
    crossing = [
        remote(n.routes.at[1 - core], n.ints.at[core], n.cross_s.at[0], n.cross_r.at[0], sibling),
        remote(n.priority.at[1 - core], n.prio.at[core], n.cross_s.at[1], n.cross_r.at[1], sibling),
        remote(n.mix_own, n.mix.at[core], n.cross_s.at[2], n.cross_r.at[2], sibling),
    ]
    arriving = [
        remote(n.routes.at[core], n.ints.at[1 - core], n.cross_s.at[0], n.cross_r.at[0], sibling),
        remote(n.priority.at[core], n.prio.at[1 - core], n.cross_s.at[1], n.cross_r.at[1], sibling),
        remote(n.mix_own, n.mix.at[1 - core], n.cross_s.at[2], n.cross_r.at[2], sibling),
    ]
    start_all(crossing)
    bring = [
        pltpu.make_async_copy(n.x_in.at[core], n.x, n.bring_sems.at[0]),
        pltpu.make_async_copy(n.cotangent.at[core], n.upstream, n.bring_sems.at[1]),
    ]
    start_all(bring)
    seg_row = n.segments[core]
    seg_col = tables_of(seg_row, n.cosine, n.sine)
    n.ints[core] = n.routes[core]
    n.prio[core] = n.priority[core]
    n.mix[core] = n.mix_own[...]
    n.r[...] = jnp.zeros(n.r.shape, BF16)
    n.r[:, :nexp] = n.gate_prev[core]
    wait_all(crossing, arriving)
    for one in bring:
        one.wait()

    @pl.when(first)
    def _():
        if inside:
            spread.pass_on()
        spread.begin_experts()
        if inside:
            spread.pass_over()

    @pl.when(second)
    def _():
        if inside:
            spread.over_ready()

    keep = [
        pltpu.make_async_copy(source, target, n.keep_sems.at[section, i])
        for section, targets in enumerate(((n.qkv_0, n.probs_0), (n.qkv_1, n.probs_1)))
        for i, (source, target) in enumerate(zip((n.qkv_here, n.probs_here), targets))
    ]
    n.small[0] = n.attn[0, :, 4 * width :]
    attend_kernel(
        dims, n.x, n.r, n.attn.at[0], n.small.at[0], n.mix.at[0], n.cosine, n.sine, seg_col, seg_row,
        n.ints.at[0], n.prio.at[0],
        n.after_0, n.qkv_here, n.probs_here, n.attended_0, n.packed_0, n.slots_0, n.r_next, n.buffer_0,
    )
    tokens.start()
    start_all(keep[:2])

    @pl.when(second)
    def _():
        if inside:
            spread.begin()

    tokens.spread()

    @pl.when(first)
    def _():
        spread.experts_ready(0)

    @pl.when(second)
    def _():
        if inside:
            spread.pass_on()
        spread.experts_ready(1)

    tokens.near_ready()
    set_half(tokens.partial, 0, experts_forward_half(half_rows(tokens.groups, 0), n.w_in.at[0], n.w_out.at[0]))
    tokens.to_sibling(0).start()
    tokens.spread_far()
    tokens.far_ready()
    set_half(tokens.partial, 1, experts_forward_half(half_rows(tokens.groups, 1), n.w_in.at[0], n.w_out.at[0]))
    tokens.to_sibling(1).start()
    tokens.return_far()

    @pl.when(second)
    def _():
        if inside:
            spread.pass_over()
        spread.begin_experts()

    tokens.return_home()
    tokens.finish_dispatch()
    tokens.finish()
    if inside:

        @pl.when(first)
        def _():
            spread.over_ready()

    n.small[1] = n.attn[1, :, 4 * width :]
    for one in keep[:2]:
        one.wait()
    middle_kernel(
        dims, n.after_0, n.packed_0, n.slots_0, n.ints.at[0], tokens.result, n.small.at[0],
        n.r_next, n.attn.at[1], n.small.at[1], n.mix.at[1], n.cosine, n.sine, seg_col, seg_row,
        n.ints.at[1], n.prio.at[1], n.upstream,
        n.out_0, n.picked_0, n.after_1, n.qkv_here, n.probs_here, n.attended_1, n.packed_1, n.slots_1, n.buffer_0, n.buffer_2,
    )
    start_all(keep[2:])
    both = (tokens_1, grads_1)
    for one in both:
        one.start()
    for one in both:
        one.spread()

    @pl.when(first)
    def _():
        spread.experts_ready(1)

    @pl.when(second)
    def _():
        spread.experts_ready(0)

    w_in, w_out = n.w_in.at[1], n.w_out.at[1]
    for half in range(2):
        if half == 0:
            for one in both:
                one.near_ready()
        else:
            for one in both:
                one.far_ready()
        parts = both_half(
            half, half_rows(tokens_1.groups, half), half_rows(grads_1.groups, half), w_in, w_out, n.hidden, n.grad_both
        )
        for one, part in zip(both, parts):
            set_half(one.partial, half, part)
            one.to_sibling(half).start()
        if half == 0:
            for one in both:
                one.spread_far()
    for one in both:
        one.return_far()
    n.grad_out[...] = mm(n.hidden[...], all_rows(grads_1.groups), TN).astype(BF16)
    for one in both:
        one.return_home()
    weight_grads_in(all_rows(tokens_1.groups), n.grad_both, n.grad_in)
    for one in both:
        one.finish_dispatch()
        one.finish()
    for one in keep[2:]:
        one.wait()
    if inside:
        spread.finish_attn()
    spread.finish_experts()


def turn_kernel(dims, inside, n):
    sums = ExpertSum(n.grad_in_1, n.grad_out_1, n.even, n.odd, n.got_out, n.sum_sems)
    loading = load_weights(n.attn, 1, n.w, n.small, n.load_sems)
    expert_loads = [
        pltpu.make_async_copy(n.w_in_all.at[0], n.w_in, n.load_sems.at[2]),
        pltpu.make_async_copy(n.w_out_all.at[0], n.w_out, n.load_sems.at[3]),
    ]
    start_all(expert_loads)
    grads = Exchange(0, n.buffer, n.groups, *n.home, n.blocks_back, n.sems)
    if inside:
        attn = AttnSum(n.grads, n.attn_buffers, n.attn_sems)
    greet_these(other_core() + along_z() + in_plane())
    start_all(sums.even())
    _, gain_second, vec_rows = small_rows_of(n.small)
    n.out[...] = combine(
        n.after[...], n.packed[...], n.slots[...], n.ints[1], n.made, gain_second, vec_rows, dims, n.picked
    ).astype(BF16)

    def between():
        give_back(n.grad_x[...].astype(BF16).astype(F32), n.packed_0[...], n.slots_0[...], dims, n.buffer)
        grads.start()

    back_body(
        dims, n.upstream, None, n.after, n.packed, n.slots, n.ints.at[1], n.picked, n.returned, n.r, n.w, n.small, n.mix.at[1],
        n.x, n.qkv, n.probs, n.attended, n.cosine, n.sine, n.grad_x, n.grad_r, n.grad_mix, n.grads, n.grad_qkv, loading,
        between,
    )
    if inside:
        attn.start()
    for one in expert_loads:
        one.wait()
    keep_forward(0, half_rows(n.arrived, 0), n.w_in, n.both, n.hidden)
    grads.spread()
    start_all(sums.odd())
    if inside:
        attn.add_cores()
    grads.near_ready()
    set_half(grads.partial, 0, back_half(0, half_rows(grads.groups, 0), n.w_in, n.w_out, n.both, n.grad_both))
    grads.to_sibling(0).start()
    grads.spread_far()
    keep_forward(1, half_rows(n.arrived, 1), n.w_in, n.both, n.hidden)
    grads.far_ready()
    set_half(grads.partial, 1, back_half(1, half_rows(grads.groups, 1), n.w_in, n.w_out, n.both, n.grad_both))
    grads.to_sibling(1).start()
    grads.return_far()
    n.grad_out_0[...] = mm(n.hidden[...], all_rows(grads.groups), TN).astype(BF16)
    if inside:
        attn.plane_ready()
        attn.add_plane()
    grads.return_home()
    weight_grads_in(all_rows(n.arrived), n.grad_both, n.grad_in_0)
    grads.finish_dispatch()
    grads.finish()
    if inside:
        attn.finish_near()
        attn.z_ready()
        attn.add_z(n.attn_sum)
        attn.finish_z()
    wait_all(sums.even() + sums.odd(), sums.even(-1) + sums.odd(-1))


def spread_columns(target, halves_at, hidden_here):
    rows, columns = target.shape
    hidden = columns // 2
    pieces = hidden // (2 * hidden_here)
    parity = lax.rem(lax.axis_index("shard"), 2)
    for first_parity in range(2):

        @pl.when(parity == first_parity)
        def _():
            for half in range(2):
                for q in range(2):
                    odd = first_parity if q == 0 else 1 - first_parity
                    for pair in range(pieces // 2):
                        for side in range(2):
                            for ahead in range(0, hidden_here, CHUNK):
                                at = side * hidden + (2 * pair + odd) * 2 * hidden_here + half * hidden_here + ahead
                                source = 2 * (pair * hidden_here + ahead) + side * CHUNK
                                target[:, at : at + CHUNK] = halves_at(half, q)[:, source : source + CHUNK].astype(F32)


def last_kernel(dims, inside, wide, n):
    core, column, place = place_of()
    pieces = lax.axis_size("shard")
    pair_count = pieces // 2
    (sibling,) = other_core()
    loading = load_weights(n.attn, 0, n.w, n.small, n.load_sems)
    sums = ExpertSum(n.grad_in_0, n.grad_out_0, n.even_0, n.odd_0, n.got_out_0, n.sum_sems)
    if inside:
        attn = AttnSum(n.grads, n.attn_buffers, n.attn_sems)
    greet_these(other_core() + along_z() + (in_plane() if inside else []))
    start_all(sums.even() + sums.odd())
    pairs = ((n.out_0, n.out_1, n.both_out), (n.grad_x_0, n.grad_x_1, n.both_x), (n.grad_r_0, n.grad_r_1, n.r_pair))

    def swaps(section):
        for i, (zero, one, both) in enumerate(pairs):
            own, other = (zero, one) if section == 0 else (one, zero)
            yield (
                remote(other, both.at[section], n.swap_s.at[i], n.swap_r.at[i], sibling),
                pltpu.make_async_copy(own, both.at[section], n.local_sem.at[i]),
            )

    def each_core(action):
        for section in range(2):

            @pl.when(core == section)
            def _():
                action(section)

    def add_experts(section, grad_in, grad_out, even, odd, got_out):
        rows, out_rows = even.shape[1], got_out.shape[1]
        own_in = grad_in[pl.ds(pl.multiple_of(place * rows, rows), rows), :]
        own_out = grad_out[pl.ds(pl.multiple_of(lax.div(place, 2) * out_rows, out_rows), out_rows), :]
        in_sum = [own_in.astype(F32), odd[0].astype(F32)]
        for i in range(pair_count - 1):
            in_sum[0] = in_sum[0] + even[i].astype(F32)
            in_sum[1] = in_sum[1] + odd[i + 1].astype(F32)
        out_sum = own_out.astype(F32)
        for i in range(pair_count - 1):
            out_sum = out_sum + got_out[i].astype(F32)

        @pl.when(core == section)
        def _():
            for q in range(2):
                n.in_mine[q] = in_sum[q]
            n.out_mine[...] = out_sum

        @pl.when(core != section)
        def _():
            for q in range(2):
                n.in_sent[q] = in_sum[q].astype(BF16)
            n.out_sent[...] = out_sum.astype(BF16)
            for one in finals:
                one.start()

    finals = [
        remote(n.in_sent, n.in_got, n.final_s.at[0], n.final_r.at[0], sibling),
        remote(n.out_sent, n.out_got, n.final_s.at[1], n.final_r.at[1], sibling),
    ]
    back_body(
        dims, n.grad_x_1, n.grad_r_1, n.after, n.packed, n.slots, n.ints.at[0], n.picked, n.returned, n.r, n.w, n.small,
        n.mix.at[0], n.x, n.qkv, n.probs, n.attended, n.cosine, n.sine, n.grad_x_0, n.grad_r_0, n.grad_mix, n.grads,
        n.grad_qkv, loading,
    )
    if inside:
        attn.start()

    @each_core
    def _(section):
        for away, here in swaps(section):
            away.start()
            here.start()

    if inside:
        attn.add_cores()
    add_experts(1, n.grad_in_1, n.grad_out_1, n.even_1, n.odd_1, n.got_out_1)
    if inside:
        attn.plane_ready()
        attn.add_plane()
    wait_all(sums.even() + sums.odd(), sums.even(-1) + sums.odd(-1))
    add_experts(0, n.grad_in_0, n.grad_out_0, n.even_0, n.odd_0, n.got_out_0)
    for one in finals:
        one.wait()
    for half in range(2):

        @pl.when(core == half)
        def _():
            if wide:
                hidden_here = n.out_mine.shape[0]
                spread_columns(n.in_total, lambda at, q: n.in_mine[q] if at == half else n.in_got[q], hidden_here)
            else:
                for q in range(2):
                    n.in_total[half, q] = n.in_mine[q]
                    n.in_total[1 - half, q] = n.in_got[q].astype(F32)
            count = n.out_mine.shape[0]
            n.out_total[half * count : (half + 1) * count] = n.out_mine[...]
            n.out_total[(1 - half) * count : (2 - half) * count] = n.out_got[...].astype(F32)

    if inside:
        attn.z_ready()
        attn.add_z(n.attn_sum_0)
        holder = attn.holds(place)
        for section in range(2):
            mine, other = (n.attn_sum_0, n.attn_sum_1) if section == 0 else (n.attn_sum_1, n.attn_sum_0)
            home = remote(other, n.attn_total, n.final_s.at[2], n.final_r.at[2], sibling)

            @pl.when(holder & (core == section))
            def _():
                home.start()
                n.attn_total[...] = mine[...]
                home.wait_send()

            @pl.when(jnp.logical_not(holder) & (core == section))
            def _():
                home.wait_recv()

        width = n.x.shape[1]
        n.qkv_total[...] = n.attn_total[:, : 3 * width]
        n.attn_out_total[...] = n.attn_total[:, 3 * width : 4 * width]
        small = n.attn_total[:, 4 * width :]
        nexp = n.mix_total.shape[0]
        n.mix_total[...] = small[:nexp, AT_MIX : AT_MIX + nexp]
        for target, at in ((n.router_total, 0), (n.proj_total, AT_PROJ), (n.vec_total, AT_VEC), (n.gain_total, AT_GAIN)):
            target[...] = small[:, at : at + target.shape[1]]

    @each_core
    def _(section):
        for away, here in swaps(section):
            away.wait()
            here.wait()

    n.both_r[...] = n.r_pair[:, :, : n.both_r.shape[2]]

    if inside:
        attn.finish_near()
        attn.finish_z()


def local(
    x_in,
    cotangent,
    gate_prev,
    segments,
    routes,
    priority,
    attn_qkv,
    attn_out,
    router,
    const_proj,
    const_vec,
    gains,
    gate_mix,
    expert_in,
    expert_out,
):
    seq_len, width = x_in.shape[2:]
    nexp = gate_prev.shape[-1]
    owners, pieces = lax.axis_size("expert"), lax.axis_size("shard")
    nffn = owners * expert_in.shape[1]
    nconst = const_vec.shape[-1]
    capacity = (5 * TOP * seq_len + 4 * nexp - 1) // (4 * nexp)
    room = -(-capacity // 16) * 16
    slots = nffn * room
    core = lax.axis_index("section")
    first_core = core == 0
    in_rows, columns = expert_in.shape[2:]
    hidden_here = expert_out.shape[2] // 2
    pairs = pieces // 2
    quarter = pairs * hidden_here
    chunks = quarter // CHUNK
    rows = attn_qkv.shape[1]
    inside, wide = rows % 16 == 0, hidden_here % CHUNK == 0

    def swap(item):
        return lax.ppermute(item, "section", [(0, 1), (1, 0)])

    def by_section(own, other):
        return jnp.where(first_core, own, other), jnp.where(first_core, other, own)

    def as_chunks(half):
        half = jnp.moveaxis(half, 3, 0).reshape(2, in_rows, 2, chunks, CHUNK)
        return jnp.swapaxes(half, 2, 3).reshape(2, in_rows, 2 * quarter)

    w_out = expert_out[0, 0].reshape(2, hidden_here, width)
    in_pieces = expert_in[0, 0]
    if not wide:
        w_in = in_pieces.reshape(in_rows, 2, pairs, 2, 2, hidden_here)
        in_pieces = jnp.stack([as_chunks(w_in[:, :, :, :, half]) for half in range(2)])
    given = None
    if not inside:
        def lanes(array, upto):
            return jnp.pad(array, ((0, 0), (0, upto - array.shape[1])))

        small = [
            lanes(router[0], AT_PROJ), lanes(const_proj[0], AT_VEC - AT_PROJ), lanes(const_vec[0], AT_GAIN - AT_VEC),
            lanes(gains[0], LANES - AT_GAIN),
        ]
        shared = jnp.concatenate([attn_qkv[0], attn_out[0]] + small, axis=1)
        shared = lax.all_gather(shared, ("expert", "shard"), axis=0, tiled=True)
        given = jnp.stack(by_section(shared, swap(shared)))
    dims = (nffn, nexp, capacity, slots, rows if inside else 0)
    heads = width // HEAD
    blocks = (owners, room, width)
    token_f32 = shaped((seq_len, width), F32)
    token_b16 = shaped((seq_len, width), BF16)
    lanes_f32 = shaped((seq_len, LANES), F32)
    lanes_i32 = shaped((seq_len, LANES), jnp.int32)
    block_shape = shaped(blocks, BF16)
    attn_shape = shaped((width, 4 * width + LANES), BF16)
    attn_columns = attn_shape.shape[1]
    pair_shape = shaped((TOP, seq_len, width), BF16)
    in_shape, out_shape = shaped((width, 2 * quarter), BF16), shaped((quarter, width), BF16)
    rows_there = 4 * slots
    dma = pltpu.SemaphoreType.DMA
    even, odd, got_out = got_shapes(pieces, in_rows, 2 * quarter, hidden_here, width)

    def vmem(shape):
        return pltpu.VMEM(shape.shape, shape.dtype)

    def attend_out(section):
        return {
            f"after_{section}": token_f32,
            f"qkv_{section}": shaped((seq_len, 3 * width), BF16),
            f"probs_{section}": shaped((heads, seq_len, seq_len), BF16),
            f"attended_{section}": token_b16,
            f"packed_{section}": lanes_f32,
            f"slots_{section}": lanes_i32,
        }

    ins = dict(
        in_pieces=in_pieces, w_out_here=w_out, x_in=x_in[:, 0], cotangent=cotangent[:, 0], gate_prev=gate_prev[:, 0],
        segments=segments, routes=routes[0, :, 0], priority=priority[0], gate_mix=gate_mix[0],
    )
    table_shapes = dict(
        mix=shaped((2, LANES, LANES), F32), cosine=lanes_f32, sine=lanes_f32, ints=shaped((2, seq_len, TOP), jnp.int32),
    )
    outs = dict(
        w_in=shaped((2, width, 2 * quarter), BF16), w_out=shaped((2, quarter, width), BF16),
        arrived=shaped((4,) + blocks, BF16), r_next=shaped((seq_len, LANES), BF16), out_0=token_b16, picked_0=pair_shape,
        made=block_shape, returned=block_shape, grad_in=in_shape, grad_out=out_shape, **attend_out(0), **attend_out(1),
        x=token_b16, r=shaped((seq_len, LANES), BF16), upstream=token_f32, **table_shapes,
    )
    if inside:
        outs["attn"] = shaped((2,) + attn_shape.shape, BF16)
        ins = dict(
            ins, w_qkv=attn_qkv[0], w_attn=attn_out[0], router=router[0], const_proj=const_proj[0], const_vec=const_vec[0],
            gains=gains[0],
        )
    else:
        ins["attn"] = given
    f = call(
        lambda n: front_kernel(dims, inside, wide, n), 0, ins, outs,
        dict(
            small=pltpu.VMEM((2, width, LANES), BF16), buffer_0=vmem(block_shape),
            buffer_2=vmem(block_shape), groups_1=pltpu.VMEM((4,) + blocks, BF16), groups_2=pltpu.VMEM((4,) + blocks, BF16),
            token_home=home_buffers(*blocks), grad_home=home_buffers(*blocks), sems=exchange_sems(3, owners),
            spread_sems=spread_scratch(owners, pieces, 2 * pairs * max(hidden_here // CHUNK, 1) if wide else 1),
            packed_w=pltpu.VMEM((rows, 4 * width + LANES), BF16), mix_own=pltpu.VMEM((LANES, LANES), F32),
            prio=pltpu.VMEM((2, 1, seq_len), jnp.int32), cross_s=dma((3,)), cross_r=dma((3,)), bring_sems=dma((2,)),
            qkv_here=pltpu.VMEM((seq_len, 3 * width), BF16), probs_here=pltpu.VMEM((heads, seq_len, seq_len), BF16),
            keep_sems=dma((2, 2)),
            hidden=pltpu.VMEM((rows_there, quarter), BF16), grad_both=pltpu.VMEM((rows_there, 2 * quarter), BF16),
        ),
        ("in_pieces", "w_out_here", "x_in", "cotangent", "qkv_0", "probs_0", "qkv_1", "probs_1"), 8 << 30,
    )
    tables = dict(mix=f.mix, cosine=f.cosine, sine=f.sine, ints=f.ints)
    attn_all = f.attn if inside else given
    scratch = dict(
        w=vmem(attn_shape), small=pltpu.VMEM((width, LANES), BF16), load_sems=dma((4,)), grad_qkv=pltpu.VMEM((seq_len, 3 * width), BF16),
        sum_sems=expert_sum_sems(pieces),
    )
    attn_scratch = {}
    block_sum = shaped((rows, attn_columns) if inside else (8, LANES), F32)
    if inside:
        buffers, sems = attn_sum_scratch(owners, pieces, rows, attn_columns)
        attn_scratch = dict(attn_buffers=buffers, attn_sems=sems)
    outs = dict(
        out=token_b16, grad_x=token_f32, grad_r=lanes_f32, grad_mix=shaped((LANES, LANES), F32), even=even, odd=odd,
        got_out=got_out, grad_in_0=in_shape, grad_out_0=out_shape, blocks_back=block_shape, attn_sum=block_sum,
    )
    more = dict(grads=vmem(attn_shape))
    if not inside:
        outs, more = dict(outs, grads=attn_shape), {}
    t = call(
        lambda n: turn_kernel(dims, inside, n), 1,
        dict(
            attn=attn_all, w_in_all=f.w_in, w_out_all=f.w_out, grad_in_1=f.grad_in, grad_out_1=f.grad_out,
            upstream=f.upstream, after=f.after_1, packed=f.packed_1, slots=f.slots_1, made=f.made, returned=f.returned, r=f.r_next,
            x=f.out_0, qkv=f.qkv_1, probs=f.probs_1, attended=f.attended_1, packed_0=f.packed_0, slots_0=f.slots_0,
            arrived=f.arrived, **tables,
        ),
        outs,
        dict(
            picked=vmem(pair_shape), buffer=vmem(block_shape), groups=pltpu.VMEM((4,) + blocks, BF16), home=home_buffers(*blocks),
            sems=exchange_sems(1, owners), w_in=vmem(in_shape), w_out=vmem(out_shape),
            both=pltpu.VMEM((rows_there, 2 * quarter), F32), hidden=pltpu.VMEM((rows_there, quarter), BF16),
            grad_both=pltpu.VMEM((rows_there, 2 * quarter), BF16), **scratch, **attn_scratch, **more,
        ),
        ("attn", "w_in_all", "w_out_all", "grad_in_1", "grad_out_1"), 12 << 30,
    )
    in_total = shaped((in_rows, columns) if wide else (2, 2, in_rows, 2 * quarter), F32)
    half_in, half_out = (2, in_rows, 2 * quarter), (hidden_here, width)
    outs = dict(
        both_out=shaped((2, seq_len, width), BF16), both_x=shaped((2, seq_len, width), F32),
        both_r=shaped((2, seq_len, nexp), F32), in_total=in_total, out_total=shaped((2 * hidden_here, width), F32),
        grad_mix=shaped((LANES, LANES), F32),
    )
    if inside:
        narrow = dict(router_total=nexp, proj_total=const_proj.shape[2], vec_total=nconst, gain_total=2)
        outs = dict(
            outs, qkv_total=shaped((rows, 3 * width), F32), attn_out_total=shaped((rows, width), F32),
            mix_total=shaped((nexp, nexp), F32), **{name: shaped((rows, lanes), F32) for name, lanes in narrow.items()},
        )
    else:
        outs = dict(outs, grads=attn_shape)
    z = call(
        lambda n: last_kernel(dims, inside, wide, n), 2,
        dict(
            attn=attn_all, grad_in_0=t.grad_in_0, grad_out_0=t.grad_out_0, grad_in_1=f.grad_in, grad_out_1=f.grad_out,
            even_1=t.even, odd_1=t.odd, got_out_1=t.got_out, attn_sum_1=t.attn_sum, out_0=f.out_0, out_1=t.out,
            grad_x_1=t.grad_x, grad_r_1=t.grad_r, after=f.after_0, packed=f.packed_0, slots=f.slots_0, picked=f.picked_0,
            returned=t.blocks_back, r=f.r, x=f.x, qkv=f.qkv_0, probs=f.probs_0, attended=f.attended_0, **tables,
        ),
        outs,
        dict(
            even_0=vmem(even), odd_0=vmem(odd), got_out_0=vmem(got_out), grad_x_0=vmem(token_f32), grad_r_0=vmem(lanes_f32),
            attn_sum_0=vmem(block_sum), attn_total=vmem(block_sum), r_pair=pltpu.VMEM((2, seq_len, LANES), F32), in_mine=pltpu.VMEM(half_in, F32), out_mine=pltpu.VMEM(half_out, F32),
            in_sent=pltpu.VMEM(half_in, BF16), out_sent=pltpu.VMEM(half_out, BF16), in_got=pltpu.VMEM(half_in, BF16),
            out_got=pltpu.VMEM(half_out, BF16), swap_s=dma((3,)), swap_r=dma((3,)), local_sem=dma((3,)), final_s=dma((3,)),
            final_r=dma((3,)), **scratch, **attn_scratch, **more,
        ),
        ("attn", "both_out", "both_x", "out_0", "out_1"), 6 << 30,
    )
    in_grad = z.in_total
    if not wide:
        odd = lax.axis_index("shard") % 2
        in_grad = jnp.where(odd == 0, in_grad, in_grad[:, ::-1])
        in_grad = jnp.swapaxes(in_grad.reshape(2, 2, in_rows, chunks, 2, CHUNK), 3, 4)
        in_grad = in_grad.reshape(2, 2, in_rows, 2, pairs, hidden_here)
        in_grad = jnp.transpose(in_grad, (2, 3, 4, 1, 0, 5)).reshape(in_rows, columns)
    if inside:
        shared_grads = (
            z.qkv_total, z.attn_out_total, z.router_total, z.proj_total, z.vec_total, z.gain_total, z.mix_total
        )
    else:
        own = jnp.where(first_core, z.grads, t.grads)
        total = own.astype(F32) + swap(jnp.where(first_core, t.grads, z.grads)).astype(F32)
        total = lax.psum_scatter(total.astype(BF16), ("expert", "shard"), scatter_dimension=0, tiled=True).astype(F32)
        own = jnp.where(first_core, z.grad_mix, t.grad_mix)
        mix_grad = own + swap(jnp.where(first_core, t.grad_mix, z.grad_mix))
        small = total[:, 4 * width :]
        shared_grads = (
            total[:, : 3 * width],
            total[:, 3 * width : 4 * width],
            small[:, :nexp],
            small[:, AT_PROJ : AT_PROJ + const_proj.shape[-1]],
            small[:, AT_VEC : AT_VEC + nconst],
            small[:, AT_GAIN : AT_GAIN + 2],
            lax.psum(mix_grad, ("expert", "shard"))[:nexp, :nexp],
        )
    return (
        z.both_out[None, :, None],
        z.both_x[None, :, None],
        z.both_r[None, :, None],
        *[grad[None] for grad in shared_grads],
        in_grad[None, None],
        z.out_total[None, None],
    )


def solution(mesh):
    placed = (
        P(None, ("expert", "shard"), None, None),
        P(None, ("expert", "shard"), None, None),
        P(None, ("expert", "shard"), None, None),
        P(None, ("expert", "shard"), None),
        P("section", None, ("expert", "shard"), None, None),
        P("section", None, ("expert", "shard"), None),
        P("section", ("expert", "shard"), None),
        P("section", ("expert", "shard"), None),
        P("section", ("expert", "shard"), None),
        P("section", ("expert", "shard"), None),
        P("section", ("expert", "shard"), None),
        P("section", ("expert", "shard"), None),
        P("section", None, None),
        P("section", "expert", "shard", None),
        P("section", "expert", "shard", None),
    )
    return jax.shard_map(
        local,
        mesh=mesh,
        in_specs=placed,
        out_specs=(
            P("section", None, ("expert", "shard"), None, None),
            P("section", None, ("expert", "shard"), None, None),
            P("section", None, ("expert", "shard"), None, None),
            P("section", ("expert", "shard"), None),
            P("section", ("expert", "shard"), None),
            P("section", ("expert", "shard"), None),
            P("section", ("expert", "shard"), None),
            P("section", ("expert", "shard"), None),
            P("section", ("expert", "shard"), None),
            P("section", None, None),
            P("section", "expert", "shard", None),
            P("section", "expert", "shard", None),
        ),
        check_vma=False,
    )
```

```python
import math
import types

import jax
import jax.numpy as jnp
from jax import lax
from jax.experimental import pallas as pl
from jax.experimental.pallas import tpu as pltpu
from jax.sharding import PartitionSpec as P

HEADS = 12
HEAD = 64
TOP = 2
CHUNK = 256
LANES = 128
AT_PROJ = 16
AT_VEC = 24
AT_GAIN = 28
AT_MIX = 32

HIGH = lax.Precision.HIGHEST
norm_eps = 1e-06
masked_score = -1e30
F32 = jnp.float32
BF16 = jnp.bfloat16


VMEM_BYTES = 60 * 1024 * 1024


def mm(a, b, contract=((1,), (0,)), precision=None):
    return lax.dot_general(a, b, (contract, ((), ())), precision=precision, preferred_element_type=F32)


NT = ((1,), (1,))
TN = ((0,), (0,))


def lane_of(rows, columns=LANES):
    return lax.broadcasted_iota(jnp.int32, (rows, columns), 1)


def inverse_norm(values):
    return lax.rsqrt(jnp.mean(values * values, axis=-1, keepdims=True) + norm_eps)


def norm_back(grad_unit, unit, inverse):
    return inverse * (grad_unit - unit * jnp.mean(grad_unit * unit, axis=-1, keepdims=True))


def roll(x, by):
    return pltpu.roll(x, by, 1)


def turned(x, lane):
    return jnp.where(lane % HEAD < HEAD // 2, roll(x, LANES - HEAD // 2), roll(x, HEAD // 2))


def hi_lo(x):
    high = x.astype(BF16)
    return high, (x - high.astype(F32)).astype(BF16)


def ones_where(condition):
    return jnp.where(condition, 1.0, 0.0).astype(BF16)


def small_rows_of(small):
    rows = small[...].astype(F32).T
    return rows[AT_GAIN : AT_GAIN + 1], rows[AT_GAIN + 1 : AT_GAIN + 2], rows[AT_VEC:AT_GAIN]


def attention(x, w, gain_first, cosine, sine, seg_col, seg_row, qkv, probs_att, attended):
    seq_len, width = x.shape
    first_b = (x * inverse_norm(x) * gain_first).astype(BF16)
    place_q = lax.broadcasted_iota(jnp.int32, (seq_len, seq_len), 0)
    place_k = lax.broadcasted_iota(jnp.int32, (seq_len, seq_len), 1)
    bias = jnp.where((seg_col == seg_row) & (place_k <= place_q), 0.0, masked_score)
    lane = lane_of(seq_len)
    low_head = lane < HEAD
    for pair in range(width // LANES):
        at = pair * LANES
        q = mm(first_b, w[:, at : at + LANES])
        k = mm(first_b, w[:, width + at : width + at + LANES])
        v = mm(first_b, w[:, 2 * width + at : 2 * width + at + LANES]).astype(BF16)
        q = q * cosine + turned(q, lane) * sine
        k = (k * cosine + turned(k, lane) * sine).astype(BF16)
        outs = []
        for half in range(2):
            one = jnp.where(low_head if half == 0 else lane >= HEAD, q, 0.0).astype(BF16)
            scores = mm(one, k, NT) * (HEAD**-0.5) + bias
            scores = jnp.exp(scores - jnp.max(scores, axis=-1, keepdims=True))
            probs = (scores * (1.0 / jnp.sum(scores, axis=-1, keepdims=True))).astype(BF16)
            probs_att[2 * pair + half] = probs
            outs.append(mm(probs, v))
        attended[:, at : at + LANES] = jnp.where(low_head, outs[0], outs[1]).astype(BF16)
        qkv[:, at : at + LANES] = q.astype(BF16)
        qkv[:, width + at : width + at + LANES] = k
        qkv[:, 2 * width + at : 2 * width + at + LANES] = v
    return x + mm(attended[...], w[:, 3 * width : 4 * width])


def gating(after, r, small, mix, gain_second, ints, prio_row, dims, packed_ref, slot_ref, r_next, buffer):
    nffn, nexp, capacity, slots, _ = dims
    rows = after.shape[0]
    second_b = (after * inverse_norm(after) * gain_second).astype(BF16)
    lane = lane_of(rows)
    logits = mm(second_b, small)
    full = logits + mm(r, mix, precision=HIGH)
    inside = lane < nexp
    full = jnp.where(inside, full, masked_score)
    raised = jnp.exp(full - jnp.max(full, axis=-1, keepdims=True))
    probs = raised / jnp.sum(raised, axis=-1, keepdims=True)
    other = jnp.where(lane % 2 == 0, roll(logits, LANES - 1), roll(logits, 1))
    bigger = jnp.maximum(logits, other)
    mine_e = jnp.exp(logits - bigger)
    mixes = mine_e / (mine_e + jnp.exp(other - bigger))
    before = ones_where(prio_row < column_of(prio_row).astype(jnp.int32))
    route = (ints[:, 0:1], ints[:, 1:2])
    routed = ones_where(((lane == route[0]) | (lane == route[1])) & (lane < nffn))
    rank = mm(before, routed)
    gates, places = [], []
    dispatch = 0.0
    stride = slots // nffn
    for k in range(TOP):
        chosen = lane == route[k]
        gates.append(jnp.sum(jnp.where(chosen, probs, 0.0), axis=-1, keepdims=True))
        rank_k = jnp.sum(jnp.where(chosen, rank, 0.0), axis=-1, keepdims=True).astype(jnp.int32)
        kept = (route[k] < nffn) & (rank_k < capacity)
        places.append(jnp.where(kept, route[k] * stride + rank_k, -1))
        dispatch = dispatch + jnp.where(places[k] == lane_of(rows, slots), 1.0, 0.0)
    buffer[...] = mm(dispatch.astype(BF16), second_b, TN).astype(BF16).reshape(buffer.shape)
    packed = jnp.where(inside, probs, jnp.where((lane >= AT_PROJ) & (lane < AT_VEC), mixes, 0.0))
    packed = jnp.where(lane == AT_VEC, gates[0], packed)
    packed_ref[...] = jnp.where(lane == AT_VEC + 1, gates[1], packed)
    slot_ref[...] = jnp.where(lane == 0, places[0], places[1])
    if r_next is not None:
        r_next[...] = jnp.where(inside, full, 0.0).astype(BF16)


def extras(packed, ints, nffn, nconst):
    gates = (packed[:, AT_VEC : AT_VEC + 1], packed[:, AT_VEC + 1 : AT_VEC + 2])

    def of(expert):
        return sum(jnp.where(ints[:, k : k + 1] == expert, gates[k], 0.0) for k in range(TOP))

    def mixes(c):
        at = AT_PROJ + 2 * c
        return packed[:, at : at + 1], packed[:, at + 1 : at + 2]

    return gates, of(nffn + 1), [of(nffn + 2 + c) for c in range(nconst)], [mixes(c) for c in range(nconst)]


def combine(after, packed, slot_pair, ints, blocks, gain_second, vec_rows, dims, picked_ref):
    nffn, nexp, _, slots, _ = dims
    nconst = nexp - nffn - 2
    rows = after.shape[0]
    second = after * inverse_norm(after) * gain_second
    gates, copied, const, mixes = extras(packed, ints, nffn, nconst)
    made = blocks[...].reshape(slots, after.shape[1])
    slot_lane = lane_of(rows, slots)
    coefficient = copied
    for c in range(nconst):
        coefficient = coefficient + const[c] * mixes[c][0]
    out = after + coefficient * second
    for k in range(TOP):
        picked = mm(ones_where(slot_pair[:, k : k + 1] == slot_lane), made)
        picked_ref[k] = picked.astype(BF16)
        out = out + gates[k] * picked
    for c in range(nconst):
        out = out + (const[c] * mixes[c][1]) * vec_rows[c : c + 1]
    return out


def give_back(grad_y, packed, slot_pair, dims, buffer):
    slots = dims[3]
    slot_lane = lane_of(grad_y.shape[0], slots)
    total = 0.0
    for k in range(TOP):
        gate = packed[:, AT_VEC + k : AT_VEC + k + 1]
        table = ones_where(slot_pair[:, k : k + 1] == slot_lane)
        total = total + mm(table, (gate * grad_y).astype(BF16), TN)
    buffer[...] = total.astype(BF16).reshape(buffer.shape)


def moe_back(
    grad_y, grad_log_in, after, packed, slot_pair, ints, picked, blocks, r, small, mix, gain_second, vec_rows, dims
):
    nffn, nexp, _, slots, _ = dims
    nconst = nexp - nffn - 2
    rows = grad_y.shape[0]
    lane = lane_of(rows)
    inverse = inverse_norm(after)
    unit = after * inverse
    second = unit * gain_second
    second_b = second.astype(BF16)
    gates, copied, const, mixes = extras(packed, ints, nffn, nconst)
    grad_buffer = blocks[...].reshape(slots, after.shape[1])
    slot_lane = lane_of(rows, slots)
    dispatch = sum(jnp.where(slot_pair[:, k : k + 1] == slot_lane, 1.0, 0.0) for k in range(TOP))
    grad_second = mm(dispatch.astype(BF16), grad_buffer)
    along_second = jnp.sum(grad_y * second, axis=-1, keepdims=True)
    coefficient = copied
    grad_extra = [(nffn + 1, along_second)]
    grad_lanes = jnp.zeros((rows, LANES), F32)
    vec_grads = []
    for c in range(nconst):
        along = jnp.sum(grad_y * vec_rows[c : c + 1], axis=-1, keepdims=True)
        m0, m1 = mixes[c]
        coefficient = coefficient + const[c] * m0
        grad_extra.append((nffn + 2 + c, m0 * along_second + m1 * along))
        d0, d1 = const[c] * along_second, const[c] * along
        mean = m0 * d0 + m1 * d1
        at = AT_PROJ + 2 * c
        grad_lanes = jnp.where(lane == at, m0 * (d0 - mean), grad_lanes)
        grad_lanes = jnp.where(lane == at + 1, m1 * (d1 - mean), grad_lanes)
        vec_grads.append(jnp.sum(grad_y * (const[c] * m1), axis=0, keepdims=True))
    grad_second = grad_second + coefficient * grad_y
    grad_probs = jnp.zeros((rows, LANES), F32)
    for k in range(TOP):
        grad_gate = jnp.sum(picked[k].astype(F32) * grad_y, axis=-1, keepdims=True)
        for expert, value in grad_extra:
            grad_gate = grad_gate + jnp.where(ints[:, k : k + 1] == expert, value, 0.0)
        grad_probs = grad_probs + jnp.where(lane == ints[:, k : k + 1], grad_gate, 0.0)
    probs = jnp.where(lane < nexp, packed, 0.0)
    grad_logits = probs * (grad_probs - jnp.sum(probs * grad_probs, axis=-1, keepdims=True)) + grad_log_in
    grad_mix = mm(jnp.where(lane < nexp, r, 0.0), jnp.where(lane < nexp, grad_logits, 0.0), TN, HIGH)
    grad_r = mm(grad_logits, mix, NT, HIGH)
    high, low = hi_lo(jnp.where(lane < nexp, grad_logits, grad_lanes))
    small_rows = mm(high, second_b, TN) + mm(low, second_b, TN)
    grad_second = grad_second + mm(high, small, NT) + mm(low, small, NT)
    grad_gain = jnp.sum(grad_second * unit, axis=0, keepdims=True)
    grad_after = grad_y + norm_back(grad_second * gain_second, unit, inverse)
    row = lax.broadcasted_iota(jnp.int32, small_rows.shape, 0)
    small_rows = jnp.where(row < AT_VEC, small_rows, 0.0)
    for c in range(nconst):
        small_rows = jnp.where(row == AT_VEC + c, vec_grads[c], small_rows)
    small_rows = jnp.where(row == AT_GAIN + 1, grad_gain, small_rows)
    return grad_after, grad_r, grad_mix, small_rows


def attention_back(
    grad_after, x, qkv, probs_att, attended, small_rows, mix_tile, w, gain_first, cosine, sine, grads, grad_qkv, grad_x, hooks
):
    seq_len, width = x.shape
    inverse = inverse_norm(x)
    unit = x * inverse
    first_b = (unit * gain_first).astype(BF16)
    grad_branch = grad_after.astype(BF16)
    lane = lane_of(seq_len)
    low_head = lane < HEAD
    masks = (ones_where(low_head), ones_where(lane >= HEAD))
    scale = HEAD**-0.5
    heads_half = width // LANES // 2
    wide = heads_half * LANES

    def weight_grads(batch):
        for part in range(3):
            columns = slice(part * width + batch * wide, part * width + (batch + 1) * wide)
            grads[batch][:, part * wide : (part + 1) * wide] = mm(first_b, grad_qkv[:, columns], TN).astype(BF16)
        if batch == 0:
            grads[0][:, 3 * wide :] = mm(attended[...], grad_branch, TN).astype(BF16)

    for pair in range(width // LANES):
        at = pair * LANES
        q = qkv[:, at : at + LANES]
        k = qkv[:, width + at : width + at + LANES]
        v = qkv[:, 2 * width + at : 2 * width + at + LANES]
        g = mm(grad_branch, w[at : at + LANES, 3 * width : 4 * width], NT).astype(BF16)
        dq, dk, dv = [], [], []
        for half in range(2):
            probs = probs_att[2 * pair + half]
            grad_p = mm(g * masks[half], v, NT)
            p = probs.astype(F32)
            grad_s = (p * (grad_p - jnp.sum(p * grad_p, axis=-1, keepdims=True))).astype(BF16)
            dv.append(mm(probs, g, TN))
            dq.append(mm(grad_s, k))
            dk.append(mm(grad_s, q, TN))
        dq = jnp.where(low_head, dq[0], dq[1]) * scale
        dk = jnp.where(low_head, dk[0], dk[1]) * scale
        grad_qkv[:, at : at + LANES] = (dq * cosine - turned(dq, lane) * sine).astype(BF16)
        grad_qkv[:, width + at : width + at + LANES] = (dk * cosine - turned(dk, lane) * sine).astype(BF16)
        grad_qkv[:, 2 * width + at : 2 * width + at + LANES] = jnp.where(low_head, dv[0], dv[1]).astype(BF16)
        if hooks.early and pair == heads_half - 1:
            weight_grads(0)
            hooks.first_done()
    if hooks.early:
        hooks.heads_done()
        weight_grads(1)
    grad_first = mm(grad_qkv[...], w[:, : 3 * width], NT)
    grad_gain = jnp.sum(grad_first * unit, axis=0, keepdims=True)
    grad_x[...] = grad_after + norm_back(grad_first * gain_first, unit, inverse)
    row = lax.broadcasted_iota(jnp.int32, small_rows.shape, 0)
    small_rows = jnp.where(row == AT_GAIN, grad_gain, small_rows)
    grads[1][:, 3 * wide :] = (small_rows.T + mix_tile).astype(BF16)
    if not hooks.early:
        hooks.rows_done()
        weight_grads(0)
        hooks.first_done()
        weight_grads(1)
    hooks.second_done()


def attend_kernel(
    dims, x, r, w, small, mix, cosine, sine, seg_col, seg_row, ints, prio_row,
    after, qkv, probs_att, attended, packed, slot_pair, r_next, buffer,
):
    gain_first, gain_second, _ = small_rows_of(small)
    after_v = attention(
        x[...].astype(F32), w, gain_first, cosine[...], sine[...], seg_col, seg_row, qkv, probs_att, attended
    )
    after[...] = after_v
    gating(
        after_v, r[...].astype(F32), small[...], mix[...], gain_second, ints[...], prio_row[...], dims,
        packed, slot_pair, r_next, buffer,
    )


def middle_kernel(
    dims, after_0, packed_0, slots_0, ints_0, blocks_0, small_0,
    r, w, small, mix, cosine, sine, seg_col, seg_row, ints, prio_row, grad_y,
    out, picked, after, qkv, probs_att, attended, packed, slot_pair, buffer, grad_buffer,
):
    _, gain_second, vec_rows = small_rows_of(small_0)
    out[...] = combine(
        after_0[...], packed_0[...], slots_0[...], ints_0[...], blocks_0, gain_second, vec_rows, dims, picked
    ).astype(BF16)
    attend_kernel(
        dims, out, r, w, small, mix, cosine, sine, seg_col, seg_row, ints, prio_row,
        after, qkv, probs_att, attended, packed, slot_pair, None, buffer,
    )
    give_back(grad_y[...], packed[...], slot_pair[...], dims, grad_buffer)


def back_body(
    dims, grad_y, grad_log, after, packed, slot_pair, ints, picked, blocks, r, w, small, mix, x, qkv, probs_att, attended,
    cosine, sine, grad_x, grad_r, grad_mix, grads, grad_qkv, loading, hooks,
):
    gain_first, gain_second, vec_rows = small_rows_of(small)
    grad_log_v = 0.0 if grad_log is None else grad_log[...].astype(BF16).astype(F32)
    grad_y_v = grad_y[...] if grad_log is None else grad_y[...].astype(BF16).astype(F32)
    grad_after, grad_r_v, grad_mix_v, small_rows = moe_back(
        grad_y_v, grad_log_v, after[...], packed[...], slot_pair[...], ints[...], picked,
        blocks, r[...].astype(F32), small[...], mix[...], gain_second, vec_rows, dims,
    )
    grad_r[...] = grad_r_v
    grad_mix[...] = grad_mix_v
    rows = dims[4]
    mix_tile = 0.0
    if rows:
        mix_tile = jnp.concatenate([roll(grad_mix_v, AT_MIX)[:rows]] * (x.shape[1] // rows), axis=0)
    loading.wait()
    attention_back(
        grad_after, x[...].astype(F32), qkv, probs_att, attended, small_rows, mix_tile, w, gain_first,
        cosine[...], sine[...], grads, grad_qkv, grad_x, hooks,
    )


def shaped(shape, dtype):
    return jax.ShapeDtypeStruct(shape, dtype)


def call(kernel, identity, ins, outs, scratch, far, flops):
    groups = {name: value if isinstance(value, list) else None for name, value in scratch.items()}
    flat = []
    for value in scratch.values():
        flat += value if isinstance(value, list) else [value]

    def body(*refs):
        refs = list(refs)
        named = {name: refs.pop(0) for name in list(ins) + list(outs)}
        for name, group in groups.items():
            named[name] = refs.pop(0) if group is None else [refs.pop(0) for _ in group]
        kernel(types.SimpleNamespace(**named))

    def spaces(names):
        return [pl.BlockSpec(memory_space=pl.ANY if name in far else pltpu.VMEM) for name in names]

    got = pl.pallas_call(
        body,
        out_shape=list(outs.values()),
        in_specs=spaces(ins),
        out_specs=spaces(outs),
        scratch_shapes=flat,
        compiler_params=pltpu.CompilerParams(
            vmem_limit_bytes=VMEM_BYTES, collective_id=identity, has_side_effects=True
        ),
        cost_estimate=pl.CostEstimate(flops=flops, bytes_accessed=40 << 20, transcendentals=0),
    )(*ins.values())
    return types.SimpleNamespace(**dict(zip(outs, got)))


MESH = pl.DeviceIdType.MESH


class Exchange:
    def __init__(self, stream, sent, groups, partial, sibling_part, onward, pair_part, summed, result, sems):
        self.stream, self.sent, self.groups = stream, sent, groups
        self.partial, self.sibling_part, self.onward = partial, sibling_part, onward
        self.pair_part, self.summed, self.result = pair_part, summed, result
        (self.column_s, self.column_r, self.pair_s, self.pair_r, self.core_s, self.core_r, self.last_s, self.last_r,
         self.local_sem, self.back_s, self.back_r, self.far_s, self.far_r, self.over_s, self.over_r,
         self.home_s, self.home_r) = sems
        self.core, self.column, self.place = lax.axis_index("section"), lax.axis_index("expert"), lax.axis_index("shard")
        self.owners = lax.axis_size("expert")
        self.sibling = (1 - self.core, self.column, self.place)
        self.pair = (self.core, self.column, self.place + 1 - 2 * lax.rem(self.place, 2))

    def peer(self, column):
        return (self.core, column, self.place)

    def turn(self, by):
        return lax.rem(self.column + by + self.owners, self.owners)

    def to_column(self, by):
        return pltpu.make_async_remote_copy(
            self.sent.at[self.turn(by)], self.groups.at[0, self.column],
            self.column_s.at[self.stream, by], self.column_r.at[self.stream, by],
            device_id=self.peer(self.turn(by)), device_id_type=MESH,
        )

    def from_column(self, by):
        source = self.turn(-by)
        return pltpu.make_async_remote_copy(
            self.sent.at[source], self.groups.at[0, source],
            self.column_s.at[self.stream, by], self.column_r.at[self.stream, by],
            device_id=self.peer(source), device_id_type=MESH,
        )

    def own_block(self):
        return pltpu.make_async_copy(
            self.sent.at[self.column], self.groups.at[0, self.column], self.local_sem.at[self.stream]
        )

    def forward(self, by, here, there, device, send, recv):
        block = self.turn(-by)
        return pltpu.make_async_remote_copy(
            self.groups.at[here, block], self.groups.at[there, block],
            send.at[self.stream, by], recv.at[self.stream, by], device_id=device, device_id_type=MESH,
        )

    def to_pair(self, by):
        return self.forward(by, 0, 2, self.pair, self.pair_s, self.pair_r)

    def to_core(self, by):
        return self.forward(by, 0, 1, self.sibling, self.core_s, self.core_r)

    def to_core_last(self, by):
        return self.forward(by, 2, 3, self.sibling, self.last_s, self.last_r)

    def start(self):
        for by in range(1, self.owners):
            self.to_column(by).start()
        self.own_block().start()

    def spread(self):
        for by in range(self.owners):
            if by:
                self.from_column(by).wait_recv()
            else:
                self.own_block().wait()
            self.to_pair(by).start()
            self.to_core(by).start()

    def near_ready(self):
        for by in range(self.owners):
            self.to_core(by).wait_recv()

    def spread_far(self, bys):
        for by in bys:
            self.to_pair(by).wait_recv()
            self.to_core_last(by).start()

    def far_ready(self, bys):
        for by in bys:
            self.to_core_last(by).wait_recv()

    def finish_dispatch(self):
        for by in range(self.owners):
            if by:
                self.to_column(by).wait_send()
            self.to_pair(by).wait_send()
            self.to_core(by).wait_send()
            self.to_core_last(by).wait_send()

    def near_back(self):
        return pltpu.make_async_remote_copy(
            self.partial.at[1], self.sibling_part.at[0], self.back_s.at[self.stream], self.back_r.at[self.stream],
            device_id=self.sibling, device_id_type=MESH,
        )

    def far_back(self, by):
        block = self.turn(-by)
        return pltpu.make_async_remote_copy(
            self.partial.at[3, block], self.sibling_part.at[1, block],
            self.far_s.at[self.stream, by], self.far_r.at[self.stream, by],
            device_id=self.sibling, device_id_type=MESH,
        )

    def over_pair(self, by):
        block = self.turn(-by)
        return pltpu.make_async_remote_copy(
            self.onward.at[block], self.pair_part.at[block],
            self.over_s.at[self.stream, by], self.over_r.at[self.stream, by],
            device_id=self.pair, device_id_type=MESH,
        )

    def home(self, by):
        return pltpu.make_async_remote_copy(
            self.summed.at[self.turn(by)], self.result.at[self.column],
            self.home_s.at[self.stream, by], self.home_r.at[self.stream, by],
            device_id=self.peer(self.turn(by)), device_id_type=MESH,
        )

    def home_here(self, by):
        source = self.turn(-by)
        return pltpu.make_async_remote_copy(
            self.summed.at[source], self.result.at[source],
            self.home_s.at[self.stream, by], self.home_r.at[self.stream, by],
            device_id=self.peer(source), device_id_type=MESH,
        )

    def return_far(self, bys):
        for by in bys:
            block = self.turn(-by)
            self.far_back(by).wait_recv()
            total = self.partial[2, block].astype(F32) + self.sibling_part[1, block].astype(F32)
            self.onward[block] = total.astype(BF16)
            self.over_pair(by).start()

    def return_home(self, bys):
        for by in bys:
            block = self.turn(-by)
            near = self.partial[0, block].astype(F32) + self.sibling_part[0, block].astype(F32)
            self.over_pair(by).wait_recv()
            self.summed[block] = (near + self.pair_part[block].astype(F32)).astype(BF16)
            if by:
                self.home(self.owners - by).start()
            else:
                self.result[block] = self.summed[block]

    def near_arrived(self):
        self.near_back().wait_recv()

    def finish(self):
        for by in range(1, self.owners):
            self.home_here(by).wait_recv()
            self.home(by).wait_send()
        for by in range(self.owners):
            self.over_pair(by).wait_send()
            self.far_back(by).wait_send()
        self.near_back().wait_send()

    def steps(self):
        cut = self.owners // 2
        return [list(range(cut)), list(range(cut, self.owners))]

    def far(self, bys):
        return [(group, self.turn(-by)) for by in bys for group in (2, 3)]


def home_buffers(owners, room, width):
    block = (owners, room, width)
    return [pltpu.VMEM((4,) + block, BF16), pltpu.VMEM((2,) + block, BF16)] + [pltpu.VMEM(block, BF16)] * 3


def exchange_sems(streams, owners):
    dma = pltpu.SemaphoreType.DMA
    return [dma((streams, owners))] * 8 + [dma((streams,))] * 3 + [dma((streams, owners))] * 6


def near_rows(ref):
    groups, owners, room, width = ref.shape
    return ref[:2].reshape(2 * owners * room, width)


def put_near(ref, value, columns=slice(None)):
    groups, owners, room, _ = ref.shape
    ref[:2, :, :, columns] = value.astype(ref.dtype).reshape(2, owners, room, value.shape[1])


def rows_at(ref, picks, columns=slice(None)):
    return jnp.concatenate([ref[group, block, :, columns] for group, block in picks], axis=0)


def put_at(ref, picks, value, columns=slice(None)):
    room = ref.shape[2]
    for i, (group, block) in enumerate(picks):
        ref[group, block, :, columns] = value[i * room : (i + 1) * room].astype(ref.dtype)


def all_rows(ref):
    groups, owners, room, width = ref.shape
    return ref[...].reshape(groups * owners * room, width)


def chunks_of(w_out):
    for chunk in range(w_out.shape[0] // CHUNK):
        yield slice(2 * CHUNK * chunk, 2 * CHUNK * (chunk + 1)), slice(CHUNK * chunk, CHUNK * (chunk + 1))


def made_by(rows, w_in, w_out):
    total = 0.0
    for columns, units in chunks_of(w_out):
        both = mm(rows, w_in[:, columns])
        gate = both[:, :CHUNK]
        hidden = (gate * jax.nn.sigmoid(gate) * both[:, CHUNK:]).astype(BF16)
        total = total + mm(hidden, w_out[units])
    return total


def forward_again(rows, w_in, w_out, put_both, put_hidden):
    for columns, units in chunks_of(w_out):
        both = mm(rows, w_in[:, columns])
        gate = both[:, :CHUNK]
        put_both(both, columns)
        put_hidden(gate * jax.nn.sigmoid(gate) * both[:, CHUNK:], units)


def back_of(grad_rows, w_in, w_out, both_at, put_grad):
    total = 0.0
    for columns, units in chunks_of(w_out):
        both = both_at(columns).astype(F32)
        gate, up = both[:, :CHUNK], both[:, CHUNK:]
        sig = jax.nn.sigmoid(gate)
        grad_hidden = mm(grad_rows, w_out[units], NT)
        grad_gate = grad_hidden * up * sig * (1.0 + gate * (1.0 - sig))
        grad_both = jnp.concatenate([grad_gate, grad_hidden * gate * sig], axis=1).astype(BF16)
        put_grad(grad_both, columns)
        total = total + mm(grad_both, w_in[:, columns], NT)
    return total


def both_ways(rows, grad_rows, w_in, w_out, put_hidden, put_grad):
    made, back = 0.0, 0.0
    for columns, units in chunks_of(w_out):
        both = mm(rows, w_in[:, columns])
        gate, up = both[:, :CHUNK], both[:, CHUNK:]
        sig = jax.nn.sigmoid(gate)
        hidden = (gate * sig * up).astype(BF16)
        put_hidden(hidden, units)
        made = made + mm(hidden, w_out[units])
        grad_hidden = mm(grad_rows, w_out[units], NT)
        grad_gate = grad_hidden * up * sig * (1.0 + gate * (1.0 - sig))
        grad_both = jnp.concatenate([grad_gate, grad_hidden * gate * sig], axis=1).astype(BF16)
        put_grad(grad_both, columns)
        back = back + mm(grad_both, w_in[:, columns], NT)
    return made, back


def near_of(ref):
    return lambda value, columns: put_near(ref, value, columns)


def far_of(ref, picks):
    return lambda value, columns: put_at(ref, picks, value, columns)


def weight_grads_in(rows, grad_ref, grad_in):
    for chunk in range(grad_in.shape[1] // (2 * CHUNK)):
        columns = slice(2 * CHUNK * chunk, 2 * CHUNK * (chunk + 1))
        grads = grad_ref[:, :, :, columns].reshape(rows.shape[0], 2 * CHUNK)
        grad_in[:, columns] = mm(rows, grads, TN).astype(BF16)


def exchange_far(streams, work):
    first, then = streams[0].steps()
    for bys in (first, then):
        for one in streams:
            one.spread_far(bys)
        if bys is then:
            for one in streams:
                one.return_far(first)
        for one in streams:
            one.far_ready(bys)
        for one, value in zip(streams, work(streams[0].far(bys))):
            put_at(one.partial, one.far(bys), value)
            for by in bys:
                one.far_back(by).start()
    for one in streams:
        one.return_far(then)


class Spread:
    def __init__(self, wide, packed, in_pieces, out_pieces, attn, w_in, w_out, sems):
        self.wide = wide
        self.packed, self.in_pieces, self.out_pieces = packed, in_pieces, out_pieces
        self.attn, self.w_in, self.w_out = attn, w_in, w_out
        (self.own_sem, self.z_s, self.z_r, self.plane_s, self.plane_r, self.core_s, self.core_r,
         self.in_s, self.in_r, self.out_s, self.out_r, self.own_in, self.own_out) = sems
        self.core, self.column, self.place = lax.axis_index("section"), lax.axis_index("expert"), lax.axis_index("shard")
        self.owners, self.pieces = lax.axis_size("expert"), lax.axis_size("shard")

    def spot(self, column, place):
        rows = self.packed.shape[0]
        return pl.ds(pl.multiple_of((column * self.pieces + place) * rows, rows), rows)

    def column_by(self, by):
        return lax.rem(self.column + by + self.owners, self.owners)

    def place_by(self, by):
        return lax.rem(self.place + by + self.pieces, self.pieces)

    def copy(self, source, target, send, recv, device):
        return pltpu.make_async_remote_copy(source, target, send, recv, device_id=device, device_id_type=MESH)

    def own(self):
        return pltpu.make_async_copy(self.packed, self.attn.at[self.core, self.spot(self.column, self.place)], self.own_sem)

    def along(self, by):
        block = self.attn.at[self.core, self.spot(self.column, self.place)]
        return self.copy(self.packed, block, self.z_s.at[by], self.z_r.at[by], (self.core, self.column, self.place_by(by)))

    def along_in(self, by):
        block = self.attn.at[self.core, self.spot(self.column, self.place_by(-by))]
        return self.copy(self.packed, block, self.z_s.at[by], self.z_r.at[by], (self.core, self.column, self.place_by(-by)))

    def plane(self, back, by):
        block = self.attn.at[self.core, self.spot(self.column, self.place_by(-back))]
        source = self.packed if back == 0 else block
        return self.copy(
            source, block, self.plane_s.at[back, by], self.plane_r.at[back, by], (self.core, self.column_by(by), self.place)
        )

    def plane_in(self, back, by):
        block = self.attn.at[self.core, self.spot(self.column_by(-by), self.place_by(-back))]
        return self.copy(
            block, block, self.plane_s.at[back, by], self.plane_r.at[back, by], (self.core, self.column_by(-by), self.place)
        )

    def over(self, back, by, section):
        block = self.attn.at[section, self.spot(self.column_by(-by), self.place_by(-back))]
        source = self.packed if back == 0 and by == 0 else block
        return self.copy(
            source, block, self.core_s.at[back, by], self.core_r.at[back, by], (1 - self.core, self.column, self.place)
        )

    def begin(self):
        self.own().start()
        for by in range(1, self.pieces):
            self.along(by).start()
        for by in range(1, self.owners):
            self.plane(0, by).start()
        self.over(0, 0, self.core).start()

    def pass_on(self):
        for back in range(1, self.pieces):
            self.along_in(back).wait_recv()
            for by in range(1, self.owners):
                self.plane(back, by).start()
            self.over(back, 0, self.core).start()

    def pass_over(self):
        for back in range(self.pieces):
            for by in range(1, self.owners):
                self.plane_in(back, by).wait_recv()
                self.over(back, by, self.core).start()
        self.own().wait()

    def over_ready(self):
        for back in range(self.pieces):
            for by in range(self.owners):
                self.over(back, by, 1 - self.core).wait_recv()

    def finish_attn(self):
        for by in range(1, self.pieces):
            self.along(by).wait_send()
        for back in range(self.pieces):
            for by in range(1, self.owners):
                self.plane(back, by).wait_send()
            for by in range(self.owners):
                self.over(back, by, self.core).wait_send()

    def in_rows(self, place):
        rows = self.w_in.shape[1] // self.pieces
        return pl.ds(pl.multiple_of(place * rows, rows), rows)

    def out_rows(self, place):
        rows = self.out_pieces.shape[1]
        return pl.ds(pl.multiple_of(lax.div(place, 2) * rows, rows), rows)

    def parts(self, core, place, section, rows):
        if not self.wide:
            return [(self.in_pieces.at[core, lax.rem(place, 2)], self.w_in.at[section, rows])]
        hidden = self.in_pieces.shape[1] // 2
        half = self.out_pieces.shape[1]
        pairs = []
        for pair in range(self.pieces // 2):
            for side in range(2):
                for ahead in range(0, half, CHUNK):
                    at = side * hidden + (2 * pair + lax.rem(place, 2)) * 2 * half + core * half + ahead
                    to = 2 * (pair * half + ahead) + side * CHUNK
                    pairs.append((
                        self.in_pieces.at[:, pl.ds(pl.multiple_of(at, CHUNK), CHUNK)],
                        self.w_in.at[section, rows, pl.ds(to, CHUNK)],
                    ))
        return pairs

    def in_copies(self, cross, by):
        core = 1 - self.core if cross else self.core
        place = self.place_by(by)
        return [
            self.copy(source, target, self.in_s.at[cross, by, i], self.in_r.at[cross, by, i], (core, self.column, place))
            for i, (source, target) in enumerate(self.parts(core, place, self.core, self.in_rows(self.place)))
        ]

    def in_here(self, cross, by):
        core = 1 - self.core if cross else self.core
        place = self.place_by(-by)
        return [
            self.copy(source, target, self.in_s.at[cross, by, i], self.in_r.at[cross, by, i], (core, self.column, place))
            for i, (source, target) in enumerate(self.parts(self.core, self.place, core, self.in_rows(place)))
        ]

    def out_copy(self, cross, by):
        core = 1 - self.core if cross else self.core
        return self.copy(
            self.out_pieces.at[core], self.w_out.at[self.core, self.out_rows(self.place)],
            self.out_s.at[cross, by // 2], self.out_r.at[cross, by // 2], (core, self.column, self.place_by(by)),
        )

    def out_here(self, cross, by):
        core = 1 - self.core if cross else self.core
        place = self.place_by(-by)
        return self.copy(
            self.out_pieces.at[core], self.w_out.at[core, self.out_rows(place)],
            self.out_s.at[cross, by // 2], self.out_r.at[cross, by // 2], (core, self.column, place),
        )

    def own_pieces(self):
        copies = [
            pltpu.make_async_copy(source, target, self.own_in.at[i])
            for i, (source, target) in enumerate(self.parts(self.core, self.place, self.core, self.in_rows(self.place)))
        ]
        return copies + [
            pltpu.make_async_copy(
                self.out_pieces.at[self.core], self.w_out.at[self.core, self.out_rows(self.place)], self.own_out
            )
        ]

    def expert_routes(self):
        for by in range(self.pieces):
            for cross in (0, 1):
                if by or cross:
                    yield cross, by

    def begin_experts(self, evens=(0, 1)):
        if 1 in evens:
            for one in self.own_pieces():
                one.start()
        for cross, by in self.expert_routes():
            if (by + 1) % 2 not in evens:
                continue
            for one in self.in_copies(cross, by):
                one.start()
            if by % 2 == 0:
                self.out_copy(cross, by).start()

    def experts_ready(self, cross):
        for way, by in self.expert_routes():
            if way == cross:
                for one in self.in_here(cross, by):
                    one.wait_recv()
                if by % 2 == 0:
                    self.out_here(cross, by).wait_recv()
        if not cross:
            for one in self.own_pieces():
                one.wait()

    def finish_experts(self):
        for cross, by in self.expert_routes():
            for one in self.in_copies(cross, by):
                one.wait_send()
            if by % 2 == 0:
                self.out_copy(cross, by).wait_send()


def spread_scratch(owners, pieces, parts):
    dma = pltpu.SemaphoreType.DMA
    return [dma, dma((pieces,)), dma((pieces,))] + [dma((pieces, owners))] * 4 + [
        dma((2, pieces, parts)), dma((2, pieces, parts)), dma((2, pieces // 2)), dma((2, pieces // 2)), dma((parts,)), dma,
    ]


def place_of():
    return lax.axis_index("section"), lax.axis_index("expert"), lax.axis_index("shard")


def remote(source, target, send, recv, device):
    return pltpu.make_async_remote_copy(source, target, send, recv, device_id=device, device_id_type=MESH)


class ExpertSum:
    def __init__(self, grad_in, grad_out, got_even, got_odd, got_out, sems):
        self.grad_in, self.grad_out = grad_in, grad_out
        self.got_even, self.got_odd, self.got_out = got_even, got_odd, got_out
        self.in_s, self.in_r, self.out_s, self.out_r = sems
        self.core, self.column, self.place = place_of()
        self.pieces = lax.axis_size("shard")

    def place_by(self, by):
        return lax.rem(self.place + by + self.pieces, self.pieces)

    def in_rows(self, place):
        rows = self.grad_in.shape[0] // self.pieces
        return pl.ds(pl.multiple_of(place * rows, rows), rows)

    def out_rows(self, place):
        rows = self.grad_out.shape[0] // (self.pieces // 2)
        return pl.ds(pl.multiple_of(lax.div(place, 2) * rows, rows), rows)

    def in_copy(self, by, way):
        place = self.place_by(way * by)
        target = self.got_even.at[by // 2 - 1] if by % 2 == 0 else self.got_odd.at[by // 2]
        return remote(
            self.grad_in.at[self.in_rows(place)], target, self.in_s.at[by - 1], self.in_r.at[by - 1],
            (self.core, self.column, place),
        )

    def out_copy(self, by, way):
        place = self.place_by(way * by)
        at = by // 2 - 1
        return remote(
            self.grad_out.at[self.out_rows(place)], self.got_out.at[at], self.out_s.at[at], self.out_r.at[at],
            (self.core, self.column, place),
        )

    def even(self, way=1):
        return [self.in_copy(by, way) for by in range(2, self.pieces, 2)]

    def odd(self, way=1):
        copies = [self.in_copy(by, way) for by in range(1, self.pieces, 2)]
        return copies + [self.out_copy(by, way) for by in range(2, self.pieces, 2)]


def start_all(copies):
    for one in copies:
        one.start()


def wait_all(sent, arriving):
    for one in arriving:
        one.wait_recv()
    for one in sent:
        one.wait_send()


def expert_sum_sems(pieces):
    dma = pltpu.SemaphoreType.DMA
    return [dma((pieces - 1,)), dma((pieces - 1,)), dma((max(pieces // 2 - 1, 1),)), dma((max(pieces // 2 - 1, 1),))]


def got_shapes(pieces, in_rows, columns, out_rows, width):
    spare = max(pieces // 2 - 1, 1)
    return (
        shaped((spare, in_rows, columns), BF16), shaped((pieces // 2, in_rows, columns), BF16),
        shaped((spare, out_rows, width), BF16),
    )


def greet_these(devices):
    barrier = pltpu.get_barrier_semaphore()
    for device in devices:
        pl.semaphore_signal(barrier, inc=1, device_id=device, device_id_type=MESH)
    pl.semaphore_wait(barrier, len(devices))


def along_z():
    core, column, place = place_of()
    pieces = lax.axis_size("shard")
    return [(core, column, lax.rem(place + by, pieces)) for by in range(1, pieces)]


def in_plane():
    core, column, place = place_of()
    owners = lax.axis_size("expert")
    return [(core, lax.rem(column + by, owners), place) for by in range(1, owners)]


def other_core():
    core, column, place = place_of()
    return [(1 - core, column, place)]


def load_weights(attn, section, w, small, sems):
    width = w.shape[0]
    first = pltpu.make_async_copy(attn.at[section, :, pl.ds(4 * width, LANES)], small, sems.at[0])
    then = pltpu.make_async_copy(attn.at[section], w, sems.at[1])
    first.start()
    then.start()
    first.wait()
    return then


class AttnSum:
    def __init__(self, grads, buffers, sems):
        self.grads = grads
        self.from_core, self.summed, self.from_plane, self.through, self.from_z = buffers
        self.core_s, self.core_r, self.plane_s, self.plane_r, self.z_s, self.z_r = sems
        self.core, self.column, self.place = place_of()
        self.owners, self.pieces = lax.axis_size("expert"), lax.axis_size("shard")

    def block(self, column, k, core):
        rows = self.summed.shape[2]
        return pl.ds(pl.multiple_of((column * self.pieces + 2 * k + core) * rows, rows), rows)

    def each(self):
        return [(column, k) for column in range(self.owners) for k in range(self.pieces // 2)]

    def to_core(self, column, k):
        return remote(
            self.grads.at[self.block(column, k, 1 - self.core)], self.from_core.at[column, k], self.core_s.at[column, k],
            self.core_r.at[column, k], (1 - self.core, self.column, self.place),
        )

    def to_plane(self, by, way=1):
        column = lax.rem(self.column + way * by + self.owners, self.owners)
        return remote(
            self.summed.at[column], self.from_plane.at[by - 1], self.plane_s.at[by - 1], self.plane_r.at[by - 1],
            (self.core, column, self.place),
        )

    def place_by(self, by):
        return lax.rem(self.place + by + self.pieces, self.pieces)

    def along(self, by, way=1):
        place = self.place_by(way * by)
        return remote(
            self.through.at[lax.div(place, 2)], self.from_z.at[by - 1], self.z_s.at[by - 1], self.z_r.at[by - 1],
            (self.core, self.column, place),
        )

    def holds(self, place):
        return lax.rem(place, 2) == self.core

    def start(self):
        for column, k in self.each():
            self.to_core(column, k).start()

    def add_cores(self):
        for column, k in self.each():
            self.to_core(column, k).wait_recv()
        for column, k in self.each():
            own = self.grads[self.block(column, k, self.core), :]
            self.summed[column, k] = (own.astype(F32) + self.from_core[column, k].astype(F32)).astype(BF16)
        for by in range(1, self.owners):
            self.to_plane(by).start()

    def plane_ready(self):
        for by in range(1, self.owners):
            self.to_plane(by, -1).wait_recv()

    def add_plane(self):
        total = self.summed[self.column].astype(F32)
        for by in range(1, self.owners):
            total = total + self.from_plane[by - 1].astype(F32)
        self.through[...] = total.astype(BF16)
        for by in range(1, self.pieces):

            @pl.when(self.holds(self.place_by(by)))
            def _():
                self.along(by).start()

    def z_ready(self):
        @pl.when(self.holds(self.place))
        def _():
            for by in range(1, self.pieces):
                self.along(by, -1).wait_recv()

    def add_z(self, target):
        @pl.when(self.holds(self.place))
        def _():
            total = self.through[lax.div(self.place, 2)].astype(F32)
            for by in range(1, self.pieces):
                total = total + self.from_z[by - 1].astype(F32)
            target[...] = total

    def finish_near(self):
        for column, k in self.each():
            self.to_core(column, k).wait_send()
        for by in range(1, self.owners):
            self.to_plane(by).wait_send()

    def finish_z(self):
        for by in range(1, self.pieces):

            @pl.when(self.holds(self.place_by(by)))
            def _():
                self.along(by).wait_send()


def attn_sum_scratch(owners, pieces, rows, columns):
    blocks = (owners, pieces // 2, rows, columns)
    dma = pltpu.SemaphoreType.DMA
    return [
        pltpu.VMEM(blocks, BF16), pltpu.VMEM(blocks, BF16), pltpu.VMEM((owners - 1,) + blocks[1:], BF16),
        pltpu.VMEM(blocks[1:], BF16), pltpu.VMEM((pieces - 1,) + blocks[2:], BF16),
    ], [dma(blocks[:2])] * 2 + [dma((owners - 1,))] * 2 + [dma((pieces - 1,))] * 2


def column_devices():
    core, column, place = place_of()
    pieces = lax.axis_size("shard")
    return [
        (one, column, lax.rem(place + by, pieces))
        for by in range(pieces)
        for one in (core, 1 - core)
    ][1:]


def column_of(row):
    return jnp.broadcast_to(row.astype(F32), (LANES, row.shape[1])).T[:, :1]


def tables_of(seg_row, cosine, sine):
    seq_len = seg_row.shape[1]
    seg_col = column_of(seg_row).astype(jnp.int32)
    start = jnp.sum(jnp.where(seg_row < seg_col, 1.0, 0.0), axis=1, keepdims=True)
    place = lax.broadcasted_iota(jnp.int32, (seq_len, LANES), 0).astype(F32)
    lane = lane_of(seq_len)
    rate = jnp.exp((lane % (HEAD // 2)).astype(F32) * (-2.0 * math.log(10000.0) / HEAD))
    angles = (place - start) * rate
    cosine[...] = jnp.cos(angles)
    sine[...] = jnp.where(lane % HEAD < HEAD // 2, -jnp.sin(angles), jnp.sin(angles))
    return seg_col


def front_kernel(dims, inside, wide, n):
    width = n.x_in.shape[2]
    core, column, place = place_of()
    nexp, owners = dims[1], lax.axis_size("expert")
    packed_w = n.packed_w
    if inside:
        packed_w[:, : 3 * width] = n.w_qkv[...]
        packed_w[:, 3 * width : 4 * width] = n.w_attn[...]
        rows = packed_w.shape[0]
        n.turning[...] = jnp.zeros(n.turning.shape, F32)
        for array, at in ((n.router, 0), (n.const_proj, AT_PROJ), (n.const_vec, AT_VEC), (n.gains, AT_GAIN)):
            n.turning[at : at + array.shape[0], :rows] = array[...].astype(F32)
        packed_w[:, 4 * width :] = n.turning[:, :LANES].T[:rows].astype(BF16)
    spread = Spread(wide, packed_w, n.in_pieces, n.w_out_here, n.attn if inside else None, n.w_in, n.w_out, n.spread_sems)
    first, second = core == 0, core == 1
    tokens = Exchange(0, n.buffer_0, n.arrived, *n.token_home, n.made, n.sems)
    tokens_1 = Exchange(1, n.buffer_0, n.groups_1, *n.token_home, n.made, n.sems)
    grads_1 = Exchange(2, n.buffer_2, n.groups_2, *n.grad_home, n.returned, n.sems)
    greet_these(column_devices() + in_plane())

    @pl.when(first)
    def _():
        if inside:
            spread.begin()

    sibling = (1 - core, column, place)
    n.mix_own[...] = jnp.zeros(n.mix_own.shape, F32)
    n.mix_own[:nexp, :nexp] = n.gate_mix[...]
    crossing = [
        remote(n.routes.at[1 - core], n.routes_all.at[core], n.cross_s.at[0], n.cross_r.at[0], sibling),
        remote(n.priority.at[1 - core], n.prio.at[core], n.cross_s.at[1], n.cross_r.at[1], sibling),
        remote(n.mix_own, n.mix.at[core], n.cross_s.at[2], n.cross_r.at[2], sibling),
    ]
    arriving = [
        remote(n.routes.at[core], n.routes_all.at[1 - core], n.cross_s.at[0], n.cross_r.at[0], sibling),
        remote(n.priority.at[core], n.prio.at[1 - core], n.cross_s.at[1], n.cross_r.at[1], sibling),
        remote(n.mix_own, n.mix.at[1 - core], n.cross_s.at[2], n.cross_r.at[2], sibling),
    ]
    start_all(crossing)
    bring = [
        pltpu.make_async_copy(n.x_in.at[core], n.x, n.bring_sems.at[0]),
        pltpu.make_async_copy(n.cotangent.at[core], n.upstream, n.bring_sems.at[1]),
    ]
    attn = (n.attn.at[0], n.attn.at[1])
    if not inside:
        attn = (n.attn_here, n.attn_here)
        loads = [pltpu.make_async_copy(n.attn.at[section], n.attn_here, n.bring_sems.at[2]) for section in range(2)]
        bring.append(loads[0])
    start_all(bring)
    seg_row = n.segments[core]
    seg_col = tables_of(seg_row, n.cosine, n.sine)
    n.routes_all[core] = n.routes[core]
    n.prio[core] = n.priority[core]
    n.mix[core] = n.mix_own[...]
    n.turning[...] = jnp.zeros(n.turning.shape, F32)
    n.turning[:nexp, :] = n.gate_prev[core].astype(F32)
    n.r[...] = n.turning[...].T.astype(BF16)
    wait_all(crossing, arriving)
    lane = lane_of(n.ints.shape[1])
    for section in range(2):
        routes = n.routes_all[section]
        first_route, second_route = (column_of(routes[k : k + 1]).astype(jnp.int32) for k in range(TOP))
        n.ints[section] = jnp.where(lane == 0, first_route, second_route)
    for one in bring:
        one.wait()

    @pl.when(first)
    def _():
        if inside:
            spread.pass_on()
        spread.begin_experts()
        if inside:
            spread.pass_over()

    @pl.when(second)
    def _():
        if inside:
            spread.over_ready()

    keep = [
        pltpu.make_async_copy(source, target, n.keep_sems.at[section, i])
        for section, targets in enumerate(((n.qkv_0, n.probs_0), (n.qkv_1, n.probs_1)))
        for i, (source, target) in enumerate(zip((n.qkv_here, n.probs_here), targets))
    ]
    leaving = [pltpu.make_async_copy(n.w_in.at[0], n.w_in_kept, n.leave_sems.at[0]),
               pltpu.make_async_copy(n.w_out.at[0], n.w_out_kept, n.leave_sems.at[1])]
    if inside:
        leaving += [
            pltpu.make_async_copy(n.attn.at[section], n.attn_kept.at[section], n.leave_sems.at[2 + section])
            for section in range(2)
        ]
    n.small[0] = attn[0][:, 4 * width :]
    attend_kernel(
        dims, n.x, n.r, attn[0], n.small.at[0], n.mix.at[0], n.cosine, n.sine, seg_col, seg_row,
        n.ints.at[0], n.prio.at[0],
        n.after_0, n.qkv_here, n.probs_here, n.attended_0, n.packed_0, n.slots_0, n.r_next, n.buffer_0,
    )
    tokens.start()
    start_all(keep[:2])
    if not inside:
        loads[1].start()

    @pl.when(second)
    def _():
        if inside:
            spread.begin()

    tokens.spread()

    @pl.when(first)
    def _():
        spread.experts_ready(0)

    @pl.when(second)
    def _():
        if inside:
            spread.pass_on()
        spread.experts_ready(1)
        spread.begin_experts((1,))

    tokens.near_ready()
    put_near(tokens.partial, made_by(near_rows(tokens.groups), n.w_in.at[0], n.w_out.at[0]))
    tokens.near_back().start()
    exchange_far([tokens], lambda picks: [made_by(rows_at(tokens.groups, picks), n.w_in.at[0], n.w_out.at[0])])

    @pl.when(second)
    def _():
        if inside:
            spread.pass_over()
        spread.begin_experts((0,))

    tokens.near_arrived()
    tokens.return_home(range(owners))
    tokens.finish_dispatch()
    tokens.finish()
    if inside:

        @pl.when(first)
        def _():
            spread.over_ready()

    if not inside:
        loads[1].wait()
    n.small[1] = attn[1][:, 4 * width :]
    for one in keep[:2]:
        one.wait()
    middle_kernel(
        dims, n.after_0, n.packed_0, n.slots_0, n.ints.at[0], tokens.result, n.small.at[0],
        n.r_next, attn[1], n.small.at[1], n.mix.at[1], n.cosine, n.sine, seg_col, seg_row,
        n.ints.at[1], n.prio.at[1], n.upstream,
        n.out_0, n.picked_0, n.after_1, n.qkv_here, n.probs_here, n.attended_1, n.packed_1, n.slots_1, n.buffer_0, n.buffer_2,
    )
    start_all(keep[2:])
    both = (tokens_1, grads_1)
    for one in both:
        one.start()
    for one in both:
        one.spread()

    @pl.when(first)
    def _():
        spread.experts_ready(1)

    @pl.when(second)
    def _():
        spread.experts_ready(0)

    w_in, w_out = n.w_in.at[1], n.w_out.at[1]
    start_all(leaving)
    for one in both:
        one.near_ready()
    parts = both_ways(
        near_rows(tokens_1.groups), near_rows(grads_1.groups), w_in, w_out, near_of(n.hidden), near_of(n.grad_both)
    )
    for one, part in zip(both, parts):
        put_near(one.partial, part)
        one.near_back().start()
    exchange_far(
        both,
        lambda picks: both_ways(
            rows_at(tokens_1.groups, picks), rows_at(grads_1.groups, picks), w_in, w_out,
            far_of(n.hidden, picks), far_of(n.grad_both, picks),
        ),
    )
    n.grad_out[...] = mm(all_rows(n.hidden), all_rows(grads_1.groups), TN).astype(BF16)
    for one in both:
        one.near_arrived()
        one.return_home(range(owners))
    weight_grads_in(all_rows(tokens_1.groups), n.grad_both, n.grad_in)
    for one in both:
        one.finish_dispatch()
        one.finish()
    for one in keep[2:] + leaving:
        one.wait()
    if inside:
        spread.finish_attn()
    spread.finish_experts()


def turn_kernel(dims, inside, n):
    sums = ExpertSum(n.grad_in_1, n.grad_out_1, n.even, n.odd, n.got_out, n.sum_sems)
    loading = load_weights(n.attn, 1, n.w, n.small, n.load_sems)
    expert_loads = [
        pltpu.make_async_copy(n.w_in_all, n.w_in, n.load_sems.at[2]),
        pltpu.make_async_copy(n.w_out_all, n.w_out, n.load_sems.at[3]),
    ]
    start_all(expert_loads)
    grads = Exchange(0, n.buffer, n.groups, *n.home, n.blocks_back, n.sems)
    attn = []
    if inside:
        attn = [AttnSum(n.grads_a, n.attn_buffers_a, n.attn_sems_a), AttnSum(n.grads_b, n.attn_buffers_b, n.attn_sems_b)]
    greet_these(other_core() + along_z() + in_plane())
    start_all(sums.even())
    _, gain_second, vec_rows = small_rows_of(n.small)
    n.out[...] = combine(
        n.after[...], n.packed[...], n.slots[...], n.ints[1], n.made, gain_second, vec_rows, dims, n.picked
    ).astype(BF16)

    def rows_done():
        give_back(n.grad_x[...].astype(BF16).astype(F32), n.packed_0[...], n.slots_0[...], dims, n.buffer)
        grads.start()

    hooks = types.SimpleNamespace(
        early=False, rows_done=rows_done, first_done=lambda: [one.start() for one in attn[:1]],
        second_done=lambda: [one.start() for one in attn[1:]],
    )
    back_body(
        dims, n.upstream, None, n.after, n.packed, n.slots, n.ints.at[1], n.picked, n.returned, n.r, n.w, n.small, n.mix.at[1],
        n.x, n.qkv, n.probs, n.attended, n.cosine, n.sine, n.grad_x, n.grad_r, n.grad_mix, (n.grads_a, n.grads_b),
        n.grad_qkv, loading, hooks,
    )
    for one in expert_loads:
        one.wait()
    forward_again(near_rows(n.arrived), n.w_in, n.w_out, near_of(n.both), near_of(n.hidden))
    grads.spread()
    start_all(sums.odd())
    for one in attn:
        one.add_cores()
    grads.near_ready()

    def near_both(columns):
        return n.both[:2, :, :, columns].reshape(near_count, 2 * CHUNK)

    near_count = n.both.shape[0] // 2 * n.both.shape[1] * n.both.shape[2]
    put_near(
        grads.partial, back_of(near_rows(grads.groups), n.w_in, n.w_out, near_both, near_of(n.grad_both))
    )
    grads.near_back().start()
    for bys in grads.steps():
        picks = grads.far(bys)
        forward_again(
            rows_at(n.arrived, picks), n.w_in, n.w_out, far_of(n.both, picks), far_of(n.hidden, picks)
        )
    exchange_far(
        [grads],
        lambda picks: [back_of(
            rows_at(grads.groups, picks), n.w_in, n.w_out, lambda columns: rows_at(n.both, picks, columns),
            far_of(n.grad_both, picks),
        )],
    )
    n.grad_out_0[...] = mm(all_rows(n.hidden), all_rows(grads.groups), TN).astype(BF16)
    for one in attn:
        one.plane_ready()
        one.add_plane()
    grads.near_arrived()
    grads.return_home(range(grads.owners))
    weight_grads_in(all_rows(n.arrived), n.grad_both, n.grad_in_0)
    grads.finish_dispatch()
    grads.finish()
    for one, target in zip(attn, (n.attn_sum_a, n.attn_sum_b)):
        one.finish_near()
        one.z_ready()
        one.add_z(target)
        one.finish_z()
    wait_all(sums.even() + sums.odd(), sums.even(-1) + sums.odd(-1))


def spread_columns(target, halves_at, hidden_here):
    rows, columns = target.shape
    hidden = columns // 2
    pieces = hidden // (2 * hidden_here)
    parity = lax.rem(lax.axis_index("shard"), 2)
    for first_parity in range(2):

        @pl.when(parity == first_parity)
        def _():
            for half in range(2):
                for q in range(2):
                    odd = first_parity if q == 0 else 1 - first_parity
                    for pair in range(pieces // 2):
                        for side in range(2):
                            for ahead in range(0, hidden_here, CHUNK):
                                at = side * hidden + (2 * pair + odd) * 2 * hidden_here + half * hidden_here + ahead
                                source = 2 * (pair * hidden_here + ahead) + side * CHUNK
                                target[:, at : at + CHUNK] = halves_at(half, q)[:, source : source + CHUNK].astype(F32)


def last_kernel(dims, inside, wide, n):
    core, column, place = place_of()
    pieces = lax.axis_size("shard")
    pair_count = pieces // 2
    (sibling,) = other_core()
    loading = load_weights(n.attn, 0, n.w, n.small, n.load_sems)
    sums = ExpertSum(n.grad_in_0, n.grad_out_0, n.even_0, n.odd_0, n.got_out_0, n.sum_sems)
    attn = []
    if inside:
        attn = [AttnSum(n.grads_a, n.attn_buffers_a, n.attn_sems_a), AttnSum(n.grads_b, n.attn_buffers_b, n.attn_sems_b)]
    greet_these(other_core() + along_z() + (in_plane() if inside else []))
    start_all(sums.even() + sums.odd())
    pairs = ((n.out_0, n.out_1, n.both_out), (n.grad_x_0, n.grad_x_1, n.both_x), (n.grad_r_0, n.grad_r_1, n.r_pair))

    def swaps(section):
        for i, (zero, one, both) in enumerate(pairs):
            own, other = (zero, one) if section == 0 else (one, zero)
            yield (
                remote(other, both.at[section], n.swap_s.at[i], n.swap_r.at[i], sibling),
                pltpu.make_async_copy(own, both.at[section], n.local_sem.at[i]),
            )

    def each_core(action):
        for section in range(2):

            @pl.when(core == section)
            def _():
                action(section)

    def add_experts(section, grad_in, grad_out, even, odd, got_out):
        rows, out_rows = even.shape[1], got_out.shape[1]
        own_in = grad_in[pl.ds(pl.multiple_of(place * rows, rows), rows), :]
        own_out = grad_out[pl.ds(pl.multiple_of(lax.div(place, 2) * out_rows, out_rows), out_rows), :]
        in_sum = [own_in.astype(F32), odd[0].astype(F32)]
        for i in range(pair_count - 1):
            in_sum[0] = in_sum[0] + even[i].astype(F32)
            in_sum[1] = in_sum[1] + odd[i + 1].astype(F32)
        out_sum = own_out.astype(F32)
        for i in range(pair_count - 1):
            out_sum = out_sum + got_out[i].astype(F32)

        @pl.when(core == section)
        def _():
            for q in range(2):
                n.in_mine[q] = in_sum[q]
            n.out_mine[...] = out_sum

        @pl.when(core != section)
        def _():
            for q in range(2):
                n.in_sent[q] = in_sum[q].astype(BF16)
            n.out_sent[...] = out_sum.astype(BF16)
            for one in finals:
                one.start()

    finals = [
        remote(n.in_sent, n.in_got, n.final_s.at[0], n.final_r.at[0], sibling),
        remote(n.out_sent, n.out_got, n.final_s.at[1], n.final_r.at[1], sibling),
    ]
    hooks = types.SimpleNamespace(
        early=True, first_done=lambda: [one.start() for one in attn[:1]],
        heads_done=lambda: [one.add_cores() for one in attn[:1]], second_done=lambda: [one.start() for one in attn[1:]],
    )
    back_body(
        dims, n.grad_x_1, n.grad_r_1, n.after, n.packed, n.slots, n.ints.at[0], n.picked, n.returned, n.r, n.w, n.small,
        n.mix.at[0], n.x, n.qkv, n.probs, n.attended, n.cosine, n.sine, n.grad_x_0, n.grad_r_0, n.grad_mix,
        (n.grads_a, n.grads_b), n.grad_qkv, loading, hooks,
    )

    @each_core
    def _(section):
        for away, here in swaps(section):
            away.start()
            here.start()

    for one in attn[1:]:
        one.add_cores()
    add_experts(1, n.grad_in_1, n.grad_out_1, n.even_1, n.odd_1, n.got_out_1)
    for one in attn:
        one.plane_ready()
        one.add_plane()
    wait_all(sums.even() + sums.odd(), sums.even(-1) + sums.odd(-1))
    add_experts(0, n.grad_in_0, n.grad_out_0, n.even_0, n.odd_0, n.got_out_0)
    for one in finals:
        one.wait()
    for half in range(2):

        @pl.when(core == half)
        def _():
            if wide:
                hidden_here = n.out_mine.shape[0]
                spread_columns(n.in_total, lambda at, q: n.in_mine[q] if at == half else n.in_got[q], hidden_here)
            else:
                for q in range(2):
                    n.in_total[half, q] = n.in_mine[q]
                    n.in_total[1 - half, q] = n.in_got[q].astype(F32)
            count = n.out_mine.shape[0]
            n.out_total[half * count : (half + 1) * count] = n.out_mine[...]
            n.out_total[(1 - half) * count : (2 - half) * count] = n.out_got[...].astype(F32)

    for i, (one, sum_0, sum_1, total) in enumerate(zip(
        attn, (n.attn_sum_0a, n.attn_sum_0b), (n.attn_sum_1a, n.attn_sum_1b), (n.attn_total_a, n.attn_total_b)
    )):
        one.z_ready()
        one.add_z(sum_0)
        holder = one.holds(place)
        for section in range(2):
            mine, other = (sum_0, sum_1) if section == 0 else (sum_1, sum_0)
            home = remote(other, total, n.final_s.at[2 + i], n.final_r.at[2 + i], sibling)

            @pl.when(holder & (core == section))
            def _():
                home.start()
                total[...] = mine[...]
                home.wait_send()

            @pl.when(jnp.logical_not(holder) & (core == section))
            def _():
                home.wait_recv()

    if inside:
        width = n.x.shape[1]
        half = width // LANES // 2 * LANES
        for batch, total in enumerate((n.attn_total_a, n.attn_total_b)):
            for part in range(3):
                at = part * width + batch * half
                n.qkv_total[:, at : at + half] = total[:, part * half : (part + 1) * half]
        n.attn_out_total[...] = n.attn_total_a[:, 3 * half :]
        small = n.attn_total_b[:, 3 * half :]
        nexp, rows = n.mix_total.shape[0], small.shape[0]
        n.mix_total[...] = small[:nexp, AT_MIX : AT_MIX + nexp]
        n.turning[...] = jnp.zeros(n.turning.shape, F32)
        n.turning[:rows] = small
        turned_small = n.turning[...].T
        for target, at in ((n.router_total, 0), (n.proj_total, AT_PROJ), (n.vec_total, AT_VEC), (n.gain_total, AT_GAIN)):
            target[...] = turned_small[at : at + target.shape[0], :rows]

    @each_core
    def _(section):
        for away, here in swaps(section):
            away.wait()
            here.wait()

    for batch in range(2):
        n.both_r[batch] = n.r_pair[batch].T[: n.both_r.shape[1]]

    for one in attn:
        one.finish_near()
        one.finish_z()


def local(
    x_in,
    cotangent,
    gate_prev,
    segments,
    routes,
    priority,
    attn_qkv,
    attn_out,
    router,
    const_proj,
    const_vec,
    gains,
    gate_mix,
    expert_in,
    expert_out,
):
    seq_len, width = x_in.shape[2:]
    nexp = gate_prev.shape[-1]
    owners, pieces = lax.axis_size("expert"), lax.axis_size("shard")
    nffn = owners * expert_in.shape[1]
    nconst = const_vec.shape[-1]
    capacity = (5 * TOP * seq_len + 4 * nexp - 1) // (4 * nexp)
    room = -(-capacity // 16) * 16
    slots = nffn * room
    core = lax.axis_index("section")
    first_core = core == 0
    in_rows, columns = expert_in.shape[2:]
    hidden_here = expert_out.shape[2] // 2
    pairs = pieces // 2
    quarter = pairs * hidden_here
    chunks = quarter // CHUNK
    rows = attn_qkv.shape[1]
    inside, wide = rows % 16 == 0, hidden_here % CHUNK == 0

    def swap(item):
        return lax.ppermute(item, "section", [(0, 1), (1, 0)])

    def by_section(own, other):
        return jnp.where(first_core, own, other), jnp.where(first_core, other, own)

    def as_chunks(half):
        half = jnp.moveaxis(half, 3, 0).reshape(2, in_rows, 2, chunks, CHUNK)
        return jnp.swapaxes(half, 2, 3).reshape(2, in_rows, 2 * quarter)

    w_out = expert_out[0, 0].reshape(2, hidden_here, width)
    in_pieces = expert_in[0, 0]
    if not wide:
        w_in = in_pieces.reshape(in_rows, 2, pairs, 2, 2, hidden_here)
        in_pieces = jnp.stack([as_chunks(w_in[:, :, :, :, half]) for half in range(2)])
    given = None
    if not inside:
        def lanes(array, upto):
            return jnp.pad(array, ((0, 0), (0, upto - array.shape[1])))

        small = [
            lanes(router[0], AT_PROJ), lanes(const_proj[0], AT_VEC - AT_PROJ), lanes(const_vec[0], AT_GAIN - AT_VEC),
            lanes(gains[0], LANES - AT_GAIN),
        ]
        shared = jnp.concatenate([attn_qkv[0], attn_out[0]] + small, axis=1)
        shared = lax.all_gather(shared, ("expert", "shard"), axis=0, tiled=True)
        given = jnp.stack(by_section(shared, swap(shared)))
    dims = (nffn, nexp, capacity, slots, rows if inside else 0)
    heads = width // HEAD
    blocks = (owners, room, width)
    token_f32 = shaped((seq_len, width), F32)
    token_b16 = shaped((seq_len, width), BF16)
    lanes_f32 = shaped((seq_len, LANES), F32)
    lanes_i32 = shaped((seq_len, LANES), jnp.int32)
    block_shape = shaped(blocks, BF16)
    attn_shape = shaped((width, 4 * width + LANES), BF16)
    attn_columns = attn_shape.shape[1]
    pair_shape = shaped((TOP, seq_len, width), BF16)
    in_shape, out_shape = shaped((width, 2 * quarter), BF16), shaped((quarter, width), BF16)
    dma = pltpu.SemaphoreType.DMA
    even, odd, got_out = got_shapes(pieces, in_rows, 2 * quarter, hidden_here, width)

    def vmem(shape):
        return pltpu.VMEM(shape.shape, shape.dtype)

    def attend_out(section):
        return {
            f"after_{section}": token_f32,
            f"qkv_{section}": shaped((seq_len, 3 * width), BF16),
            f"probs_{section}": shaped((heads, seq_len, seq_len), BF16),
            f"attended_{section}": token_b16,
            f"packed_{section}": lanes_f32,
            f"slots_{section}": lanes_i32,
        }

    ins = dict(
        in_pieces=in_pieces, w_out_here=w_out, x_in=x_in[:, 0], cotangent=cotangent[:, 0], gate_prev=jnp.swapaxes(gate_prev[:, 0], 1, 2),
        segments=segments, routes=jnp.swapaxes(routes[0, :, 0], 1, 2), priority=priority[0], gate_mix=gate_mix[0],
    )
    table_shapes = dict(
        mix=shaped((2, LANES, LANES), F32), cosine=lanes_f32, sine=lanes_f32, ints=shaped((2, seq_len, LANES), jnp.int32),
    )
    outs = dict(
        w_in_kept=in_shape, w_out_kept=out_shape, arrived=shaped((4,) + blocks, BF16), r_next=shaped((seq_len, LANES), BF16), out_0=token_b16, picked_0=pair_shape,
        made=block_shape, returned=block_shape, grad_in=in_shape, grad_out=out_shape, **attend_out(0), **attend_out(1),
        x=token_b16, r=shaped((seq_len, LANES), BF16), upstream=token_f32, **table_shapes,
    )
    if inside:
        outs["attn_kept"] = shaped((2,) + attn_shape.shape, BF16)
        ins = dict(
            ins, w_qkv=attn_qkv[0], w_attn=attn_out[0], router=router[0].T, const_proj=const_proj[0].T,
            const_vec=const_vec[0].T, gains=gains[0].T,
        )
    else:
        ins["attn"] = given
    f = call(
        lambda n: front_kernel(dims, inside, wide, n), 0, ins, outs,
        dict(
            small=pltpu.VMEM((2, width, LANES), BF16), buffer_0=vmem(block_shape),
            buffer_2=vmem(block_shape), groups_1=pltpu.VMEM((4,) + blocks, BF16), groups_2=pltpu.VMEM((4,) + blocks, BF16),
            token_home=home_buffers(*blocks), grad_home=home_buffers(*blocks), sems=exchange_sems(3, owners),
            spread_sems=spread_scratch(owners, pieces, 2 * pairs * max(hidden_here // CHUNK, 1) if wide else 1),
            packed_w=pltpu.VMEM((rows, 4 * width + LANES), BF16), mix_own=pltpu.VMEM((LANES, LANES), F32),
            prio=pltpu.VMEM((2, 1, seq_len), jnp.int32), cross_s=dma((3,)), cross_r=dma((3,)), bring_sems=dma((3,)),
            qkv_here=pltpu.VMEM((seq_len, 3 * width), BF16), probs_here=pltpu.VMEM((heads, seq_len, seq_len), BF16),
            keep_sems=dma((2, 2)), leave_sems=dma((4,)),
            w_in=pltpu.VMEM((2, width, 2 * quarter), BF16), w_out=pltpu.VMEM((2, quarter, width), BF16),
            **(dict(attn=pltpu.VMEM((2,) + attn_shape.shape, BF16)) if inside else dict(attn_here=vmem(attn_shape))), turning=pltpu.VMEM((LANES, seq_len), F32), routes_all=pltpu.VMEM((2, TOP, seq_len), jnp.int32),
            hidden=pltpu.VMEM((4,) + blocks[:2] + (quarter,), BF16), grad_both=pltpu.VMEM((4,) + blocks[:2] + (2 * quarter,), BF16),
        ),
        ("in_pieces", "w_out_here", "x_in", "cotangent", "qkv_0", "probs_0", "qkv_1", "probs_1")
        + ("w_in_kept", "w_out_kept", "attn_kept" if inside else "attn"), 8 << 30,
    )
    tables = dict(mix=f.mix, cosine=f.cosine, sine=f.sine, ints=f.ints)
    attn_all = f.attn_kept if inside else given
    scratch = dict(
        w=vmem(attn_shape), small=pltpu.VMEM((width, LANES), BF16), load_sems=dma((4,)), grad_qkv=pltpu.VMEM((seq_len, 3 * width), BF16),
        sum_sems=expert_sum_sems(pieces),
    )
    attn_scratch = {}
    half = width // LANES // 2 * LANES
    batches = dict(a=3 * half + width, b=3 * half + LANES)
    block_sums = {name: shaped((rows, lanes) if inside else (8, LANES), F32) for name, lanes in batches.items()}
    grad_shapes = {f"grads_{name}": shaped((width, lanes), BF16) for name, lanes in batches.items()}
    if inside:
        for name, lanes in batches.items():
            buffers, sems = attn_sum_scratch(owners, pieces, rows, lanes)
            attn_scratch.update({f"attn_buffers_{name}": buffers, f"attn_sems_{name}": sems})
    outs = dict(
        out=token_b16, grad_x=token_f32, grad_r=lanes_f32, grad_mix=shaped((LANES, LANES), F32), even=even, odd=odd,
        got_out=got_out, grad_in_0=in_shape, grad_out_0=out_shape, blocks_back=block_shape,
        attn_sum_a=block_sums["a"], attn_sum_b=block_sums["b"],
    )
    more = {name: vmem(shape) for name, shape in grad_shapes.items()}
    if not inside:
        outs, more = dict(outs, **grad_shapes), {}
    t = call(
        lambda n: turn_kernel(dims, inside, n), 1,
        dict(
            attn=attn_all, w_in_all=f.w_in_kept, w_out_all=f.w_out_kept, grad_in_1=f.grad_in, grad_out_1=f.grad_out,
            upstream=f.upstream, after=f.after_1, packed=f.packed_1, slots=f.slots_1, made=f.made, returned=f.returned, r=f.r_next,
            x=f.out_0, qkv=f.qkv_1, probs=f.probs_1, attended=f.attended_1, packed_0=f.packed_0, slots_0=f.slots_0,
            arrived=f.arrived, **tables,
        ),
        outs,
        dict(
            picked=vmem(pair_shape), buffer=vmem(block_shape), groups=pltpu.VMEM((4,) + blocks, BF16), home=home_buffers(*blocks),
            sems=exchange_sems(1, owners), w_in=vmem(in_shape), w_out=vmem(out_shape),
            both=pltpu.VMEM((4,) + blocks[:2] + (2 * quarter,), F32 if slots <= 384 else BF16), hidden=pltpu.VMEM((4,) + blocks[:2] + (quarter,), BF16),
            grad_both=pltpu.VMEM((4,) + blocks[:2] + (2 * quarter,), BF16), **scratch, **attn_scratch, **more,
        ),
        ("attn", "w_in_all", "w_out_all", "grad_in_1", "grad_out_1"), 12 << 30,
    )
    in_total = shaped((in_rows, columns) if wide else (2, 2, in_rows, 2 * quarter), F32)
    half_in, half_out = (2, in_rows, 2 * quarter), (hidden_here, width)
    outs = dict(
        both_out=shaped((2, seq_len, width), BF16), both_x=shaped((2, seq_len, width), F32),
        both_r=shaped((2, nexp, seq_len), F32), in_total=in_total, out_total=shaped((2 * hidden_here, width), F32),
        grad_mix=shaped((LANES, LANES), F32),
    )
    if inside:
        narrow = dict(router_total=nexp, proj_total=const_proj.shape[2], vec_total=nconst, gain_total=2)
        outs = dict(
            outs, qkv_total=shaped((rows, 3 * width), F32), attn_out_total=shaped((rows, width), F32),
            mix_total=shaped((nexp, nexp), F32), **{name: shaped((lanes, rows), F32) for name, lanes in narrow.items()},
        )
    else:
        outs = dict(outs, **grad_shapes)
    z = call(
        lambda n: last_kernel(dims, inside, wide, n), 2,
        dict(
            attn=attn_all, grad_in_0=t.grad_in_0, grad_out_0=t.grad_out_0, grad_in_1=f.grad_in, grad_out_1=f.grad_out,
            even_1=t.even, odd_1=t.odd, got_out_1=t.got_out, attn_sum_1a=t.attn_sum_a, attn_sum_1b=t.attn_sum_b, out_0=f.out_0, out_1=t.out,
            grad_x_1=t.grad_x, grad_r_1=t.grad_r, after=f.after_0, packed=f.packed_0, slots=f.slots_0, picked=f.picked_0,
            returned=t.blocks_back, r=f.r, x=f.x, qkv=f.qkv_0, probs=f.probs_0, attended=f.attended_0, **tables,
        ),
        outs,
        dict(
            even_0=vmem(even), odd_0=vmem(odd), got_out_0=vmem(got_out), grad_x_0=vmem(token_f32), grad_r_0=vmem(lanes_f32),
            attn_sum_0a=vmem(block_sums["a"]), attn_sum_0b=vmem(block_sums["b"]), attn_total_a=vmem(block_sums["a"]),
            attn_total_b=vmem(block_sums["b"]), turning=pltpu.VMEM((LANES, LANES), F32), r_pair=pltpu.VMEM((2, seq_len, LANES), F32), in_mine=pltpu.VMEM(half_in, F32), out_mine=pltpu.VMEM(half_out, F32),
            in_sent=pltpu.VMEM(half_in, BF16), out_sent=pltpu.VMEM(half_out, BF16), in_got=pltpu.VMEM(half_in, BF16),
            out_got=pltpu.VMEM(half_out, BF16), swap_s=dma((3,)), swap_r=dma((3,)), local_sem=dma((3,)), final_s=dma((4,)),
            final_r=dma((4,)), **scratch, **attn_scratch, **more,
        ),
        ("attn", "both_out", "both_x", "out_0", "out_1"), 6 << 30,
    )
    in_grad = z.in_total
    if not wide:
        odd = lax.axis_index("shard") % 2
        in_grad = jnp.where(odd == 0, in_grad, in_grad[:, ::-1])
        in_grad = jnp.swapaxes(in_grad.reshape(2, 2, in_rows, chunks, 2, CHUNK), 3, 4)
        in_grad = in_grad.reshape(2, 2, in_rows, 2, pairs, hidden_here)
        in_grad = jnp.transpose(in_grad, (2, 3, 4, 1, 0, 5)).reshape(in_rows, columns)
    if inside:
        shared_grads = (
            z.qkv_total, z.attn_out_total, z.router_total.T, z.proj_total.T, z.vec_total.T, z.gain_total.T, z.mix_total
        )
    else:
        def joined(a, b):
            parts = []
            for part in range(3):
                parts += [a[:, part * half : (part + 1) * half], b[:, part * half : (part + 1) * half]]
            return jnp.concatenate(parts + [a[:, 3 * half :], b[:, 3 * half :]], axis=1)

        grads_0, grads_1 = joined(z.grads_a, z.grads_b), joined(t.grads_a, t.grads_b)
        own = jnp.where(first_core, grads_0, grads_1)
        total = own.astype(F32) + swap(jnp.where(first_core, grads_1, grads_0)).astype(F32)
        total = lax.psum_scatter(total.astype(BF16), ("expert", "shard"), scatter_dimension=0, tiled=True).astype(F32)
        own = jnp.where(first_core, z.grad_mix, t.grad_mix)
        mix_grad = own + swap(jnp.where(first_core, t.grad_mix, z.grad_mix))
        small = total[:, 4 * width :]
        shared_grads = (
            total[:, : 3 * width],
            total[:, 3 * width : 4 * width],
            small[:, :nexp],
            small[:, AT_PROJ : AT_PROJ + const_proj.shape[-1]],
            small[:, AT_VEC : AT_VEC + nconst],
            small[:, AT_GAIN : AT_GAIN + 2],
            lax.psum(mix_grad, ("expert", "shard"))[:nexp, :nexp],
        )
    return (
        z.both_out[None, :, None],
        z.both_x[None, :, None],
        jnp.swapaxes(z.both_r, 1, 2)[None, :, None],
        *[grad[None] for grad in shared_grads],
        in_grad[None, None],
        z.out_total[None, None],
    )


def solution(mesh):
    placed = (
        P(None, ("expert", "shard"), None, None),
        P(None, ("expert", "shard"), None, None),
        P(None, ("expert", "shard"), None, None),
        P(None, ("expert", "shard"), None),
        P("section", None, ("expert", "shard"), None, None),
        P("section", None, ("expert", "shard"), None),
        P("section", ("expert", "shard"), None),
        P("section", ("expert", "shard"), None),
        P("section", ("expert", "shard"), None),
        P("section", ("expert", "shard"), None),
        P("section", ("expert", "shard"), None),
        P("section", ("expert", "shard"), None),
        P("section", None, None),
        P("section", "expert", "shard", None),
        P("section", "expert", "shard", None),
    )
    return jax.shard_map(
        local,
        mesh=mesh,
        in_specs=placed,
        out_specs=(
            P("section", None, ("expert", "shard"), None, None),
            P("section", None, ("expert", "shard"), None, None),
            P("section", None, ("expert", "shard"), None, None),
            P("section", ("expert", "shard"), None),
            P("section", ("expert", "shard"), None),
            P("section", ("expert", "shard"), None),
            P("section", ("expert", "shard"), None),
            P("section", ("expert", "shard"), None),
            P("section", ("expert", "shard"), None),
            P("section", None, None),
            P("section", "expert", "shard", None),
            P("section", "expert", "shard", None),
        ),
        check_vma=False,
    )
```

```python
import math
import types

import jax
import jax.numpy as jnp
from jax import lax
from jax.experimental import pallas as pl
from jax.experimental.pallas import tpu as pltpu
from jax.sharding import PartitionSpec as P

HEADS = 12
HEAD = 64
TOP = 2
CHUNK = 256
LANES = 128
AT_PROJ = 16
AT_VEC = 24
AT_GAIN = 28
AT_MIX = 32

HIGH = lax.Precision.HIGHEST
norm_eps = 1e-06
masked_score = -1e30
F32 = jnp.float32
BF16 = jnp.bfloat16


VMEM_BYTES = 60 * 1024 * 1024


def mm(a, b, contract=((1,), (0,)), precision=None):
    return lax.dot_general(a, b, (contract, ((), ())), precision=precision, preferred_element_type=F32)


NT = ((1,), (1,))
TN = ((0,), (0,))


def lane_of(rows, columns=LANES):
    return lax.broadcasted_iota(jnp.int32, (rows, columns), 1)


def inverse_norm(values):
    return lax.rsqrt(jnp.mean(values * values, axis=-1, keepdims=True) + norm_eps)


def norm_back(grad_unit, unit, inverse):
    return inverse * (grad_unit - unit * jnp.mean(grad_unit * unit, axis=-1, keepdims=True))


def roll(x, by):
    return pltpu.roll(x, by, 1)


def turned(x, lane):
    return jnp.where(lane % HEAD < HEAD // 2, roll(x, LANES - HEAD // 2), roll(x, HEAD // 2))


def hi_lo(x):
    high = x.astype(BF16)
    return high, (x - high.astype(F32)).astype(BF16)


def ones_where(condition):
    return jnp.where(condition, 1.0, 0.0).astype(BF16)


def small_rows_of(small):
    rows = small[...].astype(F32).T
    return rows[AT_GAIN : AT_GAIN + 1], rows[AT_GAIN + 1 : AT_GAIN + 2], rows[AT_VEC:AT_GAIN]


def attention(x, w, gain_first, cosine, sine, seg_col, seg_row, qkv, probs_att, attended):
    seq_len, width = x.shape
    first_b = (x * inverse_norm(x) * gain_first).astype(BF16)
    place_q = lax.broadcasted_iota(jnp.int32, (seq_len, seq_len), 0)
    place_k = lax.broadcasted_iota(jnp.int32, (seq_len, seq_len), 1)
    bias = jnp.where((seg_col == seg_row) & (place_k <= place_q), 0.0, masked_score)
    lane = lane_of(seq_len)
    low_head = lane < HEAD
    for pair in range(width // LANES):
        at = pair * LANES
        q = mm(first_b, w[:, at : at + LANES])
        k = mm(first_b, w[:, width + at : width + at + LANES])
        v = mm(first_b, w[:, 2 * width + at : 2 * width + at + LANES]).astype(BF16)
        q = q * cosine + turned(q, lane) * sine
        k = (k * cosine + turned(k, lane) * sine).astype(BF16)
        outs = []
        for half in range(2):
            one = jnp.where(low_head if half == 0 else lane >= HEAD, q, 0.0).astype(BF16)
            scores = mm(one, k, NT) * (HEAD**-0.5) + bias
            scores = jnp.exp(scores - jnp.max(scores, axis=-1, keepdims=True))
            probs = (scores * (1.0 / jnp.sum(scores, axis=-1, keepdims=True))).astype(BF16)
            probs_att[2 * pair + half] = probs
            outs.append(mm(probs, v))
        attended[:, at : at + LANES] = jnp.where(low_head, outs[0], outs[1]).astype(BF16)
        qkv[:, at : at + LANES] = q.astype(BF16)
        qkv[:, width + at : width + at + LANES] = k
        qkv[:, 2 * width + at : 2 * width + at + LANES] = v
    return x + mm(attended[...], w[:, 3 * width : 4 * width])


def gating(after, r, small, mix, gain_second, ints, prio_row, dims, packed_ref, slot_ref, r_next, buffer):
    nffn, nexp, capacity, slots, _ = dims
    rows = after.shape[0]
    second_b = (after * inverse_norm(after) * gain_second).astype(BF16)
    lane = lane_of(rows)
    logits = mm(second_b, small)
    full = logits + mm(r, mix, precision=HIGH)
    inside = lane < nexp
    full = jnp.where(inside, full, masked_score)
    raised = jnp.exp(full - jnp.max(full, axis=-1, keepdims=True))
    probs = raised / jnp.sum(raised, axis=-1, keepdims=True)
    other = jnp.where(lane % 2 == 0, roll(logits, LANES - 1), roll(logits, 1))
    bigger = jnp.maximum(logits, other)
    mine_e = jnp.exp(logits - bigger)
    mixes = mine_e / (mine_e + jnp.exp(other - bigger))
    before = ones_where(prio_row < column_of(prio_row).astype(jnp.int32))
    route = (ints[:, 0:1], ints[:, 1:2])
    routed = ones_where(((lane == route[0]) | (lane == route[1])) & (lane < nffn))
    rank = mm(before, routed)
    gates, places = [], []
    dispatch = 0.0
    stride = slots // nffn
    for k in range(TOP):
        chosen = lane == route[k]
        gates.append(jnp.sum(jnp.where(chosen, probs, 0.0), axis=-1, keepdims=True))
        rank_k = jnp.sum(jnp.where(chosen, rank, 0.0), axis=-1, keepdims=True).astype(jnp.int32)
        kept = (route[k] < nffn) & (rank_k < capacity)
        places.append(jnp.where(kept, route[k] * stride + rank_k, -1))
        dispatch = dispatch + jnp.where(places[k] == lane_of(rows, slots), 1.0, 0.0)
    buffer[...] = mm(dispatch.astype(BF16), second_b, TN).astype(BF16).reshape(buffer.shape)
    packed = jnp.where(inside, probs, jnp.where((lane >= AT_PROJ) & (lane < AT_VEC), mixes, 0.0))
    packed = jnp.where(lane == AT_VEC, gates[0], packed)
    packed_ref[...] = jnp.where(lane == AT_VEC + 1, gates[1], packed)
    slot_ref[...] = jnp.where(lane == 0, places[0], places[1])
    if r_next is not None:
        r_next[...] = jnp.where(inside, full, 0.0).astype(BF16)


def extras(packed, ints, nffn, nconst):
    gates = (packed[:, AT_VEC : AT_VEC + 1], packed[:, AT_VEC + 1 : AT_VEC + 2])

    def of(expert):
        return sum(jnp.where(ints[:, k : k + 1] == expert, gates[k], 0.0) for k in range(TOP))

    def mixes(c):
        at = AT_PROJ + 2 * c
        return packed[:, at : at + 1], packed[:, at + 1 : at + 2]

    return gates, of(nffn + 1), [of(nffn + 2 + c) for c in range(nconst)], [mixes(c) for c in range(nconst)]


def combine(after, packed, slot_pair, ints, blocks, gain_second, vec_rows, dims, picked_ref):
    nffn, nexp, _, slots, _ = dims
    nconst = nexp - nffn - 2
    rows = after.shape[0]
    second = after * inverse_norm(after) * gain_second
    gates, copied, const, mixes = extras(packed, ints, nffn, nconst)
    made = blocks[...].reshape(slots, after.shape[1])
    slot_lane = lane_of(rows, slots)
    coefficient = copied
    for c in range(nconst):
        coefficient = coefficient + const[c] * mixes[c][0]
    out = after + coefficient * second
    for k in range(TOP):
        picked = mm(ones_where(slot_pair[:, k : k + 1] == slot_lane), made)
        picked_ref[k] = picked.astype(BF16)
        out = out + gates[k] * picked
    for c in range(nconst):
        out = out + (const[c] * mixes[c][1]) * vec_rows[c : c + 1]
    return out


def give_back(grad_y, packed, slot_pair, dims, buffer):
    slots = dims[3]
    slot_lane = lane_of(grad_y.shape[0], slots)
    total = 0.0
    for k in range(TOP):
        gate = packed[:, AT_VEC + k : AT_VEC + k + 1]
        table = ones_where(slot_pair[:, k : k + 1] == slot_lane)
        total = total + mm(table, (gate * grad_y).astype(BF16), TN)
    buffer[...] = total.astype(BF16).reshape(buffer.shape)


def moe_back(
    grad_y, grad_log_in, after, packed, slot_pair, ints, picked, blocks, r, small, mix, gain_second, vec_rows, dims
):
    nffn, nexp, _, slots, _ = dims
    nconst = nexp - nffn - 2
    rows = grad_y.shape[0]
    lane = lane_of(rows)
    inverse = inverse_norm(after)
    unit = after * inverse
    second = unit * gain_second
    second_b = second.astype(BF16)
    gates, copied, const, mixes = extras(packed, ints, nffn, nconst)
    grad_buffer = blocks[...].reshape(slots, after.shape[1])
    slot_lane = lane_of(rows, slots)
    dispatch = sum(jnp.where(slot_pair[:, k : k + 1] == slot_lane, 1.0, 0.0) for k in range(TOP))
    grad_second = mm(dispatch.astype(BF16), grad_buffer)
    along_second = jnp.sum(grad_y * second, axis=-1, keepdims=True)
    coefficient = copied
    grad_extra = [(nffn + 1, along_second)]
    grad_lanes = jnp.zeros((rows, LANES), F32)
    vec_grads = []
    for c in range(nconst):
        along = jnp.sum(grad_y * vec_rows[c : c + 1], axis=-1, keepdims=True)
        m0, m1 = mixes[c]
        coefficient = coefficient + const[c] * m0
        grad_extra.append((nffn + 2 + c, m0 * along_second + m1 * along))
        d0, d1 = const[c] * along_second, const[c] * along
        mean = m0 * d0 + m1 * d1
        at = AT_PROJ + 2 * c
        grad_lanes = jnp.where(lane == at, m0 * (d0 - mean), grad_lanes)
        grad_lanes = jnp.where(lane == at + 1, m1 * (d1 - mean), grad_lanes)
        vec_grads.append(jnp.sum(grad_y * (const[c] * m1), axis=0, keepdims=True))
    grad_second = grad_second + coefficient * grad_y
    grad_probs = jnp.zeros((rows, LANES), F32)
    for k in range(TOP):
        grad_gate = jnp.sum(picked[k].astype(F32) * grad_y, axis=-1, keepdims=True)
        for expert, value in grad_extra:
            grad_gate = grad_gate + jnp.where(ints[:, k : k + 1] == expert, value, 0.0)
        grad_probs = grad_probs + jnp.where(lane == ints[:, k : k + 1], grad_gate, 0.0)
    probs = jnp.where(lane < nexp, packed, 0.0)
    grad_logits = probs * (grad_probs - jnp.sum(probs * grad_probs, axis=-1, keepdims=True)) + grad_log_in
    grad_mix = mm(jnp.where(lane < nexp, r, 0.0), jnp.where(lane < nexp, grad_logits, 0.0), TN, HIGH)
    grad_r = mm(grad_logits, mix, NT, HIGH)
    high, low = hi_lo(jnp.where(lane < nexp, grad_logits, grad_lanes))
    small_rows = mm(high, second_b, TN) + mm(low, second_b, TN)
    grad_second = grad_second + mm(high, small, NT) + mm(low, small, NT)
    grad_gain = jnp.sum(grad_second * unit, axis=0, keepdims=True)
    grad_after = grad_y + norm_back(grad_second * gain_second, unit, inverse)
    row = lax.broadcasted_iota(jnp.int32, small_rows.shape, 0)
    small_rows = jnp.where(row < AT_VEC, small_rows, 0.0)
    for c in range(nconst):
        small_rows = jnp.where(row == AT_VEC + c, vec_grads[c], small_rows)
    small_rows = jnp.where(row == AT_GAIN + 1, grad_gain, small_rows)
    return grad_after, grad_r, grad_mix, small_rows


def attention_back(
    grad_after, x, qkv, probs_att, attended, small_rows, mix_tile, w, gain_first, cosine, sine, grads, grad_qkv, grad_x, hooks
):
    seq_len, width = x.shape
    inverse = inverse_norm(x)
    unit = x * inverse
    first_b = (unit * gain_first).astype(BF16)
    grad_branch = grad_after.astype(BF16)
    lane = lane_of(seq_len)
    low_head = lane < HEAD
    masks = (ones_where(low_head), ones_where(lane >= HEAD))
    scale = HEAD**-0.5
    heads_half = width // LANES // 2
    wide = heads_half * LANES

    def weight_grads(batch):
        for part in range(3):
            columns = slice(part * width + batch * wide, part * width + (batch + 1) * wide)
            grads[batch][:, part * wide : (part + 1) * wide] = mm(first_b, grad_qkv[:, columns], TN).astype(BF16)
        if batch == 0:
            grads[0][:, 3 * wide :] = mm(attended[...], grad_branch, TN).astype(BF16)

    for pair in range(width // LANES):
        at = pair * LANES
        q = qkv[:, at : at + LANES]
        k = qkv[:, width + at : width + at + LANES]
        v = qkv[:, 2 * width + at : 2 * width + at + LANES]
        g = mm(grad_branch, w[at : at + LANES, 3 * width : 4 * width], NT).astype(BF16)
        dq, dk, dv = [], [], []
        for half in range(2):
            probs = probs_att[2 * pair + half]
            grad_p = mm(g * masks[half], v, NT)
            p = probs.astype(F32)
            grad_s = (p * (grad_p - jnp.sum(p * grad_p, axis=-1, keepdims=True))).astype(BF16)
            dv.append(mm(probs, g, TN))
            dq.append(mm(grad_s, k))
            dk.append(mm(grad_s, q, TN))
        dq = jnp.where(low_head, dq[0], dq[1]) * scale
        dk = jnp.where(low_head, dk[0], dk[1]) * scale
        grad_qkv[:, at : at + LANES] = (dq * cosine - turned(dq, lane) * sine).astype(BF16)
        grad_qkv[:, width + at : width + at + LANES] = (dk * cosine - turned(dk, lane) * sine).astype(BF16)
        grad_qkv[:, 2 * width + at : 2 * width + at + LANES] = jnp.where(low_head, dv[0], dv[1]).astype(BF16)
        if hooks.early and pair == heads_half - 1:
            weight_grads(0)
            hooks.first_done()
    if hooks.early:
        hooks.heads_done()
        weight_grads(1)
    grad_first = mm(grad_qkv[...], w[:, : 3 * width], NT)
    grad_gain = jnp.sum(grad_first * unit, axis=0, keepdims=True)
    grad_x[...] = grad_after + norm_back(grad_first * gain_first, unit, inverse)
    row = lax.broadcasted_iota(jnp.int32, small_rows.shape, 0)
    small_rows = jnp.where(row == AT_GAIN, grad_gain, small_rows)
    grads[1][:, 3 * wide :] = (small_rows.T + mix_tile).astype(BF16)
    if not hooks.early:
        hooks.rows_done()
        weight_grads(0)
        hooks.first_done()
        weight_grads(1)
    hooks.second_done()


def attend_kernel(
    dims, x, r, w, small, mix, cosine, sine, seg_col, seg_row, ints, prio_row,
    after, qkv, probs_att, attended, packed, slot_pair, r_next, buffer,
):
    gain_first, gain_second, _ = small_rows_of(small)
    after_v = attention(
        x[...].astype(F32), w, gain_first, cosine[...], sine[...], seg_col, seg_row, qkv, probs_att, attended
    )
    after[...] = after_v
    gating(
        after_v, r[...].astype(F32), small[...], mix[...], gain_second, ints[...], prio_row[...], dims,
        packed, slot_pair, r_next, buffer,
    )


def middle_kernel(
    dims, after_0, packed_0, slots_0, ints_0, blocks_0, small_0,
    r, w, small, mix, cosine, sine, seg_col, seg_row, ints, prio_row, grad_y,
    out, picked, after, qkv, probs_att, attended, packed, slot_pair, buffer, grad_buffer,
):
    _, gain_second, vec_rows = small_rows_of(small_0)
    out[...] = combine(
        after_0[...], packed_0[...], slots_0[...], ints_0[...], blocks_0, gain_second, vec_rows, dims, picked
    ).astype(BF16)
    attend_kernel(
        dims, out, r, w, small, mix, cosine, sine, seg_col, seg_row, ints, prio_row,
        after, qkv, probs_att, attended, packed, slot_pair, None, buffer,
    )
    give_back(grad_y[...], packed[...], slot_pair[...], dims, grad_buffer)


def back_body(
    dims, grad_y, grad_log, after, packed, slot_pair, ints, picked, blocks, r, w, small, mix, x, qkv, probs_att, attended,
    cosine, sine, grad_x, grad_r, grad_mix, grads, grad_qkv, loading, hooks,
):
    gain_first, gain_second, vec_rows = small_rows_of(small)
    grad_log_v = 0.0 if grad_log is None else grad_log[...].astype(BF16).astype(F32)
    grad_y_v = grad_y[...] if grad_log is None else grad_y[...].astype(BF16).astype(F32)
    grad_after, grad_r_v, grad_mix_v, small_rows = moe_back(
        grad_y_v, grad_log_v, after[...], packed[...], slot_pair[...], ints[...], picked,
        blocks, r[...].astype(F32), small[...], mix[...], gain_second, vec_rows, dims,
    )
    grad_r[...] = grad_r_v
    grad_mix[...] = grad_mix_v
    rows = dims[4]
    mix_tile = 0.0
    if rows:
        mix_tile = jnp.concatenate([roll(grad_mix_v, AT_MIX)[:rows]] * (x.shape[1] // rows), axis=0)
    loading.wait()
    attention_back(
        grad_after, x[...].astype(F32), qkv, probs_att, attended, small_rows, mix_tile, w, gain_first,
        cosine[...], sine[...], grads, grad_qkv, grad_x, hooks,
    )


def shaped(shape, dtype):
    return jax.ShapeDtypeStruct(shape, dtype)


def call(kernel, identity, ins, outs, scratch, far, flops):
    groups = {name: value if isinstance(value, list) else None for name, value in scratch.items()}
    flat = []
    for value in scratch.values():
        flat += value if isinstance(value, list) else [value]

    def body(*refs):
        refs = list(refs)
        named = {name: refs.pop(0) for name in list(ins) + list(outs)}
        for name, group in groups.items():
            named[name] = refs.pop(0) if group is None else [refs.pop(0) for _ in group]
        kernel(types.SimpleNamespace(**named))

    def spaces(names):
        return [pl.BlockSpec(memory_space=pl.ANY if name in far else pltpu.VMEM) for name in names]

    got = pl.pallas_call(
        body,
        out_shape=list(outs.values()),
        in_specs=spaces(ins),
        out_specs=spaces(outs),
        scratch_shapes=flat,
        compiler_params=pltpu.CompilerParams(
            vmem_limit_bytes=VMEM_BYTES, collective_id=identity, has_side_effects=True
        ),
        cost_estimate=pl.CostEstimate(flops=flops, bytes_accessed=40 << 20, transcendentals=0),
    )(*ins.values())
    return types.SimpleNamespace(**dict(zip(outs, got)))


MESH = pl.DeviceIdType.MESH


class Exchange:
    def __init__(self, stream, sent, groups, partial, sibling_part, onward, pair_part, summed, result, sems):
        self.stream, self.sent, self.groups = stream, sent, groups
        self.partial, self.sibling_part, self.onward = partial, sibling_part, onward
        self.pair_part, self.summed, self.result = pair_part, summed, result
        (self.column_s, self.column_r, self.pair_s, self.pair_r, self.core_s, self.core_r, self.last_s, self.last_r,
         self.local_sem, self.back_s, self.back_r, self.far_s, self.far_r, self.over_s, self.over_r,
         self.home_s, self.home_r) = sems
        self.core, self.column, self.place = lax.axis_index("section"), lax.axis_index("expert"), lax.axis_index("shard")
        self.owners = lax.axis_size("expert")
        self.sibling = (1 - self.core, self.column, self.place)
        self.pair = (self.core, self.column, self.place + 1 - 2 * lax.rem(self.place, 2))

    def peer(self, column):
        return (self.core, column, self.place)

    def turn(self, by):
        return lax.rem(self.column + by + self.owners, self.owners)

    def to_column(self, by):
        return pltpu.make_async_remote_copy(
            self.sent.at[self.turn(by)], self.groups.at[0, self.column],
            self.column_s.at[self.stream, by], self.column_r.at[self.stream, by],
            device_id=self.peer(self.turn(by)), device_id_type=MESH,
        )

    def from_column(self, by):
        source = self.turn(-by)
        return pltpu.make_async_remote_copy(
            self.sent.at[source], self.groups.at[0, source],
            self.column_s.at[self.stream, by], self.column_r.at[self.stream, by],
            device_id=self.peer(source), device_id_type=MESH,
        )

    def own_block(self):
        return pltpu.make_async_copy(
            self.sent.at[self.column], self.groups.at[0, self.column], self.local_sem.at[self.stream]
        )

    def forward(self, by, here, there, device, send, recv):
        block = self.turn(-by)
        return pltpu.make_async_remote_copy(
            self.groups.at[here, block], self.groups.at[there, block],
            send.at[self.stream, by], recv.at[self.stream, by], device_id=device, device_id_type=MESH,
        )

    def to_pair(self, by):
        return self.forward(by, 0, 2, self.pair, self.pair_s, self.pair_r)

    def to_core(self, by):
        return self.forward(by, 0, 1, self.sibling, self.core_s, self.core_r)

    def to_core_last(self, by):
        return self.forward(by, 2, 3, self.sibling, self.last_s, self.last_r)

    def start(self):
        for by in range(1, self.owners):
            self.to_column(by).start()
        self.own_block().start()

    def spread(self):
        for by in range(self.owners):
            if by:
                self.from_column(by).wait_recv()
            else:
                self.own_block().wait()
            self.to_pair(by).start()
            self.to_core(by).start()

    def near_ready(self):
        for by in range(self.owners):
            self.to_core(by).wait_recv()

    def spread_far(self, bys):
        for by in bys:
            self.to_pair(by).wait_recv()
            self.to_core_last(by).start()

    def far_ready(self, bys):
        for by in bys:
            self.to_core_last(by).wait_recv()

    def finish_dispatch(self):
        for by in range(self.owners):
            if by:
                self.to_column(by).wait_send()
            self.to_pair(by).wait_send()
            self.to_core(by).wait_send()
            self.to_core_last(by).wait_send()

    def near_back(self):
        return pltpu.make_async_remote_copy(
            self.partial.at[1], self.sibling_part.at[0], self.back_s.at[self.stream], self.back_r.at[self.stream],
            device_id=self.sibling, device_id_type=MESH,
        )

    def far_back(self, by):
        block = self.turn(-by)
        return pltpu.make_async_remote_copy(
            self.partial.at[3, block], self.sibling_part.at[1, block],
            self.far_s.at[self.stream, by], self.far_r.at[self.stream, by],
            device_id=self.sibling, device_id_type=MESH,
        )

    def over_pair(self, by):
        block = self.turn(-by)
        return pltpu.make_async_remote_copy(
            self.onward.at[block], self.pair_part.at[block],
            self.over_s.at[self.stream, by], self.over_r.at[self.stream, by],
            device_id=self.pair, device_id_type=MESH,
        )

    def home(self, by):
        return pltpu.make_async_remote_copy(
            self.summed.at[self.turn(by)], self.result.at[self.column],
            self.home_s.at[self.stream, by], self.home_r.at[self.stream, by],
            device_id=self.peer(self.turn(by)), device_id_type=MESH,
        )

    def home_here(self, by):
        source = self.turn(-by)
        return pltpu.make_async_remote_copy(
            self.summed.at[source], self.result.at[source],
            self.home_s.at[self.stream, by], self.home_r.at[self.stream, by],
            device_id=self.peer(source), device_id_type=MESH,
        )

    def return_far(self, bys):
        for by in bys:
            block = self.turn(-by)
            self.far_back(by).wait_recv()
            total = self.partial[2, block].astype(F32) + self.sibling_part[1, block].astype(F32)
            self.onward[block] = total.astype(BF16)
            self.over_pair(by).start()

    def return_home(self, bys):
        for by in bys:
            block = self.turn(-by)
            near = self.partial[0, block].astype(F32) + self.sibling_part[0, block].astype(F32)
            self.over_pair(by).wait_recv()
            self.summed[block] = (near + self.pair_part[block].astype(F32)).astype(BF16)
            if by:
                self.home(self.owners - by).start()
            else:
                self.result[block] = self.summed[block]

    def near_arrived(self):
        self.near_back().wait_recv()

    def finish(self):
        for by in range(1, self.owners):
            self.home_here(by).wait_recv()
            self.home(by).wait_send()
        for by in range(self.owners):
            self.over_pair(by).wait_send()
            self.far_back(by).wait_send()
        self.near_back().wait_send()

    def steps(self):
        cut = self.owners // 2
        return [list(range(cut)), list(range(cut, self.owners))]

    def far(self, bys):
        return [(group, self.turn(-by)) for by in bys for group in (2, 3)]


def home_buffers(owners, room, width):
    block = (owners, room, width)
    return [pltpu.VMEM((4,) + block, BF16), pltpu.VMEM((2,) + block, BF16)] + [pltpu.VMEM(block, BF16)] * 3


def exchange_sems(streams, owners):
    dma = pltpu.SemaphoreType.DMA
    return [dma((streams, owners))] * 8 + [dma((streams,))] * 3 + [dma((streams, owners))] * 6


def near_rows(ref):
    groups, owners, room, width = ref.shape
    return ref[:2].reshape(2 * owners * room, width)


def put_near(ref, value, columns=slice(None)):
    groups, owners, room, _ = ref.shape
    ref[:2, :, :, columns] = value.astype(ref.dtype).reshape(2, owners, room, value.shape[1])


def rows_at(ref, picks, columns=slice(None)):
    return jnp.concatenate([ref[group, block, :, columns] for group, block in picks], axis=0)


def put_at(ref, picks, value, columns=slice(None)):
    room = ref.shape[2]
    for i, (group, block) in enumerate(picks):
        ref[group, block, :, columns] = value[i * room : (i + 1) * room].astype(ref.dtype)


def all_rows(ref):
    groups, owners, room, width = ref.shape
    return ref[...].reshape(groups * owners * room, width)


def chunks_of(w_out):
    for chunk in range(w_out.shape[0] // CHUNK):
        yield slice(2 * CHUNK * chunk, 2 * CHUNK * (chunk + 1)), slice(CHUNK * chunk, CHUNK * (chunk + 1))


def made_by(rows, w_in, w_out):
    total = 0.0
    for columns, units in chunks_of(w_out):
        both = mm(rows, w_in[:, columns])
        gate = both[:, :CHUNK]
        hidden = (gate * jax.nn.sigmoid(gate) * both[:, CHUNK:]).astype(BF16)
        total = total + mm(hidden, w_out[units])
    return total


def forward_again(rows, w_in, w_out, put_both, put_hidden):
    for columns, units in chunks_of(w_out):
        both = mm(rows, w_in[:, columns])
        gate = both[:, :CHUNK]
        put_both(both, columns)
        put_hidden(gate * jax.nn.sigmoid(gate) * both[:, CHUNK:], units)


def back_of(grad_rows, w_in, w_out, both_at, put_grad):
    total = 0.0
    for columns, units in chunks_of(w_out):
        both = both_at(columns).astype(F32)
        gate, up = both[:, :CHUNK], both[:, CHUNK:]
        sig = jax.nn.sigmoid(gate)
        grad_hidden = mm(grad_rows, w_out[units], NT)
        grad_gate = grad_hidden * up * sig * (1.0 + gate * (1.0 - sig))
        grad_both = jnp.concatenate([grad_gate, grad_hidden * gate * sig], axis=1).astype(BF16)
        put_grad(grad_both, columns)
        total = total + mm(grad_both, w_in[:, columns], NT)
    return total


def both_ways(rows, grad_rows, w_in, w_out, put_hidden, put_grad):
    made, back = 0.0, 0.0
    for columns, units in chunks_of(w_out):
        both = mm(rows, w_in[:, columns])
        gate, up = both[:, :CHUNK], both[:, CHUNK:]
        sig = jax.nn.sigmoid(gate)
        hidden = (gate * sig * up).astype(BF16)
        put_hidden(hidden, units)
        made = made + mm(hidden, w_out[units])
        grad_hidden = mm(grad_rows, w_out[units], NT)
        grad_gate = grad_hidden * up * sig * (1.0 + gate * (1.0 - sig))
        grad_both = jnp.concatenate([grad_gate, grad_hidden * gate * sig], axis=1).astype(BF16)
        put_grad(grad_both, columns)
        back = back + mm(grad_both, w_in[:, columns], NT)
    return made, back


def near_of(ref):
    return lambda value, columns: put_near(ref, value, columns)


def far_of(ref, picks):
    return lambda value, columns: put_at(ref, picks, value, columns)


def weight_grads_in(rows, grad_ref, grad_in):
    for chunk in range(grad_in.shape[1] // (2 * CHUNK)):
        columns = slice(2 * CHUNK * chunk, 2 * CHUNK * (chunk + 1))
        grads = grad_ref[:, :, :, columns].reshape(rows.shape[0], 2 * CHUNK)
        grad_in[:, columns] = mm(rows, grads, TN).astype(BF16)


def exchange_far(streams, work):
    first, then = streams[0].steps()
    for bys in (first, then):
        for one in streams:
            one.spread_far(bys)
        if bys is then:
            for one in streams:
                one.return_far(first)
        for one in streams:
            one.far_ready(bys)
        for one, value in zip(streams, work(streams[0].far(bys))):
            put_at(one.partial, one.far(bys), value)
            for by in bys:
                one.far_back(by).start()
    for one in streams:
        one.return_far(then)


class Spread:
    def __init__(self, wide, packed, in_pieces, out_pieces, attn, w_in, w_out, sems):
        self.wide = wide
        self.packed, self.in_pieces, self.out_pieces = packed, in_pieces, out_pieces
        self.attn, self.w_in, self.w_out = attn, w_in, w_out
        (self.own_sem, self.z_s, self.z_r, self.plane_s, self.plane_r, self.core_s, self.core_r,
         self.in_s, self.in_r, self.out_s, self.out_r, self.own_in, self.own_out) = sems
        self.core, self.column, self.place = lax.axis_index("section"), lax.axis_index("expert"), lax.axis_index("shard")
        self.owners, self.pieces = lax.axis_size("expert"), lax.axis_size("shard")

    def spot(self, column, place):
        rows = self.packed.shape[0]
        return pl.ds(pl.multiple_of((column * self.pieces + place) * rows, rows), rows)

    def column_by(self, by):
        return lax.rem(self.column + by + self.owners, self.owners)

    def place_by(self, by):
        return lax.rem(self.place + by + self.pieces, self.pieces)

    def copy(self, source, target, send, recv, device):
        return pltpu.make_async_remote_copy(source, target, send, recv, device_id=device, device_id_type=MESH)

    def own(self):
        return pltpu.make_async_copy(self.packed, self.attn.at[self.core, self.spot(self.column, self.place)], self.own_sem)

    def along(self, back, way):
        block = self.attn.at[self.core, self.spot(self.column, self.place_by(-back))]
        there = back + 1 if way else (back - 1) % self.pieces
        return self.copy(
            self.packed if back == 0 else block, block, self.z_s.at[way, back], self.z_r.at[there],
            (self.core, self.column, self.place_by(1 if way else -1)),
        )

    def hand_on(self, back, action):
        if back < self.pieces - 1:

            @pl.when((self.place >= back) & (self.place < self.pieces - 1))
            def _():
                action(self.along(back, 1))

        if back != 1:

            @pl.when((self.place > 0) if back == 0 else (self.place > 0) & (self.place < back))
            def _():
                action(self.along(back, 0))

    def along_in(self, back):
        block = self.attn.at[self.core, self.spot(self.column, self.place_by(-back))]
        return self.copy(
            block, block, self.z_s.at[1, back], self.z_r.at[back], (self.core, self.column, self.place_by(-1))
        )

    def plane(self, back, by):
        block = self.attn.at[self.core, self.spot(self.column, self.place_by(-back))]
        source = self.packed if back == 0 else block
        return self.copy(
            source, block, self.plane_s.at[back, by], self.plane_r.at[back, by], (self.core, self.column_by(by), self.place)
        )

    def plane_in(self, back, by):
        block = self.attn.at[self.core, self.spot(self.column_by(-by), self.place_by(-back))]
        return self.copy(
            block, block, self.plane_s.at[back, by], self.plane_r.at[back, by], (self.core, self.column_by(-by), self.place)
        )

    def over(self, back, by, section):
        block = self.attn.at[section, self.spot(self.column_by(-by), self.place_by(-back))]
        source = self.packed if back == 0 and by == 0 else block
        return self.copy(
            source, block, self.core_s.at[back, by], self.core_r.at[back, by], (1 - self.core, self.column, self.place)
        )

    def begin(self):
        self.own().start()
        self.hand_on(0, lambda copy: copy.start())
        for by in range(1, self.owners):
            self.plane(0, by).start()
        self.over(0, 0, self.core).start()

    def pass_on(self):
        def arrived(back):
            self.along_in(back).wait_recv()
            self.hand_on(back, lambda copy: copy.start())
            for by in range(1, self.owners):
                self.plane(back, by).start()
            self.over(back, 0, self.core).start()

        for far in range(1, self.pieces):

            @pl.when(self.place >= far)
            def _():
                arrived(far)

            @pl.when(self.place + far < self.pieces)
            def _():
                arrived(self.pieces - far)

    def pass_over(self):
        for back in range(self.pieces):
            for by in range(1, self.owners):
                self.plane_in(back, by).wait_recv()
                self.over(back, by, self.core).start()
        self.own().wait()

    def over_ready(self):
        for back in range(self.pieces):
            for by in range(self.owners):
                self.over(back, by, 1 - self.core).wait_recv()

    def finish_attn(self):
        for back in range(self.pieces):
            self.hand_on(back, lambda copy: copy.wait_send())
        for back in range(self.pieces):
            for by in range(1, self.owners):
                self.plane(back, by).wait_send()
            for by in range(self.owners):
                self.over(back, by, self.core).wait_send()

    def in_rows(self, place):
        rows = self.w_in.shape[1] // self.pieces
        return pl.ds(pl.multiple_of(place * rows, rows), rows)

    def out_rows(self, place):
        rows = self.out_pieces.shape[1]
        return pl.ds(pl.multiple_of(lax.div(place, 2) * rows, rows), rows)

    def parts(self, core, place, section, rows):
        if not self.wide:
            return [(self.in_pieces.at[core, lax.rem(place, 2)], self.w_in.at[section, rows])]
        hidden = self.in_pieces.shape[1] // 2
        half = self.out_pieces.shape[1]
        pairs = []
        for pair in range(self.pieces // 2):
            for side in range(2):
                for ahead in range(0, half, CHUNK):
                    at = side * hidden + (2 * pair + lax.rem(place, 2)) * 2 * half + core * half + ahead
                    to = 2 * (pair * half + ahead) + side * CHUNK
                    pairs.append((
                        self.in_pieces.at[:, pl.ds(pl.multiple_of(at, CHUNK), CHUNK)],
                        self.w_in.at[section, rows, pl.ds(to, CHUNK)],
                    ))
        return pairs

    def in_copies(self, cross, by):
        core = 1 - self.core if cross else self.core
        place = self.place_by(by)
        return [
            self.copy(source, target, self.in_s.at[cross, by, i], self.in_r.at[cross, by, i], (core, self.column, place))
            for i, (source, target) in enumerate(self.parts(core, place, self.core, self.in_rows(self.place)))
        ]

    def in_here(self, cross, by):
        core = 1 - self.core if cross else self.core
        place = self.place_by(-by)
        return [
            self.copy(source, target, self.in_s.at[cross, by, i], self.in_r.at[cross, by, i], (core, self.column, place))
            for i, (source, target) in enumerate(self.parts(self.core, self.place, core, self.in_rows(place)))
        ]

    def out_copy(self, cross, by):
        core = 1 - self.core if cross else self.core
        return self.copy(
            self.out_pieces.at[core], self.w_out.at[self.core, self.out_rows(self.place)],
            self.out_s.at[cross, by // 2], self.out_r.at[cross, by // 2], (core, self.column, self.place_by(by)),
        )

    def out_here(self, cross, by):
        core = 1 - self.core if cross else self.core
        place = self.place_by(-by)
        return self.copy(
            self.out_pieces.at[core], self.w_out.at[core, self.out_rows(place)],
            self.out_s.at[cross, by // 2], self.out_r.at[cross, by // 2], (core, self.column, place),
        )

    def own_pieces(self):
        copies = [
            pltpu.make_async_copy(source, target, self.own_in.at[i])
            for i, (source, target) in enumerate(self.parts(self.core, self.place, self.core, self.in_rows(self.place)))
        ]
        return copies + [
            pltpu.make_async_copy(
                self.out_pieces.at[self.core], self.w_out.at[self.core, self.out_rows(self.place)], self.own_out
            )
        ]

    def expert_routes(self):
        for by in range(self.pieces):
            for cross in (0, 1):
                if by or cross:
                    yield cross, by

    def begin_experts(self, evens=(0, 1)):
        if 1 in evens:
            for one in self.own_pieces():
                one.start()
        for cross, by in self.expert_routes():
            if (by + 1) % 2 not in evens:
                continue
            for one in self.in_copies(cross, by):
                one.start()
            if by % 2 == 0:
                self.out_copy(cross, by).start()

    def experts_ready(self, cross):
        for way, by in self.expert_routes():
            if way == cross:
                for one in self.in_here(cross, by):
                    one.wait_recv()
                if by % 2 == 0:
                    self.out_here(cross, by).wait_recv()
        if not cross:
            for one in self.own_pieces():
                one.wait()

    def finish_experts(self):
        for cross, by in self.expert_routes():
            for one in self.in_copies(cross, by):
                one.wait_send()
            if by % 2 == 0:
                self.out_copy(cross, by).wait_send()


def spread_scratch(owners, pieces, parts):
    dma = pltpu.SemaphoreType.DMA
    return [dma, dma((2, pieces)), dma((pieces,))] + [dma((pieces, owners))] * 4 + [
        dma((2, pieces, parts)), dma((2, pieces, parts)), dma((2, pieces // 2)), dma((2, pieces // 2)), dma((parts,)), dma,
    ]


def place_of():
    return lax.axis_index("section"), lax.axis_index("expert"), lax.axis_index("shard")


def remote(source, target, send, recv, device):
    return pltpu.make_async_remote_copy(source, target, send, recv, device_id=device, device_id_type=MESH)


class ExpertSum:
    def __init__(self, grad_in, grad_out, got_even, got_odd, got_out, sems):
        self.grad_in, self.grad_out = grad_in, grad_out
        self.got_even, self.got_odd, self.got_out = got_even, got_odd, got_out
        self.in_s, self.in_r, self.out_s, self.out_r = sems
        self.core, self.column, self.place = place_of()
        self.pieces = lax.axis_size("shard")

    def place_by(self, by):
        return lax.rem(self.place + by + self.pieces, self.pieces)

    def in_rows(self, place):
        rows = self.grad_in.shape[0] // self.pieces
        return pl.ds(pl.multiple_of(place * rows, rows), rows)

    def out_rows(self, place):
        rows = self.grad_out.shape[0] // (self.pieces // 2)
        return pl.ds(pl.multiple_of(lax.div(place, 2) * rows, rows), rows)

    def in_copy(self, by, way):
        place = self.place_by(way * by)
        target = self.got_even.at[by // 2 - 1] if by % 2 == 0 else self.got_odd.at[by // 2]
        return remote(
            self.grad_in.at[self.in_rows(place)], target, self.in_s.at[by - 1], self.in_r.at[by - 1],
            (self.core, self.column, place),
        )

    def out_copy(self, by, way):
        place = self.place_by(way * by)
        at = by // 2 - 1
        return remote(
            self.grad_out.at[self.out_rows(place)], self.got_out.at[at], self.out_s.at[at], self.out_r.at[at],
            (self.core, self.column, place),
        )

    def even(self, way=1):
        return [self.in_copy(by, way) for by in range(2, self.pieces, 2)]

    def odd(self, way=1):
        copies = [self.in_copy(by, way) for by in range(1, self.pieces, 2)]
        return copies + [self.out_copy(by, way) for by in range(2, self.pieces, 2)]


def start_all(copies):
    for one in copies:
        one.start()


def wait_all(sent, arriving):
    for one in arriving:
        one.wait_recv()
    for one in sent:
        one.wait_send()


def expert_sum_sems(pieces):
    dma = pltpu.SemaphoreType.DMA
    return [dma((pieces - 1,)), dma((pieces - 1,)), dma((max(pieces // 2 - 1, 1),)), dma((max(pieces // 2 - 1, 1),))]


def got_shapes(pieces, in_rows, columns, out_rows, width):
    spare = max(pieces // 2 - 1, 1)
    return (
        shaped((spare, in_rows, columns), BF16), shaped((pieces // 2, in_rows, columns), BF16),
        shaped((spare, out_rows, width), BF16),
    )


def greet_these(devices):
    barrier = pltpu.get_barrier_semaphore()
    for device in devices:
        pl.semaphore_signal(barrier, inc=1, device_id=device, device_id_type=MESH)
    pl.semaphore_wait(barrier, len(devices))


def along_z():
    core, column, place = place_of()
    pieces = lax.axis_size("shard")
    return [(core, column, lax.rem(place + by, pieces)) for by in range(1, pieces)]


def in_plane():
    core, column, place = place_of()
    owners = lax.axis_size("expert")
    return [(core, lax.rem(column + by, owners), place) for by in range(1, owners)]


def other_core():
    core, column, place = place_of()
    return [(1 - core, column, place)]


def load_weights(attn, section, w, small, sems):
    width = w.shape[0]
    first = pltpu.make_async_copy(attn.at[section, :, pl.ds(4 * width, LANES)], small, sems.at[0])
    then = pltpu.make_async_copy(attn.at[section], w, sems.at[1])
    first.start()
    then.start()
    first.wait()
    return then


class AttnSum:
    def __init__(self, grads, buffers, sems):
        self.grads = grads
        self.from_core, self.summed, self.from_plane, self.through, self.from_z = buffers
        self.core_s, self.core_r, self.plane_s, self.plane_r, self.z_s, self.z_r = sems
        self.core, self.column, self.place = place_of()
        self.owners, self.pieces = lax.axis_size("expert"), lax.axis_size("shard")

    def block(self, column, k, core):
        rows = self.summed.shape[2]
        return pl.ds(pl.multiple_of((column * self.pieces + 2 * k + core) * rows, rows), rows)

    def each(self):
        return [(column, k) for column in range(self.owners) for k in range(self.pieces // 2)]

    def to_core(self, column, k):
        return remote(
            self.grads.at[self.block(column, k, 1 - self.core)], self.from_core.at[column, k], self.core_s.at[column, k],
            self.core_r.at[column, k], (1 - self.core, self.column, self.place),
        )

    def to_plane(self, by, way=1):
        column = lax.rem(self.column + way * by + self.owners, self.owners)
        return remote(
            self.summed.at[column], self.from_plane.at[by - 1], self.plane_s.at[by - 1], self.plane_r.at[by - 1],
            (self.core, column, self.place),
        )

    def place_by(self, by):
        return lax.rem(self.place + by + self.pieces, self.pieces)

    def along(self, by, way=1):
        place = self.place_by(way * by)
        return remote(
            self.through.at[lax.div(place, 2)], self.from_z.at[by - 1], self.z_s.at[by - 1], self.z_r.at[by - 1],
            (self.core, self.column, place),
        )

    def holds(self, place):
        return lax.rem(place, 2) == self.core

    def start(self):
        for column, k in self.each():
            self.to_core(column, k).start()

    def add_cores(self):
        for column, k in self.each():
            self.to_core(column, k).wait_recv()
        for column, k in self.each():
            own = self.grads[self.block(column, k, self.core), :]
            self.summed[column, k] = (own.astype(F32) + self.from_core[column, k].astype(F32)).astype(BF16)
        for by in range(1, self.owners):
            self.to_plane(by).start()

    def plane_ready(self):
        for by in range(1, self.owners):
            self.to_plane(by, -1).wait_recv()

    def add_plane(self):
        total = self.summed[self.column].astype(F32)
        for by in range(1, self.owners):
            total = total + self.from_plane[by - 1].astype(F32)
        self.through[...] = total.astype(BF16)
        for by in range(1, self.pieces):

            @pl.when(self.holds(self.place_by(by)))
            def _():
                self.along(by).start()

    def z_ready(self):
        @pl.when(self.holds(self.place))
        def _():
            for by in range(1, self.pieces):
                self.along(by, -1).wait_recv()

    def add_z(self, target):
        @pl.when(self.holds(self.place))
        def _():
            total = self.through[lax.div(self.place, 2)].astype(F32)
            for by in range(1, self.pieces):
                total = total + self.from_z[by - 1].astype(F32)
            target[...] = total

    def finish_near(self):
        for column, k in self.each():
            self.to_core(column, k).wait_send()
        for by in range(1, self.owners):
            self.to_plane(by).wait_send()

    def finish_z(self):
        for by in range(1, self.pieces):

            @pl.when(self.holds(self.place_by(by)))
            def _():
                self.along(by).wait_send()


def attn_sum_scratch(owners, pieces, rows, columns):
    blocks = (owners, pieces // 2, rows, columns)
    dma = pltpu.SemaphoreType.DMA
    return [
        pltpu.VMEM(blocks, BF16), pltpu.VMEM(blocks, BF16), pltpu.VMEM((owners - 1,) + blocks[1:], BF16),
        pltpu.VMEM(blocks[1:], BF16), pltpu.VMEM((pieces - 1,) + blocks[2:], BF16),
    ], [dma(blocks[:2])] * 2 + [dma((owners - 1,))] * 2 + [dma((pieces - 1,))] * 2


def column_devices():
    core, column, place = place_of()
    pieces = lax.axis_size("shard")
    return [
        (one, column, lax.rem(place + by, pieces))
        for by in range(pieces)
        for one in (core, 1 - core)
    ][1:]


def column_of(row):
    return jnp.broadcast_to(row.astype(F32), (LANES, row.shape[1])).T[:, :1]


def tables_of(seg_row, cosine, sine):
    seq_len = seg_row.shape[1]
    seg_col = column_of(seg_row).astype(jnp.int32)
    start = jnp.sum(jnp.where(seg_row < seg_col, 1.0, 0.0), axis=1, keepdims=True)
    place = lax.broadcasted_iota(jnp.int32, (seq_len, LANES), 0).astype(F32)
    lane = lane_of(seq_len)
    rate = jnp.exp((lane % (HEAD // 2)).astype(F32) * (-2.0 * math.log(10000.0) / HEAD))
    angles = (place - start) * rate
    cosine[...] = jnp.cos(angles)
    sine[...] = jnp.where(lane % HEAD < HEAD // 2, -jnp.sin(angles), jnp.sin(angles))
    return seg_col


def front_kernel(dims, inside, wide, n):
    width = n.x_in.shape[2]
    core, column, place = place_of()
    nexp, owners = dims[1], lax.axis_size("expert")
    packed_w = n.packed_w
    if inside:
        packed_w[:, : 3 * width] = n.w_qkv[...]
        packed_w[:, 3 * width : 4 * width] = n.w_attn[...]
        rows = packed_w.shape[0]
        n.turning[...] = jnp.zeros(n.turning.shape, F32)
        for array, at in ((n.router, 0), (n.const_proj, AT_PROJ), (n.const_vec, AT_VEC), (n.gains, AT_GAIN)):
            n.turning[at : at + array.shape[0], :rows] = array[...].astype(F32)
        packed_w[:, 4 * width :] = n.turning[:, :LANES].T[:rows].astype(BF16)
    spread = Spread(wide, packed_w, n.in_pieces, n.w_out_here, n.attn if inside else None, n.w_in, n.w_out, n.spread_sems)
    first, second = core == 0, core == 1
    tokens = Exchange(0, n.buffer_0, n.arrived, *n.token_home, n.made, n.sems)
    tokens_1 = Exchange(1, n.buffer_0, n.groups_1, *n.token_home, n.made, n.sems)
    grads_1 = Exchange(2, n.buffer_2, n.groups_2, *n.grad_home, n.returned, n.sems)
    greet_these(column_devices() + in_plane())

    @pl.when(first)
    def _():
        if inside:
            spread.begin()

    sibling = (1 - core, column, place)
    n.mix_own[...] = jnp.zeros(n.mix_own.shape, F32)
    n.mix_own[:nexp, :nexp] = n.gate_mix[...]
    crossing = [
        remote(n.routes.at[1 - core], n.routes_all.at[core], n.cross_s.at[0], n.cross_r.at[0], sibling),
        remote(n.priority.at[1 - core], n.prio.at[core], n.cross_s.at[1], n.cross_r.at[1], sibling),
        remote(n.mix_own, n.mix.at[core], n.cross_s.at[2], n.cross_r.at[2], sibling),
    ]
    arriving = [
        remote(n.routes.at[core], n.routes_all.at[1 - core], n.cross_s.at[0], n.cross_r.at[0], sibling),
        remote(n.priority.at[core], n.prio.at[1 - core], n.cross_s.at[1], n.cross_r.at[1], sibling),
        remote(n.mix_own, n.mix.at[1 - core], n.cross_s.at[2], n.cross_r.at[2], sibling),
    ]
    start_all(crossing)
    bring = [
        pltpu.make_async_copy(n.x_in.at[core], n.x, n.bring_sems.at[0]),
        pltpu.make_async_copy(n.cotangent.at[core], n.upstream, n.bring_sems.at[1]),
    ]
    attn = (n.attn.at[0], n.attn.at[1])
    if not inside:
        attn = (n.attn_here, n.attn_here)
        loads = [pltpu.make_async_copy(n.attn.at[section], n.attn_here, n.bring_sems.at[2]) for section in range(2)]
        bring.append(loads[0])
    start_all(bring)
    seg_row = n.segments[core]
    seg_col = tables_of(seg_row, n.cosine, n.sine)
    n.routes_all[core] = n.routes[core]
    n.prio[core] = n.priority[core]
    n.mix[core] = n.mix_own[...]
    n.turning[...] = jnp.zeros(n.turning.shape, F32)
    n.turning[:nexp, :] = n.gate_prev[core].astype(F32)
    n.r[...] = n.turning[...].T.astype(BF16)
    wait_all(crossing, arriving)
    lane = lane_of(n.ints.shape[1])
    for section in range(2):
        routes = n.routes_all[section]
        first_route, second_route = (column_of(routes[k : k + 1]).astype(jnp.int32) for k in range(TOP))
        n.ints[section] = jnp.where(lane == 0, first_route, second_route)
    for one in bring:
        one.wait()

    @pl.when(first)
    def _():
        if inside:
            spread.pass_on()
        spread.begin_experts()
        if inside:
            spread.pass_over()

    @pl.when(second)
    def _():
        if inside:
            spread.over_ready()

    keep = [
        pltpu.make_async_copy(source, target, n.keep_sems.at[section, i])
        for section, targets in enumerate(((n.qkv_0, n.probs_0), (n.qkv_1, n.probs_1)))
        for i, (source, target) in enumerate(zip((n.qkv_here, n.probs_here), targets))
    ]
    leaving = [pltpu.make_async_copy(n.w_in.at[0], n.w_in_kept, n.leave_sems.at[0]),
               pltpu.make_async_copy(n.w_out.at[0], n.w_out_kept, n.leave_sems.at[1])]
    if inside:
        leaving += [
            pltpu.make_async_copy(n.attn.at[section], n.attn_kept.at[section], n.leave_sems.at[2 + section])
            for section in range(2)
        ]
    n.small[0] = attn[0][:, 4 * width :]
    attend_kernel(
        dims, n.x, n.r, attn[0], n.small.at[0], n.mix.at[0], n.cosine, n.sine, seg_col, seg_row,
        n.ints.at[0], n.prio.at[0],
        n.after_0, n.qkv_here, n.probs_here, n.attended_0, n.packed_0, n.slots_0, n.r_next, n.buffer_0,
    )
    tokens.start()
    start_all(keep[:2])
    if not inside:
        loads[1].start()

    @pl.when(second)
    def _():
        if inside:
            spread.begin()

    tokens.spread()

    @pl.when(first)
    def _():
        spread.experts_ready(0)

    @pl.when(second)
    def _():
        if inside:
            spread.pass_on()
        spread.experts_ready(1)
        spread.begin_experts((1,))

    tokens.near_ready()
    put_near(tokens.partial, made_by(near_rows(tokens.groups), n.w_in.at[0], n.w_out.at[0]))
    tokens.near_back().start()
    exchange_far([tokens], lambda picks: [made_by(rows_at(tokens.groups, picks), n.w_in.at[0], n.w_out.at[0])])

    @pl.when(second)
    def _():
        if inside:
            spread.pass_over()
        spread.begin_experts((0,))

    tokens.near_arrived()
    tokens.return_home(range(owners))
    tokens.finish_dispatch()
    tokens.finish()
    if inside:

        @pl.when(first)
        def _():
            spread.over_ready()

    if not inside:
        loads[1].wait()
    n.small[1] = attn[1][:, 4 * width :]
    for one in keep[:2]:
        one.wait()
    middle_kernel(
        dims, n.after_0, n.packed_0, n.slots_0, n.ints.at[0], tokens.result, n.small.at[0],
        n.r_next, attn[1], n.small.at[1], n.mix.at[1], n.cosine, n.sine, seg_col, seg_row,
        n.ints.at[1], n.prio.at[1], n.upstream,
        n.out_0, n.picked_0, n.after_1, n.qkv_here, n.probs_here, n.attended_1, n.packed_1, n.slots_1, n.buffer_0, n.buffer_2,
    )
    start_all(keep[2:])
    both = (tokens_1, grads_1)
    for one in both:
        one.start()
    for one in both:
        one.spread()

    @pl.when(first)
    def _():
        spread.experts_ready(1)

    @pl.when(second)
    def _():
        spread.experts_ready(0)

    w_in, w_out = n.w_in.at[1], n.w_out.at[1]
    start_all(leaving)
    for one in both:
        one.near_ready()
    parts = both_ways(
        near_rows(tokens_1.groups), near_rows(grads_1.groups), w_in, w_out, near_of(n.hidden), near_of(n.grad_both)
    )
    for one, part in zip(both, parts):
        put_near(one.partial, part)
        one.near_back().start()
    exchange_far(
        both,
        lambda picks: both_ways(
            rows_at(tokens_1.groups, picks), rows_at(grads_1.groups, picks), w_in, w_out,
            far_of(n.hidden, picks), far_of(n.grad_both, picks),
        ),
    )
    n.grad_out[...] = mm(all_rows(n.hidden), all_rows(grads_1.groups), TN).astype(BF16)
    for one in both:
        one.near_arrived()
        one.return_home(range(owners))
    weight_grads_in(all_rows(tokens_1.groups), n.grad_both, n.grad_in)
    for one in both:
        one.finish_dispatch()
        one.finish()
    for one in keep[2:] + leaving:
        one.wait()
    if inside:
        spread.finish_attn()
    spread.finish_experts()


def turn_kernel(dims, inside, n):
    sums = ExpertSum(n.grad_in_1, n.grad_out_1, n.even, n.odd, n.got_out, n.sum_sems)
    loading = load_weights(n.attn, 1, n.w, n.small, n.load_sems)
    expert_loads = [
        pltpu.make_async_copy(n.w_in_all, n.w_in, n.load_sems.at[2]),
        pltpu.make_async_copy(n.w_out_all, n.w_out, n.load_sems.at[3]),
    ]
    start_all(expert_loads)
    grads = Exchange(0, n.buffer, n.groups, *n.home, n.blocks_back, n.sems)
    attn = []
    if inside:
        attn = [AttnSum(n.grads_a, n.attn_buffers_a, n.attn_sems_a), AttnSum(n.grads_b, n.attn_buffers_b, n.attn_sems_b)]
    greet_these(other_core() + along_z() + in_plane())
    start_all(sums.even())
    _, gain_second, vec_rows = small_rows_of(n.small)
    n.out[...] = combine(
        n.after[...], n.packed[...], n.slots[...], n.ints[1], n.made, gain_second, vec_rows, dims, n.picked
    ).astype(BF16)

    def rows_done():
        give_back(n.grad_x[...].astype(BF16).astype(F32), n.packed_0[...], n.slots_0[...], dims, n.buffer)
        grads.start()

    hooks = types.SimpleNamespace(
        early=False, rows_done=rows_done, first_done=lambda: [one.start() for one in attn[:1]],
        second_done=lambda: [one.start() for one in attn[1:]],
    )
    back_body(
        dims, n.upstream, None, n.after, n.packed, n.slots, n.ints.at[1], n.picked, n.returned, n.r, n.w, n.small, n.mix.at[1],
        n.x, n.qkv, n.probs, n.attended, n.cosine, n.sine, n.grad_x, n.grad_r, n.grad_mix, (n.grads_a, n.grads_b),
        n.grad_qkv, loading, hooks,
    )
    for one in expert_loads:
        one.wait()
    forward_again(near_rows(n.arrived), n.w_in, n.w_out, near_of(n.both), near_of(n.hidden))
    grads.spread()
    start_all(sums.odd())
    for one in attn:
        one.add_cores()
    grads.near_ready()

    def near_both(columns):
        return n.both[:2, :, :, columns].reshape(near_count, 2 * CHUNK)

    near_count = n.both.shape[0] // 2 * n.both.shape[1] * n.both.shape[2]
    put_near(
        grads.partial, back_of(near_rows(grads.groups), n.w_in, n.w_out, near_both, near_of(n.grad_both))
    )
    grads.near_back().start()
    for bys in grads.steps():
        picks = grads.far(bys)
        forward_again(
            rows_at(n.arrived, picks), n.w_in, n.w_out, far_of(n.both, picks), far_of(n.hidden, picks)
        )
    exchange_far(
        [grads],
        lambda picks: [back_of(
            rows_at(grads.groups, picks), n.w_in, n.w_out, lambda columns: rows_at(n.both, picks, columns),
            far_of(n.grad_both, picks),
        )],
    )
    n.grad_out_0[...] = mm(all_rows(n.hidden), all_rows(grads.groups), TN).astype(BF16)
    for one in attn:
        one.plane_ready()
        one.add_plane()
    grads.near_arrived()
    grads.return_home(range(grads.owners))
    weight_grads_in(all_rows(n.arrived), n.grad_both, n.grad_in_0)
    grads.finish_dispatch()
    grads.finish()
    for one, target in zip(attn, (n.attn_sum_a, n.attn_sum_b)):
        one.finish_near()
        one.z_ready()
        one.add_z(target)
        one.finish_z()
    wait_all(sums.even() + sums.odd(), sums.even(-1) + sums.odd(-1))


def spread_columns(target, halves_at, hidden_here):
    rows, columns = target.shape
    hidden = columns // 2
    pieces = hidden // (2 * hidden_here)
    parity = lax.rem(lax.axis_index("shard"), 2)
    for first_parity in range(2):

        @pl.when(parity == first_parity)
        def _():
            for half in range(2):
                for q in range(2):
                    odd = first_parity if q == 0 else 1 - first_parity
                    for pair in range(pieces // 2):
                        for side in range(2):
                            for ahead in range(0, hidden_here, CHUNK):
                                at = side * hidden + (2 * pair + odd) * 2 * hidden_here + half * hidden_here + ahead
                                source = 2 * (pair * hidden_here + ahead) + side * CHUNK
                                target[:, at : at + CHUNK] = halves_at(half, q)[:, source : source + CHUNK].astype(F32)


def last_kernel(dims, inside, wide, n):
    core, column, place = place_of()
    pieces = lax.axis_size("shard")
    pair_count = pieces // 2
    (sibling,) = other_core()
    loading = load_weights(n.attn, 0, n.w, n.small, n.load_sems)
    sums = ExpertSum(n.grad_in_0, n.grad_out_0, n.even_0, n.odd_0, n.got_out_0, n.sum_sems)
    attn = []
    if inside:
        attn = [AttnSum(n.grads_a, n.attn_buffers_a, n.attn_sems_a), AttnSum(n.grads_b, n.attn_buffers_b, n.attn_sems_b)]
    greet_these(other_core() + along_z() + (in_plane() if inside else []))
    start_all(sums.even() + sums.odd())
    pairs = ((n.out_0, n.out_1, n.both_out), (n.grad_x_0, n.grad_x_1, n.both_x), (n.grad_r_0, n.grad_r_1, n.r_pair))

    def swaps(section):
        for i, (zero, one, both) in enumerate(pairs):
            own, other = (zero, one) if section == 0 else (one, zero)
            yield (
                remote(other, both.at[section], n.swap_s.at[i], n.swap_r.at[i], sibling),
                pltpu.make_async_copy(own, both.at[section], n.local_sem.at[i]),
            )

    def each_core(action):
        for section in range(2):

            @pl.when(core == section)
            def _():
                action(section)

    def add_experts(section, grad_in, grad_out, even, odd, got_out):
        rows, out_rows = even.shape[1], got_out.shape[1]
        own_in = grad_in[pl.ds(pl.multiple_of(place * rows, rows), rows), :]
        own_out = grad_out[pl.ds(pl.multiple_of(lax.div(place, 2) * out_rows, out_rows), out_rows), :]
        in_sum = [own_in.astype(F32), odd[0].astype(F32)]
        for i in range(pair_count - 1):
            in_sum[0] = in_sum[0] + even[i].astype(F32)
            in_sum[1] = in_sum[1] + odd[i + 1].astype(F32)
        out_sum = own_out.astype(F32)
        for i in range(pair_count - 1):
            out_sum = out_sum + got_out[i].astype(F32)

        @pl.when(core == section)
        def _():
            for q in range(2):
                n.in_mine[q] = in_sum[q]
            n.out_mine[...] = out_sum

        @pl.when(core != section)
        def _():
            for q in range(2):
                n.in_sent[q] = in_sum[q].astype(BF16)
            n.out_sent[...] = out_sum.astype(BF16)
            for one in finals:
                one.start()

    finals = [
        remote(n.in_sent, n.in_got, n.final_s.at[0], n.final_r.at[0], sibling),
        remote(n.out_sent, n.out_got, n.final_s.at[1], n.final_r.at[1], sibling),
    ]
    hooks = types.SimpleNamespace(
        early=True, first_done=lambda: [one.start() for one in attn[:1]],
        heads_done=lambda: [one.add_cores() for one in attn[:1]], second_done=lambda: [one.start() for one in attn[1:]],
    )
    back_body(
        dims, n.grad_x_1, n.grad_r_1, n.after, n.packed, n.slots, n.ints.at[0], n.picked, n.returned, n.r, n.w, n.small,
        n.mix.at[0], n.x, n.qkv, n.probs, n.attended, n.cosine, n.sine, n.grad_x_0, n.grad_r_0, n.grad_mix,
        (n.grads_a, n.grads_b), n.grad_qkv, loading, hooks,
    )

    @each_core
    def _(section):
        for away, here in swaps(section):
            away.start()
            here.start()

    for one in attn[1:]:
        one.add_cores()
    add_experts(1, n.grad_in_1, n.grad_out_1, n.even_1, n.odd_1, n.got_out_1)
    for one in attn:
        one.plane_ready()
        one.add_plane()
    wait_all(sums.even() + sums.odd(), sums.even(-1) + sums.odd(-1))
    add_experts(0, n.grad_in_0, n.grad_out_0, n.even_0, n.odd_0, n.got_out_0)
    for one in finals:
        one.wait()
    for half in range(2):

        @pl.when(core == half)
        def _():
            if wide:
                hidden_here = n.out_mine.shape[0]
                spread_columns(n.in_total, lambda at, q: n.in_mine[q] if at == half else n.in_got[q], hidden_here)
            else:
                for q in range(2):
                    n.in_total[half, q] = n.in_mine[q]
                    n.in_total[1 - half, q] = n.in_got[q].astype(F32)
            count = n.out_mine.shape[0]
            n.out_total[half * count : (half + 1) * count] = n.out_mine[...]
            n.out_total[(1 - half) * count : (2 - half) * count] = n.out_got[...].astype(F32)

    for i, (one, sum_0, sum_1, total) in enumerate(zip(
        attn, (n.attn_sum_0a, n.attn_sum_0b), (n.attn_sum_1a, n.attn_sum_1b), (n.attn_total_a, n.attn_total_b)
    )):
        one.z_ready()
        one.add_z(sum_0)
        holder = one.holds(place)
        for section in range(2):
            mine, other = (sum_0, sum_1) if section == 0 else (sum_1, sum_0)
            home = remote(other, total, n.final_s.at[2 + i], n.final_r.at[2 + i], sibling)

            @pl.when(holder & (core == section))
            def _():
                home.start()
                total[...] = mine[...]
                home.wait_send()

            @pl.when(jnp.logical_not(holder) & (core == section))
            def _():
                home.wait_recv()

    if inside:
        width = n.x.shape[1]
        half = width // LANES // 2 * LANES
        for batch, total in enumerate((n.attn_total_a, n.attn_total_b)):
            for part in range(3):
                at = part * width + batch * half
                n.qkv_total[:, at : at + half] = total[:, part * half : (part + 1) * half]
        n.attn_out_total[...] = n.attn_total_a[:, 3 * half :]
        small = n.attn_total_b[:, 3 * half :]
        nexp, rows = n.mix_total.shape[0], small.shape[0]
        n.mix_total[...] = small[:nexp, AT_MIX : AT_MIX + nexp]
        n.turning[...] = jnp.zeros(n.turning.shape, F32)
        n.turning[:rows] = small
        turned_small = n.turning[...].T
        for target, at in ((n.router_total, 0), (n.proj_total, AT_PROJ), (n.vec_total, AT_VEC), (n.gain_total, AT_GAIN)):
            target[...] = turned_small[at : at + target.shape[0], :rows]

    @each_core
    def _(section):
        for away, here in swaps(section):
            away.wait()
            here.wait()

    for batch in range(2):
        n.both_r[batch] = n.r_pair[batch].T[: n.both_r.shape[1]]

    for one in attn:
        one.finish_near()
        one.finish_z()


def local(
    x_in,
    cotangent,
    gate_prev,
    segments,
    routes,
    priority,
    attn_qkv,
    attn_out,
    router,
    const_proj,
    const_vec,
    gains,
    gate_mix,
    expert_in,
    expert_out,
):
    seq_len, width = x_in.shape[2:]
    nexp = gate_prev.shape[-1]
    owners, pieces = lax.axis_size("expert"), lax.axis_size("shard")
    nffn = owners * expert_in.shape[1]
    nconst = const_vec.shape[-1]
    capacity = (5 * TOP * seq_len + 4 * nexp - 1) // (4 * nexp)
    room = -(-capacity // 16) * 16
    slots = nffn * room
    core = lax.axis_index("section")
    first_core = core == 0
    in_rows, columns = expert_in.shape[2:]
    hidden_here = expert_out.shape[2] // 2
    pairs = pieces // 2
    quarter = pairs * hidden_here
    chunks = quarter // CHUNK
    rows = attn_qkv.shape[1]
    inside, wide = rows % 16 == 0, hidden_here % CHUNK == 0

    def swap(item):
        return lax.ppermute(item, "section", [(0, 1), (1, 0)])

    def by_section(own, other):
        return jnp.where(first_core, own, other), jnp.where(first_core, other, own)

    def as_chunks(half):
        half = jnp.moveaxis(half, 3, 0).reshape(2, in_rows, 2, chunks, CHUNK)
        return jnp.swapaxes(half, 2, 3).reshape(2, in_rows, 2 * quarter)

    w_out = expert_out[0, 0].reshape(2, hidden_here, width)
    in_pieces = expert_in[0, 0]
    if not wide:
        w_in = in_pieces.reshape(in_rows, 2, pairs, 2, 2, hidden_here)
        in_pieces = jnp.stack([as_chunks(w_in[:, :, :, :, half]) for half in range(2)])
    given = None
    if not inside:
        def lanes(array, upto):
            return jnp.pad(array, ((0, 0), (0, upto - array.shape[1])))

        small = [
            lanes(router[0], AT_PROJ), lanes(const_proj[0], AT_VEC - AT_PROJ), lanes(const_vec[0], AT_GAIN - AT_VEC),
            lanes(gains[0], LANES - AT_GAIN),
        ]
        shared = jnp.concatenate([attn_qkv[0], attn_out[0]] + small, axis=1)
        shared = lax.all_gather(shared, ("expert", "shard"), axis=0, tiled=True)
        given = jnp.stack(by_section(shared, swap(shared)))
    dims = (nffn, nexp, capacity, slots, rows if inside else 0)
    heads = width // HEAD
    blocks = (owners, room, width)
    token_f32 = shaped((seq_len, width), F32)
    token_b16 = shaped((seq_len, width), BF16)
    lanes_f32 = shaped((seq_len, LANES), F32)
    lanes_i32 = shaped((seq_len, LANES), jnp.int32)
    block_shape = shaped(blocks, BF16)
    attn_shape = shaped((width, 4 * width + LANES), BF16)
    attn_columns = attn_shape.shape[1]
    pair_shape = shaped((TOP, seq_len, width), BF16)
    in_shape, out_shape = shaped((width, 2 * quarter), BF16), shaped((quarter, width), BF16)
    dma = pltpu.SemaphoreType.DMA
    even, odd, got_out = got_shapes(pieces, in_rows, 2 * quarter, hidden_here, width)

    def vmem(shape):
        return pltpu.VMEM(shape.shape, shape.dtype)

    def attend_out(section):
        return {
            f"after_{section}": token_f32,
            f"qkv_{section}": shaped((seq_len, 3 * width), BF16),
            f"probs_{section}": shaped((heads, seq_len, seq_len), BF16),
            f"attended_{section}": token_b16,
            f"packed_{section}": lanes_f32,
            f"slots_{section}": lanes_i32,
        }

    ins = dict(
        in_pieces=in_pieces, w_out_here=w_out, x_in=x_in[:, 0], cotangent=cotangent[:, 0], gate_prev=jnp.swapaxes(gate_prev[:, 0], 1, 2),
        segments=segments, routes=jnp.swapaxes(routes[0, :, 0], 1, 2), priority=priority[0], gate_mix=gate_mix[0],
    )
    table_shapes = dict(
        mix=shaped((2, LANES, LANES), F32), cosine=lanes_f32, sine=lanes_f32, ints=shaped((2, seq_len, LANES), jnp.int32),
    )
    outs = dict(
        w_in_kept=in_shape, w_out_kept=out_shape, arrived=shaped((4,) + blocks, BF16), r_next=shaped((seq_len, LANES), BF16), out_0=token_b16, picked_0=pair_shape,
        made=block_shape, returned=block_shape, grad_in=in_shape, grad_out=out_shape, **attend_out(0), **attend_out(1),
        x=token_b16, r=shaped((seq_len, LANES), BF16), upstream=token_f32, **table_shapes,
    )
    if inside:
        outs["attn_kept"] = shaped((2,) + attn_shape.shape, BF16)
        ins = dict(
            ins, w_qkv=attn_qkv[0], w_attn=attn_out[0], router=router[0].T, const_proj=const_proj[0].T,
            const_vec=const_vec[0].T, gains=gains[0].T,
        )
    else:
        ins["attn"] = given
    f = call(
        lambda n: front_kernel(dims, inside, wide, n), 0, ins, outs,
        dict(
            small=pltpu.VMEM((2, width, LANES), BF16), buffer_0=vmem(block_shape),
            buffer_2=vmem(block_shape), groups_1=pltpu.VMEM((4,) + blocks, BF16), groups_2=pltpu.VMEM((4,) + blocks, BF16),
            token_home=home_buffers(*blocks), grad_home=home_buffers(*blocks), sems=exchange_sems(3, owners),
            spread_sems=spread_scratch(owners, pieces, 2 * pairs * max(hidden_here // CHUNK, 1) if wide else 1),
            packed_w=pltpu.VMEM((rows, 4 * width + LANES), BF16), mix_own=pltpu.VMEM((LANES, LANES), F32),
            prio=pltpu.VMEM((2, 1, seq_len), jnp.int32), cross_s=dma((3,)), cross_r=dma((3,)), bring_sems=dma((3,)),
            qkv_here=pltpu.VMEM((seq_len, 3 * width), BF16), probs_here=pltpu.VMEM((heads, seq_len, seq_len), BF16),
            keep_sems=dma((2, 2)), leave_sems=dma((4,)),
            w_in=pltpu.VMEM((2, width, 2 * quarter), BF16), w_out=pltpu.VMEM((2, quarter, width), BF16),
            **(dict(attn=pltpu.VMEM((2,) + attn_shape.shape, BF16)) if inside else dict(attn_here=vmem(attn_shape))), turning=pltpu.VMEM((LANES, seq_len), F32), routes_all=pltpu.VMEM((2, TOP, seq_len), jnp.int32),
            hidden=pltpu.VMEM((4,) + blocks[:2] + (quarter,), BF16), grad_both=pltpu.VMEM((4,) + blocks[:2] + (2 * quarter,), BF16),
        ),
        ("in_pieces", "w_out_here", "x_in", "cotangent", "qkv_0", "probs_0", "qkv_1", "probs_1")
        + ("w_in_kept", "w_out_kept", "attn_kept" if inside else "attn"), 8 << 30,
    )
    tables = dict(mix=f.mix, cosine=f.cosine, sine=f.sine, ints=f.ints)
    attn_all = f.attn_kept if inside else given
    scratch = dict(
        w=vmem(attn_shape), small=pltpu.VMEM((width, LANES), BF16), load_sems=dma((4,)), grad_qkv=pltpu.VMEM((seq_len, 3 * width), BF16),
        sum_sems=expert_sum_sems(pieces),
    )
    attn_scratch = {}
    half = width // LANES // 2 * LANES
    batches = dict(a=3 * half + width, b=3 * half + LANES)
    block_sums = {name: shaped((rows, lanes) if inside else (8, LANES), F32) for name, lanes in batches.items()}
    grad_shapes = {f"grads_{name}": shaped((width, lanes), BF16) for name, lanes in batches.items()}
    if inside:
        for name, lanes in batches.items():
            buffers, sems = attn_sum_scratch(owners, pieces, rows, lanes)
            attn_scratch.update({f"attn_buffers_{name}": buffers, f"attn_sems_{name}": sems})
    outs = dict(
        out=token_b16, grad_x=token_f32, grad_r=lanes_f32, grad_mix=shaped((LANES, LANES), F32), even=even, odd=odd,
        got_out=got_out, grad_in_0=in_shape, grad_out_0=out_shape, blocks_back=block_shape,
        attn_sum_a=block_sums["a"], attn_sum_b=block_sums["b"],
    )
    more = {name: vmem(shape) for name, shape in grad_shapes.items()}
    if not inside:
        outs, more = dict(outs, **grad_shapes), {}
    t = call(
        lambda n: turn_kernel(dims, inside, n), 1,
        dict(
            attn=attn_all, w_in_all=f.w_in_kept, w_out_all=f.w_out_kept, grad_in_1=f.grad_in, grad_out_1=f.grad_out,
            upstream=f.upstream, after=f.after_1, packed=f.packed_1, slots=f.slots_1, made=f.made, returned=f.returned, r=f.r_next,
            x=f.out_0, qkv=f.qkv_1, probs=f.probs_1, attended=f.attended_1, packed_0=f.packed_0, slots_0=f.slots_0,
            arrived=f.arrived, **tables,
        ),
        outs,
        dict(
            picked=vmem(pair_shape), buffer=vmem(block_shape), groups=pltpu.VMEM((4,) + blocks, BF16), home=home_buffers(*blocks),
            sems=exchange_sems(1, owners), w_in=vmem(in_shape), w_out=vmem(out_shape),
            both=pltpu.VMEM((4,) + blocks[:2] + (2 * quarter,), F32 if slots <= 384 else BF16), hidden=pltpu.VMEM((4,) + blocks[:2] + (quarter,), BF16),
            grad_both=pltpu.VMEM((4,) + blocks[:2] + (2 * quarter,), BF16), **scratch, **attn_scratch, **more,
        ),
        ("attn", "w_in_all", "w_out_all", "grad_in_1", "grad_out_1"), 12 << 30,
    )
    in_total = shaped((in_rows, columns) if wide else (2, 2, in_rows, 2 * quarter), F32)
    half_in, half_out = (2, in_rows, 2 * quarter), (hidden_here, width)
    outs = dict(
        both_out=shaped((2, seq_len, width), BF16), both_x=shaped((2, seq_len, width), F32),
        both_r=shaped((2, nexp, seq_len), F32), in_total=in_total, out_total=shaped((2 * hidden_here, width), F32),
        grad_mix=shaped((LANES, LANES), F32),
    )
    if inside:
        narrow = dict(router_total=nexp, proj_total=const_proj.shape[2], vec_total=nconst, gain_total=2)
        outs = dict(
            outs, qkv_total=shaped((rows, 3 * width), F32), attn_out_total=shaped((rows, width), F32),
            mix_total=shaped((nexp, nexp), F32), **{name: shaped((lanes, rows), F32) for name, lanes in narrow.items()},
        )
    else:
        outs = dict(outs, **grad_shapes)
    z = call(
        lambda n: last_kernel(dims, inside, wide, n), 2,
        dict(
            attn=attn_all, grad_in_0=t.grad_in_0, grad_out_0=t.grad_out_0, grad_in_1=f.grad_in, grad_out_1=f.grad_out,
            even_1=t.even, odd_1=t.odd, got_out_1=t.got_out, attn_sum_1a=t.attn_sum_a, attn_sum_1b=t.attn_sum_b, out_0=f.out_0, out_1=t.out,
            grad_x_1=t.grad_x, grad_r_1=t.grad_r, after=f.after_0, packed=f.packed_0, slots=f.slots_0, picked=f.picked_0,
            returned=t.blocks_back, r=f.r, x=f.x, qkv=f.qkv_0, probs=f.probs_0, attended=f.attended_0, **tables,
        ),
        outs,
        dict(
            even_0=vmem(even), odd_0=vmem(odd), got_out_0=vmem(got_out), grad_x_0=vmem(token_f32), grad_r_0=vmem(lanes_f32),
            attn_sum_0a=vmem(block_sums["a"]), attn_sum_0b=vmem(block_sums["b"]), attn_total_a=vmem(block_sums["a"]),
            attn_total_b=vmem(block_sums["b"]), turning=pltpu.VMEM((LANES, LANES), F32), r_pair=pltpu.VMEM((2, seq_len, LANES), F32), in_mine=pltpu.VMEM(half_in, F32), out_mine=pltpu.VMEM(half_out, F32),
            in_sent=pltpu.VMEM(half_in, BF16), out_sent=pltpu.VMEM(half_out, BF16), in_got=pltpu.VMEM(half_in, BF16),
            out_got=pltpu.VMEM(half_out, BF16), swap_s=dma((3,)), swap_r=dma((3,)), local_sem=dma((3,)), final_s=dma((4,)),
            final_r=dma((4,)), **scratch, **attn_scratch, **more,
        ),
        ("attn", "both_out", "both_x", "out_0", "out_1"), 6 << 30,
    )
    in_grad = z.in_total
    if not wide:
        odd = lax.axis_index("shard") % 2
        in_grad = jnp.where(odd == 0, in_grad, in_grad[:, ::-1])
        in_grad = jnp.swapaxes(in_grad.reshape(2, 2, in_rows, chunks, 2, CHUNK), 3, 4)
        in_grad = in_grad.reshape(2, 2, in_rows, 2, pairs, hidden_here)
        in_grad = jnp.transpose(in_grad, (2, 3, 4, 1, 0, 5)).reshape(in_rows, columns)
    if inside:
        shared_grads = (
            z.qkv_total, z.attn_out_total, z.router_total.T, z.proj_total.T, z.vec_total.T, z.gain_total.T, z.mix_total
        )
    else:
        def joined(a, b):
            parts = []
            for part in range(3):
                parts += [a[:, part * half : (part + 1) * half], b[:, part * half : (part + 1) * half]]
            return jnp.concatenate(parts + [a[:, 3 * half :], b[:, 3 * half :]], axis=1)

        grads_0, grads_1 = joined(z.grads_a, z.grads_b), joined(t.grads_a, t.grads_b)
        own = jnp.where(first_core, grads_0, grads_1)
        total = own.astype(F32) + swap(jnp.where(first_core, grads_1, grads_0)).astype(F32)
        total = lax.psum_scatter(total.astype(BF16), ("expert", "shard"), scatter_dimension=0, tiled=True).astype(F32)
        own = jnp.where(first_core, z.grad_mix, t.grad_mix)
        mix_grad = own + swap(jnp.where(first_core, t.grad_mix, z.grad_mix))
        small = total[:, 4 * width :]
        shared_grads = (
            total[:, : 3 * width],
            total[:, 3 * width : 4 * width],
            small[:, :nexp],
            small[:, AT_PROJ : AT_PROJ + const_proj.shape[-1]],
            small[:, AT_VEC : AT_VEC + nconst],
            small[:, AT_GAIN : AT_GAIN + 2],
            lax.psum(mix_grad, ("expert", "shard"))[:nexp, :nexp],
        )
    return (
        z.both_out[None, :, None],
        z.both_x[None, :, None],
        jnp.swapaxes(z.both_r, 1, 2)[None, :, None],
        *[grad[None] for grad in shared_grads],
        in_grad[None, None],
        z.out_total[None, None],
    )


def solution(mesh):
    placed = (
        P(None, ("expert", "shard"), None, None),
        P(None, ("expert", "shard"), None, None),
        P(None, ("expert", "shard"), None, None),
        P(None, ("expert", "shard"), None),
        P("section", None, ("expert", "shard"), None, None),
        P("section", None, ("expert", "shard"), None),
        P("section", ("expert", "shard"), None),
        P("section", ("expert", "shard"), None),
        P("section", ("expert", "shard"), None),
        P("section", ("expert", "shard"), None),
        P("section", ("expert", "shard"), None),
        P("section", ("expert", "shard"), None),
        P("section", None, None),
        P("section", "expert", "shard", None),
        P("section", "expert", "shard", None),
    )
    return jax.shard_map(
        local,
        mesh=mesh,
        in_specs=placed,
        out_specs=(
            P("section", None, ("expert", "shard"), None, None),
            P("section", None, ("expert", "shard"), None, None),
            P("section", None, ("expert", "shard"), None, None),
            P("section", ("expert", "shard"), None),
            P("section", ("expert", "shard"), None),
            P("section", ("expert", "shard"), None),
            P("section", ("expert", "shard"), None),
            P("section", ("expert", "shard"), None),
            P("section", ("expert", "shard"), None),
            P("section", None, None),
            P("section", "expert", "shard", None),
            P("section", "expert", "shard", None),
        ),
        check_vma=False,
    )
```

```python
import math
import types

import jax
import jax.numpy as jnp
from jax import lax
from jax.experimental import pallas as pl
from jax.experimental.pallas import tpu as pltpu
from jax.sharding import PartitionSpec as P

HEADS = 12
HEAD = 64
TOP = 2
CHUNK = 256
LANES = 128
AT_PROJ = 16
AT_VEC = 24
AT_GAIN = 28
AT_MIX = 32

HIGH = lax.Precision.HIGHEST
norm_eps = 1e-06
masked_score = -1e30
F32 = jnp.float32
BF16 = jnp.bfloat16


VMEM_BYTES = 60 * 1024 * 1024


def mm(a, b, contract=((1,), (0,)), precision=None):
    return lax.dot_general(a, b, (contract, ((), ())), precision=precision, preferred_element_type=F32)


NT = ((1,), (1,))
TN = ((0,), (0,))


def lane_of(rows, columns=LANES):
    return lax.broadcasted_iota(jnp.int32, (rows, columns), 1)


def inverse_norm(values):
    return lax.rsqrt(jnp.mean(values * values, axis=-1, keepdims=True) + norm_eps)


def norm_back(grad_unit, unit, inverse):
    return inverse * (grad_unit - unit * jnp.mean(grad_unit * unit, axis=-1, keepdims=True))


def roll(x, by):
    return pltpu.roll(x, by, 1)


def turned(x, lane):
    return jnp.where(lane % HEAD < HEAD // 2, roll(x, LANES - HEAD // 2), roll(x, HEAD // 2))


def hi_lo(x):
    high = x.astype(BF16)
    return high, (x - high.astype(F32)).astype(BF16)


def ones_where(condition):
    return jnp.where(condition, 1.0, 0.0).astype(BF16)


def small_rows_of(small):
    rows = small[...].astype(F32).T
    return rows[AT_GAIN : AT_GAIN + 1], rows[AT_GAIN + 1 : AT_GAIN + 2], rows[AT_VEC:AT_GAIN]


def attention(x, w, gain_first, cosine, sine, seg_col, seg_row, qkv, probs_att, attended):
    seq_len, width = x.shape
    first_b = (x * inverse_norm(x) * gain_first).astype(BF16)
    place_q = lax.broadcasted_iota(jnp.int32, (seq_len, seq_len), 0)
    place_k = lax.broadcasted_iota(jnp.int32, (seq_len, seq_len), 1)
    bias = jnp.where((seg_col == seg_row) & (place_k <= place_q), 0.0, masked_score)
    lane = lane_of(seq_len)
    low_head = lane < HEAD
    for pair in range(width // LANES):
        at = pair * LANES
        q = mm(first_b, w[:, at : at + LANES])
        k = mm(first_b, w[:, width + at : width + at + LANES])
        v = mm(first_b, w[:, 2 * width + at : 2 * width + at + LANES]).astype(BF16)
        q = q * cosine + turned(q, lane) * sine
        k = (k * cosine + turned(k, lane) * sine).astype(BF16)
        outs = []
        for half in range(2):
            one = jnp.where(low_head if half == 0 else lane >= HEAD, q, 0.0).astype(BF16)
            scores = mm(one, k, NT) * (HEAD**-0.5) + bias
            scores = jnp.exp(scores - jnp.max(scores, axis=-1, keepdims=True))
            probs = (scores * (1.0 / jnp.sum(scores, axis=-1, keepdims=True))).astype(BF16)
            probs_att[2 * pair + half] = probs
            outs.append(mm(probs, v))
        attended[:, at : at + LANES] = jnp.where(low_head, outs[0], outs[1]).astype(BF16)
        qkv[:, at : at + LANES] = q.astype(BF16)
        qkv[:, width + at : width + at + LANES] = k
        qkv[:, 2 * width + at : 2 * width + at + LANES] = v
    return x + mm(attended[...], w[:, 3 * width : 4 * width])


def gating(after, r, small, mix, gain_second, ints, prio_row, dims, packed_ref, slot_ref, r_next, buffer):
    nffn, nexp, capacity, slots, _ = dims
    rows = after.shape[0]
    second_b = (after * inverse_norm(after) * gain_second).astype(BF16)
    lane = lane_of(rows)
    logits = mm(second_b, small)
    full = logits + mm(r, mix, precision=HIGH)
    inside = lane < nexp
    full = jnp.where(inside, full, masked_score)
    raised = jnp.exp(full - jnp.max(full, axis=-1, keepdims=True))
    probs = raised / jnp.sum(raised, axis=-1, keepdims=True)
    other = jnp.where(lane % 2 == 0, roll(logits, LANES - 1), roll(logits, 1))
    bigger = jnp.maximum(logits, other)
    mine_e = jnp.exp(logits - bigger)
    mixes = mine_e / (mine_e + jnp.exp(other - bigger))
    before = ones_where(prio_row < column_of(prio_row).astype(jnp.int32))
    route = (ints[:, 0:1], ints[:, 1:2])
    routed = ones_where(((lane == route[0]) | (lane == route[1])) & (lane < nffn))
    rank = mm(before, routed)
    gates, places = [], []
    dispatch = 0.0
    stride = slots // nffn
    for k in range(TOP):
        chosen = lane == route[k]
        gates.append(jnp.sum(jnp.where(chosen, probs, 0.0), axis=-1, keepdims=True))
        rank_k = jnp.sum(jnp.where(chosen, rank, 0.0), axis=-1, keepdims=True).astype(jnp.int32)
        kept = (route[k] < nffn) & (rank_k < capacity)
        places.append(jnp.where(kept, route[k] * stride + rank_k, -1))
        dispatch = dispatch + jnp.where(places[k] == lane_of(rows, slots), 1.0, 0.0)
    buffer[...] = mm(dispatch.astype(BF16), second_b, TN).astype(BF16).reshape(buffer.shape)
    packed = jnp.where(inside, probs, jnp.where((lane >= AT_PROJ) & (lane < AT_VEC), mixes, 0.0))
    packed = jnp.where(lane == AT_VEC, gates[0], packed)
    packed_ref[...] = jnp.where(lane == AT_VEC + 1, gates[1], packed)
    slot_ref[...] = jnp.where(lane == 0, places[0], places[1])
    if r_next is not None:
        r_next[...] = jnp.where(inside, full, 0.0).astype(BF16)


def extras(packed, ints, nffn, nconst):
    gates = (packed[:, AT_VEC : AT_VEC + 1], packed[:, AT_VEC + 1 : AT_VEC + 2])

    def of(expert):
        return sum(jnp.where(ints[:, k : k + 1] == expert, gates[k], 0.0) for k in range(TOP))

    def mixes(c):
        at = AT_PROJ + 2 * c
        return packed[:, at : at + 1], packed[:, at + 1 : at + 2]

    return gates, of(nffn + 1), [of(nffn + 2 + c) for c in range(nconst)], [mixes(c) for c in range(nconst)]


def combine(after, packed, slot_pair, ints, blocks, gain_second, vec_rows, dims, picked_ref):
    nffn, nexp, _, slots, _ = dims
    nconst = nexp - nffn - 2
    rows = after.shape[0]
    second = after * inverse_norm(after) * gain_second
    gates, copied, const, mixes = extras(packed, ints, nffn, nconst)
    made = blocks[...].reshape(slots, after.shape[1])
    slot_lane = lane_of(rows, slots)
    coefficient = copied
    for c in range(nconst):
        coefficient = coefficient + const[c] * mixes[c][0]
    out = after + coefficient * second
    for k in range(TOP):
        picked = mm(ones_where(slot_pair[:, k : k + 1] == slot_lane), made)
        picked_ref[k] = picked.astype(BF16)
        out = out + gates[k] * picked
    for c in range(nconst):
        out = out + (const[c] * mixes[c][1]) * vec_rows[c : c + 1]
    return out


def give_back(grad_y, packed, slot_pair, dims, buffer):
    slots = dims[3]
    slot_lane = lane_of(grad_y.shape[0], slots)
    total = 0.0
    for k in range(TOP):
        gate = packed[:, AT_VEC + k : AT_VEC + k + 1]
        table = ones_where(slot_pair[:, k : k + 1] == slot_lane)
        total = total + mm(table, (gate * grad_y).astype(BF16), TN)
    buffer[...] = total.astype(BF16).reshape(buffer.shape)


def moe_back(
    grad_y, grad_log_in, after, packed, slot_pair, ints, picked, blocks, r, small, mix, gain_second, vec_rows, dims
):
    nffn, nexp, _, slots, _ = dims
    nconst = nexp - nffn - 2
    rows = grad_y.shape[0]
    lane = lane_of(rows)
    inverse = inverse_norm(after)
    unit = after * inverse
    second = unit * gain_second
    second_b = second.astype(BF16)
    gates, copied, const, mixes = extras(packed, ints, nffn, nconst)
    grad_buffer = blocks[...].reshape(slots, after.shape[1])
    slot_lane = lane_of(rows, slots)
    dispatch = sum(jnp.where(slot_pair[:, k : k + 1] == slot_lane, 1.0, 0.0) for k in range(TOP))
    grad_second = mm(dispatch.astype(BF16), grad_buffer)
    along_second = jnp.sum(grad_y * second, axis=-1, keepdims=True)
    coefficient = copied
    grad_extra = [(nffn + 1, along_second)]
    grad_lanes = jnp.zeros((rows, LANES), F32)
    vec_grads = []
    for c in range(nconst):
        along = jnp.sum(grad_y * vec_rows[c : c + 1], axis=-1, keepdims=True)
        m0, m1 = mixes[c]
        coefficient = coefficient + const[c] * m0
        grad_extra.append((nffn + 2 + c, m0 * along_second + m1 * along))
        d0, d1 = const[c] * along_second, const[c] * along
        mean = m0 * d0 + m1 * d1
        at = AT_PROJ + 2 * c
        grad_lanes = jnp.where(lane == at, m0 * (d0 - mean), grad_lanes)
        grad_lanes = jnp.where(lane == at + 1, m1 * (d1 - mean), grad_lanes)
        vec_grads.append(jnp.sum(grad_y * (const[c] * m1), axis=0, keepdims=True))
    grad_second = grad_second + coefficient * grad_y
    grad_probs = jnp.zeros((rows, LANES), F32)
    for k in range(TOP):
        grad_gate = jnp.sum(picked[k].astype(F32) * grad_y, axis=-1, keepdims=True)
        for expert, value in grad_extra:
            grad_gate = grad_gate + jnp.where(ints[:, k : k + 1] == expert, value, 0.0)
        grad_probs = grad_probs + jnp.where(lane == ints[:, k : k + 1], grad_gate, 0.0)
    probs = jnp.where(lane < nexp, packed, 0.0)
    grad_logits = probs * (grad_probs - jnp.sum(probs * grad_probs, axis=-1, keepdims=True)) + grad_log_in
    grad_mix = mm(jnp.where(lane < nexp, r, 0.0), jnp.where(lane < nexp, grad_logits, 0.0), TN, HIGH)
    grad_r = mm(grad_logits, mix, NT, HIGH)
    high, low = hi_lo(jnp.where(lane < nexp, grad_logits, grad_lanes))
    small_rows = mm(high, second_b, TN) + mm(low, second_b, TN)
    grad_second = grad_second + mm(high, small, NT) + mm(low, small, NT)
    grad_gain = jnp.sum(grad_second * unit, axis=0, keepdims=True)
    grad_after = grad_y + norm_back(grad_second * gain_second, unit, inverse)
    row = lax.broadcasted_iota(jnp.int32, small_rows.shape, 0)
    small_rows = jnp.where(row < AT_VEC, small_rows, 0.0)
    for c in range(nconst):
        small_rows = jnp.where(row == AT_VEC + c, vec_grads[c], small_rows)
    small_rows = jnp.where(row == AT_GAIN + 1, grad_gain, small_rows)
    return grad_after, grad_r, grad_mix, small_rows


def attention_back(
    grad_after, x, qkv, probs_att, attended, small_rows, mix_tile, w, gain_first, cosine, sine, grads, grad_qkv, grad_x, hooks
):
    seq_len, width = x.shape
    inverse = inverse_norm(x)
    unit = x * inverse
    first_b = (unit * gain_first).astype(BF16)
    grad_branch = grad_after.astype(BF16)
    lane = lane_of(seq_len)
    low_head = lane < HEAD
    masks = (ones_where(low_head), ones_where(lane >= HEAD))
    scale = HEAD**-0.5
    heads_half = width // LANES // 2
    wide = heads_half * LANES

    def weight_grads(batch):
        for part in range(3):
            columns = slice(part * width + batch * wide, part * width + (batch + 1) * wide)
            grads[batch][:, part * wide : (part + 1) * wide] = mm(first_b, grad_qkv[:, columns], TN).astype(BF16)
        if batch == 0:
            grads[0][:, 3 * wide :] = mm(attended[...], grad_branch, TN).astype(BF16)

    for pair in range(width // LANES):
        at = pair * LANES
        q = qkv[:, at : at + LANES]
        k = qkv[:, width + at : width + at + LANES]
        v = qkv[:, 2 * width + at : 2 * width + at + LANES]
        g = mm(grad_branch, w[at : at + LANES, 3 * width : 4 * width], NT).astype(BF16)
        dq, dk, dv = [], [], []
        for half in range(2):
            probs = probs_att[2 * pair + half]
            grad_p = mm(g * masks[half], v, NT)
            p = probs.astype(F32)
            grad_s = (p * (grad_p - jnp.sum(p * grad_p, axis=-1, keepdims=True))).astype(BF16)
            dv.append(mm(probs, g, TN))
            dq.append(mm(grad_s, k))
            dk.append(mm(grad_s, q, TN))
        dq = jnp.where(low_head, dq[0], dq[1]) * scale
        dk = jnp.where(low_head, dk[0], dk[1]) * scale
        grad_qkv[:, at : at + LANES] = (dq * cosine - turned(dq, lane) * sine).astype(BF16)
        grad_qkv[:, width + at : width + at + LANES] = (dk * cosine - turned(dk, lane) * sine).astype(BF16)
        grad_qkv[:, 2 * width + at : 2 * width + at + LANES] = jnp.where(low_head, dv[0], dv[1]).astype(BF16)
        if hooks.early and pair == heads_half - 1:
            weight_grads(0)
            hooks.first_done()
    if hooks.early:
        hooks.heads_done()
        weight_grads(1)
    grad_first = mm(grad_qkv[...], w[:, : 3 * width], NT)
    grad_gain = jnp.sum(grad_first * unit, axis=0, keepdims=True)
    grad_x[...] = grad_after + norm_back(grad_first * gain_first, unit, inverse)
    row = lax.broadcasted_iota(jnp.int32, small_rows.shape, 0)
    small_rows = jnp.where(row == AT_GAIN, grad_gain, small_rows)
    grads[1][:, 3 * wide :] = (small_rows.T + mix_tile).astype(BF16)
    if not hooks.early:
        hooks.rows_done()
        weight_grads(0)
        hooks.first_done()
        weight_grads(1)
    hooks.second_done()


def attend_kernel(
    dims, x, r, w, small, mix, cosine, sine, seg_col, seg_row, ints, prio_row,
    after, qkv, probs_att, attended, packed, slot_pair, r_next, buffer,
):
    gain_first, gain_second, _ = small_rows_of(small)
    after_v = attention(
        x[...].astype(F32), w, gain_first, cosine[...], sine[...], seg_col, seg_row, qkv, probs_att, attended
    )
    after[...] = after_v
    gating(
        after_v, r[...].astype(F32), small[...], mix[...], gain_second, ints[...], prio_row[...], dims,
        packed, slot_pair, r_next, buffer,
    )


def middle_kernel(
    dims, after_0, packed_0, slots_0, ints_0, blocks_0, small_0,
    r, w, small, mix, cosine, sine, seg_col, seg_row, ints, prio_row, grad_y,
    out, picked, after, qkv, probs_att, attended, packed, slot_pair, buffer, grad_buffer,
):
    _, gain_second, vec_rows = small_rows_of(small_0)
    out[...] = combine(
        after_0[...], packed_0[...], slots_0[...], ints_0[...], blocks_0, gain_second, vec_rows, dims, picked
    ).astype(BF16)
    attend_kernel(
        dims, out, r, w, small, mix, cosine, sine, seg_col, seg_row, ints, prio_row,
        after, qkv, probs_att, attended, packed, slot_pair, None, buffer,
    )
    give_back(grad_y[...], packed[...], slot_pair[...], dims, grad_buffer)


def back_body(
    dims, grad_y, grad_log, after, packed, slot_pair, ints, picked, blocks, r, w, small, mix, x, qkv, probs_att, attended,
    cosine, sine, grad_x, grad_r, grad_mix, grads, grad_qkv, loading, hooks,
):
    gain_first, gain_second, vec_rows = small_rows_of(small)
    grad_log_v = 0.0 if grad_log is None else grad_log[...].astype(BF16).astype(F32)
    grad_y_v = grad_y[...] if grad_log is None else grad_y[...].astype(BF16).astype(F32)
    grad_after, grad_r_v, grad_mix_v, small_rows = moe_back(
        grad_y_v, grad_log_v, after[...], packed[...], slot_pair[...], ints[...], picked,
        blocks, r[...].astype(F32), small[...], mix[...], gain_second, vec_rows, dims,
    )
    grad_r[...] = grad_r_v
    grad_mix[...] = grad_mix_v
    rows = dims[4]
    mix_tile = 0.0
    if rows:
        mix_tile = jnp.concatenate([roll(grad_mix_v, AT_MIX)[:rows]] * (x.shape[1] // rows), axis=0)
    loading.wait()
    attention_back(
        grad_after, x[...].astype(F32), qkv, probs_att, attended, small_rows, mix_tile, w, gain_first,
        cosine[...], sine[...], grads, grad_qkv, grad_x, hooks,
    )


def shaped(shape, dtype):
    return jax.ShapeDtypeStruct(shape, dtype)


def call(kernel, identity, ins, outs, scratch, far, flops):
    groups = {name: value if isinstance(value, list) else None for name, value in scratch.items()}
    flat = []
    for value in scratch.values():
        flat += value if isinstance(value, list) else [value]

    def body(*refs):
        refs = list(refs)
        named = {name: refs.pop(0) for name in list(ins) + list(outs)}
        for name, group in groups.items():
            named[name] = refs.pop(0) if group is None else [refs.pop(0) for _ in group]
        kernel(types.SimpleNamespace(**named))

    def spaces(names):
        return [pl.BlockSpec(memory_space=pl.ANY if name in far else pltpu.VMEM) for name in names]

    got = pl.pallas_call(
        body,
        out_shape=list(outs.values()),
        in_specs=spaces(ins),
        out_specs=spaces(outs),
        scratch_shapes=flat,
        compiler_params=pltpu.CompilerParams(
            vmem_limit_bytes=VMEM_BYTES, collective_id=identity, has_side_effects=True
        ),
        cost_estimate=pl.CostEstimate(flops=flops, bytes_accessed=40 << 20, transcendentals=0),
    )(*ins.values())
    return types.SimpleNamespace(**dict(zip(outs, got)))


MESH = pl.DeviceIdType.MESH


class Exchange:
    def __init__(self, stream, sent, groups, partial, sibling_part, onward, pair_part, summed, result, sems):
        self.stream, self.sent, self.groups = stream, sent, groups
        self.partial, self.sibling_part, self.onward = partial, sibling_part, onward
        self.pair_part, self.summed, self.result = pair_part, summed, result
        (self.column_s, self.column_r, self.pair_s, self.pair_r, self.core_s, self.core_r, self.last_s, self.last_r,
         self.local_sem, self.back_s, self.back_r, self.far_s, self.far_r, self.over_s, self.over_r,
         self.home_s, self.home_r) = sems
        self.core, self.column, self.place = lax.axis_index("section"), lax.axis_index("expert"), lax.axis_index("shard")
        self.owners = lax.axis_size("expert")
        self.sibling = (1 - self.core, self.column, self.place)
        self.pair = (self.core, self.column, self.place + 1 - 2 * lax.rem(self.place, 2))

    def peer(self, column):
        return (self.core, column, self.place)

    def turn(self, by):
        return lax.rem(self.column + by + self.owners, self.owners)

    def to_column(self, by):
        return pltpu.make_async_remote_copy(
            self.sent.at[self.turn(by)], self.groups.at[0, self.column],
            self.column_s.at[self.stream, by], self.column_r.at[self.stream, by],
            device_id=self.peer(self.turn(by)), device_id_type=MESH,
        )

    def from_column(self, by):
        source = self.turn(-by)
        return pltpu.make_async_remote_copy(
            self.sent.at[source], self.groups.at[0, source],
            self.column_s.at[self.stream, by], self.column_r.at[self.stream, by],
            device_id=self.peer(source), device_id_type=MESH,
        )

    def own_block(self):
        return pltpu.make_async_copy(
            self.sent.at[self.column], self.groups.at[0, self.column], self.local_sem.at[self.stream]
        )

    def forward(self, by, here, there, device, send, recv):
        block = self.turn(-by)
        return pltpu.make_async_remote_copy(
            self.groups.at[here, block], self.groups.at[there, block],
            send.at[self.stream, by], recv.at[self.stream, by], device_id=device, device_id_type=MESH,
        )

    def to_pair(self, by):
        return self.forward(by, 0, 2, self.pair, self.pair_s, self.pair_r)

    def to_core(self, by):
        return self.forward(by, 0, 1, self.sibling, self.core_s, self.core_r)

    def to_core_last(self, by):
        return self.forward(by, 2, 3, self.sibling, self.last_s, self.last_r)

    def start(self):
        for by in range(1, self.owners):
            self.to_column(by).start()
        self.own_block().start()

    def spread(self):
        for by in range(self.owners):
            if by:
                self.from_column(by).wait_recv()
            else:
                self.own_block().wait()
            self.to_pair(by).start()
            self.to_core(by).start()

    def near_ready(self):
        for by in range(self.owners):
            self.to_core(by).wait_recv()

    def spread_far(self, bys):
        for by in bys:
            self.to_pair(by).wait_recv()
            self.to_core_last(by).start()

    def far_ready(self, bys):
        for by in bys:
            self.to_core_last(by).wait_recv()

    def finish_dispatch(self):
        for by in range(self.owners):
            if by:
                self.to_column(by).wait_send()
            self.to_pair(by).wait_send()
            self.to_core(by).wait_send()
            self.to_core_last(by).wait_send()

    def near_back(self):
        return pltpu.make_async_remote_copy(
            self.partial.at[1], self.sibling_part.at[0], self.back_s.at[self.stream], self.back_r.at[self.stream],
            device_id=self.sibling, device_id_type=MESH,
        )

    def far_back(self, by):
        block = self.turn(-by)
        return pltpu.make_async_remote_copy(
            self.partial.at[3, block], self.sibling_part.at[1, block],
            self.far_s.at[self.stream, by], self.far_r.at[self.stream, by],
            device_id=self.sibling, device_id_type=MESH,
        )

    def over_pair(self, by):
        block = self.turn(-by)
        return pltpu.make_async_remote_copy(
            self.onward.at[block], self.pair_part.at[block],
            self.over_s.at[self.stream, by], self.over_r.at[self.stream, by],
            device_id=self.pair, device_id_type=MESH,
        )

    def home(self, by):
        return pltpu.make_async_remote_copy(
            self.summed.at[self.turn(by)], self.result.at[self.column],
            self.home_s.at[self.stream, by], self.home_r.at[self.stream, by],
            device_id=self.peer(self.turn(by)), device_id_type=MESH,
        )

    def home_here(self, by):
        source = self.turn(-by)
        return pltpu.make_async_remote_copy(
            self.summed.at[source], self.result.at[source],
            self.home_s.at[self.stream, by], self.home_r.at[self.stream, by],
            device_id=self.peer(source), device_id_type=MESH,
        )

    def return_far(self, bys):
        for by in bys:
            block = self.turn(-by)
            self.far_back(by).wait_recv()
            total = self.partial[2, block].astype(F32) + self.sibling_part[1, block].astype(F32)
            self.onward[block] = total.astype(BF16)
            self.over_pair(by).start()

    def return_home(self, bys):
        for by in bys:
            block = self.turn(-by)
            near = self.partial[0, block].astype(F32) + self.sibling_part[0, block].astype(F32)
            self.over_pair(by).wait_recv()
            self.summed[block] = (near + self.pair_part[block].astype(F32)).astype(BF16)
            if by:
                self.home(self.owners - by).start()
            else:
                self.result[block] = self.summed[block]

    def near_arrived(self):
        self.near_back().wait_recv()

    def finish(self):
        for by in range(1, self.owners):
            self.home_here(by).wait_recv()
            self.home(by).wait_send()
        for by in range(self.owners):
            self.over_pair(by).wait_send()
            self.far_back(by).wait_send()
        self.near_back().wait_send()

    def steps(self):
        cut = self.owners // 2
        return [list(range(cut)), list(range(cut, self.owners))]

    def far(self, bys):
        return [(group, self.turn(-by)) for by in bys for group in (2, 3)]


def home_buffers(owners, room, width):
    block = (owners, room, width)
    return [pltpu.VMEM((4,) + block, BF16), pltpu.VMEM((2,) + block, BF16)] + [pltpu.VMEM(block, BF16)] * 3


def exchange_sems(streams, owners):
    dma = pltpu.SemaphoreType.DMA
    return [dma((streams, owners))] * 8 + [dma((streams,))] * 3 + [dma((streams, owners))] * 6


def near_rows(ref):
    groups, owners, room, width = ref.shape
    return ref[:2].reshape(2 * owners * room, width)


def put_near(ref, value, columns=slice(None)):
    groups, owners, room, _ = ref.shape
    ref[:2, :, :, columns] = value.astype(ref.dtype).reshape(2, owners, room, value.shape[1])


def rows_at(ref, picks, columns=slice(None)):
    return jnp.concatenate([ref[group, block, :, columns] for group, block in picks], axis=0)


def put_at(ref, picks, value, columns=slice(None)):
    room = ref.shape[2]
    for i, (group, block) in enumerate(picks):
        ref[group, block, :, columns] = value[i * room : (i + 1) * room].astype(ref.dtype)


def all_rows(ref):
    groups, owners, room, width = ref.shape
    return ref[...].reshape(groups * owners * room, width)


def chunks_of(w_out):
    for chunk in range(w_out.shape[0] // CHUNK):
        yield slice(2 * CHUNK * chunk, 2 * CHUNK * (chunk + 1)), slice(CHUNK * chunk, CHUNK * (chunk + 1))


def made_by(rows, w_in, w_out):
    total = 0.0
    for columns, units in chunks_of(w_out):
        both = mm(rows, w_in[:, columns])
        gate = both[:, :CHUNK]
        hidden = (gate * jax.nn.sigmoid(gate) * both[:, CHUNK:]).astype(BF16)
        total = total + mm(hidden, w_out[units])
    return total


def forward_again(rows, w_in, w_out, put_both, put_hidden):
    for columns, units in chunks_of(w_out):
        both = mm(rows, w_in[:, columns])
        gate = both[:, :CHUNK]
        put_both(both, columns)
        put_hidden(gate * jax.nn.sigmoid(gate) * both[:, CHUNK:], units)


def back_of(grad_rows, w_in, w_out, both_at, put_grad):
    total = 0.0
    for columns, units in chunks_of(w_out):
        both = both_at(columns).astype(F32)
        gate, up = both[:, :CHUNK], both[:, CHUNK:]
        sig = jax.nn.sigmoid(gate)
        grad_hidden = mm(grad_rows, w_out[units], NT)
        grad_gate = grad_hidden * up * sig * (1.0 + gate * (1.0 - sig))
        grad_both = jnp.concatenate([grad_gate, grad_hidden * gate * sig], axis=1).astype(BF16)
        put_grad(grad_both, columns)
        total = total + mm(grad_both, w_in[:, columns], NT)
    return total


def both_ways(rows, grad_rows, w_in, w_out, put_hidden, put_grad):
    made, back = 0.0, 0.0
    for columns, units in chunks_of(w_out):
        both = mm(rows, w_in[:, columns])
        gate, up = both[:, :CHUNK], both[:, CHUNK:]
        sig = jax.nn.sigmoid(gate)
        hidden = (gate * sig * up).astype(BF16)
        put_hidden(hidden, units)
        made = made + mm(hidden, w_out[units])
        grad_hidden = mm(grad_rows, w_out[units], NT)
        grad_gate = grad_hidden * up * sig * (1.0 + gate * (1.0 - sig))
        grad_both = jnp.concatenate([grad_gate, grad_hidden * gate * sig], axis=1).astype(BF16)
        put_grad(grad_both, columns)
        back = back + mm(grad_both, w_in[:, columns], NT)
    return made, back


def near_of(ref):
    return lambda value, columns: put_near(ref, value, columns)


def far_of(ref, picks):
    return lambda value, columns: put_at(ref, picks, value, columns)


def weight_grads_in(rows, grad_ref, grad_in):
    for chunk in range(grad_in.shape[1] // (2 * CHUNK)):
        columns = slice(2 * CHUNK * chunk, 2 * CHUNK * (chunk + 1))
        grads = grad_ref[:, :, :, columns].reshape(rows.shape[0], 2 * CHUNK)
        grad_in[:, columns] = mm(rows, grads, TN).astype(BF16)


def exchange_far(streams, work):
    first, then = streams[0].steps()
    for bys in (first, then):
        for one in streams:
            one.spread_far(bys)
        if bys is then:
            for one in streams:
                one.return_far(first)
        for one in streams:
            one.far_ready(bys)
        for one, value in zip(streams, work(streams[0].far(bys))):
            put_at(one.partial, one.far(bys), value)
            for by in bys:
                one.far_back(by).start()
    for one in streams:
        one.return_far(then)


class Spread:
    def __init__(self, wide, packed, in_pieces, out_pieces, attn, w_in, w_out, sems):
        self.wide = wide
        self.packed, self.in_pieces, self.out_pieces = packed, in_pieces, out_pieces
        self.attn, self.w_in, self.w_out = attn, w_in, w_out
        (self.own_sem, self.z_s, self.z_r, self.plane_s, self.plane_r, self.core_s, self.core_r,
         self.in_s, self.in_r, self.out_s, self.out_r, self.own_in, self.own_out) = sems
        self.core, self.column, self.place = lax.axis_index("section"), lax.axis_index("expert"), lax.axis_index("shard")
        self.owners, self.pieces = lax.axis_size("expert"), lax.axis_size("shard")

    def spot(self, column, place):
        rows = self.packed.shape[0]
        return pl.ds(pl.multiple_of((column * self.pieces + place) * rows, rows), rows)

    def column_by(self, by):
        return lax.rem(self.column + by + self.owners, self.owners)

    def place_by(self, by):
        return lax.rem(self.place + by + self.pieces, self.pieces)

    def copy(self, source, target, send, recv, device):
        return pltpu.make_async_remote_copy(source, target, send, recv, device_id=device, device_id_type=MESH)

    def own(self):
        return pltpu.make_async_copy(self.packed, self.attn.at[self.core, self.spot(self.column, self.place)], self.own_sem)

    def along(self, back, way):
        block = self.attn.at[self.core, self.spot(self.column, self.place_by(-back))]
        there = back + 1 if way else (back - 1) % self.pieces
        return self.copy(
            self.packed if back == 0 else block, block, self.z_s.at[way, back], self.z_r.at[there],
            (self.core, self.column, self.place_by(1 if way else -1)),
        )

    def hand_on(self, back, action):
        if back < self.pieces - 1:

            @pl.when((self.place >= back) & (self.place < self.pieces - 1))
            def _():
                action(self.along(back, 1))

        if back != 1:

            @pl.when((self.place > 0) if back == 0 else (self.place > 0) & (self.place < back))
            def _():
                action(self.along(back, 0))

    def along_in(self, back):
        block = self.attn.at[self.core, self.spot(self.column, self.place_by(-back))]
        return self.copy(
            block, block, self.z_s.at[1, back], self.z_r.at[back], (self.core, self.column, self.place_by(-1))
        )

    def plane(self, back, by):
        block = self.attn.at[self.core, self.spot(self.column, self.place_by(-back))]
        source = self.packed if back == 0 else block
        return self.copy(
            source, block, self.plane_s.at[back, by], self.plane_r.at[back, by], (self.core, self.column_by(by), self.place)
        )

    def plane_in(self, back, by):
        block = self.attn.at[self.core, self.spot(self.column_by(-by), self.place_by(-back))]
        return self.copy(
            block, block, self.plane_s.at[back, by], self.plane_r.at[back, by], (self.core, self.column_by(-by), self.place)
        )

    def over(self, back, by, section):
        block = self.attn.at[section, self.spot(self.column_by(-by), self.place_by(-back))]
        source = self.packed if back == 0 and by == 0 else block
        return self.copy(
            source, block, self.core_s.at[back, by], self.core_r.at[back, by], (1 - self.core, self.column, self.place)
        )

    def begin(self):
        self.own().start()
        self.hand_on(0, lambda copy: copy.start())
        for by in range(1, self.owners):
            self.plane(0, by).start()
        self.over(0, 0, self.core).start()

    def pass_on(self):
        def arrived(back):
            self.along_in(back).wait_recv()
            self.hand_on(back, lambda copy: copy.start())
            for by in range(1, self.owners):
                self.plane(back, by).start()
            self.over(back, 0, self.core).start()

        for far in range(1, self.pieces):

            @pl.when(self.place >= far)
            def _():
                arrived(far)

            @pl.when(self.place + far < self.pieces)
            def _():
                arrived(self.pieces - far)

    def pass_over(self):
        for back in range(self.pieces):
            for by in range(1, self.owners):
                self.plane_in(back, by).wait_recv()
                self.over(back, by, self.core).start()
        self.own().wait()

    def over_ready(self):
        for back in range(self.pieces):
            for by in range(self.owners):
                self.over(back, by, 1 - self.core).wait_recv()

    def finish_attn(self):
        for back in range(self.pieces):
            self.hand_on(back, lambda copy: copy.wait_send())
        for back in range(self.pieces):
            for by in range(1, self.owners):
                self.plane(back, by).wait_send()
            for by in range(self.owners):
                self.over(back, by, self.core).wait_send()

    def in_rows(self, place):
        rows = self.w_in.shape[1] // self.pieces
        return pl.ds(pl.multiple_of(place * rows, rows), rows)

    def out_rows(self, place):
        rows = self.out_pieces.shape[1]
        return pl.ds(pl.multiple_of(lax.div(place, 2) * rows, rows), rows)

    def parts(self, core, place, section, rows):
        if not self.wide:
            return [(self.in_pieces.at[core, lax.rem(place, 2)], self.w_in.at[section, rows])]
        hidden = self.in_pieces.shape[1] // 2
        half = self.out_pieces.shape[1]
        pairs = []
        for pair in range(self.pieces // 2):
            for side in range(2):
                for ahead in range(0, half, CHUNK):
                    at = side * hidden + (2 * pair + lax.rem(place, 2)) * 2 * half + core * half + ahead
                    to = 2 * (pair * half + ahead) + side * CHUNK
                    pairs.append((
                        self.in_pieces.at[:, pl.ds(pl.multiple_of(at, CHUNK), CHUNK)],
                        self.w_in.at[section, rows, pl.ds(to, CHUNK)],
                    ))
        return pairs

    def in_copies(self, cross, by):
        core = 1 - self.core if cross else self.core
        place = self.place_by(by)
        return [
            self.copy(source, target, self.in_s.at[cross, by, i], self.in_r.at[cross, by, i], (core, self.column, place))
            for i, (source, target) in enumerate(self.parts(core, place, self.core, self.in_rows(self.place)))
        ]

    def in_here(self, cross, by):
        core = 1 - self.core if cross else self.core
        place = self.place_by(-by)
        return [
            self.copy(source, target, self.in_s.at[cross, by, i], self.in_r.at[cross, by, i], (core, self.column, place))
            for i, (source, target) in enumerate(self.parts(self.core, self.place, core, self.in_rows(place)))
        ]

    def out_copy(self, cross, by):
        core = 1 - self.core if cross else self.core
        return self.copy(
            self.out_pieces.at[core], self.w_out.at[self.core, self.out_rows(self.place)],
            self.out_s.at[cross, by // 2], self.out_r.at[cross, by // 2], (core, self.column, self.place_by(by)),
        )

    def out_here(self, cross, by):
        core = 1 - self.core if cross else self.core
        place = self.place_by(-by)
        return self.copy(
            self.out_pieces.at[core], self.w_out.at[core, self.out_rows(place)],
            self.out_s.at[cross, by // 2], self.out_r.at[cross, by // 2], (core, self.column, place),
        )

    def own_pieces(self):
        copies = [
            pltpu.make_async_copy(source, target, self.own_in.at[i])
            for i, (source, target) in enumerate(self.parts(self.core, self.place, self.core, self.in_rows(self.place)))
        ]
        return copies + [
            pltpu.make_async_copy(
                self.out_pieces.at[self.core], self.w_out.at[self.core, self.out_rows(self.place)], self.own_out
            )
        ]

    def expert_routes(self):
        for by in range(self.pieces):
            for cross in (0, 1):
                if by or cross:
                    yield cross, by

    def begin_experts(self, evens=(0, 1)):
        if 1 in evens:
            for one in self.own_pieces():
                one.start()
        for cross, by in self.expert_routes():
            if (by + 1) % 2 not in evens:
                continue
            for one in self.in_copies(cross, by):
                one.start()
            if by % 2 == 0:
                self.out_copy(cross, by).start()

    def experts_ready(self, cross):
        for way, by in self.expert_routes():
            if way == cross:
                for one in self.in_here(cross, by):
                    one.wait_recv()
                if by % 2 == 0:
                    self.out_here(cross, by).wait_recv()
        if not cross:
            for one in self.own_pieces():
                one.wait()

    def finish_experts(self):
        for cross, by in self.expert_routes():
            for one in self.in_copies(cross, by):
                one.wait_send()
            if by % 2 == 0:
                self.out_copy(cross, by).wait_send()


def spread_scratch(owners, pieces, parts):
    dma = pltpu.SemaphoreType.DMA
    return [dma, dma((2, pieces)), dma((pieces,))] + [dma((pieces, owners))] * 4 + [
        dma((2, pieces, parts)), dma((2, pieces, parts)), dma((2, pieces // 2)), dma((2, pieces // 2)), dma((parts,)), dma,
    ]


def place_of():
    return lax.axis_index("section"), lax.axis_index("expert"), lax.axis_index("shard")


def remote(source, target, send, recv, device):
    return pltpu.make_async_remote_copy(source, target, send, recv, device_id=device, device_id_type=MESH)


class ExpertSum:
    def __init__(self, grad_in, grad_out, got_even, got_odd, got_out, sems):
        self.grad_in, self.grad_out = grad_in, grad_out
        self.got_even, self.got_odd, self.got_out = got_even, got_odd, got_out
        self.in_s, self.in_r, self.out_s, self.out_r = sems
        self.core, self.column, self.place = place_of()
        self.pieces = lax.axis_size("shard")

    def place_by(self, by):
        return lax.rem(self.place + by + self.pieces, self.pieces)

    def in_rows(self, place):
        rows = self.grad_in.shape[0] // self.pieces
        return pl.ds(pl.multiple_of(place * rows, rows), rows)

    def out_rows(self, place):
        rows = self.grad_out.shape[0] // (self.pieces // 2)
        return pl.ds(pl.multiple_of(lax.div(place, 2) * rows, rows), rows)

    def in_copy(self, by, way):
        place = self.place_by(way * by)
        target = self.got_even.at[by // 2 - 1] if by % 2 == 0 else self.got_odd.at[by // 2]
        return remote(
            self.grad_in.at[self.in_rows(place)], target, self.in_s.at[by - 1], self.in_r.at[by - 1],
            (self.core, self.column, place),
        )

    def out_copy(self, by, way):
        place = self.place_by(way * by)
        at = by // 2 - 1
        return remote(
            self.grad_out.at[self.out_rows(place)], self.got_out.at[at], self.out_s.at[at], self.out_r.at[at],
            (self.core, self.column, place),
        )

    def even(self, way=1):
        return [self.in_copy(by, way) for by in range(2, self.pieces, 2)]

    def odd(self, way=1):
        copies = [self.in_copy(by, way) for by in range(1, self.pieces, 2)]
        return copies + self.down(way)

    def down(self, way=1):
        return [self.out_copy(by, way) for by in range(2, self.pieces, 2)]


def start_all(copies):
    for one in copies:
        one.start()


def wait_all(sent, arriving):
    for one in arriving:
        one.wait_recv()
    for one in sent:
        one.wait_send()


def expert_sum_sems(pieces):
    dma = pltpu.SemaphoreType.DMA
    return [dma((pieces - 1,)), dma((pieces - 1,)), dma((max(pieces // 2 - 1, 1),)), dma((max(pieces // 2 - 1, 1),))]


def got_shapes(pieces, in_rows, columns, out_rows, width):
    spare = max(pieces // 2 - 1, 1)
    return (
        shaped((spare, in_rows, columns), BF16), shaped((pieces // 2, in_rows, columns), BF16),
        shaped((spare, out_rows, width), BF16),
    )


def greet_these(devices):
    barrier = pltpu.get_barrier_semaphore()
    for device in devices:
        pl.semaphore_signal(barrier, inc=1, device_id=device, device_id_type=MESH)
    pl.semaphore_wait(barrier, len(devices))


def along_z():
    core, column, place = place_of()
    pieces = lax.axis_size("shard")
    return [(core, column, lax.rem(place + by, pieces)) for by in range(1, pieces)]


def in_plane():
    core, column, place = place_of()
    owners = lax.axis_size("expert")
    return [(core, lax.rem(column + by, owners), place) for by in range(1, owners)]


def other_core():
    core, column, place = place_of()
    return [(1 - core, column, place)]


def load_weights(attn, section, w, small, sems):
    width = w.shape[0]
    first = pltpu.make_async_copy(attn.at[section, :, pl.ds(4 * width, LANES)], small, sems.at[0])
    then = pltpu.make_async_copy(attn.at[section], w, sems.at[1])
    first.start()
    then.start()
    first.wait()
    return then


class AttnSum:
    def __init__(self, grads, buffers, sems):
        self.grads = grads
        self.from_core, self.summed, self.from_plane, self.through, self.from_z = buffers
        self.core_s, self.core_r, self.plane_s, self.plane_r, self.z_s, self.z_r = sems
        self.core, self.column, self.place = place_of()
        self.owners, self.pieces = lax.axis_size("expert"), lax.axis_size("shard")

    def block(self, column, k, core):
        rows = self.summed.shape[2]
        return pl.ds(pl.multiple_of((column * self.pieces + 2 * k + core) * rows, rows), rows)

    def each(self):
        return [(column, k) for column in range(self.owners) for k in range(self.pieces // 2)]

    def to_core(self, column, k):
        return remote(
            self.grads.at[self.block(column, k, 1 - self.core)], self.from_core.at[column, k], self.core_s.at[column, k],
            self.core_r.at[column, k], (1 - self.core, self.column, self.place),
        )

    def to_plane(self, by, way=1):
        column = lax.rem(self.column + way * by + self.owners, self.owners)
        return remote(
            self.summed.at[column], self.from_plane.at[by - 1], self.plane_s.at[by - 1], self.plane_r.at[by - 1],
            (self.core, column, self.place),
        )

    def place_by(self, by):
        return lax.rem(self.place + by + self.pieces, self.pieces)

    def along(self, by, way=1):
        place = self.place_by(way * by)
        return remote(
            self.through.at[lax.div(place, 2)], self.from_z.at[by - 1], self.z_s.at[by - 1], self.z_r.at[by - 1],
            (self.core, self.column, place),
        )

    def holds(self, place):
        return lax.rem(place, 2) == self.core

    def start(self):
        for column, k in self.each():
            self.to_core(column, k).start()

    def add_cores(self):
        for column, k in self.each():
            self.to_core(column, k).wait_recv()
        for column, k in self.each():
            own = self.grads[self.block(column, k, self.core), :]
            self.summed[column, k] = (own.astype(F32) + self.from_core[column, k].astype(F32)).astype(BF16)
        for by in range(1, self.owners):
            self.to_plane(by).start()

    def plane_ready(self):
        for by in range(1, self.owners):
            self.to_plane(by, -1).wait_recv()

    def add_plane(self):
        total = self.summed[self.column].astype(F32)
        for by in range(1, self.owners):
            total = total + self.from_plane[by - 1].astype(F32)
        self.through[...] = total.astype(BF16)
        for by in range(1, self.pieces):

            @pl.when(self.holds(self.place_by(by)))
            def _():
                self.along(by).start()

    def z_ready(self):
        @pl.when(self.holds(self.place))
        def _():
            for by in range(1, self.pieces):
                self.along(by, -1).wait_recv()

    def add_z(self, target):
        @pl.when(self.holds(self.place))
        def _():
            total = self.through[lax.div(self.place, 2)].astype(F32)
            for by in range(1, self.pieces):
                total = total + self.from_z[by - 1].astype(F32)
            target[...] = total

    def finish_near(self):
        for column, k in self.each():
            self.to_core(column, k).wait_send()
        for by in range(1, self.owners):
            self.to_plane(by).wait_send()

    def finish_z(self):
        for by in range(1, self.pieces):

            @pl.when(self.holds(self.place_by(by)))
            def _():
                self.along(by).wait_send()


def attn_sum_scratch(owners, pieces, rows, columns):
    blocks = (owners, pieces // 2, rows, columns)
    dma = pltpu.SemaphoreType.DMA
    return [
        pltpu.VMEM(blocks, BF16), pltpu.VMEM(blocks, BF16), pltpu.VMEM((owners - 1,) + blocks[1:], BF16),
        pltpu.VMEM(blocks[1:], BF16), pltpu.VMEM((pieces - 1,) + blocks[2:], BF16),
    ], [dma(blocks[:2])] * 2 + [dma((owners - 1,))] * 2 + [dma((pieces - 1,))] * 2


def column_devices():
    core, column, place = place_of()
    pieces = lax.axis_size("shard")
    return [
        (one, column, lax.rem(place + by, pieces))
        for by in range(pieces)
        for one in (core, 1 - core)
    ][1:]


def column_of(row):
    return jnp.broadcast_to(row.astype(F32), (LANES, row.shape[1])).T[:, :1]


def tables_of(seg_row, cosine, sine):
    seq_len = seg_row.shape[1]
    seg_col = column_of(seg_row).astype(jnp.int32)
    start = jnp.sum(jnp.where(seg_row < seg_col, 1.0, 0.0), axis=1, keepdims=True)
    place = lax.broadcasted_iota(jnp.int32, (seq_len, LANES), 0).astype(F32)
    lane = lane_of(seq_len)
    rate = jnp.exp((lane % (HEAD // 2)).astype(F32) * (-2.0 * math.log(10000.0) / HEAD))
    angles = (place - start) * rate
    cosine[...] = jnp.cos(angles)
    sine[...] = jnp.where(lane % HEAD < HEAD // 2, -jnp.sin(angles), jnp.sin(angles))
    return seg_col


def front_kernel(dims, inside, wide, n):
    width = n.x_in.shape[2]
    core, column, place = place_of()
    nexp, owners = dims[1], lax.axis_size("expert")
    packed_w = n.packed_w
    if inside:
        packed_w[:, : 3 * width] = n.w_qkv[...]
        packed_w[:, 3 * width : 4 * width] = n.w_attn[...]
        rows = packed_w.shape[0]
        n.turning[...] = jnp.zeros(n.turning.shape, F32)
        for array, at in ((n.router, 0), (n.const_proj, AT_PROJ), (n.const_vec, AT_VEC), (n.gains, AT_GAIN)):
            n.turning[at : at + array.shape[0], :rows] = array[...].astype(F32)
        packed_w[:, 4 * width :] = n.turning[:, :LANES].T[:rows].astype(BF16)
    spread = Spread(wide, packed_w, n.in_pieces, n.w_out_here, n.attn if inside else None, n.w_in, n.w_out, n.spread_sems)
    first, second = core == 0, core == 1
    tokens = Exchange(0, n.buffer_0, n.arrived, *n.token_home, n.made, n.sems)
    tokens_1 = Exchange(1, n.buffer_0, n.groups_1, *n.token_home, n.made, n.sems)
    grads_1 = Exchange(2, n.buffer_2, n.groups_2, *n.grad_home, n.returned, n.sems)
    greet_these(column_devices() + in_plane())

    @pl.when(first)
    def _():
        if inside:
            spread.begin()

    sibling = (1 - core, column, place)
    n.mix_own[...] = jnp.zeros(n.mix_own.shape, F32)
    n.mix_own[:nexp, :nexp] = n.gate_mix[...]
    crossing = [
        remote(n.routes.at[1 - core], n.routes_all.at[core], n.cross_s.at[0], n.cross_r.at[0], sibling),
        remote(n.priority.at[1 - core], n.prio.at[core], n.cross_s.at[1], n.cross_r.at[1], sibling),
        remote(n.mix_own, n.mix.at[core], n.cross_s.at[2], n.cross_r.at[2], sibling),
    ]
    arriving = [
        remote(n.routes.at[core], n.routes_all.at[1 - core], n.cross_s.at[0], n.cross_r.at[0], sibling),
        remote(n.priority.at[core], n.prio.at[1 - core], n.cross_s.at[1], n.cross_r.at[1], sibling),
        remote(n.mix_own, n.mix.at[1 - core], n.cross_s.at[2], n.cross_r.at[2], sibling),
    ]
    start_all(crossing)
    bring = [
        pltpu.make_async_copy(n.x_in.at[core], n.x, n.bring_sems.at[0]),
        pltpu.make_async_copy(n.cotangent.at[core], n.upstream, n.bring_sems.at[1]),
    ]
    attn = (n.attn.at[0], n.attn.at[1])
    if not inside:
        attn = (n.attn_here, n.attn_here)
        loads = [pltpu.make_async_copy(n.attn.at[section], n.attn_here, n.bring_sems.at[2]) for section in range(2)]
        bring.append(loads[0])
    start_all(bring)
    seg_row = n.segments[core]
    seg_col = tables_of(seg_row, n.cosine, n.sine)
    n.routes_all[core] = n.routes[core]
    n.prio[core] = n.priority[core]
    n.mix[core] = n.mix_own[...]
    n.turning[...] = jnp.zeros(n.turning.shape, F32)
    n.turning[:nexp, :] = n.gate_prev[core].astype(F32)
    n.r[...] = n.turning[...].T.astype(BF16)
    wait_all(crossing, arriving)
    lane = lane_of(n.ints.shape[1])
    for section in range(2):
        routes = n.routes_all[section]
        first_route, second_route = (column_of(routes[k : k + 1]).astype(jnp.int32) for k in range(TOP))
        n.ints[section] = jnp.where(lane == 0, first_route, second_route)
    for one in bring:
        one.wait()

    @pl.when(first)
    def _():
        if inside:
            spread.pass_on()
        spread.begin_experts()
        if inside:
            spread.pass_over()

    @pl.when(second)
    def _():
        if inside:
            spread.over_ready()
            spread.begin()

    keep = [
        pltpu.make_async_copy(source, target, n.keep_sems.at[section, i])
        for section, targets in enumerate(((n.qkv_0, n.probs_0), (n.qkv_1, n.probs_1)))
        for i, (source, target) in enumerate(zip((n.qkv_here, n.probs_here), targets))
    ]
    leaving = [pltpu.make_async_copy(n.w_in.at[0], n.w_in_kept, n.leave_sems.at[0]),
               pltpu.make_async_copy(n.w_out.at[0], n.w_out_kept, n.leave_sems.at[1])]
    if inside:
        leaving += [
            pltpu.make_async_copy(n.attn.at[section], n.attn_kept.at[section], n.leave_sems.at[2 + section])
            for section in range(2)
        ]
    n.small[0] = attn[0][:, 4 * width :]
    attend_kernel(
        dims, n.x, n.r, attn[0], n.small.at[0], n.mix.at[0], n.cosine, n.sine, seg_col, seg_row,
        n.ints.at[0], n.prio.at[0],
        n.after_0, n.qkv_here, n.probs_here, n.attended_0, n.packed_0, n.slots_0, n.r_next, n.buffer_0,
    )
    tokens.start()
    start_all(keep[:2])
    if not inside:
        loads[1].start()

    tokens.spread()

    @pl.when(first)
    def _():
        spread.experts_ready(0)

    @pl.when(second)
    def _():
        if inside:
            spread.pass_on()
        spread.experts_ready(1)
        spread.begin_experts((1,))

    tokens.near_ready()
    put_near(tokens.partial, made_by(near_rows(tokens.groups), n.w_in.at[0], n.w_out.at[0]))
    tokens.near_back().start()
    exchange_far([tokens], lambda picks: [made_by(rows_at(tokens.groups, picks), n.w_in.at[0], n.w_out.at[0])])

    @pl.when(second)
    def _():
        if inside:
            spread.pass_over()
        spread.begin_experts((0,))

    tokens.near_arrived()
    tokens.return_home(range(owners))
    tokens.finish_dispatch()
    tokens.finish()
    if inside:

        @pl.when(first)
        def _():
            spread.over_ready()

    if not inside:
        loads[1].wait()
    n.small[1] = attn[1][:, 4 * width :]
    for one in keep[:2]:
        one.wait()
    middle_kernel(
        dims, n.after_0, n.packed_0, n.slots_0, n.ints.at[0], tokens.result, n.small.at[0],
        n.r_next, attn[1], n.small.at[1], n.mix.at[1], n.cosine, n.sine, seg_col, seg_row,
        n.ints.at[1], n.prio.at[1], n.upstream,
        n.out_0, n.picked_0, n.after_1, n.qkv_here, n.probs_here, n.attended_1, n.packed_1, n.slots_1, n.buffer_0, n.buffer_2,
    )
    start_all(keep[2:])
    both = (tokens_1, grads_1)
    for one in both:
        one.start()
    for one in both:
        one.spread()

    @pl.when(first)
    def _():
        spread.experts_ready(1)

    @pl.when(second)
    def _():
        spread.experts_ready(0)

    w_in, w_out = n.w_in.at[1], n.w_out.at[1]
    start_all(leaving)
    for one in both:
        one.near_ready()
    parts = both_ways(
        near_rows(tokens_1.groups), near_rows(grads_1.groups), w_in, w_out, near_of(n.hidden), near_of(n.grad_both)
    )
    for one, part in zip(both, parts):
        put_near(one.partial, part)
        one.near_back().start()
    exchange_far(
        both,
        lambda picks: both_ways(
            rows_at(tokens_1.groups, picks), rows_at(grads_1.groups, picks), w_in, w_out,
            far_of(n.hidden, picks), far_of(n.grad_both, picks),
        ),
    )
    n.grad_out[...] = mm(all_rows(n.hidden), all_rows(grads_1.groups), TN).astype(BF16)
    for one in both:
        one.near_arrived()
        one.return_home(range(owners))
    weight_grads_in(all_rows(tokens_1.groups), n.grad_both, n.grad_in)
    for one in both:
        one.finish_dispatch()
        one.finish()
    for one in keep[2:] + leaving:
        one.wait()
    if inside:
        spread.finish_attn()
    spread.finish_experts()


def turn_kernel(dims, inside, n):
    sums = ExpertSum(n.grad_in_1, n.grad_out_1, n.even, n.odd, n.got_out, n.sum_sems)
    loading = load_weights(n.attn, 1, n.w, n.small, n.load_sems)
    expert_loads = [
        pltpu.make_async_copy(n.w_in_all, n.w_in, n.load_sems.at[2]),
        pltpu.make_async_copy(n.w_out_all, n.w_out, n.load_sems.at[3]),
    ]
    start_all(expert_loads)
    grads = Exchange(0, n.buffer, n.groups, *n.home, n.blocks_back, n.sems)
    attn = []
    if inside:
        attn = [AttnSum(n.grads_a, n.attn_buffers_a, n.attn_sems_a), AttnSum(n.grads_b, n.attn_buffers_b, n.attn_sems_b)]
    greet_these(other_core() + along_z() + in_plane())
    start_all(sums.even() + sums.odd()[: -len(sums.down()) or None])
    _, gain_second, vec_rows = small_rows_of(n.small)
    n.out[...] = combine(
        n.after[...], n.packed[...], n.slots[...], n.ints[1], n.made, gain_second, vec_rows, dims, n.picked
    ).astype(BF16)

    def rows_done():
        give_back(n.grad_x[...].astype(BF16).astype(F32), n.packed_0[...], n.slots_0[...], dims, n.buffer)
        grads.start()

    hooks = types.SimpleNamespace(
        early=False, rows_done=rows_done, first_done=lambda: [one.start() for one in attn[:1]],
        second_done=lambda: [one.start() for one in attn[1:]],
    )
    back_body(
        dims, n.upstream, None, n.after, n.packed, n.slots, n.ints.at[1], n.picked, n.returned, n.r, n.w, n.small, n.mix.at[1],
        n.x, n.qkv, n.probs, n.attended, n.cosine, n.sine, n.grad_x, n.grad_r, n.grad_mix, (n.grads_a, n.grads_b),
        n.grad_qkv, loading, hooks,
    )
    for one in expert_loads:
        one.wait()
    forward_again(near_rows(n.arrived), n.w_in, n.w_out, near_of(n.both), near_of(n.hidden))
    grads.spread()
    start_all(sums.down())
    for one in attn:
        one.add_cores()
    grads.near_ready()

    def near_both(columns):
        return n.both[:2, :, :, columns].reshape(near_count, 2 * CHUNK)

    near_count = n.both.shape[0] // 2 * n.both.shape[1] * n.both.shape[2]
    put_near(
        grads.partial, back_of(near_rows(grads.groups), n.w_in, n.w_out, near_both, near_of(n.grad_both))
    )
    grads.near_back().start()
    for bys in grads.steps():
        picks = grads.far(bys)
        forward_again(
            rows_at(n.arrived, picks), n.w_in, n.w_out, far_of(n.both, picks), far_of(n.hidden, picks)
        )
    exchange_far(
        [grads],
        lambda picks: [back_of(
            rows_at(grads.groups, picks), n.w_in, n.w_out, lambda columns: rows_at(n.both, picks, columns),
            far_of(n.grad_both, picks),
        )],
    )
    n.grad_out_0[...] = mm(all_rows(n.hidden), all_rows(grads.groups), TN).astype(BF16)
    for one in attn:
        one.plane_ready()
        one.add_plane()
    grads.near_arrived()
    grads.return_home(range(grads.owners))
    weight_grads_in(all_rows(n.arrived), n.grad_both, n.grad_in_0)
    grads.finish_dispatch()
    grads.finish()
    for one, target in zip(attn, (n.attn_sum_a, n.attn_sum_b)):
        one.finish_near()
        one.z_ready()
        one.add_z(target)
        one.finish_z()
    wait_all(sums.even() + sums.odd(), sums.even(-1) + sums.odd(-1))


def spread_columns(target, halves_at, hidden_here):
    rows, columns = target.shape
    hidden = columns // 2
    pieces = hidden // (2 * hidden_here)
    parity = lax.rem(lax.axis_index("shard"), 2)
    for first_parity in range(2):

        @pl.when(parity == first_parity)
        def _():
            for half in range(2):
                for q in range(2):
                    odd = first_parity if q == 0 else 1 - first_parity
                    for pair in range(pieces // 2):
                        for side in range(2):
                            for ahead in range(0, hidden_here, CHUNK):
                                at = side * hidden + (2 * pair + odd) * 2 * hidden_here + half * hidden_here + ahead
                                source = 2 * (pair * hidden_here + ahead) + side * CHUNK
                                target[:, at : at + CHUNK] = halves_at(half, q)[:, source : source + CHUNK].astype(F32)


def last_kernel(dims, inside, wide, n):
    core, column, place = place_of()
    pieces = lax.axis_size("shard")
    pair_count = pieces // 2
    (sibling,) = other_core()
    loading = load_weights(n.attn, 0, n.w, n.small, n.load_sems)
    sums = ExpertSum(n.grad_in_0, n.grad_out_0, n.even_0, n.odd_0, n.got_out_0, n.sum_sems)
    attn = []
    if inside:
        attn = [AttnSum(n.grads_a, n.attn_buffers_a, n.attn_sems_a), AttnSum(n.grads_b, n.attn_buffers_b, n.attn_sems_b)]
    greet_these(other_core() + along_z() + (in_plane() if inside else []))
    start_all(sums.even() + sums.odd())
    pairs = ((n.out_0, n.out_1, n.both_out), (n.grad_x_0, n.grad_x_1, n.both_x), (n.grad_r_0, n.grad_r_1, n.r_pair))

    def swaps(section):
        for i, (zero, one, both) in enumerate(pairs):
            own, other = (zero, one) if section == 0 else (one, zero)
            yield (
                remote(other, both.at[section], n.swap_s.at[i], n.swap_r.at[i], sibling),
                pltpu.make_async_copy(own, both.at[section], n.local_sem.at[i]),
            )

    def each_core(action):
        for section in range(2):

            @pl.when(core == section)
            def _():
                action(section)

    def add_experts(section, grad_in, grad_out, even, odd, got_out):
        rows, out_rows = even.shape[1], got_out.shape[1]
        own_in = grad_in[pl.ds(pl.multiple_of(place * rows, rows), rows), :]
        own_out = grad_out[pl.ds(pl.multiple_of(lax.div(place, 2) * out_rows, out_rows), out_rows), :]
        in_sum = [own_in.astype(F32), odd[0].astype(F32)]
        for i in range(pair_count - 1):
            in_sum[0] = in_sum[0] + even[i].astype(F32)
            in_sum[1] = in_sum[1] + odd[i + 1].astype(F32)
        out_sum = own_out.astype(F32)
        for i in range(pair_count - 1):
            out_sum = out_sum + got_out[i].astype(F32)

        @pl.when(core == section)
        def _():
            for q in range(2):
                n.in_mine[q] = in_sum[q]
            n.out_mine[...] = out_sum

        @pl.when(core != section)
        def _():
            for q in range(2):
                n.in_sent[q] = in_sum[q].astype(BF16)
            n.out_sent[...] = out_sum.astype(BF16)
            for one in finals:
                one.start()

    finals = [
        remote(n.in_sent, n.in_got, n.final_s.at[0], n.final_r.at[0], sibling),
        remote(n.out_sent, n.out_got, n.final_s.at[1], n.final_r.at[1], sibling),
    ]
    hooks = types.SimpleNamespace(
        early=True, first_done=lambda: [one.start() for one in attn[:1]],
        heads_done=lambda: [one.add_cores() for one in attn[:1]], second_done=lambda: [one.start() for one in attn[1:]],
    )
    back_body(
        dims, n.grad_x_1, n.grad_r_1, n.after, n.packed, n.slots, n.ints.at[0], n.picked, n.returned, n.r, n.w, n.small,
        n.mix.at[0], n.x, n.qkv, n.probs, n.attended, n.cosine, n.sine, n.grad_x_0, n.grad_r_0, n.grad_mix,
        (n.grads_a, n.grads_b), n.grad_qkv, loading, hooks,
    )

    @each_core
    def _(section):
        for away, here in swaps(section):
            away.start()
            here.start()

    for one in attn[1:]:
        one.add_cores()
    add_experts(1, n.grad_in_1, n.grad_out_1, n.even_1, n.odd_1, n.got_out_1)
    for one in attn:
        one.plane_ready()
        one.add_plane()
    wait_all(sums.even() + sums.odd(), sums.even(-1) + sums.odd(-1))
    add_experts(0, n.grad_in_0, n.grad_out_0, n.even_0, n.odd_0, n.got_out_0)
    for one in finals:
        one.wait()
    for half in range(2):

        @pl.when(core == half)
        def _():
            if wide:
                hidden_here = n.out_mine.shape[0]
                spread_columns(n.in_total, lambda at, q: n.in_mine[q] if at == half else n.in_got[q], hidden_here)
            else:
                for q in range(2):
                    n.in_total[half, q] = n.in_mine[q]
                    n.in_total[1 - half, q] = n.in_got[q].astype(F32)
            count = n.out_mine.shape[0]
            n.out_total[half * count : (half + 1) * count] = n.out_mine[...]
            n.out_total[(1 - half) * count : (2 - half) * count] = n.out_got[...].astype(F32)

    for i, (one, sum_0, sum_1, total) in enumerate(zip(
        attn, (n.attn_sum_0a, n.attn_sum_0b), (n.attn_sum_1a, n.attn_sum_1b), (n.attn_total_a, n.attn_total_b)
    )):
        one.z_ready()
        one.add_z(sum_0)
        holder = one.holds(place)
        for section in range(2):
            mine, other = (sum_0, sum_1) if section == 0 else (sum_1, sum_0)
            home = remote(other, total, n.final_s.at[2 + i], n.final_r.at[2 + i], sibling)

            @pl.when(holder & (core == section))
            def _():
                home.start()
                total[...] = mine[...]
                home.wait_send()

            @pl.when(jnp.logical_not(holder) & (core == section))
            def _():
                home.wait_recv()

    if inside:
        width = n.x.shape[1]
        half = width // LANES // 2 * LANES
        for batch, total in enumerate((n.attn_total_a, n.attn_total_b)):
            for part in range(3):
                at = part * width + batch * half
                n.qkv_total[:, at : at + half] = total[:, part * half : (part + 1) * half]
        n.attn_out_total[...] = n.attn_total_a[:, 3 * half :]
        small = n.attn_total_b[:, 3 * half :]
        nexp, rows = n.mix_total.shape[0], small.shape[0]
        n.mix_total[...] = small[:nexp, AT_MIX : AT_MIX + nexp]
        n.turning[...] = jnp.zeros(n.turning.shape, F32)
        n.turning[:rows] = small
        turned_small = n.turning[...].T
        for target, at in ((n.router_total, 0), (n.proj_total, AT_PROJ), (n.vec_total, AT_VEC), (n.gain_total, AT_GAIN)):
            target[...] = turned_small[at : at + target.shape[0], :rows]

    @each_core
    def _(section):
        for away, here in swaps(section):
            away.wait()
            here.wait()

    for batch in range(2):
        n.both_r[batch] = n.r_pair[batch].T[: n.both_r.shape[1]]

    for one in attn:
        one.finish_near()
        one.finish_z()


def local(
    x_in,
    cotangent,
    gate_prev,
    segments,
    routes,
    priority,
    attn_qkv,
    attn_out,
    router,
    const_proj,
    const_vec,
    gains,
    gate_mix,
    expert_in,
    expert_out,
):
    seq_len, width = x_in.shape[2:]
    nexp = gate_prev.shape[-1]
    owners, pieces = lax.axis_size("expert"), lax.axis_size("shard")
    nffn = owners * expert_in.shape[1]
    nconst = const_vec.shape[-1]
    capacity = (5 * TOP * seq_len + 4 * nexp - 1) // (4 * nexp)
    room = -(-capacity // 16) * 16
    slots = nffn * room
    core = lax.axis_index("section")
    first_core = core == 0
    in_rows, columns = expert_in.shape[2:]
    hidden_here = expert_out.shape[2] // 2
    pairs = pieces // 2
    quarter = pairs * hidden_here
    chunks = quarter // CHUNK
    rows = attn_qkv.shape[1]
    inside, wide = rows % 16 == 0, hidden_here % CHUNK == 0

    def swap(item):
        return lax.ppermute(item, "section", [(0, 1), (1, 0)])

    def by_section(own, other):
        return jnp.where(first_core, own, other), jnp.where(first_core, other, own)

    def as_chunks(half):
        half = jnp.moveaxis(half, 3, 0).reshape(2, in_rows, 2, chunks, CHUNK)
        return jnp.swapaxes(half, 2, 3).reshape(2, in_rows, 2 * quarter)

    w_out = expert_out[0, 0].reshape(2, hidden_here, width)
    in_pieces = expert_in[0, 0]
    if not wide:
        w_in = in_pieces.reshape(in_rows, 2, pairs, 2, 2, hidden_here)
        in_pieces = jnp.stack([as_chunks(w_in[:, :, :, :, half]) for half in range(2)])
    given = None
    if not inside:
        def lanes(array, upto):
            return jnp.pad(array, ((0, 0), (0, upto - array.shape[1])))

        small = [
            lanes(router[0], AT_PROJ), lanes(const_proj[0], AT_VEC - AT_PROJ), lanes(const_vec[0], AT_GAIN - AT_VEC),
            lanes(gains[0], LANES - AT_GAIN),
        ]
        shared = jnp.concatenate([attn_qkv[0], attn_out[0]] + small, axis=1)
        shared = lax.all_gather(shared, ("expert", "shard"), axis=0, tiled=True)
        given = jnp.stack(by_section(shared, swap(shared)))
    dims = (nffn, nexp, capacity, slots, rows if inside else 0)
    heads = width // HEAD
    blocks = (owners, room, width)
    token_f32 = shaped((seq_len, width), F32)
    token_b16 = shaped((seq_len, width), BF16)
    lanes_f32 = shaped((seq_len, LANES), F32)
    lanes_i32 = shaped((seq_len, LANES), jnp.int32)
    block_shape = shaped(blocks, BF16)
    attn_shape = shaped((width, 4 * width + LANES), BF16)
    attn_columns = attn_shape.shape[1]
    pair_shape = shaped((TOP, seq_len, width), BF16)
    in_shape, out_shape = shaped((width, 2 * quarter), BF16), shaped((quarter, width), BF16)
    dma = pltpu.SemaphoreType.DMA
    even, odd, got_out = got_shapes(pieces, in_rows, 2 * quarter, hidden_here, width)

    def vmem(shape):
        return pltpu.VMEM(shape.shape, shape.dtype)

    def attend_out(section):
        return {
            f"after_{section}": token_f32,
            f"qkv_{section}": shaped((seq_len, 3 * width), BF16),
            f"probs_{section}": shaped((heads, seq_len, seq_len), BF16),
            f"attended_{section}": token_b16,
            f"packed_{section}": lanes_f32,
            f"slots_{section}": lanes_i32,
        }

    ins = dict(
        in_pieces=in_pieces, w_out_here=w_out, x_in=x_in[:, 0], cotangent=cotangent[:, 0], gate_prev=jnp.swapaxes(gate_prev[:, 0], 1, 2),
        segments=segments, routes=jnp.swapaxes(routes[0, :, 0], 1, 2), priority=priority[0], gate_mix=gate_mix[0],
    )
    table_shapes = dict(
        mix=shaped((2, LANES, LANES), F32), cosine=lanes_f32, sine=lanes_f32, ints=shaped((2, seq_len, LANES), jnp.int32),
    )
    outs = dict(
        w_in_kept=in_shape, w_out_kept=out_shape, arrived=shaped((4,) + blocks, BF16), r_next=shaped((seq_len, LANES), BF16), out_0=token_b16, picked_0=pair_shape,
        made=block_shape, returned=block_shape, grad_in=in_shape, grad_out=out_shape, **attend_out(0), **attend_out(1),
        x=token_b16, r=shaped((seq_len, LANES), BF16), upstream=token_f32, **table_shapes,
    )
    if inside:
        outs["attn_kept"] = shaped((2,) + attn_shape.shape, BF16)
        ins = dict(
            ins, w_qkv=attn_qkv[0], w_attn=attn_out[0], router=router[0].T, const_proj=const_proj[0].T,
            const_vec=const_vec[0].T, gains=gains[0].T,
        )
    else:
        ins["attn"] = given
    f = call(
        lambda n: front_kernel(dims, inside, wide, n), 0, ins, outs,
        dict(
            small=pltpu.VMEM((2, width, LANES), BF16), buffer_0=vmem(block_shape),
            buffer_2=vmem(block_shape), groups_1=pltpu.VMEM((4,) + blocks, BF16), groups_2=pltpu.VMEM((4,) + blocks, BF16),
            token_home=home_buffers(*blocks), grad_home=home_buffers(*blocks), sems=exchange_sems(3, owners),
            spread_sems=spread_scratch(owners, pieces, 2 * pairs * max(hidden_here // CHUNK, 1) if wide else 1),
            packed_w=pltpu.VMEM((rows, 4 * width + LANES), BF16), mix_own=pltpu.VMEM((LANES, LANES), F32),
            prio=pltpu.VMEM((2, 1, seq_len), jnp.int32), cross_s=dma((3,)), cross_r=dma((3,)), bring_sems=dma((3,)),
            qkv_here=pltpu.VMEM((seq_len, 3 * width), BF16), probs_here=pltpu.VMEM((heads, seq_len, seq_len), BF16),
            keep_sems=dma((2, 2)), leave_sems=dma((4,)),
            w_in=pltpu.VMEM((2, width, 2 * quarter), BF16), w_out=pltpu.VMEM((2, quarter, width), BF16),
            **(dict(attn=pltpu.VMEM((2,) + attn_shape.shape, BF16)) if inside else dict(attn_here=vmem(attn_shape))), turning=pltpu.VMEM((LANES, seq_len), F32), routes_all=pltpu.VMEM((2, TOP, seq_len), jnp.int32),
            hidden=pltpu.VMEM((4,) + blocks[:2] + (quarter,), BF16), grad_both=pltpu.VMEM((4,) + blocks[:2] + (2 * quarter,), BF16),
        ),
        ("in_pieces", "w_out_here", "x_in", "cotangent", "qkv_0", "probs_0", "qkv_1", "probs_1")
        + ("w_in_kept", "w_out_kept", "attn_kept" if inside else "attn"), 8 << 30,
    )
    tables = dict(mix=f.mix, cosine=f.cosine, sine=f.sine, ints=f.ints)
    attn_all = f.attn_kept if inside else given
    scratch = dict(
        w=vmem(attn_shape), small=pltpu.VMEM((width, LANES), BF16), load_sems=dma((4,)), grad_qkv=pltpu.VMEM((seq_len, 3 * width), BF16),
        sum_sems=expert_sum_sems(pieces),
    )
    attn_scratch = {}
    half = width // LANES // 2 * LANES
    batches = dict(a=3 * half + width, b=3 * half + LANES)
    block_sums = {name: shaped((rows, lanes) if inside else (8, LANES), F32) for name, lanes in batches.items()}
    grad_shapes = {f"grads_{name}": shaped((width, lanes), BF16) for name, lanes in batches.items()}
    if inside:
        for name, lanes in batches.items():
            buffers, sems = attn_sum_scratch(owners, pieces, rows, lanes)
            attn_scratch.update({f"attn_buffers_{name}": buffers, f"attn_sems_{name}": sems})
    outs = dict(
        out=token_b16, grad_x=token_f32, grad_r=lanes_f32, grad_mix=shaped((LANES, LANES), F32), even=even, odd=odd,
        got_out=got_out, grad_in_0=in_shape, grad_out_0=out_shape, blocks_back=block_shape,
        attn_sum_a=block_sums["a"], attn_sum_b=block_sums["b"],
    )
    more = {name: vmem(shape) for name, shape in grad_shapes.items()}
    if not inside:
        outs, more = dict(outs, **grad_shapes), {}
    t = call(
        lambda n: turn_kernel(dims, inside, n), 1,
        dict(
            attn=attn_all, w_in_all=f.w_in_kept, w_out_all=f.w_out_kept, grad_in_1=f.grad_in, grad_out_1=f.grad_out,
            upstream=f.upstream, after=f.after_1, packed=f.packed_1, slots=f.slots_1, made=f.made, returned=f.returned, r=f.r_next,
            x=f.out_0, qkv=f.qkv_1, probs=f.probs_1, attended=f.attended_1, packed_0=f.packed_0, slots_0=f.slots_0,
            arrived=f.arrived, **tables,
        ),
        outs,
        dict(
            picked=vmem(pair_shape), buffer=vmem(block_shape), groups=pltpu.VMEM((4,) + blocks, BF16), home=home_buffers(*blocks),
            sems=exchange_sems(1, owners), w_in=vmem(in_shape), w_out=vmem(out_shape),
            both=pltpu.VMEM((4,) + blocks[:2] + (2 * quarter,), F32 if slots <= 384 else BF16), hidden=pltpu.VMEM((4,) + blocks[:2] + (quarter,), BF16),
            grad_both=pltpu.VMEM((4,) + blocks[:2] + (2 * quarter,), BF16), **scratch, **attn_scratch, **more,
        ),
        ("attn", "w_in_all", "w_out_all", "grad_in_1", "grad_out_1"), 12 << 30,
    )
    in_total = shaped((in_rows, columns) if wide else (2, 2, in_rows, 2 * quarter), F32)
    half_in, half_out = (2, in_rows, 2 * quarter), (hidden_here, width)
    outs = dict(
        both_out=shaped((2, seq_len, width), BF16), both_x=shaped((2, seq_len, width), F32),
        both_r=shaped((2, nexp, seq_len), F32), in_total=in_total, out_total=shaped((2 * hidden_here, width), F32),
        grad_mix=shaped((LANES, LANES), F32),
    )
    if inside:
        narrow = dict(router_total=nexp, proj_total=const_proj.shape[2], vec_total=nconst, gain_total=2)
        outs = dict(
            outs, qkv_total=shaped((rows, 3 * width), F32), attn_out_total=shaped((rows, width), F32),
            mix_total=shaped((nexp, nexp), F32), **{name: shaped((lanes, rows), F32) for name, lanes in narrow.items()},
        )
    else:
        outs = dict(outs, **grad_shapes)
    z = call(
        lambda n: last_kernel(dims, inside, wide, n), 2,
        dict(
            attn=attn_all, grad_in_0=t.grad_in_0, grad_out_0=t.grad_out_0, grad_in_1=f.grad_in, grad_out_1=f.grad_out,
            even_1=t.even, odd_1=t.odd, got_out_1=t.got_out, attn_sum_1a=t.attn_sum_a, attn_sum_1b=t.attn_sum_b, out_0=f.out_0, out_1=t.out,
            grad_x_1=t.grad_x, grad_r_1=t.grad_r, after=f.after_0, packed=f.packed_0, slots=f.slots_0, picked=f.picked_0,
            returned=t.blocks_back, r=f.r, x=f.x, qkv=f.qkv_0, probs=f.probs_0, attended=f.attended_0, **tables,
        ),
        outs,
        dict(
            even_0=vmem(even), odd_0=vmem(odd), got_out_0=vmem(got_out), grad_x_0=vmem(token_f32), grad_r_0=vmem(lanes_f32),
            attn_sum_0a=vmem(block_sums["a"]), attn_sum_0b=vmem(block_sums["b"]), attn_total_a=vmem(block_sums["a"]),
            attn_total_b=vmem(block_sums["b"]), turning=pltpu.VMEM((LANES, LANES), F32), r_pair=pltpu.VMEM((2, seq_len, LANES), F32), in_mine=pltpu.VMEM(half_in, F32), out_mine=pltpu.VMEM(half_out, F32),
            in_sent=pltpu.VMEM(half_in, BF16), out_sent=pltpu.VMEM(half_out, BF16), in_got=pltpu.VMEM(half_in, BF16),
            out_got=pltpu.VMEM(half_out, BF16), swap_s=dma((3,)), swap_r=dma((3,)), local_sem=dma((3,)), final_s=dma((4,)),
            final_r=dma((4,)), **scratch, **attn_scratch, **more,
        ),
        ("attn", "both_out", "both_x", "out_0", "out_1"), 6 << 30,
    )
    in_grad = z.in_total
    if not wide:
        odd = lax.axis_index("shard") % 2
        in_grad = jnp.where(odd == 0, in_grad, in_grad[:, ::-1])
        in_grad = jnp.swapaxes(in_grad.reshape(2, 2, in_rows, chunks, 2, CHUNK), 3, 4)
        in_grad = in_grad.reshape(2, 2, in_rows, 2, pairs, hidden_here)
        in_grad = jnp.transpose(in_grad, (2, 3, 4, 1, 0, 5)).reshape(in_rows, columns)
    if inside:
        shared_grads = (
            z.qkv_total, z.attn_out_total, z.router_total.T, z.proj_total.T, z.vec_total.T, z.gain_total.T, z.mix_total
        )
    else:
        def joined(a, b):
            parts = []
            for part in range(3):
                parts += [a[:, part * half : (part + 1) * half], b[:, part * half : (part + 1) * half]]
            return jnp.concatenate(parts + [a[:, 3 * half :], b[:, 3 * half :]], axis=1)

        grads_0, grads_1 = joined(z.grads_a, z.grads_b), joined(t.grads_a, t.grads_b)
        own = jnp.where(first_core, grads_0, grads_1)
        total = own.astype(F32) + swap(jnp.where(first_core, grads_1, grads_0)).astype(F32)
        total = lax.psum_scatter(total.astype(BF16), ("expert", "shard"), scatter_dimension=0, tiled=True).astype(F32)
        own = jnp.where(first_core, z.grad_mix, t.grad_mix)
        mix_grad = own + swap(jnp.where(first_core, t.grad_mix, z.grad_mix))
        small = total[:, 4 * width :]
        shared_grads = (
            total[:, : 3 * width],
            total[:, 3 * width : 4 * width],
            small[:, :nexp],
            small[:, AT_PROJ : AT_PROJ + const_proj.shape[-1]],
            small[:, AT_VEC : AT_VEC + nconst],
            small[:, AT_GAIN : AT_GAIN + 2],
            lax.psum(mix_grad, ("expert", "shard"))[:nexp, :nexp],
        )
    return (
        z.both_out[None, :, None],
        z.both_x[None, :, None],
        jnp.swapaxes(z.both_r, 1, 2)[None, :, None],
        *[grad[None] for grad in shared_grads],
        in_grad[None, None],
        z.out_total[None, None],
    )


def solution(mesh):
    placed = (
        P(None, ("expert", "shard"), None, None),
        P(None, ("expert", "shard"), None, None),
        P(None, ("expert", "shard"), None, None),
        P(None, ("expert", "shard"), None),
        P("section", None, ("expert", "shard"), None, None),
        P("section", None, ("expert", "shard"), None),
        P("section", ("expert", "shard"), None),
        P("section", ("expert", "shard"), None),
        P("section", ("expert", "shard"), None),
        P("section", ("expert", "shard"), None),
        P("section", ("expert", "shard"), None),
        P("section", ("expert", "shard"), None),
        P("section", None, None),
        P("section", "expert", "shard", None),
        P("section", "expert", "shard", None),
    )
    return jax.shard_map(
        local,
        mesh=mesh,
        in_specs=placed,
        out_specs=(
            P("section", None, ("expert", "shard"), None, None),
            P("section", None, ("expert", "shard"), None, None),
            P("section", None, ("expert", "shard"), None, None),
            P("section", ("expert", "shard"), None),
            P("section", ("expert", "shard"), None),
            P("section", ("expert", "shard"), None),
            P("section", ("expert", "shard"), None),
            P("section", ("expert", "shard"), None),
            P("section", ("expert", "shard"), None),
            P("section", None, None),
            P("section", "expert", "shard", None),
            P("section", "expert", "shard", None),
        ),
        check_vma=False,
    )
```
